32 devices in a mesh: pipe: 2 (over x), dp: 16 (over z, y, core).
Axes of the slice: x: 2, y: 2, z: 4, core: 2. Of those that a mesh axis runs over, the one named last changes fastest.
Arguments:
- section_input: bfloat16 [2, 64, 512, 512], P('pipe', 'dp'), may hold values from -6 to 6
- attention_in: float32 [2, 512, 1536], P('pipe', 'dp'), may hold values from -0.25 to 0.25
- attention_out: float32 [2, 512, 512], P('pipe', 'dp'), may hold values from -1 to 1
- cross_weights: float32 [2, 512, 1024], P('pipe', 'dp')
- expand: float32 [2, 512, 2048], P('pipe', 'dp'), may hold values from -0.25 to 0.25
- contract: float32 [2, 2048, 512], P('pipe', 'dp'), may hold values from -0.125 to 0.125
- norm_gains: float32 [2, 3, 512], P('pipe', None, 'dp'), may hold values from 0.5 to 1.5
- source_lengths: int32 [64, 4], P('dp'), may hold values from 1 to 256, 512 in all within a row
- target_lengths: int32 [64, 4], P('dp'), may hold values from 1 to 256, 512 in all within a row
- cotangent: bfloat16 [64, 512, 512], P('dp'), may hold values from -6 to 6
Outputs:
- section_output: float32 [2, 64, 512, 512], P('pipe', 'dp')
- input_gradient: float32 [2, 64, 512, 512], P('pipe', 'dp')
- attention_in_gradient: float32 [2, 512, 1536], P('pipe', 'dp')
- attention_out_gradient: float32 [2, 512, 512], P('pipe', 'dp')
- cross_gradient: float32 [2, 512, 1024], P('pipe', 'dp')
- expand_gradient: float32 [2, 512, 2048], P('pipe', 'dp')
- contract_gradient: float32 [2, 2048, 512], P('pipe', 'dp')
- gains_gradient: float32 [2, 3, 512], P('pipe', None, 'dp')
The draws below stay inside these ranges and needn't reach their ends.
All inputs are finite; a program needn't handle non-finite values.
Results may differ from the reference program's by a relative error of at most 0.018.
Values may be sent and summed in bfloat16 or wider, within the bound.
A program may use at most 256 MiB of HBM per device.

```python
import math
import jax
import jax.numpy as jnp
import numpy as np
from jax import lax

D = 512
HEADS = 8
HD = 64
FF = 2048
ROW = 512
PACK = 4
ROWS = 64


def draw_cross_weights(key, part):
    key = jax.random.fold_in(key, 7)
    columns = jnp.arange(2 * D)
    scale = jnp.where(columns < D, 1.0, 2.0) * D ** (-0.5)
    base = jax.random.normal(key, (2, D, 2 * D), jnp.float32)
    return (base * scale[None, None, :]).astype(jnp.float32)


def levels(own_key, shape, shards, least, high):
    def one(position, blocks):
        steps = jax.random.uniform(jax.random.fold_in(jax.random.fold_in(own_key, 6), position), (blocks,), jnp.float32, least / len(shards), high / len(shards))
        return jnp.repeat(jnp.exp(steps), shape[position] // blocks).reshape((-1,) + (1,) * (len(shape) - position - 1))

    level = one(*shards[0])
    for cut in shards[1:]:
        level = level * one(*cut)
    return level


def length_profile(count, total, limit, skew):
    loads = [(1 << 20) // math.isqrt(rank ** skew) + 1 for rank in range(2, count + 1)]
    spare, given = total - limit - (count - 1), [1] * (count - 1)
    while spare > 0:
        free = [i for i in range(count - 1) if given[i] < limit]
        mass, budget = sum([loads[i] for i in free]), spare
        for i in free:
            addition = min(limit - given[i], max(1, budget * loads[i] // mass), spare)
            given[i] = given[i] + addition
            spare = spare - addition
    return np.array([limit] + given)


def ragged(own_key, number_of, total, limit, slope):
    if number_of == 2:
        one = jax.random.randint(own_key, (), max(1, total - limit), min(limit, total - 1) + 1)
        return jnp.stack([one, total - one])
    tallies = jnp.asarray(length_profile(number_of, total, limit, slope), jnp.int32)
    twos = (number_of - 1) // 2
    source_of, receiver = tallies[1:1 + 2 * twos:2], tallies[2:2 + 2 * twos:2]
    margin = jnp.minimum(source_of - 1, limit - receiver)
    moved = jax.random.randint(jax.random.fold_in(own_key, 1), (twos,), 0, 1 << 20) % (margin + 1)
    tallies = tallies.at[1:1 + 2 * twos:2].set(source_of - moved).at[2:2 + 2 * twos:2].set(receiver + moved)
    return tallies[jax.random.permutation(jax.random.fold_in(own_key, 2), number_of)]


def bell_draw(own_key, shape, scale, most, pieces=(), held_as=jnp.bfloat16):
    entries = jax.random.normal(own_key, shape, jnp.float32) * scale
    if len(pieces) > 0:
        entries = levels(own_key, shape, pieces, -0.22, 0.18) * entries
    return jnp.clip(entries, min=-most, max=most).astype(held_as)


def setup_inputs(seed: int = 0) -> dict:
    streams_of = jax.random.split(jax.random.key(seed), 11)
    section_input = bell_draw(streams_of[0], (2, ROWS, ROW, D), 1.0, 6.0, ((0, 2), (1, 16)))
    attention_in = bell_draw(streams_of[1], (2, D, 3 * D), D ** -0.5, 0.25, ((0, 2), (1, 16)), jnp.float32)
    attention_out = bell_draw(streams_of[2], (2, D, D), (D // 16) ** -0.5, 1.0, ((0, 2), (1, 16)), jnp.float32)
    cross_weights = draw_cross_weights(jax.random.fold_in(streams_of[10], 71), 0)
    expand = bell_draw(streams_of[4], (2, D, FF), D ** -0.5, 0.25, ((0, 2), (1, 16)), jnp.float32)
    contract = bell_draw(streams_of[5], (2, FF, D), FF ** -0.5, 0.125, ((0, 2), (1, 16)), jnp.float32)
    norm_gains = jnp.clip(1.0 + 0.1 * jax.random.normal(streams_of[6], (2, 3, D), jnp.float32), 0.5, 1.5)
    source_lengths = jax.vmap(lambda own: ragged(own, PACK, ROW, ROW // 2, 1))(jax.random.split(streams_of[7], ROWS)).reshape((ROWS, PACK)).astype(jnp.int32)
    target_lengths = jax.vmap(lambda own: ragged(own, PACK, ROW, ROW // 2, 1))(jax.random.split(streams_of[8], ROWS)).reshape((ROWS, PACK)).astype(jnp.int32)
    cotangent = bell_draw(streams_of[9], (ROWS, ROW, D), 1.0, 6.0, ((0, 16),))
    return dict(section_input=section_input, attention_in=attention_in, attention_out=attention_out, cross_weights=cross_weights, expand=expand, contract=contract, norm_gains=norm_gains, source_lengths=source_lengths, target_lengths=target_lengths, cotangent=cotangent)


EPSILON = 1e-05
MASKED = -1e+30

@jax.custom_vjp
def low(v):
    return lax.optimization_barrier(v.astype(jnp.bfloat16)).astype(jnp.float32)

@jax.custom_vjp
def low_back(v):
    return v

def low_keep(v):
    return (low(v), None)

def low_pass(kept, grad):
    return (grad,)

def back_keep(v):
    return (v, None)

def back_low(kept, grad):
    return (low(grad),)
low.defvjp(low_keep, low_pass)
low_back.defvjp(back_keep, back_low)

def matmul(left, right):
    return jnp.dot(left, right, precision=lax.Precision.HIGHEST, preferred_element_type=jnp.float32)

def layer_norm(stream, gain):
    centre = lax.optimization_barrier(jnp.mean(stream, axis=-1, keepdims=True))
    centred = stream - centre
    spread = lax.optimization_barrier(jnp.mean(centred * centred, axis=-1, keepdims=True))
    return centred * lax.rsqrt(spread + EPSILON) * gain

def segment_ids(lengths):
    ends = jnp.cumsum(lengths)
    places = jnp.arange(ROW, dtype=jnp.int32)
    return lax.optimization_barrier(jnp.sum((places[:, None] >= ends[None, :]).astype(jnp.int32), axis=1))

def make_masks(source_count, target_count):
    source_seg = segment_ids(source_count)
    target_seg = segment_ids(target_count)
    places = jnp.arange(ROW, dtype=jnp.int32)
    encoder_mask = source_seg[:, None] == source_seg[None, :]
    decoder_mask = (target_seg[:, None] == target_seg[None, :]) & (places[None, :] <= places[:, None])
    cross_mask = target_seg[:, None] == source_seg[None, :]
    return (encoder_mask, decoder_mask, cross_mask)

def attention(query, keys, values, mask):
    count = query.shape[0]
    heads_query = query.reshape(count, HEADS, HD)
    heads_keys = keys.reshape(keys.shape[0], HEADS, HD)
    heads_values = values.reshape(values.shape[0], HEADS, HD)
    raw = jnp.einsum('qhd,khd->hqk', heads_query, heads_keys, precision=lax.Precision.HIGHEST) * HD ** (-0.5)
    scores = jnp.where(mask[None], low_back(raw), MASKED)
    top = lax.optimization_barrier(jnp.max(scores, axis=-1, keepdims=True))
    weights = jnp.exp(scores - top)
    shares = weights / lax.optimization_barrier(jnp.sum(weights, axis=-1, keepdims=True))
    result = jnp.einsum('hqk,khd->qhd', low(shares), heads_values, precision=lax.Precision.HIGHEST)
    return result.reshape(count, D)

def self_block(stream, gain, project_in, project_out, mask):
    normed = low(layer_norm(stream, gain))
    triple = low_back(low(matmul(normed, project_in)))
    result = low_back(low(attention(triple[:, :D], triple[:, D:2 * D], triple[:, 2 * D:], mask)))
    return stream + low_back(matmul(result, project_out))

def feed_block(stream, gain, expand, contract):
    normed = low(layer_norm(stream, gain))
    hidden = low_back(matmul(normed, expand))
    active = low(jax.nn.gelu(hidden, approximate=False))
    return stream + low_back(matmul(active, contract))

def encoder_row(stream, mask, weights):
    project_in, project_out, cross_pair, expand, contract, gains = weights
    first = self_block(stream, gains[0], project_in, project_out, mask)
    second = feed_block(first, gains[1], expand, contract)
    memory = layer_norm(second, gains[2])
    memory_pair = low_back(low(matmul(low(memory), cross_pair)))
    return (memory, memory_pair)

def decoder_row(stream, memory_pair, self_mask, cross_mask, weights):
    project_in, project_out, cross_pair, expand, contract, gains = weights
    first = self_block(stream, gains[0], project_in, project_out, self_mask)
    normed = low(layer_norm(first, gains[1]))
    question = low_back(low(matmul(normed, cross_pair[:, :D])))
    result = low_back(low(attention(question, memory_pair[:, :D], memory_pair[:, D:], cross_mask)))
    second = first + low_back(matmul(result, cross_pair[:, D:]))
    return feed_block(second, gains[2], expand, contract)

def one_row(masters, row):
    source, target, source_count, target_count = row
    encoder_mask, decoder_mask, cross_mask = make_masks(source_count, target_count)
    encoder_weights = tuple((weight[0] for weight in masters))
    decoder_weights = tuple((weight[1] for weight in masters))
    memory, memory_pair = encoder_row(source, encoder_mask, encoder_weights)
    output = decoder_row(target, memory_pair, decoder_mask, cross_mask, decoder_weights)
    return (memory, output)

def reference(section_input, attention_in, attention_out, cross_weights, expand, contract, norm_gains, source_lengths, target_lengths, cotangent):
    inputs = section_input.astype(jnp.float32)

    def forward(streams, masters):
        rounded = tuple((low(weight) for weight in masters))
        checked = jax.checkpoint(one_row)
        return lax.map(lambda row: checked(rounded, row), (streams[0], streams[1], source_lengths, target_lengths))
    masters = (attention_in, attention_out, cross_weights, expand, contract, norm_gains)
    (memory, output), pull = jax.vjp(forward, inputs, masters)
    input_gradient, weight_grads = pull((jnp.zeros_like(memory), cotangent.astype(jnp.float32)))
    section_output = jnp.stack([memory, output])
    return (section_output, input_gradient, weight_grads[0], weight_grads[1], weight_grads[2], weight_grads[3], weight_grads[4], weight_grads[5])
```

```python
from functools import partial
import math

import jax
import jax.numpy as jnp
from jax import lax
from jax.experimental import pallas as pl
from jax.experimental.pallas import tpu as pltpu
from jax.sharding import PartitionSpec as P

D = 512
HEADS = 8
HD = 64
FF = 2048
ROW = 512
PAIRS = HEADS // 2
PACK = 4

QKV, OUT, CROSS, EXPAND, BLOCKS = 0, 3, 4, 6, 10
SLABS = FF // D

EPSILON = 1e-05
MASKED = -1e30
LOG2E = math.log2(math.e)
EXPONENT = HD**-0.5 * LOG2E
BELL = 1.0 / math.sqrt(2.0 * math.pi)
LOW = jnp.bfloat16
FULL = jnp.float32
VMEM_LIMIT = 62 * 2**20

NN = (((1,), (0,)), ((), ()))
NT = (((1,), (1,)), ((), ()))
TN = (((0,), (0,)), ((), ()))


def multiply(left, right, dims=NN):
    return lax.dot_general(left, right, dims, preferred_element_type=jnp.float32)


def columns(index, width=D):
    return pl.ds(index * width, width)


def normalize(stream):
    centred = stream - jnp.mean(stream, axis=1, keepdims=True)
    scale = lax.rsqrt(jnp.mean(centred * centred, axis=1, keepdims=True) + EPSILON)
    return centred * scale, scale


def norm_back(unit, scale, gain, delta):
    inner = delta * gain
    mean = jnp.mean(inner, axis=1, keepdims=True)
    along = jnp.mean(inner * unit, axis=1, keepdims=True)
    return scale * (inner - mean - unit * along), jnp.sum(delta * unit, axis=0, keepdims=True)


def segment(counts, row, shape, axis):
    places = lax.broadcasted_iota(jnp.int32, shape, axis)
    end = counts[row, 0]
    found = (places >= end).astype(jnp.int32)
    for piece in range(1, PACK):
        end = end + counts[row, piece]
        found = found + (places >= end).astype(jnp.int32)
    return found


def fill_bias(bias, query_counts, key_counts, row, causal):
    keep = segment(query_counts, row, (ROW, 1), 0) == segment(key_counts, row, (1, ROW), 1)
    if causal:
        query = lax.broadcasted_iota(jnp.int32, (ROW, ROW), 0)
        key = lax.broadcasted_iota(jnp.int32, (ROW, ROW), 1)
        keep = keep & (key <= query)
    bias[...] = jnp.where(keep, 0.0, MASKED)


def lanes():
    return lax.broadcasted_iota(jnp.int32, (1, 2 * HD), 1)


def only_half(value, half):
    return jnp.where(lanes() // HD == half, value, jnp.zeros_like(value))


def attend(query, keys, values, bias, shares, inverse, result):
    kept = jnp.zeros((ROW, 2 * HD), FULL)
    for pair in range(PAIRS):
        query2, keys2, values2 = query(pair), keys(pair), values(pair)
        parts = []
        for half in range(2):
            head = 2 * pair + half
            scores = multiply(only_half(query2, half), keys2, NT) + bias[...]
            top = jnp.max(scores, axis=1, keepdims=True)
            weights = jnp.exp2((scores - top) * EXPONENT)
            scale = 1.0 / jnp.sum(weights, axis=1, keepdims=True)
            low = weights.astype(LOW)
            shares[head] = low
            parts.append(multiply(low, values2) * scale)
            kept = jnp.where(lanes() == head, scale, kept)
        result[:, columns(pair, 2 * HD)] = jnp.where(lanes() < HD, parts[0], parts[1]).astype(LOW)
    inverse[...] = kept


def attend_back(query, keys, values, shares, inverse, result, delta, put):
    for pair in range(PAIRS):
        query2, keys2, values2 = query(pair), keys(pair), values(pair)
        place = slice(2 * HD * pair, 2 * HD * (pair + 1))
        scale = jnp.where(
            lanes() < HD, inverse[:, 2 * pair : 2 * pair + 1], inverse[:, 2 * pair + 1 : 2 * pair + 2]
        )
        low = (delta[:, place] * scale).astype(LOW)
        product = low.astype(FULL) * result[:, columns(pair, 2 * HD)].astype(FULL)
        query_turned, low_turned = query2.T, low.T
        delta_query = 0.0
        delta_keys, delta_values = [], []
        for half in range(2):
            weights = shares[2 * pair + half]
            along = jnp.sum(only_half(product, half), axis=1, keepdims=True)
            delta_shares = multiply(only_half(low, half), values2, NT)
            delta_scores = (weights.astype(FULL) * (delta_shares - along)).astype(LOW)
            delta_query = delta_query + multiply(delta_scores, only_half(keys2, half))
            own = slice(HD * half, HD * (half + 1))
            delta_keys.append(multiply(query_turned[own], delta_scores))
            delta_values.append(multiply(low_turned[own], weights))
        keys_turned = (jnp.concatenate(delta_keys, axis=0) * HD**-0.5).astype(LOW)
        values_turned = jnp.concatenate(delta_values, axis=0).astype(LOW)
        put(pair, (delta_query * HD**-0.5).astype(LOW), keys_turned.T, values_turned.T)


def self_parts(triple):
    return tuple(
        (lambda pair, start=part * PAIRS: triple[:, columns(start + pair, 2 * HD)]) for part in range(3)
    )


def put_triple(target):
    def put(pair, *parts):
        for part, value in enumerate(parts):
            target[:, columns(part * PAIRS + pair, 2 * HD)] = value

    return put


def feed(normed, stream, square, tall, active, slope):
    total = stream
    for slab in range(SLABS):
        hidden = multiply(normed, square[EXPAND + slab])
        under = 0.5 + 0.5 * lax.erf(hidden * math.sqrt(0.5))
        bell = BELL * jnp.exp2(hidden * hidden * (-0.5 * LOG2E))
        low = (hidden * under).astype(LOW)
        active[:, columns(slab)] = low
        slope[:, columns(slab)] = (under + hidden * bell).astype(LOW)
        total = total + multiply(low, tall[columns(slab), :])
    return total


def feed_back(delta, stream, gain, square, tall, active, slope, square_sum, tall_sum):
    unit, scale = normalize(stream)
    turned = (unit * gain).astype(LOW).T
    low = delta.astype(LOW)
    delta_normed = 0.0
    for slab in range(SLABS):
        delta_active = multiply(low, tall[columns(slab), :], NT)
        delta_hidden = (delta_active * slope[:, columns(slab)].astype(FULL)).astype(LOW)
        tall_sum[columns(slab), :] += multiply(active[:, columns(slab)], low, TN)
        square_sum[EXPAND + slab] += multiply(turned, delta_hidden)
        delta_normed = delta_normed + multiply(delta_hidden, square[EXPAND + slab], NT)
    delta_stream, delta_gain = norm_back(unit, scale, gain, delta_normed)
    return delta + delta_stream, delta_gain


def self_back(delta, stream, gain, square, triple, shares, inverse, result, delta_triple, square_sum):
    unit, scale = normalize(stream)
    low = delta.astype(LOW)
    square_sum[OUT] += multiply(result[...], low, TN)
    delta_result = multiply(low, square[OUT], NT)
    attend_back(*self_parts(triple), shares, inverse, result, delta_result, put_triple(delta_triple))
    turned = (unit * gain).astype(LOW).T
    delta_normed = 0.0
    for part in range(3):
        chunk = delta_triple[:, columns(part)]
        square_sum[QKV + part] += multiply(turned, chunk)
        delta_normed = delta_normed + multiply(chunk, square[QKV + part], NT)
    delta_stream, delta_gain = norm_back(unit, scale, gain, delta_normed)
    return delta + delta_stream, delta_gain


def project(normed, square, first, count, target):
    for part in range(count):
        target[:, columns(part)] = multiply(normed, square[first + part]).astype(LOW)


def send_sums(square_sum, tall_sum, staging, square_out, tall_out, ready):
    copies = []
    for block in range(BLOCKS + SLABS):
        if block < BLOCKS:
            value, target = square_sum[block], square_out.at[block]
        else:
            rows = columns(block - BLOCKS)
            value, target = tall_sum[rows, :], tall_out.at[rows, :]
        staging(block)[...] = value.astype(LOW)
        copy = pltpu.make_async_copy(staging(block), target, ready.at[block])
        copy.start()
        copies.append(copy)
    for copy in copies:
        copy.wait()


def encode_kernel(
    source_counts, rows, square, tall, gains,
    memory, memory_pair, triple, shares, inverse, result, first, active, slope, second,
    bias,
):
    row = pl.program_id(0)
    square, tall, gains = square.at[0], tall.at[0], gains.at[0]
    stream = rows[0].astype(FULL)
    fill_bias(bias, source_counts, source_counts, row, False)
    normed = (normalize(stream)[0] * gains[0:1, :]).astype(LOW)
    project(normed, square, QKV, 3, triple.at[0])
    attend(*self_parts(triple.at[0]), bias, shares.at[0], inverse.at[0], result.at[0])
    stream = stream + multiply(result[0], square[OUT])
    first[0] = stream
    normed = (normalize(stream)[0] * gains[1:2, :]).astype(LOW)
    stream = feed(normed, stream, square, tall, active.at[0], slope.at[0])
    second[0] = stream
    value = normalize(stream)[0] * gains[2:3, :]
    memory[0] = value
    project(value.astype(LOW), square, CROSS, 2, memory_pair.at[0])


def decode_kernel(
    source_counts, target_counts, rows, memory_pair, cotangent, square, tall, gains,
    output, gradient, delta_pair, square_out, tall_out, gain_out,
    bias, triple, question, self_shares, cross_shares, self_inverse, cross_inverse,
    self_result, cross_result, first, second, active, slope, delta_triple,
    square_sum, tall_sum, gain_sum, ready,
):
    row = pl.program_id(0)
    square, tall, gains = square.at[0], tall.at[0], gains.at[0]
    memory_pair, delta_pair = memory_pair.at[0], delta_pair.at[0]

    @pl.when(row == 0)
    def _():
        square_sum[...] = jnp.zeros(square_sum.shape, FULL)
        tall_sum[...] = jnp.zeros(tall_sum.shape, FULL)
        gain_sum[...] = jnp.zeros(gain_sum.shape, FULL)

    stream = rows[0].astype(FULL)
    fill_bias(bias, target_counts, target_counts, row, True)
    normed = (normalize(stream)[0] * gains[0:1, :]).astype(LOW)
    project(normed, square, QKV, 3, triple)
    attend(*self_parts(triple), bias, self_shares, self_inverse, self_result)
    stream = stream + multiply(self_result[...], square[OUT])
    first[...] = stream

    fill_bias(bias, target_counts, source_counts, row, False)
    normed = (normalize(stream)[0] * gains[1:2, :]).astype(LOW)
    question[...] = multiply(normed, square[CROSS]).astype(LOW)
    cross = (
        lambda pair: question[:, columns(pair, 2 * HD)],
        lambda pair: memory_pair[:, columns(pair, 2 * HD)],
        lambda pair: memory_pair[:, columns(PAIRS + pair, 2 * HD)],
    )
    attend(*cross, bias, cross_shares, cross_inverse, cross_result)
    stream = stream + multiply(cross_result[...], square[CROSS + 1])
    second[...] = stream

    normed = (normalize(stream)[0] * gains[2:3, :]).astype(LOW)
    output[0] = feed(normed, stream, square, tall, active, slope)

    delta, delta_gain = feed_back(
        cotangent[0].astype(FULL), second[...], gains[2:3, :], square, tall, active, slope, square_sum, tall_sum
    )
    gain_sum[2:3, :] += delta_gain

    unit, scale = normalize(first[...])
    low = delta.astype(LOW)
    square_sum[CROSS + 1] += multiply(cross_result[...], low, TN)
    delta_result = multiply(low, square[CROSS + 1], NT)

    def put(pair, query, keys, values):
        delta_triple[:, columns(pair, 2 * HD)] = query
        delta_pair[:, columns(pair, 2 * HD)] = keys
        delta_pair[:, columns(PAIRS + pair, 2 * HD)] = values

    attend_back(*cross, cross_shares, cross_inverse, cross_result, delta_result, put)
    delta_question = delta_triple[:, columns(0)]
    square_sum[CROSS] += multiply((unit * gains[1:2, :]).astype(LOW), delta_question, TN)
    delta_normed = multiply(delta_question, square[CROSS], NT)
    delta_stream, delta_gain = norm_back(unit, scale, gains[1:2, :], delta_normed)
    gain_sum[1:2, :] += delta_gain
    delta = delta + delta_stream

    delta, delta_gain = self_back(
        delta, rows[0].astype(FULL), gains[0:1, :], square, triple, self_shares, self_inverse, self_result,
        delta_triple, square_sum,
    )
    gain_sum[0:1, :] += delta_gain
    gradient[0] = delta

    @pl.when(row == pl.num_programs(0) - 1)
    def _():
        gain_out[...] = gain_sum[...]

        def staging(block):
            return self_shares.at[block] if block < HEADS else cross_shares.at[block - HEADS]

        send_sums(square_sum, tall_sum, staging, square_out, tall_out, ready)


def encode_back_kernel(
    rows, shares_in, triple, inverse, result, first, active, slope, second, delta_pair, square, tall, gains,
    gradient, square_out, tall_out, gain_out,
    shares, spare, delta_triple, square_sum, tall_sum, gain_sum, arrived, ready,
):
    row = pl.program_id(0)
    square, tall, gains = square.at[0], tall.at[0], gains.at[0]
    delta_pair = delta_pair.at[0]
    fetch = pltpu.make_async_copy(shares_in.at[row], shares, arrived)
    fetch.start()

    @pl.when(row == 0)
    def _():
        square_sum[...] = jnp.zeros(square_sum.shape, FULL)
        tall_sum[...] = jnp.zeros(tall_sum.shape, FULL)
        gain_sum[...] = jnp.zeros(gain_sum.shape, FULL)

    unit, scale = normalize(second[0])
    turned = (unit * gains[2:3, :]).astype(LOW).T
    delta_memory = 0.0
    for part in range(2):
        chunk = delta_pair[:, columns(part)]
        square_sum[CROSS + part] += multiply(turned, chunk)
        delta_memory = delta_memory + multiply(chunk, square[CROSS + part], NT)
    delta, delta_gain = norm_back(unit, scale, gains[2:3, :], delta_memory)
    gain_sum[2:3, :] += delta_gain

    delta, delta_gain = feed_back(
        delta, first[0], gains[1:2, :], square, tall, active.at[0], slope.at[0], square_sum, tall_sum
    )
    gain_sum[1:2, :] += delta_gain
    fetch.wait()
    delta, delta_gain = self_back(
        delta, rows[0].astype(FULL), gains[0:1, :], square, triple.at[0], shares, inverse.at[0], result.at[0],
        delta_triple, square_sum,
    )
    gain_sum[0:1, :] += delta_gain
    gradient[0] = delta

    @pl.when(row == pl.num_programs(0) - 1)
    def _():
        gain_out[...] = gain_sum[...]

        def staging(block):
            return shares.at[block] if block < HEADS else spare.at[block - HEADS]

        send_sums(square_sum, tall_sum, staging, square_out, tall_out, ready)


def per_row(*shape):
    return pl.BlockSpec((1,) + shape, lambda row: (row,) + (0,) * len(shape))


def of_layer(layer, *shape):
    return pl.BlockSpec(
        (1,) + shape, lambda row: (layer,) + (0,) * len(shape), pipeline_mode=pl.Buffered(1)
    )


def weight_specs(layer):
    return [of_layer(layer, BLOCKS, D, D), of_layer(layer, FF, D), of_layer(layer, 3, D)]


ANYWHERE = pl.BlockSpec(memory_space=pl.ANY)
SCALARS = pl.BlockSpec(memory_space=pltpu.SMEM)
PARAMS = pltpu.CompilerParams(vmem_limit_bytes=VMEM_LIMIT)


def shape_of(shape, kind):
    return jax.ShapeDtypeStruct(shape, kind)


def sums_scratch():
    return [pltpu.VMEM((BLOCKS, D, D), FULL), pltpu.VMEM((FF, D), FULL), pltpu.VMEM((8, D), FULL)]


def sums_shapes():
    return [shape_of((BLOCKS, D, D), LOW), shape_of((FF, D), LOW), shape_of((8, D), FULL)]


def sums_specs():
    return [ANYWHERE, ANYWHERE, pl.BlockSpec((8, D), lambda row: (0, 0))]


def encode(source_counts, rows, weights):
    count = rows.shape[0]
    kept = [
        ((ROW, D), FULL),
        ((ROW, 2 * D), LOW),
        ((ROW, 3 * D), LOW),
        ((HEADS, ROW, ROW), LOW),
        ((ROW, 2 * HD), FULL),
        ((ROW, D), LOW),
        ((ROW, D), FULL),
        ((ROW, FF), LOW),
        ((ROW, FF), LOW),
        ((ROW, D), FULL),
    ]
    return pl.pallas_call(
        encode_kernel,
        grid=(count,),
        in_specs=[SCALARS, per_row(ROW, D)] + weight_specs(0),
        out_specs=[per_row(*shape) for shape, _ in kept],
        out_shape=[shape_of((count,) + shape, kind) for shape, kind in kept],
        scratch_shapes=[pltpu.VMEM((ROW, ROW), FULL)],
        compiler_params=PARAMS,
        name="encode",
    )(source_counts, rows, *weights)


def decode(source_counts, target_counts, rows, memory_pair, cotangent, weights):
    count = rows.shape[0]
    shares = pltpu.VMEM((HEADS, ROW, ROW), LOW)
    inverse = pltpu.VMEM((ROW, 2 * HD), FULL)
    low = pltpu.VMEM((ROW, D), LOW)
    full = pltpu.VMEM((ROW, D), FULL)
    wide = pltpu.VMEM((ROW, FF), LOW)
    triple = pltpu.VMEM((ROW, 3 * D), LOW)
    return pl.pallas_call(
        decode_kernel,
        grid=(count,),
        in_specs=[SCALARS, SCALARS, per_row(ROW, D), per_row(ROW, 2 * D), per_row(ROW, D)] + weight_specs(1),
        out_specs=[per_row(ROW, D), per_row(ROW, D), per_row(ROW, 2 * D)] + sums_specs(),
        out_shape=[
            shape_of((count, ROW, D), FULL),
            shape_of((count, ROW, D), FULL),
            shape_of((count, ROW, 2 * D), LOW),
        ]
        + sums_shapes(),
        scratch_shapes=[
            pltpu.VMEM((ROW, ROW), FULL), triple, low, shares, shares, inverse, inverse,
            low, low, full, full, wide, wide, triple,
        ]
        + sums_scratch()
        + [pltpu.SemaphoreType.DMA((BLOCKS + SLABS,))],
        compiler_params=PARAMS,
        name="decode",
    )(source_counts, target_counts, rows, memory_pair, cotangent, *weights)


def encode_back(rows, kept, delta_pair, weights):
    count = rows.shape[0]
    triple, shares, inverse, result, first, active, slope, second = kept
    return pl.pallas_call(
        encode_back_kernel,
        grid=(count,),
        in_specs=[
            per_row(ROW, D), ANYWHERE, per_row(ROW, 3 * D), per_row(ROW, 2 * HD), per_row(ROW, D),
            per_row(ROW, D), per_row(ROW, FF), per_row(ROW, FF), per_row(ROW, D), per_row(ROW, 2 * D),
        ]
        + weight_specs(0),
        out_specs=[per_row(ROW, D)] + sums_specs(),
        out_shape=[shape_of((count, ROW, D), FULL)] + sums_shapes(),
        scratch_shapes=[
            pltpu.VMEM((HEADS, ROW, ROW), LOW),
            pltpu.VMEM((BLOCKS + SLABS - HEADS, D, D), LOW),
            pltpu.VMEM((ROW, 3 * D), LOW),
        ]
        + sums_scratch()
        + [pltpu.SemaphoreType.DMA, pltpu.SemaphoreType.DMA((BLOCKS + SLABS,))],
        compiler_params=PARAMS,
        name="encode_back",
    )(rows, shares, triple, inverse, result, first, active, slope, second, delta_pair, *weights)


def gather_weights(square, tall, gains, shards):
    axes = ("pipe", "dp")
    every_square = lax.all_gather(square, axes, axis=0, tiled=False)
    every_tall = lax.all_gather(tall, axes, axis=0, tiled=False)
    every_gain = lax.all_gather(gains.astype(LOW), axes, axis=0, tiled=False)
    every_square = every_square.reshape(2, shards, BLOCKS, D // shards, D)
    every_gain = every_gain.reshape(2, shards, 3, D // shards)
    return (
        jnp.swapaxes(every_square, 1, 2).reshape(2, BLOCKS, D, D),
        every_tall.reshape(2, FF, D),
        jnp.swapaxes(every_gain, 1, 2).reshape(2, 3, D).astype(FULL),
    )


def scatter_sums(square, tall, gains, shards):
    axes = ("pipe", "dp")
    square = jnp.swapaxes(square.reshape(2, BLOCKS, shards, D // shards, D), 1, 2)
    gains = jnp.swapaxes(gains.reshape(2, 3, shards, D // shards), 1, 2)
    square = square.reshape(2 * shards, BLOCKS, D // shards, D)
    tall = tall.reshape(2 * shards, FF // shards, D)
    gains = gains.reshape(2 * shards, 3, D // shards)
    return tuple(
        lax.psum_scatter(value, axes, scatter_dimension=0, tiled=False).astype(FULL)
        for value in (square, tall, gains)
    )


def swap(value):
    return lax.ppermute(value, "pipe", [(0, 1), (1, 0)])


def blocks_of(value):
    return [value[:, start : start + D] for start in range(0, value.shape[1], D)]


def local(
    section_input,
    attention_in,
    attention_out,
    cross_weights,
    expand,
    contract,
    norm_gains,
    source_lengths,
    target_lengths,
    cotangent,
):
    section = lax.axis_index("pipe")
    shards = lax.axis_size("dp")
    rows = section_input[0]
    count = rows.shape[0] // 2
    start = section * count

    def part(value, first):
        return lax.dynamic_slice_in_dim(value, first, count, axis=0)

    mine = part(rows, start)
    other = swap(part(rows, count - start))
    source_rows = jnp.where(section == 0, mine, other)
    target_rows = jnp.where(section == 0, other, mine)
    source_counts = part(source_lengths, start)
    target_counts = part(target_lengths, start)

    square = jnp.stack(
        blocks_of(attention_in[0]) + [attention_out[0]] + blocks_of(cross_weights[0]) + blocks_of(expand[0])
    ).astype(LOW)
    weights = gather_weights(square, contract[0].astype(LOW), norm_gains[0], shards)

    memory, memory_pair, *kept = encode(source_counts, source_rows, weights)
    output, target_gradient, delta_pair, *decoder_sums = decode(
        source_counts, target_counts, target_rows, memory_pair, part(cotangent, start), weights
    )
    source_gradient, *encoder_sums = encode_back(source_rows, kept, delta_pair, weights)

    def settle(source, target):
        own = jnp.where(section == 0, source, target)
        away = swap(jnp.where(section == 0, target, source).astype(LOW)).astype(FULL)
        whole = jnp.zeros((2 * count, ROW, D), FULL)
        whole = lax.dynamic_update_slice_in_dim(whole, own, start, axis=0)
        return lax.dynamic_update_slice_in_dim(whole, away, count - start, axis=0)[None]

    section_output = settle(memory, output)
    input_gradient = settle(source_gradient, target_gradient)

    square, tall, gains = (jnp.stack(pair) for pair in zip(encoder_sums, decoder_sums))
    square, tall, gains = scatter_sums(square, tall, gains[:, :3], shards)

    def joined(first, last):
        return jnp.concatenate([square[block] for block in range(first, last)], axis=1)[None]

    return (
        section_output,
        input_gradient,
        joined(QKV, OUT),
        joined(OUT, CROSS),
        joined(CROSS, EXPAND),
        joined(EXPAND, BLOCKS),
        tall[None],
        gains[None],
    )


def solution(mesh):
    in_specs = (
        P("pipe", "dp", None, None),
        P("pipe", "dp", None),
        P("pipe", "dp", None),
        P("pipe", "dp", None),
        P("pipe", "dp", None),
        P("pipe", "dp", None),
        P("pipe", None, "dp"),
        P("dp", None),
        P("dp", None),
        P("dp", None, None),
    )
    out_specs = (
        P("pipe", "dp", None, None),
        P("pipe", "dp", None, None),
        P("pipe", "dp", None),
        P("pipe", "dp", None),
        P("pipe", "dp", None),
        P("pipe", "dp", None),
        P("pipe", "dp", None),
        P("pipe", None, "dp"),
    )
    return jax.shard_map(local, mesh=mesh, in_specs=in_specs, out_specs=out_specs, check_vma=False)
```

```python
from functools import partial
import math

import jax
import jax.numpy as jnp
from jax import lax
from jax.experimental import pallas as pl
from jax.experimental.pallas import tpu as pltpu
from jax.sharding import PartitionSpec as P

D = 512
HEADS = 8
HD = 64
FF = 2048
ROW = 512
PAIRS = HEADS // 2
PACK = 4

QKV, OUT, CROSS, EXPAND, BLOCKS = 0, 3, 4, 6, 10
SLABS = FF // D

EPSILON = 1e-05
MASKED = -1e30
LOG2E = math.log2(math.e)
EXPONENT = HD**-0.5 * LOG2E
BELL = 1.0 / math.sqrt(2.0 * math.pi)
LOW = jnp.bfloat16
FULL = jnp.float32
VMEM_LIMIT = 62 * 2**20

NN = (((1,), (0,)), ((), ()))
NT = (((1,), (1,)), ((), ()))
TN = (((0,), (0,)), ((), ()))


def multiply(left, right, dims=NN):
    return lax.dot_general(left, right, dims, preferred_element_type=jnp.float32)


def columns(index, width=D):
    return pl.ds(index * width, width)


def normalize(stream):
    centred = stream - jnp.mean(stream, axis=1, keepdims=True)
    scale = lax.rsqrt(jnp.mean(centred * centred, axis=1, keepdims=True) + EPSILON)
    return centred * scale, scale


def norm_back(unit, scale, gain, delta):
    inner = delta * gain
    mean = jnp.mean(inner, axis=1, keepdims=True)
    along = jnp.mean(inner * unit, axis=1, keepdims=True)
    return scale * (inner - mean - unit * along), jnp.sum(delta * unit, axis=0, keepdims=True)


def segment(counts, row, shape, axis):
    places = lax.broadcasted_iota(jnp.int32, shape, axis)
    end = counts[row, 0]
    found = (places >= end).astype(jnp.int32)
    for piece in range(1, PACK):
        end = end + counts[row, piece]
        found = found + (places >= end).astype(jnp.int32)
    return found


def fill_bias(bias, query_counts, key_counts, row, causal):
    keep = segment(query_counts, row, (ROW, 1), 0) == segment(key_counts, row, (1, ROW), 1)
    if causal:
        query = lax.broadcasted_iota(jnp.int32, (ROW, ROW), 0)
        key = lax.broadcasted_iota(jnp.int32, (ROW, ROW), 1)
        keep = keep & (key <= query)
    bias[...] = jnp.where(keep, 0.0, MASKED)


def lanes():
    return lax.broadcasted_iota(jnp.int32, (1, 2 * HD), 1)


def only_half(value, half):
    return jnp.where(lanes() // HD == half, value, jnp.zeros_like(value))


def attend(query, keys, values, bias, shares, inverse, result):
    kept = jnp.zeros((ROW, 2 * HD), FULL)
    for pair in range(PAIRS):
        query2, keys2, values2 = query(pair), keys(pair), values(pair)
        parts = []
        for half in range(2):
            head = 2 * pair + half
            scores = multiply(only_half(query2, half), keys2, NT) + bias[...]
            top = jnp.max(scores, axis=1, keepdims=True)
            weights = jnp.exp2((scores - top) * EXPONENT)
            scale = 1.0 / jnp.sum(weights, axis=1, keepdims=True)
            low = weights.astype(LOW)
            shares[head] = low
            parts.append(multiply(low, values2) * scale)
            kept = jnp.where(lanes() == head, scale, kept)
        result[:, columns(pair, 2 * HD)] = jnp.where(lanes() < HD, parts[0], parts[1]).astype(LOW)
    inverse[...] = kept


def attend_back(query, keys, values, shares, inverse, result, delta, put):
    for pair in range(PAIRS):
        query2, keys2, values2 = query(pair), keys(pair), values(pair)
        place = slice(2 * HD * pair, 2 * HD * (pair + 1))
        scale = jnp.where(
            lanes() < HD, inverse[:, 2 * pair : 2 * pair + 1], inverse[:, 2 * pair + 1 : 2 * pair + 2]
        )
        low = (delta[:, place] * scale).astype(LOW)
        product = low.astype(FULL) * result[:, columns(pair, 2 * HD)].astype(FULL)
        query_turned, low_turned = query2.T, low.T
        delta_query = 0.0
        delta_keys, delta_values = [], []
        for half in range(2):
            weights = shares[2 * pair + half]
            along = jnp.sum(only_half(product, half), axis=1, keepdims=True)
            delta_shares = multiply(only_half(low, half), values2, NT)
            delta_scores = (weights.astype(FULL) * (delta_shares - along)).astype(LOW)
            delta_query = delta_query + multiply(delta_scores, only_half(keys2, half))
            own = slice(HD * half, HD * (half + 1))
            delta_keys.append(multiply(query_turned[own], delta_scores))
            delta_values.append(multiply(low_turned[own], weights))
        keys_turned = (jnp.concatenate(delta_keys, axis=0) * HD**-0.5).astype(LOW)
        values_turned = jnp.concatenate(delta_values, axis=0).astype(LOW)
        put(pair, (delta_query * HD**-0.5).astype(LOW), keys_turned.T, values_turned.T)


def self_parts(triple):
    return tuple(
        (lambda pair, start=part * PAIRS: triple[:, columns(start + pair, 2 * HD)]) for part in range(3)
    )


def put_triple(target):
    def put(pair, *parts):
        for part, value in enumerate(parts):
            target[:, columns(part * PAIRS + pair, 2 * HD)] = value

    return put


def feed(normed, stream, square, tall, active, slope):
    total = stream
    for slab in range(SLABS):
        hidden = multiply(normed, square[EXPAND + slab])
        under = 0.5 + 0.5 * lax.erf(hidden * math.sqrt(0.5))
        bell = BELL * jnp.exp2(hidden * hidden * (-0.5 * LOG2E))
        low = (hidden * under).astype(LOW)
        active[:, columns(slab)] = low
        slope[:, columns(slab)] = (under + hidden * bell).astype(LOW)
        total = total + multiply(low, tall[columns(slab), :])
    return total


def feed_back(delta, stream, gain, square, tall, active, slope, square_sum, tall_sum):
    unit, scale = normalize(stream)
    turned = (unit * gain).astype(LOW).T
    low = delta.astype(LOW)
    delta_normed = 0.0
    for slab in range(SLABS):
        delta_active = multiply(low, tall[columns(slab), :], NT)
        delta_hidden = (delta_active * slope[:, columns(slab)].astype(FULL)).astype(LOW)
        tall_sum[columns(slab), :] += multiply(active[:, columns(slab)], low, TN)
        square_sum[EXPAND + slab] += multiply(turned, delta_hidden)
        delta_normed = delta_normed + multiply(delta_hidden, square[EXPAND + slab], NT)
    delta_stream, delta_gain = norm_back(unit, scale, gain, delta_normed)
    return delta + delta_stream, delta_gain


def self_back(delta, stream, gain, square, triple, shares, inverse, result, delta_triple, square_sum):
    unit, scale = normalize(stream)
    low = delta.astype(LOW)
    square_sum[OUT] += multiply(result[...], low, TN)
    delta_result = multiply(low, square[OUT], NT)
    attend_back(*self_parts(triple), shares, inverse, result, delta_result, put_triple(delta_triple))
    turned = (unit * gain).astype(LOW).T
    delta_normed = 0.0
    for part in range(3):
        chunk = delta_triple[:, columns(part)]
        square_sum[QKV + part] += multiply(turned, chunk)
        delta_normed = delta_normed + multiply(chunk, square[QKV + part], NT)
    delta_stream, delta_gain = norm_back(unit, scale, gain, delta_normed)
    return delta + delta_stream, delta_gain


def project(normed, square, first, count, target):
    for part in range(count):
        target[:, columns(part)] = multiply(normed, square[first + part]).astype(LOW)


def send_sums(square_sum, tall_sum, staging, square_out, tall_out, ready):
    copies = []
    for block in range(BLOCKS + SLABS):
        if block < BLOCKS:
            value, target = square_sum[block], square_out.at[block]
        else:
            rows = columns(block - BLOCKS)
            value, target = tall_sum[rows, :], tall_out.at[rows, :]
        staging(block)[...] = value.astype(LOW)
        copy = pltpu.make_async_copy(staging(block), target, ready.at[block])
        copy.start()
        copies.append(copy)
    for copy in copies:
        copy.wait()


def encode_kernel(
    source_counts, rows, square, tall, gains,
    memory, memory_pair, triple, shares, inverse, result, first, active, slope, second,
    bias,
):
    row = pl.program_id(0)
    square, tall, gains = square.at[0], tall.at[0], gains.at[0]
    stream = rows[0].astype(FULL)
    fill_bias(bias, source_counts, source_counts, row, False)
    normed = (normalize(stream)[0] * gains[0:1, :]).astype(LOW)
    project(normed, square, QKV, 3, triple.at[0])
    attend(*self_parts(triple.at[0]), bias, shares.at[0], inverse.at[0], result.at[0])
    stream = stream + multiply(result[0], square[OUT])
    first[0] = stream
    normed = (normalize(stream)[0] * gains[1:2, :]).astype(LOW)
    stream = feed(normed, stream, square, tall, active.at[0], slope.at[0])
    second[0] = stream
    value = normalize(stream)[0] * gains[2:3, :]
    memory[0] = value
    project(value.astype(LOW), square, CROSS, 2, memory_pair.at[0])


def decode_kernel(
    source_counts, target_counts, rows, memory_pair, cotangent, square, tall, gains,
    output, gradient, delta_pair, square_out, tall_out, gain_out,
    bias, triple, question, self_shares, cross_shares, self_inverse, cross_inverse,
    self_result, cross_result, first, second, active, slope, delta_triple,
    square_sum, tall_sum, gain_sum, ready,
):
    row = pl.program_id(0)
    square, tall, gains = square.at[0], tall.at[0], gains.at[0]
    memory_pair, delta_pair = memory_pair.at[0], delta_pair.at[0]

    @pl.when(row == 0)
    def _():
        square_sum[...] = jnp.zeros(square_sum.shape, FULL)
        tall_sum[...] = jnp.zeros(tall_sum.shape, FULL)
        gain_sum[...] = jnp.zeros(gain_sum.shape, FULL)

    stream = rows[0].astype(FULL)
    fill_bias(bias, target_counts, target_counts, row, True)
    normed = (normalize(stream)[0] * gains[0:1, :]).astype(LOW)
    project(normed, square, QKV, 3, triple)
    attend(*self_parts(triple), bias, self_shares, self_inverse, self_result)
    stream = stream + multiply(self_result[...], square[OUT])
    first[...] = stream

    fill_bias(bias, target_counts, source_counts, row, False)
    normed = (normalize(stream)[0] * gains[1:2, :]).astype(LOW)
    question[...] = multiply(normed, square[CROSS]).astype(LOW)
    cross = (
        lambda pair: question[:, columns(pair, 2 * HD)],
        lambda pair: memory_pair[:, columns(pair, 2 * HD)],
        lambda pair: memory_pair[:, columns(PAIRS + pair, 2 * HD)],
    )
    attend(*cross, bias, cross_shares, cross_inverse, cross_result)
    stream = stream + multiply(cross_result[...], square[CROSS + 1])
    second[...] = stream

    normed = (normalize(stream)[0] * gains[2:3, :]).astype(LOW)
    output[0] = feed(normed, stream, square, tall, active, slope)

    delta, delta_gain = feed_back(
        cotangent[0].astype(FULL), second[...], gains[2:3, :], square, tall, active, slope, square_sum, tall_sum
    )
    gain_sum[2:3, :] += delta_gain

    unit, scale = normalize(first[...])
    low = delta.astype(LOW)
    square_sum[CROSS + 1] += multiply(cross_result[...], low, TN)
    delta_result = multiply(low, square[CROSS + 1], NT)

    def put(pair, query, keys, values):
        delta_triple[:, columns(pair, 2 * HD)] = query
        delta_pair[:, columns(pair, 2 * HD)] = keys
        delta_pair[:, columns(PAIRS + pair, 2 * HD)] = values

    attend_back(*cross, cross_shares, cross_inverse, cross_result, delta_result, put)
    delta_question = delta_triple[:, columns(0)]
    square_sum[CROSS] += multiply((unit * gains[1:2, :]).astype(LOW), delta_question, TN)
    delta_normed = multiply(delta_question, square[CROSS], NT)
    delta_stream, delta_gain = norm_back(unit, scale, gains[1:2, :], delta_normed)
    gain_sum[1:2, :] += delta_gain
    delta = delta + delta_stream

    delta, delta_gain = self_back(
        delta, rows[0].astype(FULL), gains[0:1, :], square, triple, self_shares, self_inverse, self_result,
        delta_triple, square_sum,
    )
    gain_sum[0:1, :] += delta_gain
    gradient[0] = delta

    @pl.when(row == pl.num_programs(0) - 1)
    def _():
        gain_out[...] = gain_sum[...]

        def staging(block):
            return self_shares.at[block] if block < HEADS else cross_shares.at[block - HEADS]

        send_sums(square_sum, tall_sum, staging, square_out, tall_out, ready)


def encode_back_kernel(
    rows, shares_in, triple, inverse, result, first, active, slope, second, delta_pair, square, tall, gains,
    gradient, square_out, tall_out, gain_out,
    shares, spare, delta_triple, square_sum, tall_sum, gain_sum, arrived, ready,
):
    row = pl.program_id(0)
    square, tall, gains = square.at[0], tall.at[0], gains.at[0]
    delta_pair = delta_pair.at[0]
    fetch = pltpu.make_async_copy(shares_in.at[row], shares, arrived)
    fetch.start()

    @pl.when(row == 0)
    def _():
        square_sum[...] = jnp.zeros(square_sum.shape, FULL)
        tall_sum[...] = jnp.zeros(tall_sum.shape, FULL)
        gain_sum[...] = jnp.zeros(gain_sum.shape, FULL)

    unit, scale = normalize(second[0])
    turned = (unit * gains[2:3, :]).astype(LOW).T
    delta_memory = 0.0
    for part in range(2):
        chunk = delta_pair[:, columns(part)]
        square_sum[CROSS + part] += multiply(turned, chunk)
        delta_memory = delta_memory + multiply(chunk, square[CROSS + part], NT)
    delta, delta_gain = norm_back(unit, scale, gains[2:3, :], delta_memory)
    gain_sum[2:3, :] += delta_gain

    delta, delta_gain = feed_back(
        delta, first[0], gains[1:2, :], square, tall, active.at[0], slope.at[0], square_sum, tall_sum
    )
    gain_sum[1:2, :] += delta_gain
    fetch.wait()
    delta, delta_gain = self_back(
        delta, rows[0].astype(FULL), gains[0:1, :], square, triple.at[0], shares, inverse.at[0], result.at[0],
        delta_triple, square_sum,
    )
    gain_sum[0:1, :] += delta_gain
    gradient[0] = delta

    @pl.when(row == pl.num_programs(0) - 1)
    def _():
        gain_out[...] = gain_sum[...]

        def staging(block):
            return shares.at[block] if block < HEADS else spare.at[block - HEADS]

        send_sums(square_sum, tall_sum, staging, square_out, tall_out, ready)


def per_row(*shape):
    return pl.BlockSpec((1,) + shape, lambda row: (row,) + (0,) * len(shape))


def of_layer(layer, *shape):
    return pl.BlockSpec(
        (1,) + shape, lambda row: (layer,) + (0,) * len(shape), pipeline_mode=pl.Buffered(1)
    )


def weight_specs(layer):
    return [of_layer(layer, BLOCKS, D, D), of_layer(layer, FF, D), of_layer(layer, 3, D)]


ANYWHERE = pl.BlockSpec(memory_space=pl.ANY)
SCALARS = pl.BlockSpec(memory_space=pltpu.SMEM)
PARAMS = pltpu.CompilerParams(vmem_limit_bytes=VMEM_LIMIT)


def shape_of(shape, kind):
    return jax.ShapeDtypeStruct(shape, kind)


def sums_scratch():
    return [pltpu.VMEM((BLOCKS, D, D), FULL), pltpu.VMEM((FF, D), FULL), pltpu.VMEM((8, D), FULL)]


def sums_shapes():
    return [shape_of((BLOCKS, D, D), LOW), shape_of((FF, D), LOW), shape_of((8, D), FULL)]


def sums_specs():
    return [ANYWHERE, ANYWHERE, pl.BlockSpec((8, D), lambda row: (0, 0))]


def encode(source_counts, rows, weights):
    count = rows.shape[0]
    kept = [
        ((ROW, D), FULL),
        ((ROW, 2 * D), LOW),
        ((ROW, 3 * D), LOW),
        ((HEADS, ROW, ROW), LOW),
        ((ROW, 2 * HD), FULL),
        ((ROW, D), LOW),
        ((ROW, D), FULL),
        ((ROW, FF), LOW),
        ((ROW, FF), LOW),
        ((ROW, D), FULL),
    ]
    return pl.pallas_call(
        encode_kernel,
        grid=(count,),
        in_specs=[SCALARS, per_row(ROW, D)] + weight_specs(0),
        out_specs=[per_row(*shape) for shape, _ in kept],
        out_shape=[shape_of((count,) + shape, kind) for shape, kind in kept],
        scratch_shapes=[pltpu.VMEM((ROW, ROW), FULL)],
        compiler_params=PARAMS,
        name="encode",
    )(source_counts, rows, *weights)


def decode(source_counts, target_counts, rows, memory_pair, cotangent, weights):
    count = rows.shape[0]
    shares = pltpu.VMEM((HEADS, ROW, ROW), LOW)
    inverse = pltpu.VMEM((ROW, 2 * HD), FULL)
    low = pltpu.VMEM((ROW, D), LOW)
    full = pltpu.VMEM((ROW, D), FULL)
    wide = pltpu.VMEM((ROW, FF), LOW)
    triple = pltpu.VMEM((ROW, 3 * D), LOW)
    return pl.pallas_call(
        decode_kernel,
        grid=(count,),
        in_specs=[SCALARS, SCALARS, per_row(ROW, D), per_row(ROW, 2 * D), per_row(ROW, D)] + weight_specs(1),
        out_specs=[per_row(ROW, D), per_row(ROW, D), per_row(ROW, 2 * D)] + sums_specs(),
        out_shape=[
            shape_of((count, ROW, D), FULL),
            shape_of((count, ROW, D), FULL),
            shape_of((count, ROW, 2 * D), LOW),
        ]
        + sums_shapes(),
        scratch_shapes=[
            pltpu.VMEM((ROW, ROW), FULL), triple, low, shares, shares, inverse, inverse,
            low, low, full, full, wide, wide, triple,
        ]
        + sums_scratch()
        + [pltpu.SemaphoreType.DMA((BLOCKS + SLABS,))],
        compiler_params=PARAMS,
        name="decode",
    )(source_counts, target_counts, rows, memory_pair, cotangent, *weights)


def encode_back(rows, kept, delta_pair, weights):
    count = rows.shape[0]
    triple, shares, inverse, result, first, active, slope, second = kept
    return pl.pallas_call(
        encode_back_kernel,
        grid=(count,),
        in_specs=[
            per_row(ROW, D), ANYWHERE, per_row(ROW, 3 * D), per_row(ROW, 2 * HD), per_row(ROW, D),
            per_row(ROW, D), per_row(ROW, FF), per_row(ROW, FF), per_row(ROW, D), per_row(ROW, 2 * D),
        ]
        + weight_specs(0),
        out_specs=[per_row(ROW, D)] + sums_specs(),
        out_shape=[shape_of((count, ROW, D), FULL)] + sums_shapes(),
        scratch_shapes=[
            pltpu.VMEM((HEADS, ROW, ROW), LOW),
            pltpu.VMEM((BLOCKS + SLABS - HEADS, D, D), LOW),
            pltpu.VMEM((ROW, 3 * D), LOW),
        ]
        + sums_scratch()
        + [pltpu.SemaphoreType.DMA, pltpu.SemaphoreType.DMA((BLOCKS + SLABS,))],
        compiler_params=PARAMS,
        name="encode_back",
    )(rows, shares, triple, inverse, result, first, active, slope, second, delta_pair, *weights)


MESH = pl.DeviceIdType.MESH
UNITS = BLOCKS + SLABS
UNIT = 32
DEPTHS, SIDES, CORES = 4, 2, 2


class Place:
    def __init__(self):
        self.layer = lax.axis_index("pipe")
        self.rank = lax.axis_index("dp")
        self.core = self.rank % CORES
        self.side = self.rank // CORES % SIDES
        self.depth = self.rank // (CORES * SIDES)

    def sibling(self):
        return (self.layer, self.rank + 1 - 2 * self.core)

    def across_side(self):
        return (self.layer, self.rank + CORES * (1 - 2 * self.side))

    def across_layer(self):
        return (1 - self.layer, self.rank)

    def other_depth(self, step):
        return (self.depth + step) % DEPTHS

    def along_depth(self, step):
        return (self.layer, self.rank + CORES * SIDES * (self.other_depth(step) - self.depth))

    def greet(self):
        partners = [self.sibling(), self.across_side(), self.across_layer()]
        partners += [self.along_depth(step) for step in range(1, DEPTHS)]
        barrier = pltpu.get_barrier_semaphore()
        for partner in partners:
            pl.semaphore_signal(barrier, inc=1, device_id=partner, device_id_type=MESH)
        pl.semaphore_wait(barrier, len(partners))


def push(source, target, sent, arrived, device):
    copy = pltpu.make_async_remote_copy(
        src_ref=source, dst_ref=target, send_sem=sent, recv_sem=arrived, device_id=device, device_id_type=MESH
    )
    copy.start()
    return copy


def layer_first(unit):
    return unit % 4 != 3


def gather_kernel(
    attention_in, attention_out, cross, expand, contract, gains, rows,
    square, tall, every_gain, away,
    own, own_done, depth_sent, depth_done, first_sent, first_done, last_sent, last_done,
    core_sent, core_done, gain_sent, gain_done, gain_own, row_sent, row_done,
):
    place = Place()
    layer, depth, side, core = place.layer, place.depth, place.side, place.core
    count = away.shape[0]
    sources = [attention_in.at[:, columns(j)] for j in range(3)] + [attention_out]
    sources += [cross.at[:, columns(j)] for j in range(2)] + [expand.at[:, columns(j)] for j in range(SLABS)]
    sources += [contract.at[columns(j, UNIT), :] for j in range(SLABS)]

    def spot(unit, *index):
        if unit < BLOCKS:
            return square.at[(index[0], unit) + index[1:]]
        return tall.at[index + (unit - BLOCKS,)]

    place.greet()
    swap_rows = push(
        rows.at[pl.ds(count - layer * count, count)], away, row_sent, row_done, place.across_layer()
    )
    everything = slice(None)
    owned, deep, first, last, shared = [], [], [], [], []

    mine = every_gain.at[layer, depth, side, core]
    gain_copy = pltpu.make_async_copy(gains, mine, gain_own)
    gain_copy.start()
    gain_pushes = [
        push(gains, mine, gain_sent.at[step - 1], gain_done.at[step - 1], place.along_depth(step))
        for step in range(1, DEPTHS)
    ]

    def begin(unit):
        own[unit] = sources[unit][...].astype(LOW)
        target = spot(unit, layer, depth, side, core)
        copy = pltpu.make_async_copy(own.at[unit], target, own_done.at[unit])
        copy.start()
        owned.append(copy)
        deep.append(
            [
                push(
                    own.at[unit], target, depth_sent.at[unit, step - 1], depth_done.at[unit, step - 1],
                    place.along_depth(step),
                )
                for step in range(1, DEPTHS)
            ]
        )

    def cross_first(unit):
        owned[unit].wait()
        for copy in deep[unit]:
            copy.wait_recv()
        block = spot(unit, layer, everything, side, core)
        target = place.across_layer() if layer_first(unit) else place.across_side()
        first.append(push(block, block, first_sent.at[unit], first_done.at[unit], target))

    def cross_last(unit):
        first[unit].wait_recv()
        if layer_first(unit):
            block, target = spot(unit, everything, everything, side, core), place.across_side()
        else:
            block, target = spot(unit, layer, everything, everything, core), place.across_layer()
        last.append(push(block, block, last_sent.at[unit], last_done.at[unit], target))

    def share(unit):
        last[unit].wait_recv()
        block = spot(unit, everything, everything, everything, core)
        shared.append(push(block, block, core_sent.at[unit], core_done.at[unit], place.sibling()))

    def gain_step(position):
        whole = every_gain.at[layer, :, side, core]
        if position == 0:
            gain_copy.wait()
            for copy in gain_pushes:
                copy.wait_recv()
            target = place.across_layer()
        elif position == 1:
            gain_pushes[-1].wait_recv()
            whole, target = every_gain.at[:, :, side, core], place.across_side()
        else:
            gain_pushes[-1].wait_recv()
            whole, target = every_gain.at[:, :, :, core], place.sibling()
        slot = DEPTHS - 1 + position
        gain_pushes.append(push(whole, whole, gain_sent.at[slot], gain_done.at[slot], target))

    ahead, gap = 4, 2
    for unit in range(ahead):
        begin(unit)
    for step in range(UNITS + 2 * gap):
        if step + ahead < UNITS:
            begin(step + ahead)
        if step < UNITS:
            cross_first(step)
        if 0 <= step - gap < UNITS:
            cross_last(step - gap)
        if 0 <= step - 2 * gap < UNITS:
            share(step - 2 * gap)
        if step < 3:
            gain_step(step)
    for unit in range(UNITS):
        shared[unit].wait()
        last[unit].wait_send()
        first[unit].wait_send()
        for copy in deep[unit]:
            copy.wait_send()
    gain_pushes[-1].wait_recv()
    for copy in gain_pushes:
        copy.wait_send()
    swap_rows.wait()


def gather_near(weights, gains, rows):
    count = rows.shape[0] // 2
    shards = DEPTHS * SIDES * CORES
    tile = jnp.tile(gains.astype(LOW), (1, 4))
    lane_part = lax.broadcasted_iota(jnp.int32, tile.shape, 1) // UNIT
    tile = jnp.where(lane_part == lax.axis_index("dp") % 4, tile, jnp.zeros_like(tile))
    tile = jnp.pad(tile, ((0, 16 - tile.shape[0]), (0, 0)))
    dma = pltpu.SemaphoreType.DMA
    vmem = pl.BlockSpec(memory_space=pltpu.VMEM)
    square, tall, every_gain, away = pl.pallas_call(
        gather_kernel,
        in_specs=[vmem] * 6 + [ANYWHERE],
        out_specs=[ANYWHERE] * 4,
        out_shape=[
            shape_of((2, BLOCKS, DEPTHS, SIDES, CORES, UNIT, D), LOW),
            shape_of((2, DEPTHS, SIDES, CORES, SLABS, UNIT, D), LOW),
            shape_of((2, DEPTHS, SIDES, CORES, 16, 128), LOW),
            shape_of((count, ROW, D), LOW),
        ],
        scratch_shapes=[
            pltpu.VMEM((UNITS, UNIT, D), LOW), dma((UNITS,)),
            dma((UNITS, 3)), dma((UNITS, 3)), dma((UNITS,)), dma((UNITS,)), dma((UNITS,)), dma((UNITS,)),
            dma((UNITS,)), dma((UNITS,)), dma((6,)), dma((6,)), dma, dma, dma,
        ],
        compiler_params=pltpu.CompilerParams(
            vmem_limit_bytes=VMEM_LIMIT, collective_id=0, has_side_effects=True
        ),
        name="gather",
    )(*weights, tile, rows)
    every_gain = every_gain.reshape(2, 4, 4, 16, 128).astype(FULL).sum(axis=2)[:, :, :3]
    every_gain = jnp.swapaxes(every_gain, 1, 2).reshape(2, 3, D)
    return (square.reshape(2, BLOCKS, D, D), tall.reshape(2, FF, D), every_gain), away


def gather_weights(weights, gains, shards):
    attention_in, attention_out, cross, expand, contract = weights
    square = jnp.stack(blocks_of(attention_in) + [attention_out] + blocks_of(cross) + blocks_of(expand)).astype(LOW)
    axes = ("pipe", "dp")
    every_square = lax.all_gather(square, axes, axis=0, tiled=False)
    every_tall = lax.all_gather(contract.astype(LOW), axes, axis=0, tiled=False)
    every_gain = lax.all_gather(gains.astype(LOW), axes, axis=0, tiled=False)
    every_square = every_square.reshape(2, shards, BLOCKS, D // shards, D)
    every_gain = every_gain.reshape(2, shards, 3, D // shards)
    return (
        jnp.swapaxes(every_square, 1, 2).reshape(2, BLOCKS, D, D),
        every_tall.reshape(2, FF, D),
        jnp.swapaxes(every_gain, 1, 2).reshape(2, 3, D).astype(FULL),
    )


def add_low(left, right):
    return (left.astype(FULL) + right.astype(FULL)).astype(LOW)


def scatter_kernel(
    source_square, source_tall, source_gain, target_square, target_tall, target_gain,
    square_out, tall_out, gain_out,
    total, from_core, from_side, from_layer, middle, from_last, ending, from_depth, gain_total, gain_parts,
    loaded, core_sent, core_done, first_sent, first_done, last_sent, last_done, depth_sent, depth_done,
    gain_sent, gain_done,
):
    place = Place()
    layer, depth, side, core = place.layer, place.depth, place.side, place.core
    everything = slice(None)

    def spot(which, unit, owner):
        if unit < BLOCKS:
            return (source_square, target_square)[which].at[unit, :, :, owner]
        return (source_tall, target_tall)[which].at[:, :, owner, unit - BLOCKS]

    loads, cores, first, last, deep, gains = [], [], [], [], [], []

    def begin(unit):
        for which in range(2):
            cores.append(
                push(
                    spot(which, unit, 1 - core), from_core.at[unit, which], core_sent.at[unit, which],
                    core_done.at[unit, which], place.sibling(),
                )
            )
            load = pltpu.make_async_copy(spot(which, unit, core), total.at[unit, which], loaded.at[unit, which])
            load.start()
            loads.append(load)

    def cross_first(unit):
        for which in range(2):
            loads[2 * unit + which].wait()
            cores[2 * unit + which].wait_recv()

            def add(step, carry):
                total[unit, which, step] = add_low(total[unit, which, step], from_core[unit, which, step])
                return carry

            lax.fori_loop(0, DEPTHS, add, 0)
        if layer_first(unit):
            block, landing, target = total.at[unit, :, :, 1 - side], from_side.at[unit], place.across_side()
        else:
            block, landing, target = total.at[unit, 1 - layer], from_layer.at[unit], place.across_layer()
        first.append(push(block, landing, first_sent.at[unit], first_done.at[unit], target))

    def cross_last(unit):
        first[unit].wait_recv()
        if layer_first(unit):

            def add(step, carry):
                which, row = step // DEPTHS, step % DEPTHS
                middle[unit, which, row] = add_low(total[unit, which, row, side], from_side[unit, which, row])
                return carry

            target = place.across_layer()
            source = middle.at[unit, 1 - layer]
        else:

            def add(step, carry):
                which, row = step // DEPTHS, step % DEPTHS
                middle[unit, which, row] = add_low(total[unit, layer, row, which], from_layer[unit, row, which])
                return carry

            target = place.across_side()
            source = middle.at[unit, 1 - side]
        lax.fori_loop(0, 2 * DEPTHS, add, 0)
        last.append(push(source, from_last.at[unit], last_sent.at[unit], last_done.at[unit], target))

    def along_depth(unit):
        last[unit].wait_recv()
        kept = layer if layer_first(unit) else side
        ending[unit] = add_low(middle[unit, kept], from_last[unit])
        deep.append(
            [
                push(
                    ending.at[unit, place.other_depth(step)], from_depth.at[unit, step - 1],
                    depth_sent.at[unit, step - 1], depth_done.at[unit, step - 1], place.along_depth(step),
                )
                for step in range(1, DEPTHS)
            ]
        )

    def finish(unit):
        value = ending[unit, depth].astype(FULL)
        for step in range(1, DEPTHS):
            deep[unit][step - 1].wait_recv()
            value = value + from_depth[unit, step - 1].astype(FULL)
        if unit < BLOCKS:
            square_out[unit] = value
        else:
            tall_out[columns(unit - BLOCKS, UNIT), :] = value

    def gain_step(position):
        if position == 0:
            for which, gain in enumerate((source_gain, target_gain)):
                for row in range(DEPTHS):
                    gain_total[0, which, row] = gain[:, columns(row, 128)]
            source, target = gain_total.at[0], place.sibling()
        elif position == 1:
            gains[0].wait_recv()
            gain_total[1] = gain_total[0] + gain_parts[0]
            source, target = gain_total.at[1], place.across_side()
        else:
            gains[1].wait_recv()
            gain_total[2] = gain_total[1] + gain_parts[1]
            source, target = gain_total.at[2, 1 - layer], place.across_layer()
        part = gain_parts.at[position] if position < 2 else gain_parts.at[2, 0]
        gains.append(push(source, part, gain_sent.at[position], gain_done.at[position], target))

    def gain_last():
        gains[2].wait_recv()
        gain_total[0, 0] = gain_total[2, layer] + gain_parts[2, 0]
        for step in range(1, DEPTHS):
            gains.append(
                push(
                    gain_total.at[0, 0, place.other_depth(step)], gain_parts.at[2, 1, step],
                    gain_sent.at[2 + step], gain_done.at[2 + step], place.along_depth(step),
                )
            )

    def gain_finish():
        value = gain_total[0, 0, depth]
        for step in range(1, DEPTHS):
            gains[2 + step].wait_recv()
            value = value + gain_parts[2, 1, step]
        gain_out[...] = value

    place.greet()
    ahead, gap = 3, 2
    for unit in range(ahead):
        begin(unit)
    for step in range(UNITS + 3 * gap):
        if step + ahead < UNITS:
            begin(step + ahead)
        if step < UNITS:
            cross_first(step)
        if 0 <= step - gap < UNITS:
            cross_last(step - gap)
        if 0 <= step - 2 * gap < UNITS:
            along_depth(step - 2 * gap)
        if 0 <= step - 3 * gap < UNITS:
            finish(step - 3 * gap)
        if step < 3:
            gain_step(step)
        elif step == 3:
            gains[0].wait_send()
            gain_last()
        elif step == 4:
            gain_finish()
    for copy in cores + first + last + sum(deep, []) + gains[1:]:
        copy.wait_send()


def scatter_near(source_sums, target_sums):
    dma = pltpu.SemaphoreType.DMA
    vmem = pl.BlockSpec(memory_space=pltpu.VMEM)
    shards = DEPTHS * SIDES * CORES
    operands = []
    for square, tall, gain in (source_sums, target_sums):
        operands.append(square.reshape(BLOCKS, DEPTHS, SIDES, CORES, UNIT, D))
        operands.append(tall.reshape(DEPTHS, SIDES, CORES, SLABS, UNIT, D))
        operands.append(gain)
    square, tall, gain = pl.pallas_call(
        scatter_kernel,
        in_specs=[ANYWHERE, ANYWHERE, vmem] * 2,
        out_specs=[vmem] * 3,
        out_shape=[shape_of((BLOCKS, UNIT, D), FULL), shape_of((SLABS * UNIT, D), FULL), shape_of((8, 128), FULL)],
        scratch_shapes=[
            pltpu.VMEM((UNITS, 2, DEPTHS, SIDES, UNIT, D), LOW),
            pltpu.VMEM((UNITS, 2, DEPTHS, SIDES, UNIT, D), LOW),
            pltpu.VMEM((UNITS, 2, DEPTHS, UNIT, D), LOW),
            pltpu.VMEM((UNITS, DEPTHS, 2, UNIT, D), LOW),
            pltpu.VMEM((UNITS, 2, DEPTHS, UNIT, D), LOW),
            pltpu.VMEM((UNITS, DEPTHS, UNIT, D), LOW),
            pltpu.VMEM((UNITS, DEPTHS, UNIT, D), LOW),
            pltpu.VMEM((UNITS, 3, UNIT, D), LOW),
            pltpu.VMEM((3, 2, DEPTHS, 8, 128), FULL),
            pltpu.VMEM((3, 2, DEPTHS, 8, 128), FULL),
            dma((UNITS, 2)), dma((UNITS, 2)), dma((UNITS, 2)), dma((UNITS,)), dma((UNITS,)), dma((UNITS,)),
            dma((UNITS,)), dma((UNITS, 3)), dma((UNITS, 3)), dma((6,)), dma((6,)),
        ],
        compiler_params=pltpu.CompilerParams(
            vmem_limit_bytes=VMEM_LIMIT, collective_id=1, has_side_effects=True
        ),
        name="scatter",
    )(*operands)
    start = lax.axis_index("dp") % 4 * UNIT
    return square, tall, lax.dynamic_slice_in_dim(gain[:3], start, UNIT, axis=1)


def scatter_sums(source_sums, target_sums, shards):
    square, tall, gains = (jnp.stack(pair) for pair in zip(source_sums, target_sums))
    axes = ("pipe", "dp")
    square = jnp.swapaxes(square.reshape(2, BLOCKS, shards, D // shards, D), 1, 2)
    gains = jnp.swapaxes(gains[:, :3].reshape(2, 3, shards, D // shards), 1, 2)
    square = square.reshape(2 * shards, BLOCKS, D // shards, D)
    tall = tall.reshape(2 * shards, FF // shards, D)
    gains = gains.reshape(2 * shards, 3, D // shards)
    return tuple(
        lax.psum_scatter(value, axes, scatter_dimension=0, tiled=False).astype(FULL)
        for value in (square, tall, gains)
    )


def swap(value):
    return lax.ppermute(value, "pipe", [(0, 1), (1, 0)])


def blocks_of(value):
    return [value[:, start : start + D] for start in range(0, value.shape[1], D)]


def local(
    section_input,
    attention_in,
    attention_out,
    cross_weights,
    expand,
    contract,
    norm_gains,
    source_lengths,
    target_lengths,
    cotangent,
):
    section = lax.axis_index("pipe")
    shards = lax.axis_size("dp")
    rows = section_input[0]
    count = rows.shape[0] // 2
    start = section * count

    def part(value, first):
        return lax.dynamic_slice_in_dim(value, first, count, axis=0)

    mine = part(rows, start)
    source_counts = part(source_lengths, start)
    target_counts = part(target_lengths, start)
    shares = tuple(value[0] for value in (attention_in, attention_out, cross_weights, expand, contract))
    if shards == DEPTHS * SIDES * CORES:
        weights, other = gather_near(shares, norm_gains[0], rows)
    else:
        weights, other = gather_weights(shares, norm_gains[0], shards), swap(part(rows, count - start))
    source_rows = jnp.where(section == 0, mine, other)
    target_rows = jnp.where(section == 0, other, mine)

    memory, memory_pair, *kept = encode(source_counts, source_rows, weights)
    output, target_gradient, delta_pair, *target_sums = decode(
        source_counts, target_counts, target_rows, memory_pair, part(cotangent, start), weights
    )
    away_output = swap(jnp.where(section == 0, output, memory).astype(LOW))
    away_target = lax.ppermute(target_gradient.astype(LOW), "pipe", [(0, 1)])
    source_gradient, *source_sums = encode_back(source_rows, kept, delta_pair, weights)
    away_source = lax.ppermute(source_gradient.astype(LOW), "pipe", [(1, 0)])
    if shards == DEPTHS * SIDES * CORES:
        square, tall, gains = scatter_near(source_sums, target_sums)
    else:
        square, tall, gains = scatter_sums(source_sums, target_sums, shards)

    def settle(source, target, from_source, from_target):
        upper = jnp.concatenate([source, from_source.astype(FULL)], axis=0)
        lower = jnp.concatenate([from_target.astype(FULL), target], axis=0)
        return jnp.where(section == 0, upper, lower)[None]

    section_output = settle(memory, output, away_output, away_output)
    input_gradient = settle(source_gradient, target_gradient, away_source, away_target)

    def joined(first, last):
        return jnp.concatenate([square[block] for block in range(first, last)], axis=1)[None]

    return (
        section_output,
        input_gradient,
        joined(QKV, OUT),
        joined(OUT, CROSS),
        joined(CROSS, EXPAND),
        joined(EXPAND, BLOCKS),
        tall[None],
        gains[None],
    )


def solution(mesh):
    in_specs = (
        P("pipe", "dp", None, None),
        P("pipe", "dp", None),
        P("pipe", "dp", None),
        P("pipe", "dp", None),
        P("pipe", "dp", None),
        P("pipe", "dp", None),
        P("pipe", None, "dp"),
        P("dp", None),
        P("dp", None),
        P("dp", None, None),
    )
    out_specs = (
        P("pipe", "dp", None, None),
        P("pipe", "dp", None, None),
        P("pipe", "dp", None),
        P("pipe", "dp", None),
        P("pipe", "dp", None),
        P("pipe", "dp", None),
        P("pipe", "dp", None),
        P("pipe", None, "dp"),
    )
    return jax.shard_map(local, mesh=mesh, in_specs=in_specs, out_specs=out_specs, check_vma=False)
```

```python
from functools import partial
import math

import jax
import jax.numpy as jnp
from jax import lax
from jax.experimental import pallas as pl
from jax.experimental.pallas import tpu as pltpu
from jax.sharding import PartitionSpec as P

D = 512
HEADS = 8
HD = 64
FF = 2048
ROW = 512
PAIRS = HEADS // 2
PACK = 4

QKV, OUT, SELFS = 0, 3, 4
CROSS, EXPAND, BLOCKS = 0, 2, 6
SLABS = FF // D
UNITS = BLOCKS + SLABS

EPSILON = 1e-05
MASKED = -1e30
LOG2E = math.log2(math.e)
EXPONENT = HD**-0.5 * LOG2E
BELL = 1.0 / math.sqrt(2.0 * math.pi)
LOW = jnp.bfloat16
FULL = jnp.float32
VMEM_LIMIT = 63 * 2**20

NN = (((1,), (0,)), ((), ()))
NT = (((1,), (1,)), ((), ()))
TN = (((0,), (0,)), ((), ()))


def multiply(left, right, dims=NN):
    return lax.dot_general(left, right, dims, preferred_element_type=jnp.float32)


def columns(index, width=D):
    return pl.ds(index * width, width)


def normalize(stream):
    centred = stream - jnp.mean(stream, axis=1, keepdims=True)
    scale = lax.rsqrt(jnp.mean(centred * centred, axis=1, keepdims=True) + EPSILON)
    return centred * scale, scale


def norm_back(unit, scale, gain, delta):
    inner = delta * gain
    mean = jnp.mean(inner, axis=1, keepdims=True)
    along = jnp.mean(inner * unit, axis=1, keepdims=True)
    return scale * (inner - mean - unit * along), jnp.sum(delta * unit, axis=0, keepdims=True)


def segment(counts, shape, axis):
    places = lax.broadcasted_iota(jnp.int32, shape, axis)
    end = counts[0]
    found = (places >= end).astype(jnp.int32)
    for count in counts[1:]:
        end = end + count
        found = found + (places >= end).astype(jnp.int32)
    return found


def segments(counts):
    return segment(counts, (ROW, 1), 0), segment(counts, (1, ROW), 1)


def fill_bias(bias, query_segment, key_segment, causal=None):
    keep = query_segment == key_segment
    if causal is not None:
        query = lax.broadcasted_iota(jnp.int32, (ROW, ROW), 0)
        key = lax.broadcasted_iota(jnp.int32, (ROW, ROW), 1)
        keep = keep & (key <= query + jnp.where(causal, 0, ROW))
    bias[...] = jnp.where(keep, 0.0, MASKED).astype(bias.dtype)


def lanes():
    return lax.broadcasted_iota(jnp.int32, (1, 2 * HD), 1)


def only_half(value, half):
    return jnp.where(lanes() // HD == half, value, jnp.zeros_like(value))


def attend(query, keys, values, bias, shares, inverse, result, hook):
    kept = jnp.zeros((ROW, 2 * HD), FULL)
    for pair in range(PAIRS):
        query2, keys2, values2 = query(pair), keys(pair), values(pair)
        parts = []
        for half in range(2):
            head = 2 * pair + half
            scores = multiply(only_half(query2, half), keys2, NT) + bias[...]
            top = jnp.max(scores, axis=1, keepdims=True)
            weights = jnp.exp2((scores - top) * EXPONENT)
            scale = 1.0 / jnp.sum(weights, axis=1, keepdims=True)
            low = weights.astype(LOW)
            shares[head] = low
            parts.append(multiply(low, values2) * scale)
            kept = jnp.where(lanes() == head, scale, kept)
        result[:, columns(pair, 2 * HD)] = jnp.where(lanes() < HD, parts[0], parts[1]).astype(LOW)
        hook()
    inverse[...] = kept


def attend_back(query, keys, values, shares, inverse, result, delta, put, hook):
    for pair in range(PAIRS):
        query2, keys2, values2 = query(pair), keys(pair), values(pair)
        place = slice(2 * HD * pair, 2 * HD * (pair + 1))
        scale = jnp.where(
            lanes() < HD, inverse[:, 2 * pair : 2 * pair + 1], inverse[:, 2 * pair + 1 : 2 * pair + 2]
        )
        low = (delta[:, place] * scale).astype(LOW)
        product = low.astype(FULL) * result[:, columns(pair, 2 * HD)].astype(FULL)
        query_turned, low_turned = query2.T, low.T
        delta_query = 0.0
        delta_keys, delta_values = [], []
        for half in range(2):
            weights = shares[2 * pair + half]
            along = jnp.sum(only_half(product, half), axis=1, keepdims=True)
            delta_shares = multiply(only_half(low, half), values2, NT)
            delta_scores = (weights.astype(FULL) * (delta_shares - along)).astype(LOW)
            delta_query = delta_query + multiply(delta_scores, only_half(keys2, half))
            own = slice(HD * half, HD * (half + 1))
            delta_keys.append(multiply(query_turned[own], delta_scores))
            delta_values.append(multiply(low_turned[own], weights))
        keys_turned = (jnp.concatenate(delta_keys, axis=0) * HD**-0.5).astype(LOW)
        values_turned = jnp.concatenate(delta_values, axis=0).astype(LOW)
        put(pair, (delta_query * HD**-0.5).astype(LOW), keys_turned.T, values_turned.T)
        hook()


def self_parts(triple):
    return tuple(
        (lambda pair, start=part * PAIRS: triple[:, columns(start + pair, 2 * HD)]) for part in range(3)
    )


def put_triple(target):
    def put(pair, *parts):
        for part, value in enumerate(parts):
            target[:, columns(part * PAIRS + pair, 2 * HD)] = value

    return put


def feed(normed, stream, square, tall, active, slope):
    total = stream
    for slab in range(SLABS):
        hidden = multiply(normed, square[EXPAND + slab])
        under = 0.5 + 0.5 * lax.erf(hidden * math.sqrt(0.5))
        bell = BELL * jnp.exp2(hidden * hidden * (-0.5 * LOG2E))
        low = (hidden * under).astype(LOW)
        active[:, columns(slab)] = low
        slope[:, columns(slab)] = (under + hidden * bell).astype(LOW)
        total = total + multiply(low, tall[columns(slab), :])
    return total


def feed_back(delta, stream, gain, square, tall, change):
    unit, scale = normalize(stream)
    low = delta.astype(LOW)
    delta_normed = 0.0
    for slab in range(SLABS):
        delta_active = multiply(low, tall[columns(slab), :], NT)
        delta_hidden = (delta_active * change[:, columns(slab)].astype(FULL)).astype(LOW)
        change[:, columns(slab)] = delta_hidden
        delta_normed = delta_normed + multiply(delta_hidden, square[EXPAND + slab], NT)
    delta_stream, delta_gain = norm_back(unit, scale, gain, delta_normed)
    return delta + delta_stream, delta_gain


def self_forward(stream, gain, square, bias, triple, shares, inverse, result, hook):
    normed = (normalize(stream)[0] * gain).astype(LOW)
    for part in range(3):
        triple[:, columns(part)] = multiply(normed, square(QKV + part)).astype(LOW)
    hook()
    attend(*self_parts(triple), bias, shares, inverse, result, hook)
    return stream + multiply(result[...], square(OUT))


def self_back(low, stream, gain, square, triple, shares, inverse, result, delta_triple, sums, hook):
    unit, scale = normalize(stream)
    sums[OUT] += multiply(result[...], low, TN)
    delta_result = multiply(low, square(OUT), NT)
    hook()
    attend_back(*self_parts(triple), shares, inverse, result, delta_result, put_triple(delta_triple), hook)
    turned = (unit * gain).astype(LOW).T
    delta_normed = 0.0
    for part in range(3):
        chunk = delta_triple[:, columns(part)]
        sums[QKV + part] += multiply(turned, chunk)
        delta_normed = delta_normed + multiply(chunk, square(QKV + part), NT)
    delta_stream, delta_gain = norm_back(unit, scale, gain, delta_normed)
    return low.astype(FULL) + delta_stream, delta_gain


def middle_kernel(
    source_counts, target_counts, first, away, cotangent, square, tall, gains,
    section_output, sent_output, kept_delta, sent_delta, square_out, tall_out, gain_out,
    bias, shares, inverse, cross_result, source_end, target_mid, value,
    source_normed, source_active, memory_low, cross_normed, feed_normed, target_active,
    source_change, source_low, delta_pair, delta_question, cross_low, target_change, target_low,
    gain_sum, loaded, stored, ready,
):
    step = pl.program_id(0)
    layer = lax.axis_index("pipe")
    count = loaded.shape[0]
    source_square, target_square = square.at[0], square.at[1]
    source_tall, target_tall = tall.at[0], tall.at[1]

    def load(row):
        return pltpu.make_async_copy(
            cotangent.at[layer * count + row], target_low.at[columns(row, ROW), :], loaded.at[row]
        )

    def store(row):
        return pltpu.make_async_copy(value, section_output.at[layer * count + row], stored)

    @pl.when(step == 0)
    def _():
        gain_sum[...] = jnp.zeros(gain_sum.shape, FULL)
        for row in range(loaded.shape[0]):
            load(row).start()

    @pl.when(step < count)
    def _():
        row = step
        place = pl.ds(pl.multiple_of(row * ROW, ROW), ROW)
        own, other = first[0], away[0].astype(FULL)
        source_stream = jnp.where(layer == 0, own, other)
        target_stream = jnp.where(layer == 0, other, own)
        whole = layer * count + row
        source_segment = segments([source_counts[whole, piece] for piece in range(PACK)])
        target_segment = segments([target_counts[whole, piece] for piece in range(PACK)])

        unit, _ = normalize(source_stream)
        normed = (unit * gains[0, 1:2, :]).astype(LOW)
        source_normed[place, :] = normed
        end = feed(
            normed, source_stream, source_square, source_tall, source_active.at[place, :], source_change.at[place, :]
        )
        source_end[...] = end
        memory = normalize(end)[0] * gains[0, 2:3, :]
        low = memory.astype(LOW)
        memory_low[place, :] = low
        for part in range(2):
            delta_pair[place, columns(part)] = multiply(low, source_square[CROSS + part]).astype(LOW)

        fill_bias(bias, target_segment[0], source_segment[1])
        unit, _ = normalize(target_stream)
        normed = (unit * gains[1, 1:2, :]).astype(LOW)
        cross_normed[place, :] = normed
        delta_question[place, :] = multiply(normed, target_square[CROSS]).astype(LOW)
        cross = (
            lambda pair: delta_question[place, columns(pair, 2 * HD)],
            lambda pair: delta_pair[place, columns(pair, 2 * HD)],
            lambda pair: delta_pair[place, columns(PAIRS + pair, 2 * HD)],
        )
        result = cross_result.at[place, :]
        attend(*cross, bias, shares, inverse, result, no_hook)
        stream = target_stream + multiply(result[...], target_square[CROSS + 1])
        target_mid[...] = stream
        normed = (normalize(stream)[0] * gains[1, 2:3, :]).astype(LOW)
        feed_normed[place, :] = normed
        output = feed(
            normed, stream, target_square, target_tall, target_active.at[place, :], target_change.at[place, :]
        )

        @pl.when(row > 0)
        def _():
            store(row).wait()

        value[...] = jnp.where(layer == 0, memory, output)
        store(row).start()
        sent_output[0] = jnp.where(layer == 0, output, memory).astype(LOW)

        load(row).wait()
        delta, delta_gain = feed_back(
            target_low[place, :].astype(FULL), target_mid[...], gains[1, 2:3, :], target_square, target_tall,
            target_change.at[place, :],
        )
        gain_sum[1, 2:3, :] += delta_gain

        unit, scale = normalize(target_stream)
        low = delta.astype(LOW)
        cross_low[place, :] = low
        delta_result = multiply(low, target_square[CROSS + 1], NT)

        def put(pair, query, keys, values):
            delta_question[place, columns(pair, 2 * HD)] = query
            delta_pair[place, columns(pair, 2 * HD)] = keys
            delta_pair[place, columns(PAIRS + pair, 2 * HD)] = values

        attend_back(*cross, shares, inverse, result, delta_result, put, no_hook)
        delta_normed = multiply(delta_question[place, :], target_square[CROSS], NT)
        delta_stream, delta_gain = norm_back(unit, scale, gains[1, 1:2, :], delta_normed)
        gain_sum[1, 1:2, :] += delta_gain
        target_delta = (delta + delta_stream).astype(LOW)

        unit, scale = normalize(source_end[...])
        delta_memory = 0.0
        for part in range(2):
            delta_memory = delta_memory + multiply(delta_pair[place, columns(part)], source_square[CROSS + part], NT)
        delta, delta_gain = norm_back(unit, scale, gains[0, 2:3, :], delta_memory)
        gain_sum[0, 2:3, :] += delta_gain
        source_low[place, :] = delta.astype(LOW)
        delta, delta_gain = feed_back(
            delta, source_stream, gains[0, 1:2, :], source_square, source_tall, source_change.at[place, :]
        )
        gain_sum[0, 1:2, :] += delta_gain
        source_delta = delta.astype(LOW)
        kept_delta[0] = jnp.where(layer == 0, source_delta, target_delta)
        sent_delta[0] = jnp.where(layer == 0, target_delta, source_delta)

    @pl.when(step == count)
    def _():
        store(0).wait()
        gain_out[...] = gain_sum[...]
        copies = []

        def emit(result, target):
            slot = len(copies) % HEADS
            if len(copies) >= HEADS:
                copies[len(copies) - HEADS].wait()
            shares[slot] = result.astype(LOW)
            copy = pltpu.make_async_copy(shares.at[slot], target, ready.at[slot])
            copy.start()
            copies.append(copy)

        for which, normed, change, active, low in (
            (1, feed_normed, target_change, target_active, target_low),
            (0, source_normed, source_change, source_active, source_low),
        ):
            turned = normed[...].T
            for slab in range(SLABS):
                emit(multiply(turned, change[:, columns(slab)]), square_out.at[which, EXPAND + slab])
            for slab in range(SLABS):
                emit(multiply(active[:, columns(slab)], low[...], TN), tall_out.at[which, columns(slab), :])
        emit(multiply(cross_normed[...], delta_question[...], TN), square_out.at[1, CROSS])
        emit(multiply(cross_result[...], cross_low[...], TN), square_out.at[1, CROSS + 1])
        turned = memory_low[...].T
        for part in range(2):
            emit(multiply(turned, delta_pair[:, columns(part)]), square_out.at[0, CROSS + part])
        for copy in copies[-HEADS:]:
            copy.wait()


def no_hook():
    pass


def per_row(*shape, last=None, start=0, buffers=2):
    def index(row):
        return (start + (row if last is None else jnp.minimum(row, last)),) + (0,) * len(shape)

    return pl.BlockSpec((1,) + shape, index, pipeline_mode=pl.Buffered(buffers) if buffers != 2 else None)


def constant(*shape):
    return pl.BlockSpec(shape, lambda row: (0,) * len(shape), pipeline_mode=pl.Buffered(1))


ANYWHERE = pl.BlockSpec(memory_space=pl.ANY)
SCALARS = pl.BlockSpec(memory_space=pltpu.SMEM)
PARAMS = pltpu.CompilerParams(vmem_limit_bytes=VMEM_LIMIT)


def shape_of(shape, kind):
    return jax.ShapeDtypeStruct(shape, kind)


def middle(source_counts, target_counts, first, away, cotangent, square, tall, gains):
    count = away.shape[0]
    tokens = count * ROW
    full = pltpu.VMEM((ROW, D), FULL)
    kept, pair, wide = (pltpu.VMEM((tokens, width), LOW) for width in (D, 2 * D, FF))
    last = count - 1
    return pl.pallas_call(
        middle_kernel,
        grid=(count + 1,),
        in_specs=[
            SCALARS, SCALARS, per_row(ROW, D, last=last, start=count, buffers=1),
            per_row(ROW, D, last=last, buffers=1), ANYWHERE,
            constant(2, BLOCKS, D, D), constant(2, FF, D), constant(2, 8, D),
        ],
        out_specs=[ANYWHERE]
        + [per_row(ROW, D, last=last)] * 3
        + [ANYWHERE, ANYWHERE, pl.BlockSpec((2, 8, D), lambda row: (0, 0, 0))],
        out_shape=[shape_of((2 * count, ROW, D), FULL)]
        + [shape_of((count, ROW, D), LOW)] * 3
        + [shape_of((2, BLOCKS, D, D), LOW), shape_of((2, FF, D), LOW), shape_of((2, 8, D), FULL)],
        scratch_shapes=[
            pltpu.VMEM((ROW, ROW), LOW), pltpu.VMEM((HEADS, ROW, ROW), LOW),
            pltpu.VMEM((ROW, 2 * HD), FULL), kept, full, full, full,
            kept, wide, kept, kept, kept, wide,
            wide, kept, pair, kept, kept, wide, kept,
            pltpu.VMEM((2, 8, D), FULL), pltpu.SemaphoreType.DMA((count,)), pltpu.SemaphoreType.DMA,
            pltpu.SemaphoreType.DMA((HEADS,)),
        ],
        compiler_params=PARAMS,
        name="middle",
    )(source_counts, target_counts, first, away, cotangent, square, tall, gains)


MESH = pl.DeviceIdType.MESH
UNITS = BLOCKS + SLABS
UNIT = 32
DEPTHS, SIDES, CORES = 4, 2, 2


class Place:
    def __init__(self):
        self.layer = lax.axis_index("pipe")
        self.rank = lax.axis_index("dp")
        self.core = self.rank % CORES
        self.side = self.rank // CORES % SIDES
        self.depth = self.rank // (CORES * SIDES)

    def sibling(self):
        return (self.layer, self.rank + 1 - 2 * self.core)

    def across_side(self):
        return (self.layer, self.rank + CORES * (1 - 2 * self.side))

    def across_layer(self):
        return (1 - self.layer, self.rank)

    def other_depth(self, step):
        return (self.depth + step) % DEPTHS

    def along_depth(self, step):
        return (self.layer, self.rank + CORES * SIDES * (self.other_depth(step) - self.depth))

    def greet(self):
        partners = [self.sibling(), self.across_side(), self.across_layer()]
        partners += [self.along_depth(step) for step in range(1, DEPTHS)]
        barrier = pltpu.get_barrier_semaphore()
        for partner in partners:
            pl.semaphore_signal(barrier, inc=1, device_id=partner, device_id_type=MESH)
        pl.semaphore_wait(barrier, len(partners))


def layer_first(unit):
    return unit % 4 != 3


def row_of(layer, slot, count):
    return (slot + count * (1 - layer)) % (2 * count)


class Plan:
    def __init__(self, rate, hooks):
        self.rate, self.hooks = rate, hooks
        self.steps = {}
        self.index = 0

    def fill(self, thunks, rows):
        for number, thunk in enumerate(thunks):
            place = min(int(number * self.rate), rows * self.hooks - 1)
            self.steps.setdefault(divmod(place, self.hooks), []).append(thunk)

    def hook(self):
        index, self.index = self.index, self.index + 1
        step = pl.program_id(0)
        for (row, place), thunks in sorted(self.steps.items(), key=lambda item: item[0]):
            if place == index:

                @pl.when(step == row)
                def _(thunks=thunks):
                    for thunk in thunks:
                        thunk()


class Copies:
    def __init__(self):
        self.made = {}

    def define(self, key, parts):
        def make():
            source, target, sent, arrived, device = parts()
            return pltpu.make_async_remote_copy(
                src_ref=source, dst_ref=target, send_sem=sent, recv_sem=arrived, device_id=device,
                device_id_type=MESH,
            )

        self.made[key] = make

    def start(self, *keys):
        for key in keys:
            self.made[key]().start()

    def arrived(self, *keys):
        for key in keys:
            self.made[key]().wait_recv()

    def finish(self):
        for make in self.made.values():
            make().wait_send()


GATHER_RATE, GATHER_AHEAD, GATHER_GAP = 1.5, 4, 2
SCATTER_RATE, SCATTER_AHEAD, SCATTER_GAP = 1.4, 3, 2
ORDER = (2, 3, 4, 5, 6, 7, 8, 9, 0, 1)
HOOKS = PAIRS + 2


def near_self_kernel(
    source_counts, target_counts, attention_in, attention_out, cross, expand, contract, gains, rows,
    square, tall, own_square, every_gain, away, triple, shares, inverse, result, first,
    blocks, tiles, streams, sending, bias, own,
    own_done, fetched, block_sent, block_done, block_out, tile_sent, tile_done,
    depth_sent, depth_done, first_sent, first_done, last_sent, last_done, core_sent, core_done,
    away_sent, away_done,
):
    place = Place()
    layer, depth, side, core = place.layer, place.depth, place.side, place.core
    step, total = pl.program_id(0), 2 * away.shape[0]
    count = away.shape[0]
    everything = slice(None)
    copies = Copies()
    selfs = [attention_in.at[:, columns(j)] for j in range(3)] + [attention_out]
    sources = [cross.at[:, columns(j)] for j in range(2)] + [expand.at[:, columns(j)] for j in range(SLABS)]
    sources += [contract.at[columns(j, UNIT), :] for j in range(SLABS)]

    def spot(unit, *index):
        if unit < BLOCKS:
            return square.at[(index[0], unit) + index[1:]]
        return tall.at[index + (unit - BLOCKS,)]

    def from_layers(unit):
        return spot(unit, everything, everything, side, core)

    def from_sides(unit):
        return spot(unit, layer, everything, everything, core)

    def deep_parts(unit, away_by):
        slot = (unit, away_by - 1)
        target = spot(unit, layer, depth, side, core)
        return own.at[unit], target, depth_sent.at[slot], depth_done.at[slot], place.along_depth(away_by)

    def first_parts(unit):
        block = spot(unit, layer, everything, side, core)
        target = place.across_layer() if layer_first(unit) else place.across_side()
        return block, block, first_sent.at[unit], first_done.at[unit], target

    def last_parts(unit):
        if layer_first(unit):
            block, target = from_layers(unit), place.across_side()
        else:
            block, target = from_sides(unit), place.across_layer()
        return block, block, last_sent.at[unit], last_done.at[unit], target

    def core_parts(unit):
        block = spot(unit, everything, everything, everything, core)
        return block, block, core_sent.at[unit], core_done.at[unit], place.sibling()

    for unit in range(UNITS):
        for away_by in range(1, DEPTHS):
            copies.define(("deep", unit, away_by), partial(deep_parts, unit, away_by))
        copies.define(("first", unit), partial(first_parts, unit))
        copies.define(("last", unit), partial(last_parts, unit))
        copies.define(("core", unit), partial(core_parts, unit))

    def away_parts(slot):
        return sending.at[slot], away.at[slot], away_sent.at[slot], away_done.at[slot], place.across_layer()

    def block_parts(unit, stage):
        if stage == 0:
            block, target = blocks.at[unit, :, :, core], place.sibling()
        elif stage < DEPTHS:
            block, target = blocks.at[unit, depth, side, core], place.along_depth(stage)
        else:
            block, target = blocks.at[unit, :, side, core], place.across_side()
        return block, block, block_sent.at[unit, stage], block_done.at[unit, stage], target

    def tile_parts(stage):
        if stage == 0:
            block, target = tiles.at[layer], place.across_layer()
        elif stage < DEPTHS:
            block, target = tiles.at[layer, depth, side, core], place.along_depth(stage)
        elif stage == DEPTHS:
            block, target = tiles.at[layer, :, side, core], place.across_side()
        else:
            block, target = tiles.at[layer, :, :, core], place.sibling()
        return block, block, tile_sent.at[stage], tile_done.at[stage], target

    for stage in range(DEPTHS + 2):
        copies.define(("tile", stage), partial(tile_parts, stage))
    for unit in range(SELFS):
        for stage in range(DEPTHS + 1):
            copies.define(("block", unit, stage), partial(block_parts, unit, stage))
    for slot in range(count):
        copies.define(("away", slot), partial(away_parts, slot))

    def keep(unit):
        return pltpu.make_async_copy(own.at[unit], spot(unit, layer, depth, side, core), own_done.at[unit])

    def deep(unit):
        return [("deep", unit, away_by) for away_by in range(1, DEPTHS)]

    def begin(unit):
        own[unit] = sources[unit][...].astype(LOW)
        keep(unit).start()
        copies.start(*deep(unit))

    def cross_first(unit):
        keep(unit).wait()
        copies.arrived(*deep(unit))
        copies.start(("first", unit))

    def cross_last(unit):
        copies.arrived(("first", unit))
        copies.start(("last", unit))

    def share(unit):
        copies.arrived(("last", unit))
        copies.start(("core", unit))

    def steps():
        gap, ahead = GATHER_GAP, GATHER_AHEAD

        def one(number):
            if ahead <= number + ahead < UNITS:
                begin(ORDER[number + ahead])
            if number < UNITS:
                cross_first(ORDER[number])
            if 0 <= number - gap < UNITS:
                cross_last(ORDER[number - gap])
            if 0 <= number - 2 * gap < UNITS:
                share(ORDER[number - 2 * gap])

        return [partial(one, number) for number in range(UNITS + 2 * gap)]

    def lay_gains(which):
        for row in range(DEPTHS):
            value = tiles[which, row, 0, 0].astype(FULL)
            for other in ((0, 1), (1, 0), (1, 1)):
                value = value + tiles[(which, row) + other].astype(FULL)
            every_gain[which, :, columns(row, 128)] = value[:8]

    def fetch(slot):
        return pltpu.make_async_copy(
            rows.at[row_of(layer, slot, count)], streams.at[slot % 2], fetched.at[slot % 2]
        )

    @pl.when(step == 0)
    def _():
        fetch(step).start()
        for unit in range(SELFS):
            blocks[unit, depth, side, core] = selfs[unit][...].astype(LOW)
        tiles[layer, depth, side, core] = gains[...]
        place.greet()
        across = range(1, DEPTHS)
        copies.start(*[("tile", stage) for stage in across])
        for unit in range(SELFS):
            copies.start(*[("block", unit, stage) for stage in across])
        for number in range(GATHER_AHEAD):
            begin(ORDER[number])
        copies.arrived(*[("tile", stage) for stage in across])
        copies.start(("tile", DEPTHS))
        for unit in range(SELFS):
            copies.arrived(*[("block", unit, stage) for stage in across])
            copies.start(("block", unit, DEPTHS))
        copies.arrived(("tile", DEPTHS))
        copies.start(("tile", DEPTHS + 1))
        for unit in range(SELFS):
            copies.arrived(("block", unit, DEPTHS))
            copies.start(("block", unit, 0))
        copies.arrived(("tile", DEPTHS + 1))
        copies.start(("tile", 0))
        lay_gains(layer)
        copies.arrived(*[("block", unit, 0) for unit in range(SELFS)])
        pltpu.make_async_copy(blocks, own_square, block_out).start()

    plan = Plan(GATHER_RATE, HOOKS)
    plan.fill(steps(), total)

    @pl.when(step + 1 < total)
    def _():
        fetch(step + 1).start()

    row = row_of(layer, step, count)
    causal = layer == 1
    both = [jnp.where(causal, target_counts[row, piece], source_counts[row, piece]) for piece in range(PACK)]
    fill_bias(bias, *segments(both), causal)
    fetch(step).wait()
    stream = self_forward(
        streams[step % 2].astype(FULL), every_gain[layer, 0:1, :], lambda unit: blocks[unit].reshape(D, D), bias,
        triple.at[0], shares.at[0], inverse.at[0], result.at[0], plan.hook,
    )
    first[0] = stream

    for slot in range(count):

        @pl.when(step == slot)
        def _(slot=slot):
            sending[slot] = stream.astype(LOW)
            copies.start(("away", slot))

    plan.hook()

    @pl.when(step == total - 1)
    def _():
        copies.arrived(("tile", 0))
        lay_gains(1 - layer)
        copies.arrived(*[("core", unit) for unit in range(UNITS)])
        copies.arrived(*[("away", slot) for slot in range(count)])
        copies.finish()
        pltpu.make_async_copy(blocks, own_square, block_out).wait()


def kept_shapes():
    return [
        ((ROW, 3 * D), LOW), ((HEADS, ROW, ROW), LOW), ((ROW, 2 * HD), FULL), ((ROW, D), LOW), ((ROW, D), FULL)
    ]


def near_self(source_counts, target_counts, weights, gains, rows):
    total = rows.shape[0]
    tile = jnp.tile(gains.astype(LOW), (1, 4))
    lane_part = lax.broadcasted_iota(jnp.int32, tile.shape, 1) // UNIT
    tile = jnp.where(lane_part == lax.axis_index("dp") % 4, tile, jnp.zeros_like(tile))
    tile = jnp.pad(tile, ((0, 16 - tile.shape[0]), (0, 0)))
    dma = pltpu.SemaphoreType.DMA
    kept = kept_shapes()
    outs = [
        shape_of((2, BLOCKS, DEPTHS, SIDES, CORES, UNIT, D), LOW),
        shape_of((2, DEPTHS, SIDES, CORES, SLABS, UNIT, D), LOW),
        shape_of((SELFS, DEPTHS, SIDES, CORES, UNIT, D), LOW),
        shape_of((2, 8, D), FULL),
        shape_of((total // 2, ROW, D), LOW),
    ]
    square, tall, own_square, every_gain, away, *kept = pl.pallas_call(
        near_self_kernel,
        grid=(total,),
        in_specs=[SCALARS, SCALARS] + [constant(*value.shape) for value in weights] + [constant(16, 128), ANYWHERE],
        out_specs=[ANYWHERE] * 3
        + [pl.BlockSpec((2, 8, D), lambda row: (0, 0, 0)), ANYWHERE]
        + [per_row(*shape) for shape, _ in kept],
        out_shape=outs + [shape_of((total,) + shape, kind) for shape, kind in kept],
        scratch_shapes=[
            pltpu.VMEM((SELFS, DEPTHS, SIDES, CORES, UNIT, D), LOW),
            pltpu.VMEM((2, DEPTHS, SIDES, CORES, 16, 128), LOW),
            pltpu.VMEM((2, ROW, D), LOW),
            pltpu.VMEM((total // 2, ROW, D), LOW),
            pltpu.VMEM((ROW, ROW), FULL),
            pltpu.VMEM((UNITS, UNIT, D), LOW),
            dma((UNITS,)), dma((2,)), dma((SELFS, 5)), dma((SELFS, 5)), dma, dma((6,)), dma((6,)),
            dma((UNITS, 3)), dma((UNITS, 3)), dma((UNITS,)), dma((UNITS,)), dma((UNITS,)), dma((UNITS,)),
            dma((UNITS,)), dma((UNITS,)), dma((total // 2,)), dma((total // 2,)),
        ],
        compiler_params=pltpu.CompilerParams(
            vmem_limit_bytes=VMEM_LIMIT, collective_id=0, has_side_effects=True
        ),
        name="self_forward",
    )(source_counts, target_counts, *weights, tile, rows)
    return square.reshape(2, BLOCKS, D, D), tall.reshape(2, FF, D), own_square, every_gain, away, kept


def add_low(left, right):
    return (left.astype(FULL) + right.astype(FULL)).astype(LOW)


def near_back_kernel(
    kept_delta, sent_delta, rows, own_square, gains, triple, shares, inverse, result,
    square_sums, tall_sums, gain_sums,
    gradient, attention_in, attention_out, cross, expand, contract, gain_out,
    deltas, streams, value, delta_triple, sums, low_sums, own_gain,
    total, from_core, from_side, from_layer, middle, from_last, ending, from_depth,
    own_total, own_from_core, own_middle, own_from_side, own_from_depth,
    gain_total, gain_parts, gain_from_layer,
    delta_done, delta_sent, delta_arrived, fetched, stored,
    loaded, core_sent, core_done, first_sent, first_done, last_sent, last_done, depth_sent, depth_done,
    own_sent, own_done, gain_sent, gain_done,
):
    place = Place()
    layer, depth, side, core = place.layer, place.depth, place.side, place.core
    count = kept_delta.shape[0]
    step, steps_in_all = pl.program_id(0), 2 * count
    copies = Copies()

    def spot(which, unit, owner):
        if unit < BLOCKS:
            return square_sums.at[which, unit, :, :, owner]
        return tall_sums.at[which, :, :, owner, unit - BLOCKS]

    def load(unit, which):
        return pltpu.make_async_copy(spot(which, unit, core), total.at[unit, which], loaded.at[unit, which])

    def core_parts(unit, which):
        slot = (unit, which)
        return (
            spot(which, unit, 1 - core), from_core.at[slot], core_sent.at[slot], core_done.at[slot], place.sibling()
        )

    def first_parts(unit):
        if layer_first(unit):
            source, target, device = total.at[unit, :, :, 1 - side], from_side.at[unit], place.across_side()
        else:
            source, target, device = total.at[unit, 1 - layer], from_layer.at[unit], place.across_layer()
        return source, target, first_sent.at[unit], first_done.at[unit], device

    def last_parts(unit):
        if layer_first(unit):
            source, device = middle.at[unit, 1 - layer], place.across_layer()
        else:
            source, device = middle.at[unit, 1 - side], place.across_side()
        return source, from_last.at[unit], last_sent.at[unit], last_done.at[unit], device

    def deep_parts(unit, away_by):
        slot = (unit, away_by - 1)
        return (
            ending.at[unit, place.other_depth(away_by)], from_depth.at[slot], depth_sent.at[slot],
            depth_done.at[slot], place.along_depth(away_by),
        )

    def delta_parts(slot):
        return (
            sent_delta.at[slot], deltas.at[count + slot], delta_sent.at[slot], delta_arrived.at[slot],
            place.across_layer(),
        )

    def own_core_parts(unit):
        return (
            low_sums.at[unit, :, :, 1 - core], own_from_core.at[unit], own_sent.at[unit, 0], own_done.at[unit, 0],
            place.sibling(),
        )

    def own_side_parts(unit):
        return (
            own_total.at[unit, :, 1 - side], own_from_side.at[unit], own_sent.at[unit, 1], own_done.at[unit, 1],
            place.across_side(),
        )

    def own_deep_parts(unit, away_by):
        return (
            own_middle.at[unit, place.other_depth(away_by)], own_from_depth.at[unit, away_by - 1],
            own_sent.at[unit, 1 + away_by], own_done.at[unit, 1 + away_by], place.along_depth(away_by),
        )

    def gain_parts_of(stage):
        if stage == 0:
            source, target, device = gain_sums.at[1 - layer], gain_from_layer, place.across_layer()
        elif stage == 1:
            source, target, device = gain_total.at[0], gain_parts.at[0], place.sibling()
        elif stage == 2:
            source, target, device = gain_total.at[1], gain_parts.at[1], place.across_side()
        else:
            away_by = stage - 2
            source, target = gain_total.at[2, place.other_depth(away_by)], gain_parts.at[2, away_by]
            device = place.along_depth(away_by)
        return source, target, gain_sent.at[stage], gain_done.at[stage], device

    across = range(1, DEPTHS)
    for unit in range(UNITS):
        for which in range(2):
            copies.define(("core", unit, which), partial(core_parts, unit, which))
        copies.define(("first", unit), partial(first_parts, unit))
        copies.define(("last", unit), partial(last_parts, unit))
        for away_by in across:
            copies.define(("deep", unit, away_by), partial(deep_parts, unit, away_by))
    for slot in range(count):
        copies.define(("delta", slot), partial(delta_parts, slot))
    for unit in range(SELFS):
        copies.define(("own core", unit), partial(own_core_parts, unit))
        copies.define(("own side", unit), partial(own_side_parts, unit))
        for away_by in across:
            copies.define(("own deep", unit, away_by), partial(own_deep_parts, unit, away_by))
    for stage in range(3 + DEPTHS - 1):
        copies.define(("gain", stage), partial(gain_parts_of, stage))

    def begin(unit):
        for which in range(2):
            copies.start(("core", unit, which))
            load(unit, which).start()

    def cross_first(unit):
        for which in range(2):
            load(unit, which).wait()
            copies.arrived(("core", unit, which))

            def add(row, carry):
                total[unit, which, row] = add_low(total[unit, which, row], from_core[unit, which, row])
                return carry

            lax.fori_loop(0, DEPTHS, add, 0)
        copies.start(("first", unit))

    def cross_last(unit):
        copies.arrived(("first", unit))
        if layer_first(unit):

            def add(index, carry):
                which, row = index // DEPTHS, index % DEPTHS
                middle[unit, which, row] = add_low(total[unit, which, row, side], from_side[unit, which, row])
                return carry

        else:

            def add(index, carry):
                which, row = index // DEPTHS, index % DEPTHS
                middle[unit, which, row] = add_low(total[unit, layer, row, which], from_layer[unit, row, which])
                return carry

        lax.fori_loop(0, 2 * DEPTHS, add, 0)
        copies.start(("last", unit))

    def along_depth(unit):
        copies.arrived(("last", unit))
        kept = layer if layer_first(unit) else side
        ending[unit] = add_low(middle[unit, kept], from_last[unit])
        copies.start(*[("deep", unit, away_by) for away_by in range(1, DEPTHS)])

    def finish(unit):
        whole = ending[unit, depth].astype(FULL)
        for away_by in range(1, DEPTHS):
            copies.arrived(("deep", unit, away_by))
            whole = whole + from_depth[unit, away_by - 1].astype(FULL)
        if unit < EXPAND:
            cross[:, columns(unit - CROSS)] = whole
        elif unit < BLOCKS:
            expand[:, columns(unit - EXPAND)] = whole
        else:
            contract[columns(unit - BLOCKS, UNIT), :] = whole

    def steps():
        gap, ahead = SCATTER_GAP, SCATTER_AHEAD

        def one(number):
            if ahead <= number + ahead < UNITS:
                begin(ORDER[number + ahead])
            if number < UNITS:
                cross_first(ORDER[number])
            if 0 <= number - gap < UNITS:
                cross_last(ORDER[number - gap])
            if 0 <= number - 2 * gap < UNITS:
                along_depth(ORDER[number - 2 * gap])
            if 0 <= number - 3 * gap < UNITS:
                finish(ORDER[number - 3 * gap])

        return [partial(one, number) for number in range(UNITS + 3 * gap)]

    def fetch(index):
        slot = (index + count) % steps_in_all
        return pltpu.make_async_copy(
            rows.at[row_of(layer, slot, count)], streams.at[index % 2], fetched.at[index % 2]
        )

    def store(index):
        slot = (index + count) % steps_in_all
        return pltpu.make_async_copy(
            value.at[index % 2], gradient.at[row_of(layer, slot, count)], stored.at[index % 2]
        )

    take = pltpu.make_async_copy(kept_delta, deltas.at[pl.ds(0, count)], delta_done)

    @pl.when(step == 0)
    def _():
        take.start()
        fetch(step).start()
        sums[...] = jnp.zeros(sums.shape, FULL)
        own_gain[...] = jnp.zeros(own_gain.shape, FULL)
        place.greet()
        for number in range(SCATTER_AHEAD):
            begin(ORDER[number])
        copies.start(*[("delta", slot) for slot in range(count)])
        copies.start(("gain", 0))
        take.wait()

    for slot in range(count):

        @pl.when(step == count + slot)
        def _(slot=slot):
            copies.arrived(("delta", slot))

    plan = Plan(SCATTER_RATE, HOOKS)
    plan.fill(steps(), steps_in_all)

    @pl.when(step + 1 < steps_in_all)
    def _():
        fetch(step + 1).start()

    fetch(step).wait()
    delta, delta_gain = self_back(
        deltas[step], streams[step % 2].astype(FULL), gains[layer, 0:1, :],
        lambda unit: own_square[unit].reshape(D, D),
        triple.at[0], shares.at[0], inverse.at[0], result.at[0], delta_triple, sums, plan.hook,
    )
    own_gain[0:1, :] += delta_gain

    @pl.when(step >= 2)
    def _():
        store(step).wait()

    value[step % 2] = delta
    store(step).start()
    plan.hook()

    @pl.when(step == steps_in_all - 1)
    def _():
        for unit in range(SELFS):
            low_sums[unit] = sums[unit].astype(LOW).reshape(DEPTHS, SIDES, CORES, UNIT, D)
            copies.start(("own core", unit))
        copies.arrived(("gain", 0))
        whole = gain_sums[layer] + gain_from_layer[...] + own_gain[...]
        for row in range(DEPTHS):
            gain_total[0, row] = whole[:, 128 * row : 128 * (row + 1)]
        copies.start(("gain", 1))
        for unit in range(SELFS):
            copies.arrived(("own core", unit))

            def add(row, carry):
                own_total[unit, row] = add_low(low_sums[unit, row, :, core], own_from_core[unit, row])
                return carry

            lax.fori_loop(0, DEPTHS, add, 0)
            copies.start(("own side", unit))
        copies.arrived(("gain", 1))
        gain_total[1] = gain_total[0] + gain_parts[0]
        copies.start(("gain", 2))
        for unit in range(SELFS):
            copies.arrived(("own side", unit))
            own_middle[unit] = add_low(own_total[unit, :, side], own_from_side[unit])
            copies.start(*[("own deep", unit, away_by) for away_by in across])
        copies.arrived(("gain", 2))
        gain_total[2] = gain_total[1] + gain_parts[1]
        copies.start(*[("gain", 2 + away_by) for away_by in across])
        for unit in range(SELFS):
            whole = own_middle[unit, depth].astype(FULL)
            for away_by in range(1, DEPTHS):
                copies.arrived(("own deep", unit, away_by))
                whole = whole + own_from_depth[unit, away_by - 1].astype(FULL)
            if unit < OUT:
                attention_in[:, columns(unit)] = whole
            else:
                attention_out[...] = whole
        whole = gain_total[2, depth]
        for away_by in range(1, DEPTHS):
            copies.arrived(("gain", 2 + away_by))
            whole = whole + gain_parts[2, away_by]
        gain_out[...] = whole
        store(step - 1).wait()
        store(step).wait()
        copies.finish()


def near_back(kept_delta, sent_delta, rows, own_square, gains, kept, square_sums, tall_sums, gain_sums):
    count, total = kept_delta.shape[0], rows.shape[0]
    dma = pltpu.SemaphoreType.DMA
    vmem = pl.BlockSpec(memory_space=pltpu.VMEM)
    shapes = kept_shapes()[:4]

    def rotated(*shape):
        return pl.BlockSpec((1,) + shape, lambda step: ((step + count) % total,) + (0,) * len(shape))

    weight_shapes = [(UNIT, 3 * D), (UNIT, D), (UNIT, 2 * D), (UNIT, FF), (SLABS * UNIT, D), (8, 128)]
    low = lambda *shape: pltpu.VMEM(shape, LOW)
    full = lambda *shape: pltpu.VMEM(shape, FULL)
    gradient, *weights, gain = pl.pallas_call(
        near_back_kernel,
        grid=(total,),
        in_specs=[ANYWHERE, ANYWHERE, ANYWHERE, constant(SELFS, DEPTHS, SIDES, CORES, UNIT, D), constant(2, 8, D)]
        + [rotated(*shape) for shape, _ in shapes]
        + [ANYWHERE, ANYWHERE, constant(2, 8, D)],
        out_specs=[ANYWHERE] + [pl.BlockSpec(shape, lambda step: (0, 0)) for shape in weight_shapes],
        out_shape=[shape_of((total, ROW, D), FULL)] + [shape_of(shape, FULL) for shape in weight_shapes],
        scratch_shapes=[
            low(total, ROW, D), low(2, ROW, D), full(2, ROW, D), low(ROW, 3 * D), full(SELFS, D, D),
            low(SELFS, DEPTHS, SIDES, CORES, UNIT, D), full(8, D),
            low(UNITS, 2, DEPTHS, SIDES, UNIT, D), low(UNITS, 2, DEPTHS, SIDES, UNIT, D),
            low(UNITS, 2, DEPTHS, UNIT, D), low(UNITS, DEPTHS, 2, UNIT, D), low(UNITS, 2, DEPTHS, UNIT, D),
            low(UNITS, DEPTHS, UNIT, D), low(UNITS, DEPTHS, UNIT, D), low(UNITS, 3, UNIT, D),
            low(SELFS, DEPTHS, SIDES, UNIT, D), low(SELFS, DEPTHS, SIDES, UNIT, D),
            low(SELFS, DEPTHS, UNIT, D), low(SELFS, DEPTHS, UNIT, D), low(SELFS, 3, UNIT, D),
            full(3, DEPTHS, 8, 128), full(3, DEPTHS, 8, 128), full(8, D),
            dma, dma((count,)), dma((count,)), dma((2,)), dma((2,)),
            dma((UNITS, 2)), dma((UNITS, 2)), dma((UNITS, 2)), dma((UNITS,)), dma((UNITS,)), dma((UNITS,)),
            dma((UNITS,)), dma((UNITS, 3)), dma((UNITS, 3)),
            dma((SELFS, 5)), dma((SELFS, 5)), dma((6,)), dma((6,)),
        ],
        compiler_params=pltpu.CompilerParams(
            vmem_limit_bytes=VMEM_LIMIT, collective_id=1, has_side_effects=True
        ),
        name="self_back",
    )(
        kept_delta, sent_delta, rows, own_square, gains, *kept[:4],
        square_sums.reshape(2, BLOCKS, DEPTHS, SIDES, CORES, UNIT, D),
        tall_sums.reshape(2, DEPTHS, SIDES, CORES, SLABS, UNIT, D), gain_sums,
    )
    start = lax.axis_index("dp") % 4 * UNIT
    return gradient, *weights, lax.dynamic_slice_in_dim(gain[:3], start, UNIT, axis=1)


def far_self_kernel(
    source_counts, target_counts, rows, square, gains, triple, shares, inverse, result, first, bias
):
    layer, step, count = lax.axis_index("pipe"), pl.program_id(0), pl.num_programs(0) // 2
    row = row_of(layer, step, count)
    causal = layer == 1
    both = [jnp.where(causal, target_counts[row, piece], source_counts[row, piece]) for piece in range(PACK)]
    fill_bias(bias, *segments(both), causal)
    first[0] = self_forward(
        rows[0].astype(FULL), gains[layer, 0:1, :], lambda unit: square[unit], bias,
        triple.at[0], shares.at[0], inverse.at[0], result.at[0], no_hook,
    )


def far_self(source_counts, target_counts, square, gains, rows):
    total = rows.shape[0]
    kept = kept_shapes()
    return pl.pallas_call(
        far_self_kernel,
        grid=(total,),
        in_specs=[SCALARS, SCALARS, per_row(ROW, D), constant(SELFS, D, D), constant(2, 8, D)],
        out_specs=[per_row(*shape) for shape, _ in kept],
        out_shape=[shape_of((total,) + shape, kind) for shape, kind in kept],
        scratch_shapes=[pltpu.VMEM((ROW, ROW), FULL)],
        compiler_params=PARAMS,
        name="self_forward",
    )(source_counts, target_counts, rows, square, gains)


def far_back_kernel(
    deltas, rows, square, gains, triple, shares, inverse, result, gradient, sums, gain_out, delta_triple
):
    layer, step = lax.axis_index("pipe"), pl.program_id(0)

    @pl.when(step == 0)
    def _():
        sums[...] = jnp.zeros(sums.shape, FULL)
        gain_out[...] = jnp.zeros(gain_out.shape, FULL)

    delta, delta_gain = self_back(
        deltas[0], rows[0].astype(FULL), gains[layer, 0:1, :], lambda unit: square[unit],
        triple.at[0], shares.at[0], inverse.at[0], result.at[0], delta_triple, sums, no_hook,
    )
    gain_out[0:1, :] += delta_gain
    gradient[0] = delta


def far_back(deltas, rows, square, gains, kept):
    total = rows.shape[0]
    return pl.pallas_call(
        far_back_kernel,
        grid=(total,),
        in_specs=[per_row(ROW, D), per_row(ROW, D), constant(SELFS, D, D), constant(2, 8, D)]
        + [per_row(*shape) for shape, _ in kept_shapes()[:4]],
        out_specs=[per_row(ROW, D), constant(SELFS, D, D), constant(8, D)],
        out_shape=[shape_of((total, ROW, D), FULL), shape_of((SELFS, D, D), FULL), shape_of((8, D), FULL)],
        scratch_shapes=[pltpu.VMEM((ROW, 3 * D), LOW)],
        compiler_params=PARAMS,
        name="self_back",
    )(deltas, rows, square, gains, *kept[:4])


def spotsof(value):
    return [value[:, start : start + D] for start in range(0, value.shape[1], D)]


def gather_all(value, axes):
    return lax.all_gather(value, axes, axis=0, tiled=False)


def far_weights(weights, gains, shards):
    attention_in, attention_out, cross, expand, contract = (value.astype(LOW) for value in weights)
    both = ("pipe", "dp")
    own = jnp.stack(spotsof(attention_in) + [attention_out])
    own = jnp.swapaxes(gather_all(own, "dp"), 0, 1).reshape(SELFS, D, D)
    square = gather_all(jnp.stack(spotsof(cross) + spotsof(expand)), both)
    square = jnp.swapaxes(square.reshape(2, shards, BLOCKS, D // shards, D), 1, 2)
    tall = gather_all(contract, both)
    gains = gather_all(gains.astype(LOW), both).reshape(2, shards, 3, D // shards)
    gains = jnp.swapaxes(gains, 1, 2).reshape(2, 3, D).astype(FULL)
    return own, square.reshape(2, BLOCKS, D, D), tall.reshape(2, FF, D), jnp.pad(gains, ((0, 0), (0, 5), (0, 0)))


def scattered(value, axes):
    return lax.psum_scatter(value, axes, scatter_dimension=0, tiled=False).astype(FULL)


def far_sums(own, own_gain, square, tall, gains, section, shards):
    both = ("pipe", "dp")
    share = D // shards
    own = scattered(jnp.swapaxes(own.reshape(SELFS, shards, share, D), 0, 1), "dp")
    square = jnp.swapaxes(square.reshape(2, BLOCKS, shards, share, D), 1, 2)
    square = scattered(square.reshape(2 * shards, BLOCKS, share, D), both)
    tall = scattered(tall.reshape(2 * shards, FF // shards, D), both)
    gains = gains + jnp.where(jnp.arange(2)[:, None, None] == section, own_gain[None], 0.0)
    gains = jnp.swapaxes(gains[:, :3].reshape(2, 3, shards, share), 1, 2)
    gains = scattered(gains.reshape(2 * shards, 3, share), both)

    def joined(value, first, last):
        return jnp.concatenate([value[block] for block in range(first, last)], axis=1)

    return (
        joined(own, QKV, OUT), own[OUT], joined(square, CROSS, EXPAND), joined(square, EXPAND, BLOCKS), tall, gains
    )


def swap(value):
    return lax.ppermute(value, "pipe", [(0, 1), (1, 0)])


def local(
    section_input,
    attention_in,
    attention_out,
    cross_weights,
    expand,
    contract,
    norm_gains,
    source_lengths,
    target_lengths,
    cotangent,
):
    section = lax.axis_index("pipe")
    shards = lax.axis_size("dp")
    near = shards == DEPTHS * SIDES * CORES
    rows = section_input[0]
    count = rows.shape[0] // 2
    weights = tuple(value[0] for value in (attention_in, attention_out, cross_weights, expand, contract))
    if near:
        square, tall, own_square, gains, away, kept = near_self(
            source_lengths, target_lengths, weights, norm_gains[0], rows
        )
    else:
        turn = jnp.where(section == 0, count, 0)
        own_square, square, tall, gains = far_weights(weights, norm_gains[0], shards)
        slots = jnp.roll(rows, turn, axis=0)
        kept = far_self(source_lengths, target_lengths, own_square, gains, slots)
        away = swap(kept[-1][:count].astype(LOW))
    section_output, sent_output, kept_delta, sent_delta, square_sums, tall_sums, gain_sums = middle(
        source_lengths, target_lengths, kept[-1], away, cotangent, square, tall, gains
    )
    away_output = swap(sent_output)
    if near:
        gradient, *weight_sums = near_back(
            kept_delta, sent_delta, rows, own_square, gains, kept, square_sums, tall_sums, gain_sums
        )
    else:
        deltas = jnp.concatenate([swap(sent_delta), kept_delta], axis=0)
        gradient, own_sums, own_gain = far_back(deltas, slots, own_square, gains, kept)
        gradient = jnp.roll(gradient, -turn, axis=0)
        weight_sums = far_sums(own_sums, own_gain, square_sums, tall_sums, gain_sums, section, shards)
    section_output = lax.dynamic_update_slice_in_dim(
        section_output, away_output.astype(FULL), count * (1 - section), axis=0
    )
    return (section_output[None], gradient[None]) + tuple(value[None] for value in weight_sums)


def solution(mesh):
    in_specs = (
        P("pipe", "dp", None, None),
        P("pipe", "dp", None),
        P("pipe", "dp", None),
        P("pipe", "dp", None),
        P("pipe", "dp", None),
        P("pipe", "dp", None),
        P("pipe", None, "dp"),
        P("dp", None),
        P("dp", None),
        P("dp", None, None),
    )
    out_specs = (
        P("pipe", "dp", None, None),
        P("pipe", "dp", None, None),
        P("pipe", "dp", None),
        P("pipe", "dp", None),
        P("pipe", "dp", None),
        P("pipe", "dp", None),
        P("pipe", "dp", None),
        P("pipe", None, "dp"),
    )
    return jax.shard_map(local, mesh=mesh, in_specs=in_specs, out_specs=out_specs, check_vma=False)
```

```python
from functools import partial
import math

import jax
import jax.numpy as jnp
from jax import lax
from jax.experimental import pallas as pl
from jax.experimental.pallas import tpu as pltpu
from jax.sharding import PartitionSpec as P

D = 512
HEADS = 8
HD = 64
FF = 2048
ROW = 512
PAIRS = HEADS // 2
PACK = 4

QKV, OUT, SELFS = 0, 3, 4
CROSS, EXPAND, BLOCKS = 0, 2, 6
SLABS = FF // D
UNITS = BLOCKS + SLABS

EPSILON = 1e-05
MASKED = -1e30
LOG2E = math.log2(math.e)
EXPONENT = HD**-0.5 * LOG2E
BELL = 1.0 / math.sqrt(2.0 * math.pi)
LOW = jnp.bfloat16
FULL = jnp.float32
VMEM_LIMIT = 63 * 2**20

NN = (((1,), (0,)), ((), ()))
NT = (((1,), (1,)), ((), ()))
TN = (((0,), (0,)), ((), ()))


def multiply(left, right, dims=NN):
    return lax.dot_general(left, right, dims, preferred_element_type=jnp.float32)


def columns(index, width=D):
    return pl.ds(index * width, width)


def normalize(stream):
    centred = stream - jnp.mean(stream, axis=1, keepdims=True)
    scale = lax.rsqrt(jnp.mean(centred * centred, axis=1, keepdims=True) + EPSILON)
    return centred * scale, scale


def norm_back(unit, scale, gain, delta):
    inner = delta * gain
    mean = jnp.mean(inner, axis=1, keepdims=True)
    along = jnp.mean(inner * unit, axis=1, keepdims=True)
    return scale * (inner - mean - unit * along), jnp.sum(delta * unit, axis=0, keepdims=True)


def segment(counts, shape, axis):
    places = lax.broadcasted_iota(jnp.int32, shape, axis)
    end = counts[0]
    found = (places >= end).astype(jnp.int32)
    for count in counts[1:]:
        end = end + count
        found = found + (places >= end).astype(jnp.int32)
    return found


def segments(counts):
    return segment(counts, (ROW, 1), 0), segment(counts, (1, ROW), 1)


def fill_bias(bias, query_segment, key_segment, causal=None):
    keep = query_segment == key_segment
    if causal is not None:
        query = lax.broadcasted_iota(jnp.int32, (ROW, ROW), 0)
        key = lax.broadcasted_iota(jnp.int32, (ROW, ROW), 1)
        keep = keep & (key <= query + jnp.where(causal, 0, ROW))
    bias[...] = jnp.where(keep, 0.0, MASKED).astype(bias.dtype)


def lanes():
    return lax.broadcasted_iota(jnp.int32, (1, 2 * HD), 1)


def only_half(value, half):
    return jnp.where(lanes() // HD == half, value, jnp.zeros_like(value))


def attend(query, keys, values, bias, shares, inverse, result, hook):
    kept = jnp.zeros((ROW, 2 * HD), FULL)
    for pair in range(PAIRS):
        query2, keys2, values2 = query(pair), keys(pair), values(pair)
        parts = []
        for half in range(2):
            head = 2 * pair + half
            scores = multiply(only_half(query2, half), keys2, NT) + bias[...]
            top = jnp.max(scores, axis=1, keepdims=True)
            weights = jnp.exp2((scores - top) * EXPONENT)
            scale = 1.0 / jnp.sum(weights, axis=1, keepdims=True)
            low = weights.astype(LOW)
            shares[head] = low
            parts.append(multiply(low, values2) * scale)
            kept = jnp.where(lanes() == head, scale, kept)
        result[:, columns(pair, 2 * HD)] = jnp.where(lanes() < HD, parts[0], parts[1]).astype(LOW)
        hook()
    inverse[...] = kept


def attend_back(query, keys, values, shares, inverse, result, delta, put, hook):
    for pair in range(PAIRS):
        query2, keys2, values2 = query(pair), keys(pair), values(pair)
        place = slice(2 * HD * pair, 2 * HD * (pair + 1))
        scale = jnp.where(
            lanes() < HD, inverse[:, 2 * pair : 2 * pair + 1], inverse[:, 2 * pair + 1 : 2 * pair + 2]
        )
        low = (delta[:, place] * scale).astype(LOW)
        product = low.astype(FULL) * result[:, columns(pair, 2 * HD)].astype(FULL)
        query_turned, low_turned = query2.T, low.T
        delta_query = 0.0
        delta_keys, delta_values = [], []
        for half in range(2):
            weights = shares[2 * pair + half]
            along = jnp.sum(only_half(product, half), axis=1, keepdims=True)
            delta_shares = multiply(only_half(low, half), values2, NT)
            delta_scores = (weights.astype(FULL) * (delta_shares - along)).astype(LOW)
            delta_query = delta_query + multiply(delta_scores, only_half(keys2, half))
            own = slice(HD * half, HD * (half + 1))
            delta_keys.append(multiply(query_turned[own], delta_scores))
            delta_values.append(multiply(low_turned[own], weights))
        keys_turned = (jnp.concatenate(delta_keys, axis=0) * HD**-0.5).astype(LOW)
        values_turned = jnp.concatenate(delta_values, axis=0).astype(LOW)
        put(pair, (delta_query * HD**-0.5).astype(LOW), keys_turned.T, values_turned.T)
        hook()


def self_parts(triple):
    return tuple(
        (lambda pair, start=part * PAIRS: triple[:, columns(start + pair, 2 * HD)]) for part in range(3)
    )


def put_triple(target):
    def put(pair, *parts):
        for part, value in enumerate(parts):
            target[:, columns(part * PAIRS + pair, 2 * HD)] = value

    return put


def feed(normed, stream, expand, contract, active, slope, hook):
    total = stream
    for slab in range(SLABS):
        hidden = multiply(normed, expand(slab))
        under = 0.5 + 0.5 * lax.erf(hidden * math.sqrt(0.5))
        bell = BELL * jnp.exp2(hidden * hidden * (-0.5 * LOG2E))
        low = (hidden * under).astype(LOW)
        active[:, columns(slab)] = low
        slope[:, columns(slab)] = (under + hidden * bell).astype(LOW)
        total = total + multiply(low, contract(slab))
        hook()
    return total


def feed_back(delta, stream, gain, expand, contract, change):
    unit, scale = normalize(stream)
    low = delta.astype(LOW)
    delta_normed = 0.0
    for slab in range(SLABS):
        delta_active = multiply(low, contract(slab), NT)
        delta_hidden = (delta_active * change[:, columns(slab)].astype(FULL)).astype(LOW)
        change[:, columns(slab)] = delta_hidden
        delta_normed = delta_normed + multiply(delta_hidden, expand(slab), NT)
    delta_stream, delta_gain = norm_back(unit, scale, gain, delta_normed)
    return delta + delta_stream, delta_gain


def self_forward(stream, gain, square, bias, triple, shares, inverse, result, hook):
    normed = (normalize(stream)[0] * gain).astype(LOW)
    for part in range(3):
        triple[:, columns(part)] = multiply(normed, square(QKV + part)).astype(LOW)
    hook()
    attend(*self_parts(triple), bias, shares, inverse, result, hook)
    return stream + multiply(result[...], square(OUT))


def self_back(low, stream, gain, square, triple, shares, inverse, result, delta_triple, sums, hook):
    unit, scale = normalize(stream)
    sums[OUT] += multiply(result[...], low, TN)
    delta_result = multiply(low, square(OUT), NT)
    hook()
    attend_back(*self_parts(triple), shares, inverse, result, delta_result, put_triple(delta_triple), hook)
    turned = (unit * gain).astype(LOW).T
    delta_normed = 0.0
    for part in range(3):
        chunk = delta_triple[:, columns(part)]
        sums[QKV + part] += multiply(turned, chunk)
        delta_normed = delta_normed + multiply(chunk, square(QKV + part), NT)
    delta_stream, delta_gain = norm_back(unit, scale, gain, delta_normed)
    return low.astype(FULL) + delta_stream, delta_gain


def no_hook():
    pass


def per_row(*shape, last=None, start=0, buffers=2):
    def index(row):
        return (start + (row if last is None else jnp.minimum(row, last)),) + (0,) * len(shape)

    return pl.BlockSpec((1,) + shape, index, pipeline_mode=pl.Buffered(buffers) if buffers != 2 else None)


def constant(*shape):
    return pl.BlockSpec(shape, lambda row: (0,) * len(shape), pipeline_mode=pl.Buffered(1))


ANYWHERE = pl.BlockSpec(memory_space=pl.ANY)
SCALARS = pl.BlockSpec(memory_space=pltpu.SMEM)
PARAMS = pltpu.CompilerParams(vmem_limit_bytes=VMEM_LIMIT)


def shape_of(shape, kind):
    return jax.ShapeDtypeStruct(shape, kind)


MESH = pl.DeviceIdType.MESH
UNITS = BLOCKS + SLABS
UNIT = 32
DEPTHS, SIDES, CORES = 4, 2, 2


class Place:
    def __init__(self):
        self.layer = lax.axis_index("pipe")
        self.rank = lax.axis_index("dp")
        self.core = self.rank % CORES
        self.side = self.rank // CORES % SIDES
        self.depth = self.rank // (CORES * SIDES)

    def sibling(self):
        return (self.layer, self.rank + 1 - 2 * self.core)

    def across_side(self):
        return (self.layer, self.rank + CORES * (1 - 2 * self.side))

    def across_layer(self):
        return (1 - self.layer, self.rank)

    def other_depth(self, step):
        return (self.depth + step) % DEPTHS

    def along_depth(self, step):
        return (self.layer, self.rank + CORES * SIDES * (self.other_depth(step) - self.depth))

    def greet(self):
        partners = [self.sibling(), self.across_side(), self.across_layer()]
        partners += [self.along_depth(step) for step in range(1, DEPTHS)]
        barrier = pltpu.get_barrier_semaphore()
        for partner in partners:
            pl.semaphore_signal(barrier, inc=1, device_id=partner, device_id_type=MESH)
        pl.semaphore_wait(barrier, len(partners))


def layer_first(unit):
    return unit % 2 == 0


def row_of(layer, slot, count):
    return (slot + count * (1 - layer)) % (2 * count)


class Plan:
    def __init__(self, rate, hooks):
        self.rate, self.hooks = rate, hooks
        self.steps = {}
        self.index = 0

    def fill(self, thunks, rows):
        for number, thunk in enumerate(thunks):
            place = min(int(number * self.rate), rows * self.hooks - 1)
            self.steps.setdefault(divmod(place, self.hooks), []).append(thunk)

    def hook(self, step):
        index, self.index = self.index, self.index + 1
        for (row, place), thunks in sorted(self.steps.items(), key=lambda item: item[0]):
            if place == index:

                @pl.when(step == row)
                def _(thunks=thunks):
                    for thunk in thunks:
                        thunk()


class Copies:
    def __init__(self):
        self.made = {}

    def define(self, key, parts):
        def make():
            source, target, sent, arrived, device = parts()
            return pltpu.make_async_remote_copy(
                src_ref=source, dst_ref=target, send_sem=sent, recv_sem=arrived, device_id=device,
                device_id_type=MESH,
            )

        self.made[key] = make

    def start(self, *keys):
        for key in keys:
            self.made[key]().start()

    def arrived(self, *keys):
        for key in keys:
            self.made[key]().wait_recv()

    def finish(self, *keys):
        for key in keys or self.made:
            self.made[key]().wait_send()


class Spread:
    LAYER, SIDE, CORE, RELAY = 3, 4, 5, 6

    def __init__(self, place, copies, units, sent, done, kept):
        self.place, self.copies, self.units = place, copies, units
        self.sent, self.done, self.kept = sent, done, kept
        for number in range(len(units)):
            for stage in range(self.RELAY + DEPTHS - 1):
                copies.define((self, number, stage), partial(self.parts, number, stage))

    def parts(self, number, stage):
        place, (_, source, spot) = self.place, self.units[number]
        own, slot = spot(place.depth, place.side, place.core), stage
        if stage < self.LAYER:
            block, target, device = source(), own, place.along_depth(stage + 1)
        elif stage == self.LAYER:
            block, target, device = source(), own, place.across_layer()
        elif stage == self.SIDE:
            block = target = spot(slice(None), place.side, place.core)
            device = place.across_side()
        elif stage == self.CORE:
            block = target = spot(slice(None), slice(None), place.core)
            device = place.sibling()
        else:
            slot = stage - self.RELAY
            block, target, device = own, own, place.along_depth(slot + 1)
        return block, target, self.sent.at[number, slot], self.done.at[number, slot], device

    def keys(self, number, *stages):
        return [(self, number, stage) for stage in stages]

    def along(self, number):
        return self.keys(number, *range(DEPTHS - 1))

    def relayed(self, number):
        return self.keys(number, *range(self.RELAY, self.RELAY + DEPTHS - 1))

    def keep(self, number):
        _, source, spot = self.units[number]
        place = self.place
        return pltpu.make_async_copy(source(), spot(place.depth, place.side, place.core), self.kept.at[number])

    def owned(self, number):
        return pl.when(self.place.layer == self.units[number][0])

    def begin(self, number):
        @self.owned(number)
        def _():
            self.copies.start(*self.keys(number, self.LAYER))
            self.copies.start(*self.along(number))
            self.keep(number).start()

    def relay(self, number):
        @pl.when(self.place.layer != self.units[number][0])
        def _():
            self.copies.arrived(*self.keys(number, self.LAYER))
            self.copies.start(*self.relayed(number))

    def cross(self, number):
        @self.owned(number)
        def _():
            self.keep(number).wait()

        self.copies.arrived(*self.along(number))
        self.copies.start(*self.keys(number, self.SIDE))

    def share(self, number):
        self.copies.arrived(*self.keys(number, self.SIDE))
        self.copies.start(*self.keys(number, self.CORE))

    def end(self, number):
        self.copies.arrived(*self.keys(number, self.CORE))

    def finish(self):
        for number in range(len(self.units)):

            @self.owned(number)
            def _(number=number):
                self.copies.finish(*self.keys(number, self.LAYER))

            self.copies.finish(*self.along(number), *self.keys(number, self.SIDE, self.CORE))

    def steps(self, ahead, gap):
        def one(number):
            if ahead <= number + ahead < len(self.units):
                self.begin(number + ahead)
            if ahead - 1 <= number + ahead - 1 < len(self.units):
                self.relay(number + ahead - 1)
            if number < len(self.units):
                self.cross(number)
            if 0 <= number - gap < len(self.units):
                self.share(number - gap)

        return [partial(one, number) for number in range(len(self.units) + gap)]


GATHER_RATE, GATHER_AHEAD, GATHER_GAP, GATHER_EARLY = 2.0, 4, 3, 4
GATHER_ORDER = tuple((0, unit) for unit in (2, 3, 4, 5, 6, 7, 8, 9, 0, 1)) + ((1, 0), (1, 1))
MIDDLE_RATE, MIDDLE_AHEAD, MIDDLE_GAP = 1.4, 8, 3
MIDDLE_ORDER = (4, 5, 6, 7, 0, 1, 2, 3)
MIDDLE_HOOKS = SLABS + PAIRS + 1
SCATTER_RATE, SCATTER_AHEAD, SCATTER_GAP = 1.4, 3, 2
ORDER = (2, 3, 4, 5, 6, 7, 8, 9, 0, 1)
HOOKS = PAIRS + 2


def near_self_kernel(
    source_counts, target_counts, attention_in, attention_out, cross, expand, contract, gains, rows,
    square, tall, target_cross, own_rest, own_square, every_gain, away, triple, shares, inverse, result, first,
    blocks, tiles, streams, sending, bias, own,
    fetched, block_sent, block_done, block_out, tile_sent, tile_done, rest_out,
    spread_sent, spread_done, spread_kept, away_sent, away_done,
):
    place = Place()
    layer, depth, side, core = place.layer, place.depth, place.side, place.core
    step, total = pl.program_id(0), 2 * away.shape[0]
    count = away.shape[0]
    copies = Copies()
    selfs = [attention_in.at[:, columns(j)] for j in range(3)] + [attention_out]
    sources = [cross.at[:, columns(j)] for j in range(2)] + [expand.at[:, columns(j)] for j in range(SLABS)]
    sources += [contract.at[columns(j, UNIT), :] for j in range(SLABS)]

    def source_spot(unit, *index):
        if unit < BLOCKS:
            return square.at[(unit,) + index]
        return tall.at[index + (unit - BLOCKS,)]

    def target_spot(unit, *index):
        return target_cross.at[(unit,) + index]

    units = [
        (owner, partial(own.at.__getitem__, unit), partial((source_spot, target_spot)[owner], unit))
        for owner, unit in GATHER_ORDER
    ]
    spread = Spread(place, copies, units, spread_sent, spread_done, spread_kept)
    rest = pltpu.make_async_copy(own.at[pl.ds(2, UNITS - 2)], own_rest, rest_out)

    def away_parts(slot):
        return sending.at[slot], away.at[slot], away_sent.at[slot], away_done.at[slot], place.across_layer()

    def block_parts(unit, stage):
        if stage == 0:
            block, target = blocks.at[unit, :, :, core], place.sibling()
        elif stage < DEPTHS:
            block, target = blocks.at[unit, depth, side, core], place.along_depth(stage)
        else:
            block, target = blocks.at[unit, :, side, core], place.across_side()
        return block, block, block_sent.at[unit, stage], block_done.at[unit, stage], target

    def tile_parts(stage):
        if stage == 0:
            block, target = tiles.at[layer], place.across_layer()
        elif stage < DEPTHS:
            block, target = tiles.at[layer, depth, side, core], place.along_depth(stage)
        elif stage == DEPTHS:
            block, target = tiles.at[layer, :, side, core], place.across_side()
        else:
            block, target = tiles.at[layer, :, :, core], place.sibling()
        return block, block, tile_sent.at[stage], tile_done.at[stage], target

    for stage in range(DEPTHS + 2):
        copies.define(("tile", stage), partial(tile_parts, stage))
    for unit in range(SELFS):
        for stage in range(DEPTHS + 1):
            copies.define(("block", unit, stage), partial(block_parts, unit, stage))
    for slot in range(count):
        copies.define(("away", slot), partial(away_parts, slot))

    def lay_gains(which):
        for row in range(DEPTHS):
            value = tiles[which, row, 0, 0].astype(FULL)
            for other in ((0, 1), (1, 0), (1, 1)):
                value = value + tiles[(which, row) + other].astype(FULL)
            every_gain[which, :, columns(row, 128)] = value[:8]

    def fetch(slot):
        return pltpu.make_async_copy(
            rows.at[row_of(layer, slot, count)], streams.at[slot % 2], fetched.at[slot % 2]
        )

    @pl.when(step == 0)
    def _():
        fetch(step).start()
        for unit in range(SELFS):
            blocks[unit, depth, side, core] = selfs[unit][...].astype(LOW)
        for unit in range(UNITS):
            own[unit] = sources[unit][...].astype(LOW)
        rest.start()
        tiles[layer, depth, side, core] = gains[...]
        place.greet()
        across = range(1, DEPTHS)
        early = iter(spread.steps(GATHER_AHEAD, GATHER_GAP)[:GATHER_EARLY])
        copies.start(*[("tile", stage) for stage in across])
        for unit in range(SELFS):
            copies.start(*[("block", unit, stage) for stage in across])
        for number in range(GATHER_AHEAD):
            spread.begin(number)
        copies.arrived(*[("tile", stage) for stage in across])
        copies.start(("tile", DEPTHS))
        for number in range(GATHER_AHEAD - 1):
            spread.relay(number)
        for unit in range(SELFS):
            copies.arrived(*[("block", unit, stage) for stage in across])
            copies.start(("block", unit, DEPTHS))
        copies.arrived(("tile", DEPTHS))
        copies.start(("tile", DEPTHS + 1))
        for unit in range(SELFS):
            for _ in range(GATHER_EARLY // SELFS):
                next(early)()
            copies.arrived(("block", unit, DEPTHS))
            copies.start(("block", unit, 0))
        copies.arrived(("tile", DEPTHS + 1))
        copies.start(("tile", 0))
        lay_gains(layer)
        copies.arrived(*[("block", unit, 0) for unit in range(OUT)])

    def last_block():
        copies.arrived(("block", OUT, 0))
        pltpu.make_async_copy(blocks, own_square, block_out).start()

    plan = Plan(GATHER_RATE, HOOKS)
    plan.fill([last_block] + spread.steps(GATHER_AHEAD, GATHER_GAP)[GATHER_EARLY:], total)

    @pl.when(step + 1 < total)
    def _():
        fetch(step + 1).start()

    row = row_of(layer, step, count)
    causal = layer == 1
    both = [jnp.where(causal, target_counts[row, piece], source_counts[row, piece]) for piece in range(PACK)]
    fill_bias(bias, *segments(both), causal)
    fetch(step).wait()
    stream = self_forward(
        streams[step % 2].astype(FULL), every_gain[layer, 0:1, :], lambda unit: blocks[unit].reshape(D, D), bias,
        triple.at[0], shares.at[0], inverse.at[0], result.at[0], partial(plan.hook, step),
    )
    stream = stream.astype(LOW)
    first[0] = stream

    for slot in range(count):

        @pl.when(step == slot)
        def _(slot=slot):
            sending[slot] = stream
            copies.start(("away", slot))

    plan.hook(step)

    @pl.when(step == total - 1)
    def _():
        copies.arrived(("tile", 0))
        lay_gains(1 - layer)
        for number in range(len(units)):
            spread.end(number)
        copies.arrived(*[("away", slot) for slot in range(count)])
        copies.finish(*[("away", slot) for slot in range(count)])
        copies.finish(*[("tile", stage) for stage in range(DEPTHS + 2)])
        copies.finish(*[("block", unit, stage) for unit in range(SELFS) for stage in range(DEPTHS + 1)])
        spread.finish()
        pltpu.make_async_copy(blocks, own_square, block_out).wait()
        rest.wait()


def kept_shapes():
    return [
        ((ROW, 3 * D), LOW), ((HEADS, ROW, ROW), LOW), ((ROW, 2 * HD), FULL), ((ROW, D), LOW), ((ROW, D), LOW)
    ]


def near_self(source_counts, target_counts, weights, gains, rows):
    total = rows.shape[0]
    tile = jnp.tile(gains.astype(LOW), (1, 4))
    lane_part = lax.broadcasted_iota(jnp.int32, tile.shape, 1) // UNIT
    tile = jnp.where(lane_part == lax.axis_index("dp") % 4, tile, jnp.zeros_like(tile))
    tile = jnp.pad(tile, ((0, 16 - tile.shape[0]), (0, 0)))
    dma = pltpu.SemaphoreType.DMA
    kept = kept_shapes()
    outs = [
        shape_of((BLOCKS, DEPTHS, SIDES, CORES, UNIT, D), LOW),
        shape_of((DEPTHS, SIDES, CORES, SLABS, UNIT, D), LOW),
        shape_of((2, DEPTHS, SIDES, CORES, UNIT, D), LOW),
        shape_of((UNITS - 2, UNIT, D), LOW),
        shape_of((SELFS, DEPTHS, SIDES, CORES, UNIT, D), LOW),
        shape_of((2, 8, D), FULL),
        shape_of((total // 2, ROW, D), LOW),
    ]
    square, tall, cross, own_rest, own_square, every_gain, away, *kept = pl.pallas_call(
        near_self_kernel,
        grid=(total,),
        in_specs=[SCALARS, SCALARS] + [constant(*value.shape) for value in weights] + [constant(16, 128), ANYWHERE],
        out_specs=[ANYWHERE] * 5
        + [pl.BlockSpec((2, 8, D), lambda row: (0, 0, 0)), ANYWHERE]
        + [per_row(*shape) for shape, _ in kept],
        out_shape=outs + [shape_of((total,) + shape, kind) for shape, kind in kept],
        scratch_shapes=[
            pltpu.VMEM((SELFS, DEPTHS, SIDES, CORES, UNIT, D), LOW),
            pltpu.VMEM((2, DEPTHS, SIDES, CORES, 16, 128), LOW),
            pltpu.VMEM((2, ROW, D), LOW),
            pltpu.VMEM((total // 2, ROW, D), LOW),
            pltpu.VMEM((ROW, ROW), FULL),
            pltpu.VMEM((UNITS, UNIT, D), LOW),
            dma((2,)), dma((SELFS, 5)), dma((SELFS, 5)), dma, dma((6,)), dma((6,)), dma,
            dma((len(GATHER_ORDER), 6)), dma((len(GATHER_ORDER), 6)), dma((len(GATHER_ORDER),)),
            dma((total // 2,)), dma((total // 2,)),
        ],
        compiler_params=pltpu.CompilerParams(
            vmem_limit_bytes=VMEM_LIMIT, collective_id=0, has_side_effects=True
        ),
        name="self_forward",
    )(source_counts, target_counts, *weights, tile, rows)
    weights = square.reshape(BLOCKS, D, D), tall.reshape(FF, D), cross.reshape(2, D, D), own_rest
    return weights, own_square, every_gain, away, kept


def middle_kernel(
    near,
    source_counts, target_counts, first, away, cotangent, source_square, source_tall, target_cross, rest, rest_tall,
    gains,
    section_output, sent_output, kept_delta, sent_delta, square_out, tall_out, gain_out, saved_shares, saved_active,
    target_expand, target_contract, bias, shares, inverse, cross_result, source_end, target_mid, value, sending, keeping,
    source_normed, active, memory_low, cross_normed, feed_normed,
    source_change, source_low, delta_pair, delta_question, cross_low, target_change, target_low,
    loaded, stored, kept, spilled, ready, output_sent, output_done, delta_sent, delta_done,
    spread_sent, spread_done, spread_kept,
):
    place = Place()
    layer = place.layer
    count = away.shape[0]
    copies = Copies()

    def source_expand(slab):
        return source_square[EXPAND + slab]

    def source_contract(slab):
        return source_tall[columns(slab), :]

    if near:

        def spot(unit, *index):
            if unit < SLABS:
                return target_expand.at[(unit,) + index]
            return target_contract.at[index + (unit - SLABS,)]

        units = [(1, partial(rest.at.__getitem__, unit), partial(spot, unit)) for unit in MIDDLE_ORDER]
        spread = Spread(place, copies, units, spread_sent, spread_done, spread_kept)

        def expand_of(slab):
            return target_expand[slab].reshape(D, D)

        def contract_of(slab):
            return target_contract[slab].reshape(D, D)

    else:

        def expand_of(slab):
            return target_expand[slab]

        def contract_of(slab):
            return target_contract[columns(slab), :]

        whole_rest = [
            pltpu.make_async_copy(rest, target_expand, spread_kept.at[0]),
            pltpu.make_async_copy(rest_tall, target_contract, spread_kept.at[1]),
        ]

    def rows_of(row):
        return pl.ds(pl.multiple_of(row * ROW, ROW), ROW)

    def load(row):
        return pltpu.make_async_copy(
            cotangent.at[layer * count + row], target_low.at[columns(row, ROW), :], loaded.at[row]
        )

    def store(row):
        return pltpu.make_async_copy(value, section_output.at[layer * count + row], stored)

    def keep(row):
        return pltpu.make_async_copy(keeping.at[row], kept_delta.at[row], kept.at[row])

    class Parcels:
        def __init__(self, name, target, sent, done):
            self.name, self.target, self.sent, self.done = name, target, sent, done
            for row in range(count):
                copies.define((name, row), partial(self.parts, row))

        def parts(self, row):
            return sending.at[row], self.target.at[row], self.sent.at[row], self.done.at[row], place.across_layer()

        def local(self, row):
            return pltpu.make_async_copy(sending.at[row], self.target.at[row], self.sent.at[row])

        def put(self, row, block):
            for static in range(count):

                @pl.when(row == static)
                def _(static=static):
                    sending[static] = block
                    if near:
                        copies.start((self.name, static))
                    else:
                        self.local(static).start()

        def left(self, row):
            for static in range(count):

                @pl.when(row == static)
                def _(static=static):
                    if near:
                        copies.finish((self.name, static))
                    else:
                        self.local(static).wait()

    outputs = Parcels("output", sent_output, output_sent, output_done)
    deltas = Parcels("delta", sent_delta, delta_sent, delta_done)

    def streams(row):
        own, other = first[row].astype(FULL), away[row].astype(FULL)
        return jnp.where(layer == 0, own, other), jnp.where(layer == 0, other, own)

    def publish(row, owner, block):
        @pl.when(layer == owner)
        def _():
            @pl.when(row > 0)
            def _():
                store(row - 1).wait()

            value[...] = block
            store(row).start()

        @pl.when(layer != owner)
        def _():
            outputs.put(row, block.astype(LOW))

    for row in range(count):
        load(row).start()
    gain_out[...] = jnp.zeros(gain_out.shape, FULL)
    if near:
        place.greet()
        for number in range(MIDDLE_AHEAD):
            spread.begin(number)
        for number in range(MIDDLE_AHEAD - 1):
            spread.relay(number)
        plan = Plan(MIDDLE_RATE, MIDDLE_HOOKS)
        plan.fill(spread.steps(MIDDLE_AHEAD, MIDDLE_GAP), count)
    else:
        for copy in whole_rest:
            copy.start()

    def cross_parts(row):
        at = rows_of(row)
        return (
            lambda pair: delta_question[at, columns(pair, 2 * HD)],
            lambda pair: delta_pair[at, columns(pair, 2 * HD)],
            lambda pair: delta_pair[at, columns(PAIRS + pair, 2 * HD)],
        )

    spill = pltpu.make_async_copy(shares, saved_shares, spilled.at[0])
    unspill = pltpu.make_async_copy(saved_shares, shares, spilled.at[0])

    def forward(row, carry):
        at = rows_of(row)
        hook = partial(plan.hook, row) if near else no_hook
        source_stream, target_stream = streams(row)
        whole = layer * count + row
        source_segment = segments([source_counts[whole, piece] for piece in range(PACK)])
        target_segment = segments([target_counts[whole, piece] for piece in range(PACK)])

        normed = (normalize(source_stream)[0] * gains[0, 1:2, :]).astype(LOW)
        source_normed[at, :] = normed
        end = feed(
            normed, source_stream, source_expand, source_contract, active.at[at, :], source_change.at[at, :], hook
        )
        source_end[row] = end
        memory = normalize(end)[0] * gains[0, 2:3, :]
        low = memory.astype(LOW)
        memory_low[at, :] = low
        for part in range(2):
            delta_pair[at, columns(part)] = multiply(low, source_square[CROSS + part]).astype(LOW)
        publish(row, 0, memory)
        hook()

        fill_bias(bias, target_segment[0], source_segment[1])
        normed = (normalize(target_stream)[0] * gains[1, 1:2, :]).astype(LOW)
        cross_normed[at, :] = normed
        delta_question[at, :] = multiply(normed, target_cross[0]).astype(LOW)

        @pl.when(row > 0)
        def _():
            spill.wait()

        result = cross_result.at[at, :]
        attend(*cross_parts(row), bias, shares, inverse.at[row], result, hook)

        @pl.when(row < count - 1)
        def _():
            spill.start()

        target_mid[row] = target_stream + multiply(result[...], target_cross[1])
        return carry

    lax.fori_loop(0, count, forward, 0)
    spill_active = pltpu.make_async_copy(active, saved_active, spilled.at[1])
    unspill_active = pltpu.make_async_copy(saved_active, active, spilled.at[1])
    spill_active.start()
    if near:
        for number in range(SLABS):
            spread.end(number)
    else:
        for copy in whole_rest:
            copy.wait()
    spill_active.wait()

    @pl.when(layer == 0)
    def _():
        store(count - 1).wait()

    def turn(row, carry):
        at = rows_of(row)
        stream = target_mid[row]
        normed = (normalize(stream)[0] * gains[1, 2:3, :]).astype(LOW)
        feed_normed[at, :] = normed
        slabs = iter(range(SLABS))

        def expand_ready(slab):
            if near:

                @pl.when(row == 0)
                def _():
                    spread.end(SLABS + slab)

            return expand_of(slab)

        output = feed(
            normed, stream, expand_ready, contract_of, active.at[at, :], target_change.at[at, :], no_hook
        )
        publish(row, 1, output)
        for static in range(count):

            @pl.when(row == static)
            def _(static=static):
                load(static).wait()

        delta, delta_gain = feed_back(
            target_low[at, :].astype(FULL), stream, gains[1, 2:3, :], expand_of, contract_of, target_change.at[at, :]
        )
        gain_out[1, 2:3, :] += delta_gain
        target_mid[row] = delta
        return carry

    lax.fori_loop(0, count, turn, 0)

    emitted = []

    def emit(block, holder, target):
        holder[...] = block.astype(LOW)
        copy = pltpu.make_async_copy(holder, target, ready.at[len(emitted)])
        copy.start()
        emitted.append(copy)

    def feed_grads(which, normed, change, low):
        turned = normed[...].T
        for slab in range(SLABS):
            grown = multiply(turned, change[:, columns(slab)])
            shrunk = multiply(active[:, columns(slab)], low[...], TN)
            emit(grown, change.at[pl.ds(0, D), columns(slab)], square_out.at[which, EXPAND + slab])
            emit(shrunk, change.at[pl.ds(D, D), columns(slab)], tall_out.at[which, columns(slab), :])

    feed_grads(1, feed_normed, target_change, target_low)
    unspill_active.start()

    def backward(number, carry):
        row = count - 1 - number
        at = rows_of(row)
        source_stream, target_stream = streams(row)

        @pl.when(number > 0)
        def _():
            unspill.wait()

        delta = target_mid[row]
        low = delta.astype(LOW)
        cross_low[at, :] = low
        delta_result = multiply(low, target_cross[1], NT)

        def put(pair, query, keys, values):
            delta_question[at, columns(pair, 2 * HD)] = query
            delta_pair[at, columns(pair, 2 * HD)] = keys
            delta_pair[at, columns(PAIRS + pair, 2 * HD)] = values

        attend_back(
            *cross_parts(row), shares, inverse.at[row], cross_result.at[at, :], delta_result, put, no_hook
        )

        @pl.when(number < count - 1)
        def _():
            unspill.start()

        unit, scale = normalize(target_stream)
        delta_normed = multiply(delta_question[at, :], target_cross[0], NT)
        delta_stream, delta_gain = norm_back(unit, scale, gains[1, 1:2, :], delta_normed)
        gain_out[1, 1:2, :] += delta_gain
        target_delta = (delta + delta_stream).astype(LOW)

        unit, scale = normalize(source_end[row])
        delta_memory = 0.0
        for part in range(2):
            delta_memory = delta_memory + multiply(delta_pair[at, columns(part)], source_square[CROSS + part], NT)
        delta, delta_gain = norm_back(unit, scale, gains[0, 2:3, :], delta_memory)
        gain_out[0, 2:3, :] += delta_gain
        source_low[at, :] = delta.astype(LOW)
        delta, delta_gain = feed_back(
            delta, source_stream, gains[0, 1:2, :], source_expand, source_contract, source_change.at[at, :]
        )
        gain_out[0, 1:2, :] += delta_gain
        source_delta = delta.astype(LOW)
        keeping[row] = jnp.where(layer == 0, source_delta, target_delta)
        for static in range(count):

            @pl.when(row == static)
            def _(static=static):
                keep(static).start()

        outputs.left(row)
        deltas.put(row, jnp.where(layer == 0, target_delta, source_delta))
        return carry

    lax.fori_loop(0, count, backward, 0)
    unspill_active.wait()
    feed_grads(0, source_normed, source_change, source_low)
    turned = memory_low[...].T
    for part in range(2):
        grown = multiply(turned, delta_pair[:, columns(part)])
        emit(grown, delta_pair.at[pl.ds(0, D), columns(part)], square_out.at[0, CROSS + part])
    for part, (left, right) in enumerate(((cross_normed, delta_question), (cross_result, cross_low))):
        emit(multiply(left[...], right[...], TN), right.at[pl.ds(0, D), :], square_out.at[1, CROSS + part])
    for copy in emitted:
        copy.wait()

    @pl.when(layer == 1)
    def _():
        store(count - 1).wait()

    for row in range(count):
        keep(row).wait()
        deltas.left(row)
    if near:
        copies.arrived(*[(name, row) for name in ("output", "delta") for row in range(count)])
        spread.finish()


def middle(near, source_counts, target_counts, first, away, cotangent, weights, gains):
    count = away.shape[0]
    tokens = count * ROW
    dma = pltpu.SemaphoreType.DMA
    low = lambda *shape: pltpu.VMEM(shape, LOW)
    full = lambda *shape: pltpu.VMEM(shape, FULL)
    square, tall, cross, rest = weights[:4]
    rest_tall = weights[4] if not near else rest
    if near:
        expand = low(SLABS, DEPTHS, SIDES, CORES, UNIT, D)
        contract = low(DEPTHS, SIDES, CORES, SLABS, UNIT, D)
    else:
        expand, contract = low(SLABS, D, D), low(FF, D)
    row_shape = shape_of((count, ROW, D), LOW)
    remote = dict(collective_id=2, has_side_effects=True) if near else {}
    outs = pl.pallas_call(
        partial(middle_kernel, near),
        grid=(1,),
        in_specs=[
            SCALARS, SCALARS,
            pl.BlockSpec((count, ROW, D), lambda step: (1, 0, 0), pipeline_mode=pl.Buffered(1)),
            constant(count, ROW, D), ANYWHERE, constant(BLOCKS, D, D), constant(FF, D), constant(2, D, D),
            ANYWHERE, ANYWHERE, constant(2, 8, D),
        ],
        out_specs=[ANYWHERE] * 6 + [pl.BlockSpec((2, 8, D), lambda step: (0, 0, 0)), ANYWHERE, ANYWHERE],
        out_shape=[shape_of((2 * count, ROW, D), FULL), row_shape, row_shape, row_shape]
        + [shape_of((2, BLOCKS, D, D), LOW), shape_of((2, FF, D), LOW), shape_of((2, 8, D), FULL)]
        + [shape_of((HEADS, ROW, ROW), LOW), shape_of((tokens, FF), LOW)],
        scratch_shapes=[
            expand, contract, low(ROW, ROW), low(HEADS, ROW, ROW), full(count, ROW, 2 * HD), low(tokens, D),
            full(count, ROW, D), full(count, ROW, D), full(ROW, D), low(count, ROW, D), low(count, ROW, D),
            low(tokens, D), low(tokens, FF), low(tokens, D), low(tokens, D), low(tokens, D),
            low(tokens, FF), low(tokens, D), low(tokens, 2 * D), low(tokens, D), low(tokens, D), low(tokens, FF),
            low(tokens, D),
            dma((count,)), dma, dma((count,)), dma((2,)), dma((2 * UNITS,)),
            dma((count,)), dma((count,)), dma((count,)), dma((count,)),
            dma((2 * SLABS, 6)), dma((2 * SLABS, 6)), dma((2 * SLABS,)),
        ],
        compiler_params=pltpu.CompilerParams(vmem_limit_bytes=VMEM_LIMIT, **remote),
        name="middle",
    )(source_counts, target_counts, first, away, cotangent, square, tall, cross, rest, rest_tall, gains)
    return outs[:7]


def add_low(left, right):
    return (left.astype(FULL) + right.astype(FULL)).astype(LOW)


def near_back_kernel(
    kept_delta, away_delta, rows, own_square, gains, triple, shares, inverse, result,
    square_sums, tall_sums, gain_sums,
    gradient, attention_in, attention_out, cross, expand, contract, gain_out,
    deltas, streams, value, delta_triple, sums, low_sums, own_gain,
    total, from_core, from_side, from_layer, middle, from_last, ending, from_depth,
    own_total, own_from_core, own_middle, own_from_side, own_from_depth,
    gain_total, gain_parts, gain_from_layer,
    delta_done, fetched, stored,
    loaded, core_sent, core_done, first_sent, first_done, last_sent, last_done, depth_sent, depth_done,
    own_sent, own_done, gain_sent, gain_done,
):
    place = Place()
    layer, depth, side, core = place.layer, place.depth, place.side, place.core
    count = kept_delta.shape[0]
    step, steps_in_all = pl.program_id(0), 2 * count
    copies = Copies()

    def spot(which, unit, owner):
        if unit < BLOCKS:
            return square_sums.at[which, unit, :, :, owner]
        return tall_sums.at[which, :, :, owner, unit - BLOCKS]

    def load(unit, which):
        return pltpu.make_async_copy(spot(which, unit, core), total.at[unit, which], loaded.at[unit, which])

    def core_parts(unit, which):
        slot = (unit, which)
        return (
            spot(which, unit, 1 - core), from_core.at[slot], core_sent.at[slot], core_done.at[slot], place.sibling()
        )

    def first_parts(unit):
        if layer_first(unit):
            source, target, device = total.at[unit, :, :, 1 - side], from_side.at[unit], place.across_side()
        else:
            source, target, device = total.at[unit, 1 - layer], from_layer.at[unit], place.across_layer()
        return source, target, first_sent.at[unit], first_done.at[unit], device

    def last_parts(unit):
        if layer_first(unit):
            source, device = middle.at[unit, 1 - layer], place.across_layer()
        else:
            source, device = middle.at[unit, 1 - side], place.across_side()
        return source, from_last.at[unit], last_sent.at[unit], last_done.at[unit], device

    def deep_parts(unit, away_by):
        slot = (unit, away_by - 1)
        return (
            ending.at[unit, place.other_depth(away_by)], from_depth.at[slot], depth_sent.at[slot],
            depth_done.at[slot], place.along_depth(away_by),
        )

    def own_core_parts(unit):
        return (
            low_sums.at[unit, :, :, 1 - core], own_from_core.at[unit], own_sent.at[unit, 0], own_done.at[unit, 0],
            place.sibling(),
        )

    def own_side_parts(unit):
        return (
            own_total.at[unit, :, 1 - side], own_from_side.at[unit], own_sent.at[unit, 1], own_done.at[unit, 1],
            place.across_side(),
        )

    def own_deep_parts(unit, away_by):
        return (
            own_middle.at[unit, place.other_depth(away_by)], own_from_depth.at[unit, away_by - 1],
            own_sent.at[unit, 1 + away_by], own_done.at[unit, 1 + away_by], place.along_depth(away_by),
        )

    def gain_parts_of(stage):
        if stage == 0:
            source, target, device = gain_sums.at[1 - layer], gain_from_layer, place.across_layer()
        elif stage == 1:
            source, target, device = gain_total.at[0], gain_parts.at[0], place.sibling()
        elif stage == 2:
            source, target, device = gain_total.at[1], gain_parts.at[1], place.across_side()
        else:
            away_by = stage - 2
            source, target = gain_total.at[2, place.other_depth(away_by)], gain_parts.at[2, away_by]
            device = place.along_depth(away_by)
        return source, target, gain_sent.at[stage], gain_done.at[stage], device

    across = range(1, DEPTHS)
    for unit in range(UNITS):
        for which in range(2):
            copies.define(("core", unit, which), partial(core_parts, unit, which))
        copies.define(("first", unit), partial(first_parts, unit))
        copies.define(("last", unit), partial(last_parts, unit))
        for away_by in across:
            copies.define(("deep", unit, away_by), partial(deep_parts, unit, away_by))
    for unit in range(SELFS):
        copies.define(("own core", unit), partial(own_core_parts, unit))
        copies.define(("own side", unit), partial(own_side_parts, unit))
        for away_by in across:
            copies.define(("own deep", unit, away_by), partial(own_deep_parts, unit, away_by))
    for stage in range(3 + DEPTHS - 1):
        copies.define(("gain", stage), partial(gain_parts_of, stage))

    def begin(unit):
        for which in range(2):
            copies.start(("core", unit, which))
            load(unit, which).start()

    def cross_first(unit):
        for which in range(2):
            load(unit, which).wait()
            copies.arrived(("core", unit, which))

            def add(row, carry):
                total[unit, which, row] = add_low(total[unit, which, row], from_core[unit, which, row])
                return carry

            lax.fori_loop(0, DEPTHS, add, 0)
        copies.start(("first", unit))

    def cross_last(unit):
        copies.arrived(("first", unit))
        if layer_first(unit):

            def add(index, carry):
                which, row = index // DEPTHS, index % DEPTHS
                middle[unit, which, row] = add_low(total[unit, which, row, side], from_side[unit, which, row])
                return carry

        else:

            def add(index, carry):
                which, row = index // DEPTHS, index % DEPTHS
                middle[unit, which, row] = add_low(total[unit, layer, row, which], from_layer[unit, row, which])
                return carry

        lax.fori_loop(0, 2 * DEPTHS, add, 0)
        copies.start(("last", unit))

    def along_depth(unit):
        copies.arrived(("last", unit))
        kept = layer if layer_first(unit) else side
        ending[unit] = add_low(middle[unit, kept], from_last[unit])
        copies.start(*[("deep", unit, away_by) for away_by in range(1, DEPTHS)])

    def finish(unit):
        whole = ending[unit, depth].astype(FULL)
        for away_by in range(1, DEPTHS):
            copies.arrived(("deep", unit, away_by))
            whole = whole + from_depth[unit, away_by - 1].astype(FULL)
        if unit < EXPAND:
            cross[:, columns(unit - CROSS)] = whole
        elif unit < BLOCKS:
            expand[:, columns(unit - EXPAND)] = whole
        else:
            contract[columns(unit - BLOCKS, UNIT), :] = whole

    def steps():
        gap, ahead = SCATTER_GAP, SCATTER_AHEAD

        def one(number):
            if ahead <= number + ahead < UNITS:
                begin(ORDER[number + ahead])
            if number < UNITS:
                cross_first(ORDER[number])
            if 0 <= number - gap < UNITS:
                cross_last(ORDER[number - gap])
            if 0 <= number - 2 * gap < UNITS:
                along_depth(ORDER[number - 2 * gap])
            if 0 <= number - 3 * gap < UNITS:
                finish(ORDER[number - 3 * gap])

        return [partial(one, number) for number in range(UNITS + 3 * gap)]

    def fetch(index):
        slot = (index + count) % steps_in_all
        return pltpu.make_async_copy(
            rows.at[row_of(layer, slot, count)], streams.at[index % 2], fetched.at[index % 2]
        )

    def store(index):
        slot = (index + count) % steps_in_all
        return pltpu.make_async_copy(
            value.at[index % 2], gradient.at[row_of(layer, slot, count)], stored.at[index % 2]
        )

    takes = [
        pltpu.make_async_copy(source, deltas.at[pl.ds(count * half, count)], delta_done.at[half])
        for half, source in enumerate((kept_delta, away_delta))
    ]

    @pl.when(step == 0)
    def _():
        for take in takes:
            take.start()
        fetch(step).start()
        sums[...] = jnp.zeros(sums.shape, FULL)
        own_gain[...] = jnp.zeros(own_gain.shape, FULL)
        place.greet()
        for number in range(SCATTER_AHEAD):
            begin(ORDER[number])
        copies.start(("gain", 0))
        for take in takes:
            take.wait()

    plan = Plan(SCATTER_RATE, HOOKS)
    plan.fill(steps(), steps_in_all)

    @pl.when(step + 1 < steps_in_all)
    def _():
        fetch(step + 1).start()

    fetch(step).wait()
    delta, delta_gain = self_back(
        deltas[step], streams[step % 2].astype(FULL), gains[layer, 0:1, :],
        lambda unit: own_square[unit].reshape(D, D),
        triple.at[0], shares.at[0], inverse.at[0], result.at[0], delta_triple, sums, partial(plan.hook, step),
    )
    own_gain[0:1, :] += delta_gain

    @pl.when(step >= 2)
    def _():
        store(step).wait()

    value[step % 2] = delta
    store(step).start()
    plan.hook(step)

    @pl.when(step == steps_in_all - 1)
    def _():
        for unit in range(SELFS):
            low_sums[unit] = sums[unit].astype(LOW).reshape(DEPTHS, SIDES, CORES, UNIT, D)
            copies.start(("own core", unit))
        copies.arrived(("gain", 0))
        whole = gain_sums[layer] + gain_from_layer[...] + own_gain[...]
        for row in range(DEPTHS):
            gain_total[0, row] = whole[:, 128 * row : 128 * (row + 1)]
        copies.start(("gain", 1))
        for unit in range(SELFS):
            copies.arrived(("own core", unit))

            def add(row, carry):
                own_total[unit, row] = add_low(low_sums[unit, row, :, core], own_from_core[unit, row])
                return carry

            lax.fori_loop(0, DEPTHS, add, 0)
            copies.start(("own side", unit))
        copies.arrived(("gain", 1))
        gain_total[1] = gain_total[0] + gain_parts[0]
        copies.start(("gain", 2))
        for unit in range(SELFS):
            copies.arrived(("own side", unit))
            own_middle[unit] = add_low(own_total[unit, :, side], own_from_side[unit])
            copies.start(*[("own deep", unit, away_by) for away_by in across])
        copies.arrived(("gain", 2))
        gain_total[2] = gain_total[1] + gain_parts[1]
        copies.start(*[("gain", 2 + away_by) for away_by in across])
        for unit in range(SELFS):
            whole = own_middle[unit, depth].astype(FULL)
            for away_by in range(1, DEPTHS):
                copies.arrived(("own deep", unit, away_by))
                whole = whole + own_from_depth[unit, away_by - 1].astype(FULL)
            if unit < OUT:
                attention_in[:, columns(unit)] = whole
            else:
                attention_out[...] = whole
        whole = gain_total[2, depth]
        for away_by in range(1, DEPTHS):
            copies.arrived(("gain", 2 + away_by))
            whole = whole + gain_parts[2, away_by]
        gain_out[...] = whole
        store(step - 1).wait()
        store(step).wait()
        copies.finish()


def near_back(kept_delta, away_delta, rows, own_square, gains, kept, square_sums, tall_sums, gain_sums):
    count, total = kept_delta.shape[0], rows.shape[0]
    dma = pltpu.SemaphoreType.DMA
    vmem = pl.BlockSpec(memory_space=pltpu.VMEM)
    shapes = kept_shapes()[:4]

    def rotated(*shape):
        return pl.BlockSpec((1,) + shape, lambda step: ((step + count) % total,) + (0,) * len(shape))

    weight_shapes = [(UNIT, 3 * D), (UNIT, D), (UNIT, 2 * D), (UNIT, FF), (SLABS * UNIT, D), (8, 128)]
    low = lambda *shape: pltpu.VMEM(shape, LOW)
    full = lambda *shape: pltpu.VMEM(shape, FULL)
    gradient, *weights, gain = pl.pallas_call(
        near_back_kernel,
        grid=(total,),
        in_specs=[ANYWHERE, ANYWHERE, ANYWHERE, constant(SELFS, DEPTHS, SIDES, CORES, UNIT, D), constant(2, 8, D)]
        + [rotated(*shape) for shape, _ in shapes]
        + [ANYWHERE, ANYWHERE, constant(2, 8, D)],
        out_specs=[ANYWHERE] + [pl.BlockSpec(shape, lambda step: (0, 0)) for shape in weight_shapes],
        out_shape=[shape_of((total, ROW, D), FULL)] + [shape_of(shape, FULL) for shape in weight_shapes],
        scratch_shapes=[
            low(total, ROW, D), low(2, ROW, D), full(2, ROW, D), low(ROW, 3 * D), full(SELFS, D, D),
            low(SELFS, DEPTHS, SIDES, CORES, UNIT, D), full(8, D),
            low(UNITS, 2, DEPTHS, SIDES, UNIT, D), low(UNITS, 2, DEPTHS, SIDES, UNIT, D),
            low(UNITS, 2, DEPTHS, UNIT, D), low(UNITS, DEPTHS, 2, UNIT, D), low(UNITS, 2, DEPTHS, UNIT, D),
            low(UNITS, DEPTHS, UNIT, D), low(UNITS, DEPTHS, UNIT, D), low(UNITS, 3, UNIT, D),
            low(SELFS, DEPTHS, SIDES, UNIT, D), low(SELFS, DEPTHS, SIDES, UNIT, D),
            low(SELFS, DEPTHS, UNIT, D), low(SELFS, DEPTHS, UNIT, D), low(SELFS, 3, UNIT, D),
            full(3, DEPTHS, 8, 128), full(3, DEPTHS, 8, 128), full(8, D),
            dma((2,)), dma((2,)), dma((2,)),
            dma((UNITS, 2)), dma((UNITS, 2)), dma((UNITS, 2)), dma((UNITS,)), dma((UNITS,)), dma((UNITS,)),
            dma((UNITS,)), dma((UNITS, 3)), dma((UNITS, 3)),
            dma((SELFS, 5)), dma((SELFS, 5)), dma((6,)), dma((6,)),
        ],
        compiler_params=pltpu.CompilerParams(
            vmem_limit_bytes=VMEM_LIMIT, collective_id=1, has_side_effects=True
        ),
        name="self_back",
    )(
        kept_delta, away_delta, rows, own_square, gains, *kept[:4],
        square_sums.reshape(2, BLOCKS, DEPTHS, SIDES, CORES, UNIT, D),
        tall_sums.reshape(2, DEPTHS, SIDES, CORES, SLABS, UNIT, D), gain_sums,
    )
    start = lax.axis_index("dp") % 4 * UNIT
    return gradient, *weights, lax.dynamic_slice_in_dim(gain[:3], start, UNIT, axis=1)


def far_self_kernel(
    source_counts, target_counts, rows, square, gains, triple, shares, inverse, result, first, bias
):
    layer, step, count = lax.axis_index("pipe"), pl.program_id(0), pl.num_programs(0) // 2
    row = row_of(layer, step, count)
    causal = layer == 1
    both = [jnp.where(causal, target_counts[row, piece], source_counts[row, piece]) for piece in range(PACK)]
    fill_bias(bias, *segments(both), causal)
    first[0] = self_forward(
        rows[0].astype(FULL), gains[layer, 0:1, :], lambda unit: square[unit], bias,
        triple.at[0], shares.at[0], inverse.at[0], result.at[0], no_hook,
    ).astype(LOW)


def far_self(source_counts, target_counts, square, gains, rows):
    total = rows.shape[0]
    kept = kept_shapes()
    return pl.pallas_call(
        far_self_kernel,
        grid=(total,),
        in_specs=[SCALARS, SCALARS, per_row(ROW, D), constant(SELFS, D, D), constant(2, 8, D)],
        out_specs=[per_row(*shape) for shape, _ in kept],
        out_shape=[shape_of((total,) + shape, kind) for shape, kind in kept],
        scratch_shapes=[pltpu.VMEM((ROW, ROW), FULL)],
        compiler_params=PARAMS,
        name="self_forward",
    )(source_counts, target_counts, rows, square, gains)


def far_back_kernel(
    deltas, rows, square, gains, triple, shares, inverse, result, gradient, sums, gain_out, delta_triple
):
    layer, step = lax.axis_index("pipe"), pl.program_id(0)

    @pl.when(step == 0)
    def _():
        sums[...] = jnp.zeros(sums.shape, FULL)
        gain_out[...] = jnp.zeros(gain_out.shape, FULL)

    delta, delta_gain = self_back(
        deltas[0], rows[0].astype(FULL), gains[layer, 0:1, :], lambda unit: square[unit],
        triple.at[0], shares.at[0], inverse.at[0], result.at[0], delta_triple, sums, no_hook,
    )
    gain_out[0:1, :] += delta_gain
    gradient[0] = delta


def far_back(deltas, rows, square, gains, kept):
    total = rows.shape[0]
    return pl.pallas_call(
        far_back_kernel,
        grid=(total,),
        in_specs=[per_row(ROW, D), per_row(ROW, D), constant(SELFS, D, D), constant(2, 8, D)]
        + [per_row(*shape) for shape, _ in kept_shapes()[:4]],
        out_specs=[per_row(ROW, D), constant(SELFS, D, D), constant(8, D)],
        out_shape=[shape_of((total, ROW, D), FULL), shape_of((SELFS, D, D), FULL), shape_of((8, D), FULL)],
        scratch_shapes=[pltpu.VMEM((ROW, 3 * D), LOW)],
        compiler_params=PARAMS,
        name="self_back",
    )(deltas, rows, square, gains, *kept[:4])


def spotsof(value):
    return [value[:, start : start + D] for start in range(0, value.shape[1], D)]


def gather_all(value, axes):
    return lax.all_gather(value, axes, axis=0, tiled=False)


def far_weights(weights, gains, shards):
    attention_in, attention_out, cross, expand, contract = (value.astype(LOW) for value in weights)
    both = ("pipe", "dp")
    own = jnp.stack(spotsof(attention_in) + [attention_out])
    own = jnp.swapaxes(gather_all(own, "dp"), 0, 1).reshape(SELFS, D, D)
    square = gather_all(jnp.stack(spotsof(cross) + spotsof(expand)), both)
    square = jnp.swapaxes(square.reshape(2, shards, BLOCKS, D // shards, D), 1, 2)
    tall = gather_all(contract, both)
    gains = gather_all(gains.astype(LOW), both).reshape(2, shards, 3, D // shards)
    gains = jnp.swapaxes(gains, 1, 2).reshape(2, 3, D).astype(FULL)
    return own, square.reshape(2, BLOCKS, D, D), tall.reshape(2, FF, D), jnp.pad(gains, ((0, 0), (0, 5), (0, 0)))


def scattered(value, axes):
    return lax.psum_scatter(value, axes, scatter_dimension=0, tiled=False).astype(FULL)


def far_sums(own, own_gain, square, tall, gains, section, shards):
    both = ("pipe", "dp")
    share = D // shards
    own = scattered(jnp.swapaxes(own.reshape(SELFS, shards, share, D), 0, 1), "dp")
    square = jnp.swapaxes(square.reshape(2, BLOCKS, shards, share, D), 1, 2)
    square = scattered(square.reshape(2 * shards, BLOCKS, share, D), both)
    tall = scattered(tall.reshape(2 * shards, FF // shards, D), both)
    gains = gains + jnp.where(jnp.arange(2)[:, None, None] == section, own_gain[None], 0.0)
    gains = jnp.swapaxes(gains[:, :3].reshape(2, 3, shards, share), 1, 2)
    gains = scattered(gains.reshape(2 * shards, 3, share), both)

    def joined(value, first, last):
        return jnp.concatenate([value[block] for block in range(first, last)], axis=1)

    return (
        joined(own, QKV, OUT), own[OUT], joined(square, CROSS, EXPAND), joined(square, EXPAND, BLOCKS), tall, gains
    )


def swap(value):
    return lax.ppermute(value, "pipe", [(0, 1), (1, 0)])


def local(
    section_input,
    attention_in,
    attention_out,
    cross_weights,
    expand,
    contract,
    norm_gains,
    source_lengths,
    target_lengths,
    cotangent,
):
    section = lax.axis_index("pipe")
    shards = lax.axis_size("dp")
    near = shards == DEPTHS * SIDES * CORES
    rows = section_input[0]
    count = rows.shape[0] // 2
    weights = tuple(value[0] for value in (attention_in, attention_out, cross_weights, expand, contract))
    if near:
        weights, own_square, gains, away, kept = near_self(
            source_lengths, target_lengths, weights, norm_gains[0], rows
        )
    else:
        turn = jnp.where(section == 0, count, 0)
        own_square, square, tall, gains = far_weights(weights, norm_gains[0], shards)
        weights = square[0], tall[0], square[1, CROSS:EXPAND], square[1, EXPAND:], tall[1]
        slots = jnp.roll(rows, turn, axis=0)
        kept = far_self(source_lengths, target_lengths, own_square, gains, slots)
        away = swap(kept[-1][:count])
    section_output, away_output, kept_delta, away_delta, square_sums, tall_sums, gain_sums = middle(
        near, source_lengths, target_lengths, kept[-1], away, cotangent, weights, gains
    )
    if near:
        gradient, *weight_sums = near_back(
            kept_delta, away_delta, rows, own_square, gains, kept, square_sums, tall_sums, gain_sums
        )
    else:
        away_output, away_delta = swap(away_output), swap(away_delta)
        deltas = jnp.concatenate([away_delta, kept_delta], axis=0)
        gradient, own_sums, own_gain = far_back(deltas, slots, own_square, gains, kept)
        gradient = jnp.roll(gradient, -turn, axis=0)
        weight_sums = far_sums(own_sums, own_gain, square_sums, tall_sums, gain_sums, section, shards)
    section_output = lax.dynamic_update_slice_in_dim(
        section_output, away_output.astype(FULL), count * (1 - section), axis=0
    )
    return (section_output[None], gradient[None]) + tuple(value[None] for value in weight_sums)


def solution(mesh):
    in_specs = (
        P("pipe", "dp", None, None),
        P("pipe", "dp", None),
        P("pipe", "dp", None),
        P("pipe", "dp", None),
        P("pipe", "dp", None),
        P("pipe", "dp", None),
        P("pipe", None, "dp"),
        P("dp", None),
        P("dp", None),
        P("dp", None, None),
    )
    out_specs = (
        P("pipe", "dp", None, None),
        P("pipe", "dp", None, None),
        P("pipe", "dp", None),
        P("pipe", "dp", None),
        P("pipe", "dp", None),
        P("pipe", "dp", None),
        P("pipe", "dp", None),
        P("pipe", None, "dp"),
    )
    return jax.shard_map(local, mesh=mesh, in_specs=in_specs, out_specs=out_specs, check_vma=False)
```

```python
from functools import partial
import math

import jax
import jax.numpy as jnp
from jax import lax
from jax.experimental import pallas as pl
from jax.experimental.pallas import tpu as pltpu
from jax.sharding import PartitionSpec as P

D = 512
HEADS = 8
HD = 64
FF = 2048
ROW = 512
PAIRS = HEADS // 2
PACK = 4

QKV, OUT, SELFS = 0, 3, 4
CROSS, EXPAND, BLOCKS = 0, 2, 6
SLABS = FF // D
UNITS = BLOCKS + SLABS

EPSILON = 1e-05
MASKED = -1e30
LOG2E = math.log2(math.e)
EXPONENT = HD**-0.5 * LOG2E
BELL = 1.0 / math.sqrt(2.0 * math.pi)
LOW = jnp.bfloat16
FULL = jnp.float32
VMEM_LIMIT = 63 * 2**20

NN = (((1,), (0,)), ((), ()))
NT = (((1,), (1,)), ((), ()))
TN = (((0,), (0,)), ((), ()))


def multiply(left, right, dims=NN):
    return lax.dot_general(left, right, dims, preferred_element_type=jnp.float32)


def columns(index, width=D):
    return pl.ds(index * width, width)


def normalize(stream):
    centred = stream - jnp.mean(stream, axis=1, keepdims=True)
    scale = lax.rsqrt(jnp.mean(centred * centred, axis=1, keepdims=True) + EPSILON)
    return centred * scale, scale


def norm_back(unit, scale, gain, delta):
    inner = delta * gain
    mean = jnp.mean(inner, axis=1, keepdims=True)
    along = jnp.mean(inner * unit, axis=1, keepdims=True)
    return scale * (inner - mean - unit * along), jnp.sum(delta * unit, axis=0, keepdims=True)


def segment(counts, shape, axis):
    places = lax.broadcasted_iota(jnp.int32, shape, axis)
    end = counts[0]
    found = (places >= end).astype(jnp.int32)
    for count in counts[1:]:
        end = end + count
        found = found + (places >= end).astype(jnp.int32)
    return found


def segments(counts):
    return segment(counts, (ROW, 1), 0), segment(counts, (1, ROW), 1)


def fill_bias(bias, query_segment, key_segment, causal=None):
    keep = query_segment == key_segment
    if causal is not None:
        query = lax.broadcasted_iota(jnp.int32, (ROW, ROW), 0)
        key = lax.broadcasted_iota(jnp.int32, (ROW, ROW), 1)
        keep = keep & (key <= query + jnp.where(causal, 0, ROW))
    bias[...] = jnp.where(keep, 0.0, MASKED).astype(bias.dtype)


def lanes():
    return lax.broadcasted_iota(jnp.int32, (1, 2 * HD), 1)


def only_half(value, half):
    return jnp.where(lanes() // HD == half, value, jnp.zeros_like(value))


def attend(query, keys, values, bias, shares, inverse, result, hook):
    kept = jnp.zeros((ROW, 2 * HD), FULL)
    for pair in range(PAIRS):
        query2, keys2, values2 = query(pair), keys(pair), values(pair)
        parts = []
        for half in range(2):
            head = 2 * pair + half
            scores = multiply(only_half(query2, half), keys2, NT) + bias[...]
            top = jnp.max(scores, axis=1, keepdims=True)
            weights = jnp.exp2((scores - top) * EXPONENT)
            scale = 1.0 / jnp.sum(weights, axis=1, keepdims=True)
            low = weights.astype(LOW)
            shares[head] = low
            parts.append(multiply(low, values2) * scale)
            kept = jnp.where(lanes() == head, scale, kept)
        result[:, columns(pair, 2 * HD)] = jnp.where(lanes() < HD, parts[0], parts[1]).astype(LOW)
        hook()
    inverse[...] = kept


def attend_back(query, keys, values, shares, inverse, result, delta, put, hook):
    for pair in range(PAIRS):
        query2, keys2, values2 = query(pair), keys(pair), values(pair)
        place = slice(2 * HD * pair, 2 * HD * (pair + 1))
        scale = jnp.where(
            lanes() < HD, inverse[:, 2 * pair : 2 * pair + 1], inverse[:, 2 * pair + 1 : 2 * pair + 2]
        )
        low = (delta[:, place] * scale).astype(LOW)
        product = low.astype(FULL) * result[:, columns(pair, 2 * HD)].astype(FULL)
        query_turned, low_turned = query2.T, low.T
        delta_query = 0.0
        delta_keys, delta_values = [], []
        for half in range(2):
            weights = shares[2 * pair + half]
            along = jnp.sum(only_half(product, half), axis=1, keepdims=True)
            delta_shares = multiply(only_half(low, half), values2, NT)
            delta_scores = (weights.astype(FULL) * (delta_shares - along)).astype(LOW)
            delta_query = delta_query + multiply(delta_scores, only_half(keys2, half))
            own = slice(HD * half, HD * (half + 1))
            delta_keys.append(multiply(query_turned[own], delta_scores))
            delta_values.append(multiply(low_turned[own], weights))
        keys_turned = (jnp.concatenate(delta_keys, axis=0) * HD**-0.5).astype(LOW)
        values_turned = jnp.concatenate(delta_values, axis=0).astype(LOW)
        put(pair, (delta_query * HD**-0.5).astype(LOW), keys_turned.T, values_turned.T)
        hook()


def self_parts(triple):
    return tuple(
        (lambda pair, start=part * PAIRS: triple[:, columns(start + pair, 2 * HD)]) for part in range(3)
    )


def put_triple(target):
    def put(pair, *parts):
        for part, value in enumerate(parts):
            target[:, columns(part * PAIRS + pair, 2 * HD)] = value

    return put


def feed(normed, stream, expand, contract, active, slope, hook):
    total = stream
    for slab in range(SLABS):
        hidden = multiply(normed, expand(slab))
        under = 0.5 + 0.5 * lax.erf(hidden * math.sqrt(0.5))
        bell = BELL * jnp.exp2(hidden * hidden * (-0.5 * LOG2E))
        low = (hidden * under).astype(LOW)
        active[:, columns(slab)] = low
        slope[:, columns(slab)] = (under + hidden * bell).astype(LOW)
        total = total + multiply(low, contract(slab))
        hook()
    return total


def feed_back(delta, stream, gain, expand, contract, change):
    unit, scale = normalize(stream)
    low = delta.astype(LOW)
    delta_normed = 0.0
    for slab in range(SLABS):
        delta_active = multiply(low, contract(slab), NT)
        delta_hidden = (delta_active * change[:, columns(slab)].astype(FULL)).astype(LOW)
        change[:, columns(slab)] = delta_hidden
        delta_normed = delta_normed + multiply(delta_hidden, expand(slab), NT)
    delta_stream, delta_gain = norm_back(unit, scale, gain, delta_normed)
    return delta + delta_stream, delta_gain


def self_forward(stream, gain, square, bias, triple, shares, inverse, result, hook):
    normed = (normalize(stream)[0] * gain).astype(LOW)
    for part in range(3):
        triple[:, columns(part)] = multiply(normed, square(QKV + part)).astype(LOW)
    hook()
    attend(*self_parts(triple), bias, shares, inverse, result, hook)
    return stream + multiply(result[...], square(OUT))


def self_back(low, stream, gain, square, triple, shares, inverse, result, delta_triple, sums, hook):
    unit, scale = normalize(stream)
    sums[OUT] += multiply(result[...], low, TN)
    delta_result = multiply(low, square(OUT), NT)
    hook()
    attend_back(*self_parts(triple), shares, inverse, result, delta_result, put_triple(delta_triple), hook)
    turned = (unit * gain).astype(LOW).T
    delta_normed = 0.0
    for part in range(3):
        chunk = delta_triple[:, columns(part)]
        sums[QKV + part] += multiply(turned, chunk)
        delta_normed = delta_normed + multiply(chunk, square(QKV + part), NT)
    delta_stream, delta_gain = norm_back(unit, scale, gain, delta_normed)
    return low.astype(FULL) + delta_stream, delta_gain


def forward(
    layer, own, other, source_segment, target_segment, gains, expand, contract, pair_weights, cross, bias, kept, hook
):
    end_out, mid_out, normed_out, active, change, pair, cross_normed, question, shares, inverse, result = kept
    source_stream = jnp.where(layer == 0, own, other).astype(FULL)
    target_stream = jnp.where(layer == 0, other, own).astype(FULL)
    normed = (normalize(source_stream)[0] * gains[0, 1:2, :]).astype(LOW)
    normed_out[...] = normed
    end = feed(normed, source_stream, expand, contract, active, change, hook)
    end_out[...] = end
    low = (normalize(end)[0] * gains[0, 2:3, :]).astype(LOW)
    for part in range(2):
        pair[:, columns(part)] = multiply(low, pair_weights(part)).astype(LOW)
    hook()
    fill_bias(bias, target_segment[0], source_segment[1])
    normed = (normalize(target_stream)[0] * gains[1, 1:2, :]).astype(LOW)
    cross_normed[...] = normed
    question[...] = multiply(normed, cross(0)).astype(LOW)
    attend(*cross_refs(question, pair), bias, shares, inverse, result, hook)
    mid_out[...] = target_stream + multiply(result[...], cross(1))


def forward_shapes():
    return [
        ((ROW, D), FULL), ((ROW, D), FULL), ((ROW, D), LOW), ((ROW, FF), LOW), ((ROW, FF), LOW), ((ROW, 2 * D), LOW),
        ((ROW, D), LOW), ((ROW, D), LOW), ((HEADS, ROW, ROW), LOW), ((ROW, 2 * HD), FULL), ((ROW, D), LOW),
    ]


def cross_refs(question, pair):
    return (
        lambda number: question[:, columns(number, 2 * HD)],
        lambda number: pair[:, columns(number, 2 * HD)],
        lambda number: pair[:, columns(PAIRS + number, 2 * HD)],
    )


def counts_of(source_counts, target_counts, row):
    return [[counts[row, piece] for piece in range(PACK)] for counts in (source_counts, target_counts)]


def no_hook():
    pass


def per_row(*shape, last=None, start=0, buffers=2):
    def index(row):
        return (start + (row if last is None else jnp.minimum(row, last)),) + (0,) * len(shape)

    return pl.BlockSpec((1,) + shape, index, pipeline_mode=pl.Buffered(buffers) if buffers != 2 else None)


def constant(*shape):
    return pl.BlockSpec(shape, lambda row: (0,) * len(shape), pipeline_mode=pl.Buffered(1))


ANYWHERE = pl.BlockSpec(memory_space=pl.ANY)
SCALARS = pl.BlockSpec(memory_space=pltpu.SMEM)
PARAMS = pltpu.CompilerParams(vmem_limit_bytes=VMEM_LIMIT)


def shape_of(shape, kind):
    return jax.ShapeDtypeStruct(shape, kind)


MESH = pl.DeviceIdType.MESH
UNITS = BLOCKS + SLABS
UNIT = 32
DEPTHS, SIDES, CORES = 4, 2, 2


class Place:
    def __init__(self):
        self.layer = lax.axis_index("pipe")
        self.rank = lax.axis_index("dp")
        self.core = self.rank % CORES
        self.side = self.rank // CORES % SIDES
        self.depth = self.rank // (CORES * SIDES)

    def sibling(self):
        return (self.layer, self.rank + 1 - 2 * self.core)

    def across_side(self):
        return (self.layer, self.rank + CORES * (1 - 2 * self.side))

    def across_layer(self):
        return (1 - self.layer, self.rank)

    def other_depth(self, step):
        return (self.depth + step) % DEPTHS

    def along_depth(self, step):
        return (self.layer, self.rank + CORES * SIDES * (self.other_depth(step) - self.depth))

    def greet(self):
        partners = [self.sibling(), self.across_side(), self.across_layer()]
        partners += [self.along_depth(step) for step in range(1, DEPTHS)]
        barrier = pltpu.get_barrier_semaphore()
        for partner in partners:
            pl.semaphore_signal(barrier, inc=1, device_id=partner, device_id_type=MESH)
        pl.semaphore_wait(barrier, len(partners))


def row_of(layer, slot, count):
    return (slot + count * (1 - layer)) % (2 * count)


class Plan:
    def __init__(self, rate, hooks):
        self.rate, self.hooks = rate, hooks
        self.steps = {}
        self.index = 0

    def fill(self, thunks, rows):
        late = []
        for number, thunk in enumerate(thunks):
            place = int(number * self.rate)
            if place < rows * self.hooks:
                self.steps.setdefault(divmod(place, self.hooks), []).append(thunk)
            else:
                late.append(thunk)
        return late

    def hook(self, step):
        index, self.index = self.index, self.index + 1
        for (row, place), thunks in sorted(self.steps.items(), key=lambda item: item[0]):
            if place == index:

                @pl.when(step == row)
                def _(thunks=thunks):
                    for thunk in thunks:
                        thunk()


class Copies:
    def __init__(self):
        self.made = {}

    def define(self, key, parts):
        def make():
            source, target, sent, arrived, device = parts()
            return pltpu.make_async_remote_copy(
                src_ref=source, dst_ref=target, send_sem=sent, recv_sem=arrived, device_id=device,
                device_id_type=MESH,
            )

        self.made[key] = make

    def start(self, *keys):
        for key in keys:
            self.made[key]().start()

    def arrived(self, *keys):
        for key in keys:
            self.made[key]().wait_recv()

    def finish(self, *keys):
        for key in keys or self.made:
            self.made[key]().wait_send()


class Spread:
    LAYER, SIDE, CORE, RELAY = 3, 4, 5, 6

    def __init__(self, place, copies, units, sent, done, kept):
        self.place, self.copies, self.units = place, copies, units
        self.sent, self.done, self.kept = sent, done, kept
        for number in range(len(units)):
            for stage in range(self.RELAY + DEPTHS - 1):
                copies.define((self, number, stage), partial(self.parts, number, stage))

    def parts(self, number, stage):
        place, (_, late, source, spot) = self.place, self.units[number]
        own, slot, everything = spot(place.depth, place.side, place.core), stage, slice(None)
        if stage < self.LAYER:
            block, target, device = source(), own, place.along_depth(stage + 1)
        elif stage == self.LAYER:
            block, target, device = source(), own, place.across_layer()
            if late:
                block = target = spot(everything, everything, place.core)
        elif stage == self.SIDE:
            block = target = spot(everything, place.side, place.core)
            device = place.across_side()
        elif stage == self.CORE:
            block = target = spot(everything, everything, place.core)
            device = place.sibling()
        else:
            slot = stage - self.RELAY
            block, target, device = own, own, place.along_depth(slot + 1)
        return block, target, self.sent.at[number, slot], self.done.at[number, slot], device

    def keys(self, number, *stages):
        return [(self, number, stage) for stage in stages]

    def along(self, number):
        return self.keys(number, *range(DEPTHS - 1))

    def relayed(self, number):
        return self.keys(number, *range(self.RELAY, self.RELAY + DEPTHS - 1))

    def keep(self, number):
        _, _, source, spot = self.units[number]
        place = self.place
        return pltpu.make_async_copy(source(), spot(place.depth, place.side, place.core), self.kept.at[number])

    def owned(self, number):
        return pl.when(self.place.layer == self.units[number][0])

    def foreign(self, number):
        return pl.when(self.place.layer != self.units[number][0])

    def late(self, number):
        return self.units[number][1]

    def begin(self, number):
        @self.owned(number)
        def _():
            if not self.late(number):
                self.copies.start(*self.keys(number, self.LAYER))
            self.copies.start(*self.along(number))
            self.keep(number).start()

    def relay(self, number):
        if not self.late(number):

            @self.foreign(number)
            def _():
                self.copies.arrived(*self.keys(number, self.LAYER))
                self.copies.start(*self.relayed(number))

    def cross(self, number):
        def work():
            self.copies.arrived(*self.along(number))
            self.copies.start(*self.keys(number, self.SIDE))

        @self.owned(number)
        def _():
            self.keep(number).wait()
            if self.late(number):
                work()

        if not self.late(number):
            work()

    def share(self, number):
        def work():
            self.copies.arrived(*self.keys(number, self.SIDE))
            self.copies.start(*self.keys(number, self.CORE))

        if self.late(number):

            @self.owned(number)
            def _():
                work()
                self.copies.start(*self.keys(number, self.LAYER))

        else:
            work()

    def pass_on(self, number):
        if self.late(number):

            @self.foreign(number)
            def _():
                self.copies.arrived(*self.keys(number, self.LAYER))
                self.copies.start(*self.keys(number, self.CORE))

    def end(self, number):
        self.copies.arrived(*self.keys(number, self.CORE))

    def finish(self):
        for number in range(len(self.units)):
            first = self.along(number) + self.keys(number, self.SIDE)

            @self.owned(number)
            def _(number=number, first=first):
                self.copies.finish(*self.keys(number, self.LAYER))
                if self.late(number):
                    self.copies.finish(*first)

            if not self.late(number):
                self.copies.finish(*first)
            self.copies.finish(*self.keys(number, self.CORE))

    def steps(self, ahead, gap):
        def one(number):
            if ahead <= number + ahead < len(self.units):
                self.begin(number + ahead)
            if ahead - 1 <= number + ahead - 1 < len(self.units):
                self.relay(number + ahead - 1)
            if number < len(self.units):
                self.cross(number)
            if 0 <= number - gap < len(self.units):
                self.share(number - gap)
            if 0 <= number - 2 * gap < len(self.units):
                self.pass_on(number - 2 * gap)

        return [partial(one, number) for number in range(len(self.units) + 2 * gap)]


def add_low(left, right):
    return (left.astype(FULL) + right.astype(FULL)).astype(LOW)


class Collect:
    SIDE, DEPTH, LAYER = 1, 2, 5

    def __init__(self, place, copies, units, buffers, sent, done):
        self.place, self.copies, self.units = place, copies, units
        self.from_core, self.from_side, self.from_depth, self.from_layer = buffers
        self.sent, self.done = sent, done
        for number in range(len(units)):
            for stage in range(self.LAYER + 1):
                copies.define((self, number, stage), partial(self.parts, number, stage))

    def parts(self, number, stage):
        place, (_, outgoing, total, _, _) = self.place, self.units[number]
        if stage == 0:
            source, target, device = outgoing(), self.from_core.at[number], place.sibling()
        elif stage == self.SIDE:
            source = total(slice(None), 1 - place.side)
            target, device = self.from_side.at[number], place.across_side()
        elif stage < self.LAYER:
            away_by = stage - self.DEPTH + 1
            source = total(place.other_depth(away_by), place.side)
            target, device = self.from_depth.at[number, away_by - 1], place.along_depth(away_by)
        else:
            source, target = total(place.depth, place.side), self.from_layer.at[number]
            device = place.across_layer()
        return source, target, self.sent.at[number, stage], self.done.at[number, stage], device

    def keys(self, number, *stages):
        return [(self, number, stage) for stage in stages]

    def along(self, number):
        return self.keys(number, *range(self.DEPTH, self.LAYER))

    def begin(self, number):
        load = self.units[number][3]
        if load is not None:
            load().start()
        self.copies.start(*self.keys(number, 0))

    def chip(self, number):
        _, _, total, load, _ = self.units[number]
        if load is not None:
            load().wait()
        self.copies.arrived(*self.keys(number, 0))

        def add(depth, carry):
            share = total(depth, slice(None))
            share[...] = add_low(share[...], self.from_core[number, depth])
            return carry

        lax.fori_loop(0, DEPTHS, add, 0)
        self.copies.start(*self.keys(number, self.SIDE))

    def sides(self, number):
        total = self.units[number][2]
        self.copies.arrived(*self.keys(number, self.SIDE))

        def add(depth, carry):
            share = total(depth, self.place.side)
            share[...] = add_low(share[...], self.from_side[number, depth])
            return carry

        lax.fori_loop(0, DEPTHS, add, 0)
        self.copies.start(*self.along(number))

    def depths(self, number):
        owner, _, total, _, target = self.units[number]
        self.copies.arrived(*self.along(number))
        share = total(self.place.depth, self.place.side)
        value = share[...].astype(FULL)
        for other in range(DEPTHS - 1):
            value = value + self.from_depth[number, other].astype(FULL)
        if owner is None:
            target()[...] = value
            return

        @pl.when(self.place.layer == owner)
        def _():
            target()[...] = value

        @pl.when(self.place.layer != owner)
        def _():
            share[...] = value.astype(LOW)
            self.copies.start(*self.keys(number, self.LAYER))

    def layers(self, number):
        owner, target = self.units[number][0], self.units[number][4]
        if owner is not None:

            @pl.when(self.place.layer == owner)
            def _():
                self.copies.arrived(*self.keys(number, self.LAYER))
                target()[...] = target()[...] + self.from_layer[number].astype(FULL)

    def finish(self):
        for number, unit in enumerate(self.units):
            self.copies.finish(*self.keys(number, 0, self.SIDE), *self.along(number))
            if unit[0] is not None:

                @pl.when(self.place.layer != unit[0])
                def _(number=number):
                    self.copies.finish(*self.keys(number, self.LAYER))

    def steps(self, ahead, gap):
        count = len(self.units)

        def one(number):
            if ahead <= number + ahead < count:
                self.begin(number + ahead)
            for place, work in enumerate((self.chip, self.sides, self.depths, self.layers)):
                if 0 <= number - place * gap < count:
                    work(number - place * gap)

        return [partial(one, number) for number in range(count + 3 * gap)]


def collect_scratch(count, layers=True):
    low = lambda *shape: pltpu.VMEM(shape, LOW)
    return [
        low(count, DEPTHS, SIDES, UNIT, D), low(count, DEPTHS, UNIT, D), low(count, DEPTHS - 1, UNIT, D),
        low(count if layers else 1, UNIT, D),
        pltpu.SemaphoreType.DMA((count, 6)), pltpu.SemaphoreType.DMA((count, 6)),
    ]


GATHER_RATE, GATHER_AHEAD, GATHER_GAP, GATHER_EARLY, FORWARD_RATE = 1.9, 6, 3, 4, 3.0
GATHER_ORDER = (
    tuple((0, unit, False) for unit in (2, 6, 3, 7, 4, 8, 5, 9, 0, 1))
    + ((1, 0, False), (1, 1, False))
    + tuple((1, unit, False) for unit in (6, 7, 8, 9, 2, 3, 4, 5))
)
SOON = 12
FORWARD_HOOKS = SLABS + PAIRS + 1
SCATTER_RATE, SCATTER_AHEAD, SCATTER_GAP = 2.0, 4, 3
SCATTER_ORDER = ((1, 0), (1, 1)) + tuple((0, unit) for unit in (2, 6, 3, 7, 4, 8, 5, 9, 0, 1))
TURN_RATE, TURN_GAP, TURN_HOOKS = 1.3, 5, PAIRS + 3
HOOKS = PAIRS + 2


def near_self_kernel(
    source_counts, target_counts, attention_in, attention_out, cross, expand, contract, gains, rows,
    square_out, tall_out, cross_out, target_rest, target_tall, own_square, every_gain, away,
    triple, shares, inverse, result, first,
    end, mid, source_normed, active, change, pair, cross_normed, question, cross_shares, cross_inverse, cross_result,
    blocks, tiles, streams, firsts, landing, bias, own, source_square, source_tall, target_cross, share_rows,
    share_done, fetched, block_sent, block_done, block_out, tile_sent, tile_done,
    spread_sent, spread_done, spread_kept, away_sent, away_done, copied,
):
    place = Place()
    layer, depth, side, core = place.layer, place.depth, place.side, place.core
    step, total = pl.program_id(0), 2 * away.shape[0]
    count = away.shape[0]
    copies = Copies()
    share_row = share_rows.at[step % 2]

    def kept_share(target):
        return pltpu.make_async_copy(share_row, target, share_done.at[step % 2])

    kept = [
        ref.at[0]
        for ref in (end, mid, source_normed, active, change, pair, cross_normed, question, cross_inverse, cross_result)
    ]
    kept.insert(8, share_row)
    selfs = [attention_in.at[:, columns(j)] for j in range(3)] + [attention_out]
    sources = [cross.at[:, columns(j)] for j in range(2)] + [expand.at[:, columns(j)] for j in range(SLABS)]
    sources += [contract.at[columns(j, UNIT), :] for j in range(SLABS)]

    def spot(owner, unit, *index):
        if owner == 0:
            if unit < BLOCKS:
                return source_square.at[(unit,) + index]
            return source_tall.at[index + (unit - BLOCKS,)]
        if unit < EXPAND:
            return target_cross.at[(unit,) + index]
        if unit < BLOCKS:
            return target_rest.at[(unit - EXPAND,) + index]
        return target_tall.at[index + (unit - BLOCKS,)]

    units = [
        (owner, late, partial(own.at.__getitem__, unit), partial(spot, owner, unit))
        for owner, unit, late in GATHER_ORDER
    ]
    spread = Spread(place, copies, units, spread_sent, spread_done, spread_kept)

    def away_parts(slot):
        return firsts.at[slot], landing.at[slot], away_sent.at[slot], away_done.at[slot], place.across_layer()

    def block_parts(unit, stage):
        if stage == 0:
            block, target = blocks.at[unit, :, :, core], place.sibling()
        elif stage < DEPTHS:
            block, target = blocks.at[unit, depth, side, core], place.along_depth(stage)
        else:
            block, target = blocks.at[unit, :, side, core], place.across_side()
        return block, block, block_sent.at[unit, stage], block_done.at[unit, stage], target

    def tile_parts(stage):
        if stage == 0:
            block, target = tiles.at[layer], place.across_layer()
        elif stage < DEPTHS:
            block, target = tiles.at[layer, depth, side, core], place.along_depth(stage)
        elif stage == DEPTHS:
            block, target = tiles.at[layer, :, side, core], place.across_side()
        else:
            block, target = tiles.at[layer, :, :, core], place.sibling()
        return block, block, tile_sent.at[stage], tile_done.at[stage], target

    for stage in range(DEPTHS + 2):
        copies.define(("tile", stage), partial(tile_parts, stage))
    for unit in range(SELFS):
        for stage in range(DEPTHS + 1):
            copies.define(("block", unit, stage), partial(block_parts, unit, stage))
    for slot in range(count):
        copies.define(("away", slot), partial(away_parts, slot))

    def lay_gains(which):
        for row in range(DEPTHS):
            value = tiles[which, row, 0, 0].astype(FULL)
            for other in ((0, 1), (1, 0), (1, 1)):
                value = value + tiles[(which, row) + other].astype(FULL)
            every_gain[which, :, columns(row, 128)] = value[:8]

    def fetch(slot):
        return pltpu.make_async_copy(
            rows.at[row_of(layer, slot, count)], streams.at[slot % 2], fetched.at[slot % 2]
        )

    @pl.when(step == 0)
    def _():
        fetch(step).start()
        for unit in range(SELFS):
            blocks[unit, depth, side, core] = selfs[unit][...].astype(LOW)
        for unit in range(UNITS):
            own[unit] = sources[unit][...].astype(LOW)
        tiles[layer, depth, side, core] = gains[...]
        place.greet()
        across = range(1, DEPTHS)
        early = iter(spread.steps(GATHER_AHEAD, GATHER_GAP)[:GATHER_EARLY])
        copies.start(*[("tile", stage) for stage in across])
        for unit in range(SELFS):
            copies.start(*[("block", unit, stage) for stage in across])
        for number in range(GATHER_AHEAD):
            spread.begin(number)
        copies.arrived(*[("tile", stage) for stage in across])
        copies.start(("tile", DEPTHS))
        for number in range(GATHER_AHEAD - 1):
            spread.relay(number)
        for unit in range(SELFS):
            copies.arrived(*[("block", unit, stage) for stage in across])
            copies.start(("block", unit, DEPTHS))
        copies.arrived(("tile", DEPTHS))
        copies.start(("tile", DEPTHS + 1))
        for unit in range(SELFS):
            for _ in range(GATHER_EARLY // SELFS):
                next(early)()
            copies.arrived(("block", unit, DEPTHS))
            copies.start(("block", unit, 0))
        copies.arrived(("tile", DEPTHS + 1))
        copies.start(("tile", 0))
        lay_gains(layer)
        copies.arrived(*[("block", unit, 0) for unit in range(OUT)])

    def last_block():
        copies.arrived(("block", OUT, 0))
        pltpu.make_async_copy(blocks, own_square, block_out).start()

    plan = Plan(GATHER_RATE, HOOKS)
    late = plan.fill([last_block] + spread.steps(GATHER_AHEAD, GATHER_GAP)[GATHER_EARLY:], total)
    forward_plan = Plan(FORWARD_RATE, FORWARD_HOOKS)
    late = forward_plan.fill(late, count)

    @pl.when(step + 1 < total)
    def _():
        fetch(step + 1).start()

    @pl.when(step >= 2)
    def _():
        kept_share(shares.at[0]).wait()

    @pl.when(step < total)
    def _():
        row = row_of(layer, step, count)
        causal = layer == 1
        both = [jnp.where(causal, *pair_of) for pair_of in zip(*counts_of(target_counts, source_counts, row))]
        fill_bias(bias, *segments(both), causal)
        fetch(step).wait()
        stream = self_forward(
            streams[step % 2].astype(FULL), every_gain[layer, 0:1, :], lambda unit: blocks[unit].reshape(D, D), bias,
            triple.at[0], share_row, inverse.at[0], result.at[0], partial(plan.hook, step),
        )
        kept_share(shares.at[step]).start()
        stream = stream.astype(LOW)
        first[0] = stream
        firsts[step] = stream
        for slot in range(count):

            @pl.when(step == slot)
            def _(slot=slot):
                copies.start(("away", slot))

        plan.hook(step)

    outward = [
        pltpu.make_async_copy(source, target, copied.at[index])
        for index, (source, target) in enumerate(
            ((source_square, square_out), (source_tall, tall_out), (target_cross, cross_out), (landing, away))
        )
    ]

    @pl.when(step == total)
    def _():
        copies.arrived(("tile", 0))
        lay_gains(1 - layer)
        for number in range(SOON):
            spread.end(number)
        copies.arrived(*[("away", slot) for slot in range(count)])
        for copy in outward:
            copy.start()

    @pl.when(step >= total)
    def _():
        index = step - total
        source_pieces, target_pieces = counts_of(source_counts, target_counts, layer * count + index)
        forward(
            layer, firsts[step - count], landing[index], segments(source_pieces), segments(target_pieces), every_gain,
            lambda slab: source_square[EXPAND + slab].reshape(D, D), lambda slab: source_tall[slab].reshape(D, D),
            lambda part: source_square[CROSS + part].reshape(D, D), lambda part: target_cross[part].reshape(D, D),
            bias, kept, partial(forward_plan.hook, index),
        )
        kept_share(cross_shares.at[index]).start()

    @pl.when(step == total + count - 1)
    def _():
        for thunk in late:
            thunk()
        for number in range(SOON, len(units)):
            spread.end(number)
        copies.finish(*[("away", slot) for slot in range(count)])
        copies.finish(*[("tile", stage) for stage in range(DEPTHS + 2)])
        copies.finish(*[("block", unit, stage) for unit in range(SELFS) for stage in range(DEPTHS + 1)])
        spread.finish()
        pltpu.make_async_copy(blocks, own_square, block_out).wait()
        for copy in outward:
            copy.wait()
        for number in range(2):
            pltpu.make_async_copy(share_rows.at[number], cross_shares.at[number], share_done.at[number]).wait()


def kept_shapes():
    return [
        ((ROW, 3 * D), LOW), ((HEADS, ROW, ROW), LOW), ((ROW, 2 * HD), FULL), ((ROW, D), LOW), ((ROW, D), LOW)
    ]


def near_self(source_counts, target_counts, weights, gains, rows):
    total = rows.shape[0]
    tile = jnp.tile(gains.astype(LOW), (1, 4))
    lane_part = lax.broadcasted_iota(jnp.int32, tile.shape, 1) // UNIT
    tile = jnp.where(lane_part == lax.axis_index("dp") % 4, tile, jnp.zeros_like(tile))
    tile = jnp.pad(tile, ((0, 16 - tile.shape[0]), (0, 0)))
    dma = pltpu.SemaphoreType.DMA
    kept, ahead = kept_shapes(), forward_shapes()
    count = total // 2
    square_shape = (BLOCKS, DEPTHS, SIDES, CORES, UNIT, D)
    tall_shape = (DEPTHS, SIDES, CORES, SLABS, UNIT, D)
    cross_shape, rest_shape = (2,) + square_shape[1:], (SLABS,) + square_shape[1:]
    own_shape = (SELFS,) + square_shape[1:]
    outs = [
        shape_of(shape, LOW) for shape in (square_shape, tall_shape, cross_shape, rest_shape, tall_shape, own_shape)
    ] + [shape_of((2, 8, D), FULL), shape_of((count, ROW, D), LOW)]
    low = lambda *shape: pltpu.VMEM(shape, LOW)

    def later(*shape):
        return pl.BlockSpec((1,) + shape, lambda step: (jnp.maximum(step - total, 0),) + (0,) * len(shape))

    def spec(shape, make):
        return ANYWHERE if shape == (HEADS, ROW, ROW) else make(*shape)

    results = pl.pallas_call(
        near_self_kernel,
        grid=(total + count,),
        in_specs=[SCALARS, SCALARS] + [constant(*value.shape) for value in weights] + [constant(16, 128), ANYWHERE],
        out_specs=[ANYWHERE] * 6
        + [pl.BlockSpec((2, 8, D), lambda row: (0, 0, 0)), ANYWHERE]
        + [spec(shape, partial(per_row, last=total - 1)) for shape, _ in kept]
        + [spec(shape, later) for shape, _ in ahead],
        out_shape=outs
        + [shape_of((total,) + shape, kind) for shape, kind in kept]
        + [shape_of((count,) + shape, kind) for shape, kind in ahead],
        scratch_shapes=[
            low(*own_shape), low(2, DEPTHS, SIDES, CORES, 16, 128), low(2, ROW, D), low(total, ROW, D),
            low(count, ROW, D), low(ROW, ROW), low(UNITS, UNIT, D), low(*square_shape), low(*tall_shape),
            low(*cross_shape), low(2, HEADS, ROW, ROW),
            dma((2,)), dma((2,)), dma((SELFS, 5)), dma((SELFS, 5)), dma, dma((6,)), dma((6,)),
            dma((len(GATHER_ORDER), 6)), dma((len(GATHER_ORDER), 6)), dma((len(GATHER_ORDER),)),
            dma((count,)), dma((count,)), dma((4,)),
        ],
        compiler_params=pltpu.CompilerParams(
            vmem_limit_bytes=VMEM_LIMIT, collective_id=0, has_side_effects=True
        ),
        name="self_forward",
    )(source_counts, target_counts, *weights, tile, rows)
    weights, (own_square, every_gain, away), results = results[:5], results[5:8], results[8:]
    weights = weights[0].reshape(BLOCKS, D, D), weights[1].reshape(FF, D), weights[2].reshape(2, D, D), *weights[3:]
    return weights, own_square, every_gain, away, results[: len(kept)], results[len(kept) :]


def middle_kernel(
    near,
    first, away, cotangent, source_square, source_tall, target_cross, rest, rest_tall, gains,
    kept_end, kept_mid, kept_normed, kept_active, kept_change, kept_pair, kept_cross, kept_question, kept_shares,
    kept_inverse, kept_result,
    section_output, sent_output, kept_delta, sent_delta, square_out, tall_out, gain_out, expand_out, contract_out,
    target_expand, target_contract, shares, inverse, cross_result, source_end, target_mid, value, sending, keeping,
    source_normed, active, memory_low, cross_normed, feed_normed,
    source_change, source_low, delta_pair, delta_question, cross_low, target_change, target_low,
    loaded, stored, kept, ready, output_sent, output_done, delta_sent, delta_done, fetched,
    turn_core, turn_side, turn_depth, turn_layer, turn_sent, turn_done,
):
    place = Place()
    layer = place.layer
    count = away.shape[0]
    copies = Copies()

    def source_expand(slab):
        return source_square[EXPAND + slab]

    def source_contract(slab):
        return source_tall[columns(slab), :]

    if near:

        def spot(unit, *index):
            if unit < SLABS:
                return target_expand.at[(unit,) + index]
            return target_contract.at[index + (unit - SLABS,)]

        def turn_unit(unit):
            def target():
                if unit < SLABS:
                    return expand_out.at[:, columns(unit)]
                return contract_out.at[columns(unit - SLABS, UNIT), :]

            return (
                1,
                lambda: spot(unit, slice(None), slice(None), 1 - place.core),
                lambda *index: spot(unit, *index, place.core),
                None,
                target,
            )

        collect = Collect(
            place, copies, [turn_unit(unit) for unit in range(2 * SLABS)],
            (turn_core, turn_side, turn_depth, turn_layer), turn_sent, turn_done,
        )

        def expand_of(slab):
            return target_expand[slab].reshape(D, D)

        def contract_of(slab):
            return target_contract[slab].reshape(D, D)

    else:

        def expand_of(slab):
            return target_expand[slab]

        def contract_of(slab):
            return target_contract[columns(slab), :]

    whole_rest = [
        pltpu.make_async_copy(rest, target_expand, fetched.at[0]),
        pltpu.make_async_copy(rest_tall, target_contract, fetched.at[1]),
    ]

    def rows_of(row):
        return pl.ds(pl.multiple_of(row * ROW, ROW), ROW)

    def load(row):
        return pltpu.make_async_copy(
            cotangent.at[layer * count + row], target_low.at[columns(row, ROW), :], loaded.at[row]
        )

    def store(row):
        return pltpu.make_async_copy(value, section_output.at[layer * count + row], stored)

    def keep(row):
        return pltpu.make_async_copy(keeping.at[row], kept_delta.at[row], kept.at[row])

    class Parcels:
        def __init__(self, name, target, sent, done):
            self.name, self.target, self.sent, self.done = name, target, sent, done
            for row in range(count):
                copies.define((name, row), partial(self.parts, row))

        def parts(self, row):
            return sending.at[row], self.target.at[row], self.sent.at[row], self.done.at[row], place.across_layer()

        def local(self, row):
            return pltpu.make_async_copy(sending.at[row], self.target.at[row], self.sent.at[row])

        def put(self, row, block):
            for static in range(count):

                @pl.when(row == static)
                def _(static=static):
                    sending[static] = block
                    if near:
                        copies.start((self.name, static))
                    else:
                        self.local(static).start()

        def left(self, row):
            for static in range(count):

                @pl.when(row == static)
                def _(static=static):
                    if near:
                        copies.finish((self.name, static))
                    else:
                        self.local(static).wait()

    outputs = Parcels("output", sent_output, output_sent, output_done)
    deltas = Parcels("delta", sent_delta, delta_sent, delta_done)

    def streams(row):
        own, other = first[row].astype(FULL), away[row].astype(FULL)
        return jnp.where(layer == 0, own, other), jnp.where(layer == 0, other, own)

    def publish(row, owner, block):
        @pl.when(layer == owner)
        def _():
            @pl.when(jnp.asarray(row) > 0)
            def _():
                store(row - 1).wait()

            value[...] = block
            store(row).start()

        @pl.when(layer != owner)
        def _():
            outputs.put(row, block.astype(LOW))

    for row in range(count):
        load(row).start()
    gain_out[...] = jnp.zeros(gain_out.shape, FULL)
    if near:
        place.greet()
    takes = [
        pltpu.make_async_copy(source, target, fetched.at[2 + index])
        for index, (source, target) in enumerate(
            (
                (kept_end, source_end), (kept_mid, target_mid), (kept_normed, source_normed), (kept_cross, cross_normed),
                (kept_result, cross_result), (kept_pair, delta_pair), (kept_question, delta_question),
                (kept_inverse, inverse), (kept_shares.at[count - 1], shares), (kept_change, source_change),
            )
        )
    ]
    take_active = pltpu.make_async_copy(kept_active, active, fetched.at[12])
    for copy in takes[:2] + whole_rest + takes[2:]:
        copy.start()

    def cross_parts(row):
        at = rows_of(row)
        return cross_refs(delta_question.at[at, :], delta_pair.at[at, :])

    def take_shares(row):
        return pltpu.make_async_copy(kept_shares.at[row], shares, fetched.at[13])

    takes[0].wait()
    for row in range(count):
        memory = normalize(source_end[row])[0] * gains[0, 2:3, :]
        memory_low[columns(row, ROW), :] = memory.astype(LOW)
        publish(row, 0, memory)
    for copy in takes[1:2] + whole_rest:
        copy.wait()

    @pl.when(layer == 0)
    def _():
        store(count - 1).wait()

    def turn(row, carry):
        at = rows_of(row)
        stream = target_mid[row]
        normed = (normalize(stream)[0] * gains[1, 2:3, :]).astype(LOW)
        feed_normed[at, :] = normed
        output = feed(
            normed, stream, expand_of, contract_of, active.at[at, :], target_change.at[at, :], no_hook
        )
        publish(row, 1, output)
        for static in range(count):

            @pl.when(row == static)
            def _(static=static):
                load(static).wait()

        delta, delta_gain = feed_back(
            target_low[at, :].astype(FULL), stream, gains[1, 2:3, :], expand_of, contract_of, target_change.at[at, :]
        )
        gain_out[1, 2:3, :] += delta_gain
        target_mid[row] = delta
        return carry

    lax.fori_loop(0, count, turn, 0)

    emitted, late = [], []

    def emit(block, holder, target):
        holder[...] = block.astype(LOW)
        copy = pltpu.make_async_copy(holder, target, ready.at[len(emitted)])
        copy.start()
        emitted.append(copy)
        if late:
            late.pop(0)()

    def feed_grads(which, normed, change, low):
        turned = normed[...].T
        for slab in range(SLABS):
            grown = multiply(turned, change[:, columns(slab)])
            shrunk = multiply(active[:, columns(slab)], low[...], TN)
            emit(grown, change.at[pl.ds(0, D), columns(slab)], square_out.at[which, EXPAND + slab])
            emit(shrunk, change.at[pl.ds(D, D), columns(slab)], tall_out.at[which, columns(slab), :])

    if near:
        turned = feed_normed[...].T
        for slab in range(SLABS):
            grown = multiply(turned, target_change[:, columns(slab)])
            target_expand[slab] = grown.astype(LOW).reshape(DEPTHS, SIDES, CORES, UNIT, D)
            collect.begin(slab)
            shrunk = multiply(active[:, columns(slab)], target_low[...], TN)
            target_contract[slab] = shrunk.astype(LOW).reshape(SIDES, CORES, SLABS, UNIT, D)
        for slab in range(SLABS):
            collect.begin(SLABS + slab)
        plan = Plan(TURN_RATE, TURN_HOOKS)
        late = plan.fill(collect.steps(2 * SLABS, TURN_GAP), count)
    else:
        feed_grads(1, feed_normed, target_change, target_low)
    take_active.start()
    for copy in takes[2:]:
        copy.wait()

    def backward(number, carry):
        row = count - 1 - number
        at = rows_of(row)
        hook = partial(plan.hook, number) if near else no_hook
        source_stream, target_stream = streams(row)

        @pl.when(number > 0)
        def _():
            take_shares(row).wait()

        delta = target_mid[row]
        low = delta.astype(LOW)
        cross_low[at, :] = low
        delta_result = multiply(low, target_cross[1], NT)

        def put(pair, query, keys, values):
            delta_question[at, columns(pair, 2 * HD)] = query
            delta_pair[at, columns(pair, 2 * HD)] = keys
            delta_pair[at, columns(PAIRS + pair, 2 * HD)] = values

        attend_back(
            *cross_parts(row), shares, inverse.at[row], cross_result.at[at, :], delta_result, put, hook
        )

        @pl.when(number < count - 1)
        def _():
            take_shares(row - 1).start()

        unit, scale = normalize(target_stream)
        delta_normed = multiply(delta_question[at, :], target_cross[0], NT)
        delta_stream, delta_gain = norm_back(unit, scale, gains[1, 1:2, :], delta_normed)
        gain_out[1, 1:2, :] += delta_gain
        target_delta = (delta + delta_stream).astype(LOW)
        hook()

        unit, scale = normalize(source_end[row])
        delta_memory = 0.0
        for part in range(2):
            delta_memory = delta_memory + multiply(delta_pair[at, columns(part)], source_square[CROSS + part], NT)
        delta, delta_gain = norm_back(unit, scale, gains[0, 2:3, :], delta_memory)
        gain_out[0, 2:3, :] += delta_gain
        source_low[at, :] = delta.astype(LOW)
        hook()
        delta, delta_gain = feed_back(
            delta, source_stream, gains[0, 1:2, :], source_expand, source_contract, source_change.at[at, :]
        )
        gain_out[0, 1:2, :] += delta_gain
        source_delta = delta.astype(LOW)
        keeping[row] = jnp.where(layer == 0, source_delta, target_delta)
        for static in range(count):

            @pl.when(row == static)
            def _(static=static):
                keep(static).start()

        outputs.left(row)
        deltas.put(row, jnp.where(layer == 0, target_delta, source_delta))
        hook()
        return carry

    lax.fori_loop(0, count, backward, 0)
    take_active.wait()
    feed_grads(0, source_normed, source_change, source_low)
    turned = memory_low[...].T
    for part in range(2):
        grown = multiply(turned, delta_pair[:, columns(part)])
        emit(grown, delta_pair.at[pl.ds(0, D), columns(part)], square_out.at[0, CROSS + part])
    for part, (left, right) in enumerate(((cross_normed, delta_question), (cross_result, cross_low))):
        emit(multiply(left[...], right[...], TN), right.at[pl.ds(0, D), :], square_out.at[1, CROSS + part])
    for thunk in late:
        thunk()
    for copy in emitted:
        copy.wait()

    @pl.when(layer == 1)
    def _():
        store(count - 1).wait()

    for row in range(count):
        keep(row).wait()
        deltas.left(row)
    if near:
        copies.arrived(*[(name, row) for name in ("output", "delta") for row in range(count)])
        collect.finish()


def middle(near, first, away, cotangent, weights, gains, ahead):
    count = away.shape[0]
    tokens = count * ROW
    dma = pltpu.SemaphoreType.DMA
    low = lambda *shape: pltpu.VMEM(shape, LOW)
    full = lambda *shape: pltpu.VMEM(shape, FULL)
    square, tall, cross, rest, rest_tall = weights
    if near:
        expand = low(SLABS, DEPTHS, SIDES, CORES, UNIT, D)
        contract = low(DEPTHS, SIDES, CORES, SLABS, UNIT, D)
    else:
        expand, contract = low(SLABS, D, D), low(FF, D)
    rows_apart = (0, 1, 8, 9)
    ahead = [
        value if place in rows_apart else value.reshape(tokens, value.shape[-1]) for place, value in enumerate(ahead)
    ]
    row_shape = shape_of((count, ROW, D), LOW)
    early_shapes = [(UNIT, FF), (SLABS * UNIT, D)]
    remote = dict(collective_id=2, has_side_effects=True) if near else {}
    outs = pl.pallas_call(
        partial(middle_kernel, near),
        grid=(1,),
        in_specs=[
            pl.BlockSpec((count, ROW, D), lambda step: (1, 0, 0), pipeline_mode=pl.Buffered(1)),
            constant(count, ROW, D), ANYWHERE, constant(BLOCKS, D, D), constant(FF, D), constant(2, D, D),
            ANYWHERE, ANYWHERE, constant(2, 8, D),
        ]
        + [ANYWHERE] * len(ahead),
        out_specs=[ANYWHERE] * 6
        + [pl.BlockSpec((2, 8, D), lambda step: (0, 0, 0))]
        + [pl.BlockSpec(shape, lambda step: (0, 0)) for shape in early_shapes],
        out_shape=[shape_of((2 * count, ROW, D), FULL), row_shape, row_shape, row_shape]
        + [shape_of((2, BLOCKS, D, D), LOW), shape_of((2, FF, D), LOW), shape_of((2, 8, D), FULL)]
        + [shape_of(shape, FULL) for shape in early_shapes],
        scratch_shapes=[
            expand, contract, low(HEADS, ROW, ROW), full(count, ROW, 2 * HD), low(tokens, D),
            full(count, ROW, D), full(count, ROW, D), full(ROW, D), low(count, ROW, D), low(count, ROW, D),
            low(tokens, D), low(tokens, FF), low(tokens, D), low(tokens, D), low(tokens, D),
            low(tokens, FF), low(tokens, D), low(tokens, 2 * D), low(tokens, D), low(tokens, D), low(tokens, FF),
            low(tokens, D),
            dma((count,)), dma, dma((count,)), dma((2 * UNITS,)),
            dma((count,)), dma((count,)), dma((count,)), dma((count,)), dma((14,)),
        ]
        + collect_scratch(2 * SLABS if near else 1),
        compiler_params=pltpu.CompilerParams(vmem_limit_bytes=VMEM_LIMIT, **remote),
        name="middle",
    )(first, away, cotangent, square, tall, cross, rest, rest_tall, gains, *ahead)
    return outs[:7], outs[7:]


def near_back_kernel(
    kept_delta, away_delta, rows, own_square, gains, triple, shares, inverse, result,
    square_sums, tall_sums, gain_sums, early_expand, early_contract,
    gradient, attention_in, attention_out, cross, expand, contract, gain_out,
    deltas, streams, value, delta_triple, sums, low_sums, own_gain, total,
    gain_total, gain_parts, gain_from_layer,
    delta_done, fetched, stored, loaded, gain_sent, gain_done,
    other_core, other_side, other_depth, other_layer, other_sent, other_done,
    own_core, own_side, own_depth, own_layer, own_sent, own_done,
):
    place = Place()
    layer, depth, core = place.layer, place.depth, place.core
    count = kept_delta.shape[0]
    step, steps_in_all = pl.program_id(0), 2 * count
    copies = Copies()

    def other_unit(number):
        which, unit = SCATTER_ORDER[number]

        def share(owner):
            if unit < BLOCKS:
                return square_sums.at[which, unit, :, :, owner]
            return tall_sums.at[which, :, :, owner, unit - BLOCKS]

        def target():
            if unit < EXPAND:
                return cross.at[:, columns(unit - CROSS)]
            if unit < BLOCKS:
                return expand.at[:, columns(unit - EXPAND)]
            return contract.at[columns(unit - BLOCKS, UNIT), :]

        return (
            which,
            lambda: share(1 - core),
            lambda *index: total.at[(number,) + index],
            lambda: pltpu.make_async_copy(share(core), total.at[number], loaded.at[number]),
            target,
        )

    def own_unit(unit):
        return (
            None,
            lambda: low_sums.at[unit, :, :, 1 - core],
            lambda *index: low_sums.at[(unit,) + index + (core,)],
            None,
            lambda: attention_in.at[:, columns(unit)] if unit < OUT else attention_out,
        )

    others = Collect(
        place, copies, [other_unit(number) for number in range(len(SCATTER_ORDER))],
        (other_core, other_side, other_depth, other_layer), other_sent, other_done,
    )
    selfs = Collect(
        place, copies, [own_unit(unit) for unit in range(SELFS)], (own_core, own_side, own_depth, own_layer),
        own_sent, own_done,
    )

    def gain_parts_of(stage):
        if stage == 0:
            source, target, device = gain_sums.at[1 - layer], gain_from_layer, place.across_layer()
        elif stage == 1:
            source, target, device = gain_total.at[0], gain_parts.at[0], place.sibling()
        elif stage == 2:
            source, target, device = gain_total.at[1], gain_parts.at[1], place.across_side()
        else:
            away_by = stage - 2
            source, target = gain_total.at[2, place.other_depth(away_by)], gain_parts.at[2, away_by]
            device = place.along_depth(away_by)
        return source, target, gain_sent.at[stage], gain_done.at[stage], device

    gain_stages = range(3 + DEPTHS - 1)
    for stage in gain_stages:
        copies.define(("gain", stage), partial(gain_parts_of, stage))

    def fetch(index):
        slot = (index + count) % steps_in_all
        return pltpu.make_async_copy(
            rows.at[row_of(layer, slot, count)], streams.at[index % 2], fetched.at[index % 2]
        )

    def store(index):
        slot = (index + count) % steps_in_all
        return pltpu.make_async_copy(
            value.at[index % 2], gradient.at[row_of(layer, slot, count)], stored.at[index % 2]
        )

    takes = [
        pltpu.make_async_copy(source, deltas.at[pl.ds(count * half, count)], delta_done.at[half])
        for half, source in enumerate((kept_delta, away_delta))
    ]

    @pl.when(step == 0)
    def _():
        for take in takes:
            take.start()
        fetch(step).start()
        sums[...] = jnp.zeros(sums.shape, FULL)
        own_gain[...] = jnp.zeros(own_gain.shape, FULL)
        place.greet()
        for number in range(SCATTER_AHEAD):
            others.begin(number)
        copies.start(("gain", 0))

        @pl.when(layer == 1)
        def _():
            expand[...] = early_expand[...]
            contract[...] = early_contract[...]

        for take in takes:
            take.wait()

    plan = Plan(SCATTER_RATE, HOOKS)
    late = plan.fill(others.steps(SCATTER_AHEAD, SCATTER_GAP), steps_in_all)

    @pl.when(step + 1 < steps_in_all)
    def _():
        fetch(step + 1).start()

    fetch(step).wait()
    delta, delta_gain = self_back(
        deltas[step], streams[step % 2].astype(FULL), gains[layer, 0:1, :],
        lambda unit: own_square[unit].reshape(D, D),
        triple.at[0], shares.at[0], inverse.at[0], result.at[0], delta_triple, sums, partial(plan.hook, step),
    )
    own_gain[0:1, :] += delta_gain

    @pl.when(step >= 2)
    def _():
        store(step).wait()

    value[step % 2] = delta
    store(step).start()
    plan.hook(step)

    @pl.when(step == steps_in_all - 1)
    def _():
        def more():
            if late:
                late.pop(0)()

        for unit in range(SELFS):
            low_sums[unit] = sums[unit].astype(LOW).reshape(DEPTHS, SIDES, CORES, UNIT, D)
            selfs.begin(unit)
        copies.arrived(("gain", 0))
        whole = gain_sums[layer] + gain_from_layer[...] + own_gain[...]
        for row in range(DEPTHS):
            gain_total[0, row] = whole[:, 128 * row : 128 * (row + 1)]
        copies.start(("gain", 1))
        more()
        for unit in range(SELFS):
            selfs.chip(unit)
        copies.arrived(("gain", 1))
        gain_total[1] = gain_total[0] + gain_parts[0]
        copies.start(("gain", 2))
        for unit in range(SELFS):
            more()
            selfs.sides(unit)
        copies.arrived(("gain", 2))
        gain_total[2] = gain_total[1] + gain_parts[1]
        copies.start(*[("gain", 2 + away_by) for away_by in range(1, DEPTHS)])
        for unit in range(SELFS):
            more()
            selfs.depths(unit)
        while late:
            more()
        whole = gain_total[2, depth]
        for away_by in range(1, DEPTHS):
            copies.arrived(("gain", 2 + away_by))
            whole = whole + gain_parts[2, away_by]
        gain_out[...] = whole
        store(step - 1).wait()
        store(step).wait()
        copies.finish(*[("gain", stage) for stage in gain_stages])
        others.finish()
        selfs.finish()


def near_back(kept_delta, away_delta, rows, own_square, gains, kept, square_sums, tall_sums, gain_sums, early):
    count, total = kept_delta.shape[0], rows.shape[0]
    dma = pltpu.SemaphoreType.DMA
    vmem = pl.BlockSpec(memory_space=pltpu.VMEM)
    shapes = kept_shapes()[:4]

    def rotated(*shape):
        return pl.BlockSpec((1,) + shape, lambda step: ((step + count) % total,) + (0,) * len(shape))

    units = len(SCATTER_ORDER)
    weight_shapes = [(UNIT, 3 * D), (UNIT, D), (UNIT, 2 * D), (UNIT, FF), (SLABS * UNIT, D), (8, 128)]
    low = lambda *shape: pltpu.VMEM(shape, LOW)
    full = lambda *shape: pltpu.VMEM(shape, FULL)
    gradient, *weights, gain = pl.pallas_call(
        near_back_kernel,
        grid=(total,),
        in_specs=[ANYWHERE, ANYWHERE, ANYWHERE, constant(SELFS, DEPTHS, SIDES, CORES, UNIT, D), constant(2, 8, D)]
        + [rotated(*shape) for shape, _ in shapes]
        + [ANYWHERE, ANYWHERE, constant(2, 8, D), constant(UNIT, FF), constant(SLABS * UNIT, D)],
        out_specs=[ANYWHERE] + [pl.BlockSpec(shape, lambda step: (0, 0)) for shape in weight_shapes],
        out_shape=[shape_of((total, ROW, D), FULL)] + [shape_of(shape, FULL) for shape in weight_shapes],
        scratch_shapes=[
            low(total, ROW, D), low(2, ROW, D), full(2, ROW, D), low(ROW, 3 * D), full(SELFS, D, D),
            low(SELFS, DEPTHS, SIDES, CORES, UNIT, D), full(8, D), low(units, DEPTHS, SIDES, UNIT, D),
            full(3, DEPTHS, 8, 128), full(3, DEPTHS, 8, 128), full(8, D),
            dma((2,)), dma((2,)), dma((2,)), dma((units,)), dma((6,)), dma((6,)),
        ]
        + collect_scratch(units)
        + collect_scratch(SELFS, False),
        compiler_params=pltpu.CompilerParams(
            vmem_limit_bytes=VMEM_LIMIT, collective_id=1, has_side_effects=True
        ),
        name="self_back",
    )(
        kept_delta, away_delta, rows, own_square, gains, *kept[:4],
        square_sums.reshape(2, BLOCKS, DEPTHS, SIDES, CORES, UNIT, D),
        tall_sums.reshape(2, DEPTHS, SIDES, CORES, SLABS, UNIT, D), gain_sums, *early,
    )
    start = lax.axis_index("dp") % 4 * UNIT
    return gradient, *weights, lax.dynamic_slice_in_dim(gain[:3], start, UNIT, axis=1)


def far_self_kernel(
    source_counts, target_counts, rows, square, gains, triple, shares, inverse, result, first, bias
):
    layer, step, count = lax.axis_index("pipe"), pl.program_id(0), pl.num_programs(0) // 2
    row = row_of(layer, step, count)
    causal = layer == 1
    both = [jnp.where(causal, target_counts[row, piece], source_counts[row, piece]) for piece in range(PACK)]
    fill_bias(bias, *segments(both), causal)
    first[0] = self_forward(
        rows[0].astype(FULL), gains[layer, 0:1, :], lambda unit: square[unit], bias,
        triple.at[0], shares.at[0], inverse.at[0], result.at[0], no_hook,
    ).astype(LOW)


def far_self(source_counts, target_counts, square, gains, rows):
    total = rows.shape[0]
    kept = kept_shapes()
    return pl.pallas_call(
        far_self_kernel,
        grid=(total,),
        in_specs=[SCALARS, SCALARS, per_row(ROW, D), constant(SELFS, D, D), constant(2, 8, D)],
        out_specs=[per_row(*shape) for shape, _ in kept],
        out_shape=[shape_of((total,) + shape, kind) for shape, kind in kept],
        scratch_shapes=[pltpu.VMEM((ROW, ROW), FULL)],
        compiler_params=PARAMS,
        name="self_forward",
    )(source_counts, target_counts, rows, square, gains)


def far_forward_kernel(
    source_counts, target_counts, first, away, square, tall, cross, gains, *refs
):
    layer, step, count = lax.axis_index("pipe"), pl.program_id(0), pl.num_programs(0)
    source_pieces, target_pieces = counts_of(source_counts, target_counts, layer * count + step)
    forward(
        layer, first[0], away[0], segments(source_pieces), segments(target_pieces), gains,
        lambda slab: square[EXPAND + slab], lambda slab: tall[columns(slab), :],
        lambda part: square[CROSS + part], lambda part: cross[part], refs[-1], [ref.at[0] for ref in refs[:-1]], no_hook,
    )


def far_forward(source_counts, target_counts, first, away, square, tall, cross, gains):
    count = away.shape[0]
    kept = forward_shapes()
    return pl.pallas_call(
        far_forward_kernel,
        grid=(count,),
        in_specs=[
            SCALARS, SCALARS, per_row(ROW, D, start=count), per_row(ROW, D), constant(BLOCKS, D, D), constant(FF, D),
            constant(2, D, D), constant(2, 8, D),
        ],
        out_specs=[per_row(*shape) for shape, _ in kept],
        out_shape=[shape_of((count,) + shape, kind) for shape, kind in kept],
        scratch_shapes=[pltpu.VMEM((ROW, ROW), LOW)],
        compiler_params=PARAMS,
        name="forward",
    )(source_counts, target_counts, first, away, square, tall, cross, gains)


def far_back_kernel(
    deltas, rows, square, gains, triple, shares, inverse, result, gradient, sums, gain_out, delta_triple
):
    layer, step = lax.axis_index("pipe"), pl.program_id(0)

    @pl.when(step == 0)
    def _():
        sums[...] = jnp.zeros(sums.shape, FULL)
        gain_out[...] = jnp.zeros(gain_out.shape, FULL)

    delta, delta_gain = self_back(
        deltas[0], rows[0].astype(FULL), gains[layer, 0:1, :], lambda unit: square[unit],
        triple.at[0], shares.at[0], inverse.at[0], result.at[0], delta_triple, sums, no_hook,
    )
    gain_out[0:1, :] += delta_gain
    gradient[0] = delta


def far_back(deltas, rows, square, gains, kept):
    total = rows.shape[0]
    return pl.pallas_call(
        far_back_kernel,
        grid=(total,),
        in_specs=[per_row(ROW, D), per_row(ROW, D), constant(SELFS, D, D), constant(2, 8, D)]
        + [per_row(*shape) for shape, _ in kept_shapes()[:4]],
        out_specs=[per_row(ROW, D), constant(SELFS, D, D), constant(8, D)],
        out_shape=[shape_of((total, ROW, D), FULL), shape_of((SELFS, D, D), FULL), shape_of((8, D), FULL)],
        scratch_shapes=[pltpu.VMEM((ROW, 3 * D), LOW)],
        compiler_params=PARAMS,
        name="self_back",
    )(deltas, rows, square, gains, *kept[:4])


def spotsof(value):
    return [value[:, start : start + D] for start in range(0, value.shape[1], D)]


def gather_all(value, axes):
    return lax.all_gather(value, axes, axis=0, tiled=False)


def far_weights(weights, gains, shards):
    attention_in, attention_out, cross, expand, contract = (value.astype(LOW) for value in weights)
    both = ("pipe", "dp")
    own = jnp.stack(spotsof(attention_in) + [attention_out])
    own = jnp.swapaxes(gather_all(own, "dp"), 0, 1).reshape(SELFS, D, D)
    square = gather_all(jnp.stack(spotsof(cross) + spotsof(expand)), both)
    square = jnp.swapaxes(square.reshape(2, shards, BLOCKS, D // shards, D), 1, 2)
    tall = gather_all(contract, both)
    gains = gather_all(gains.astype(LOW), both).reshape(2, shards, 3, D // shards)
    gains = jnp.swapaxes(gains, 1, 2).reshape(2, 3, D).astype(FULL)
    return own, square.reshape(2, BLOCKS, D, D), tall.reshape(2, FF, D), jnp.pad(gains, ((0, 0), (0, 5), (0, 0)))


def scattered(value, axes):
    return lax.psum_scatter(value, axes, scatter_dimension=0, tiled=False).astype(FULL)


def far_sums(own, own_gain, square, tall, gains, section, shards):
    both = ("pipe", "dp")
    share = D // shards
    own = scattered(jnp.swapaxes(own.reshape(SELFS, shards, share, D), 0, 1), "dp")
    square = jnp.swapaxes(square.reshape(2, BLOCKS, shards, share, D), 1, 2)
    square = scattered(square.reshape(2 * shards, BLOCKS, share, D), both)
    tall = scattered(tall.reshape(2 * shards, FF // shards, D), both)
    gains = gains + jnp.where(jnp.arange(2)[:, None, None] == section, own_gain[None], 0.0)
    gains = jnp.swapaxes(gains[:, :3].reshape(2, 3, shards, share), 1, 2)
    gains = scattered(gains.reshape(2 * shards, 3, share), both)

    def joined(value, first, last):
        return jnp.concatenate([value[block] for block in range(first, last)], axis=1)

    return (
        joined(own, QKV, OUT), own[OUT], joined(square, CROSS, EXPAND), joined(square, EXPAND, BLOCKS), tall, gains
    )


def swap(value):
    return lax.ppermute(value, "pipe", [(0, 1), (1, 0)])


def local(
    section_input,
    attention_in,
    attention_out,
    cross_weights,
    expand,
    contract,
    norm_gains,
    source_lengths,
    target_lengths,
    cotangent,
):
    section = lax.axis_index("pipe")
    shards = lax.axis_size("dp")
    near = shards == DEPTHS * SIDES * CORES
    rows = section_input[0]
    count = rows.shape[0] // 2
    weights = tuple(value[0] for value in (attention_in, attention_out, cross_weights, expand, contract))
    if near:
        weights, own_square, gains, away, kept, ahead = near_self(
            source_lengths, target_lengths, weights, norm_gains[0], rows
        )
    else:
        turn = jnp.where(section == 0, count, 0)
        own_square, square, tall, gains = far_weights(weights, norm_gains[0], shards)
        weights = square[0], tall[0], square[1, CROSS:EXPAND], square[1, EXPAND:], tall[1]
        slots = jnp.roll(rows, turn, axis=0)
        kept = far_self(source_lengths, target_lengths, own_square, gains, slots)
        away = swap(kept[-1][:count])
        ahead = far_forward(source_lengths, target_lengths, kept[-1], away, *weights[:3], gains)
    (section_output, away_output, kept_delta, away_delta, *sums), early = middle(
        near, kept[-1], away, cotangent, weights, gains, ahead
    )
    if near:
        gradient, *weight_sums = near_back(
            kept_delta, away_delta, rows, own_square, gains, kept, *sums, early
        )
    else:
        away_output, away_delta = swap(away_output), swap(away_delta)
        deltas = jnp.concatenate([away_delta, kept_delta], axis=0)
        gradient, own_sums, own_gain = far_back(deltas, slots, own_square, gains, kept)
        gradient = jnp.roll(gradient, -turn, axis=0)
        weight_sums = far_sums(own_sums, own_gain, *sums, section, shards)
    section_output = lax.dynamic_update_slice_in_dim(
        section_output, away_output.astype(FULL), count * (1 - section), axis=0
    )
    return (section_output[None], gradient[None]) + tuple(value[None] for value in weight_sums)


def solution(mesh):
    in_specs = (
        P("pipe", "dp", None, None),
        P("pipe", "dp", None),
        P("pipe", "dp", None),
        P("pipe", "dp", None),
        P("pipe", "dp", None),
        P("pipe", "dp", None),
        P("pipe", None, "dp"),
        P("dp", None),
        P("dp", None),
        P("dp", None, None),
    )
    out_specs = (
        P("pipe", "dp", None, None),
        P("pipe", "dp", None, None),
        P("pipe", "dp", None),
        P("pipe", "dp", None),
        P("pipe", "dp", None),
        P("pipe", "dp", None),
        P("pipe", "dp", None),
        P("pipe", None, "dp"),
    )
    return jax.shard_map(local, mesh=mesh, in_specs=in_specs, out_specs=out_specs, check_vma=False)
```

```python
from functools import partial
import math

import jax
import jax.numpy as jnp
from jax import lax
from jax.experimental import pallas as pl
from jax.experimental.pallas import tpu as pltpu
from jax.sharding import PartitionSpec as P

D = 512
HEADS = 8
HD = 64
FF = 2048
ROW = 512
PAIRS = HEADS // 2
PACK = 4

QKV, OUT, SELFS = 0, 3, 4
CROSS, EXPAND, BLOCKS = 0, 2, 6
SLABS = FF // D
UNITS = BLOCKS + SLABS

EPSILON = 1e-05
MASKED = -1e30
LOG2E = math.log2(math.e)
EXPONENT = HD**-0.5 * LOG2E
BELL = 1.0 / math.sqrt(2.0 * math.pi)
LOW = jnp.bfloat16
FULL = jnp.float32
VMEM_LIMIT = 63 * 2**20

NN = (((1,), (0,)), ((), ()))
NT = (((1,), (1,)), ((), ()))
TN = (((0,), (0,)), ((), ()))


def multiply(left, right, dims=NN):
    return lax.dot_general(left, right, dims, preferred_element_type=jnp.float32)


def columns(index, width=D):
    return pl.ds(index * width, width)


def normalize(stream):
    centred = stream - jnp.mean(stream, axis=1, keepdims=True)
    scale = lax.rsqrt(jnp.mean(centred * centred, axis=1, keepdims=True) + EPSILON)
    return centred * scale, scale


def norm_back(unit, scale, gain, delta):
    inner = delta * gain
    mean = jnp.mean(inner, axis=1, keepdims=True)
    along = jnp.mean(inner * unit, axis=1, keepdims=True)
    return scale * (inner - mean - unit * along), jnp.sum(delta * unit, axis=0, keepdims=True)


def segment(counts, shape, axis):
    places = lax.broadcasted_iota(jnp.int32, shape, axis)
    end = counts[0]
    found = (places >= end).astype(jnp.int32)
    for count in counts[1:]:
        end = end + count
        found = found + (places >= end).astype(jnp.int32)
    return found


def segments(counts):
    return segment(counts, (ROW, 1), 0), segment(counts, (1, ROW), 1)


def fill_bias(bias, query_segment, key_segment, causal=None):
    keep = query_segment == key_segment
    if causal is not None:
        query = lax.broadcasted_iota(jnp.int32, (ROW, ROW), 0)
        key = lax.broadcasted_iota(jnp.int32, (ROW, ROW), 1)
        keep = keep & (key <= query + jnp.where(causal, 0, ROW))
    bias[...] = jnp.where(keep, 0.0, MASKED).astype(bias.dtype)


def lanes():
    return lax.broadcasted_iota(jnp.int32, (1, 2 * HD), 1)


def only_half(value, half):
    return jnp.where(lanes() // HD == half, value, jnp.zeros_like(value))


def attend(query, keys, values, bias, shares, inverse, result, hook):
    kept = jnp.zeros((ROW, 2 * HD), FULL)
    for pair in range(PAIRS):
        query2, keys2, values2 = query(pair), keys(pair), values(pair)
        parts = []
        for half in range(2):
            head = 2 * pair + half
            scores = multiply(only_half(query2, half), keys2, NT) + bias[...]
            top = jnp.max(scores, axis=1, keepdims=True)
            weights = jnp.exp2((scores - top) * EXPONENT)
            scale = 1.0 / jnp.sum(weights, axis=1, keepdims=True)
            low = weights.astype(LOW)
            shares[head] = low
            parts.append(multiply(low, values2) * scale)
            kept = jnp.where(lanes() == head, scale, kept)
        result[:, columns(pair, 2 * HD)] = jnp.where(lanes() < HD, parts[0], parts[1]).astype(LOW)
        hook()
    inverse[...] = kept


def attend_back(query, keys, values, shares, inverse, result, delta, put, hook):
    for pair in range(PAIRS):
        query2, keys2, values2 = query(pair), keys(pair), values(pair)
        place = slice(2 * HD * pair, 2 * HD * (pair + 1))
        scale = jnp.where(
            lanes() < HD, inverse[:, 2 * pair : 2 * pair + 1], inverse[:, 2 * pair + 1 : 2 * pair + 2]
        )
        low = (delta[:, place] * scale).astype(LOW)
        product = low.astype(FULL) * result[:, columns(pair, 2 * HD)].astype(FULL)
        query_turned, low_turned = query2.T, low.T
        delta_query = 0.0
        delta_keys, delta_values = [], []
        for half in range(2):
            weights = shares[2 * pair + half]
            along = jnp.sum(only_half(product, half), axis=1, keepdims=True)
            delta_shares = multiply(only_half(low, half), values2, NT)
            delta_scores = (weights.astype(FULL) * (delta_shares - along)).astype(LOW)
            delta_query = delta_query + multiply(delta_scores, only_half(keys2, half))
            own = slice(HD * half, HD * (half + 1))
            delta_keys.append(multiply(query_turned[own], delta_scores))
            delta_values.append(multiply(low_turned[own], weights))
        keys_turned = (jnp.concatenate(delta_keys, axis=0) * HD**-0.5).astype(LOW)
        values_turned = jnp.concatenate(delta_values, axis=0).astype(LOW)
        put(pair, (delta_query * HD**-0.5).astype(LOW), keys_turned.T, values_turned.T)
        hook()


def self_parts(triple):
    return tuple(
        (lambda pair, start=part * PAIRS: triple[:, columns(start + pair, 2 * HD)]) for part in range(3)
    )


def put_triple(target):
    def put(pair, *parts):
        for part, value in enumerate(parts):
            target[:, columns(part * PAIRS + pair, 2 * HD)] = value

    return put


def feed(normed, stream, expand, contract, active, slope, hook):
    total = stream
    for slab in range(SLABS):
        hidden = multiply(normed, expand(slab))
        under = 0.5 + 0.5 * lax.erf(hidden * math.sqrt(0.5))
        bell = BELL * jnp.exp2(hidden * hidden * (-0.5 * LOG2E))
        low = (hidden * under).astype(LOW)
        active[:, columns(slab)] = low
        slope[:, columns(slab)] = (under + hidden * bell).astype(LOW)
        total = total + multiply(low, contract(slab))
        hook()
    return total


def feed_back(delta, stream, gain, expand, contract, change):
    unit, scale = normalize(stream)
    low = delta.astype(LOW)
    delta_normed = 0.0
    for slab in range(SLABS):
        delta_active = multiply(low, contract(slab), NT)
        delta_hidden = (delta_active * change[:, columns(slab)].astype(FULL)).astype(LOW)
        change[:, columns(slab)] = delta_hidden
        delta_normed = delta_normed + multiply(delta_hidden, expand(slab), NT)
    delta_stream, delta_gain = norm_back(unit, scale, gain, delta_normed)
    return delta + delta_stream, delta_gain


def self_forward(stream, gain, square, bias, triple, shares, inverse, result, hook):
    normed = (normalize(stream)[0] * gain).astype(LOW)
    for part in range(3):
        triple[:, columns(part)] = multiply(normed, square(QKV + part)).astype(LOW)
    hook()
    attend(*self_parts(triple), bias, shares, inverse, result, hook)
    return stream + multiply(result[...], square(OUT))


def self_back(low, stream, gain, square, triple, shares, inverse, result, delta_triple, sums, hook):
    unit, scale = normalize(stream)
    sums[OUT] += multiply(result[...], low, TN)
    delta_result = multiply(low, square(OUT), NT)
    hook()
    attend_back(*self_parts(triple), shares, inverse, result, delta_result, put_triple(delta_triple), hook)
    turned = (unit * gain).astype(LOW).T
    delta_normed = 0.0
    for part in range(3):
        chunk = delta_triple[:, columns(part)]
        sums[QKV + part] += multiply(turned, chunk)
        delta_normed = delta_normed + multiply(chunk, square(QKV + part), NT)
    delta_stream, delta_gain = norm_back(unit, scale, gain, delta_normed)
    return low.astype(FULL) + delta_stream, delta_gain


def forward(
    layer, own, other, source_segment, target_segment, gains, expand, contract, pair_weights, cross, bias, kept, hook
):
    end_out, mid_out, normed_out, active, change, pair, cross_normed, question, shares, inverse, result = kept
    source_stream = jnp.where(layer == 0, own, other).astype(FULL)
    target_stream = jnp.where(layer == 0, other, own).astype(FULL)
    normed = (normalize(source_stream)[0] * gains[0, 1:2, :]).astype(LOW)
    normed_out[...] = normed
    end = feed(normed, source_stream, expand, contract, active, change, hook)
    end_out[...] = end
    low = (normalize(end)[0] * gains[0, 2:3, :]).astype(LOW)
    for part in range(2):
        pair[:, columns(part)] = multiply(low, pair_weights(part)).astype(LOW)
    hook()
    fill_bias(bias, target_segment[0], source_segment[1])
    normed = (normalize(target_stream)[0] * gains[1, 1:2, :]).astype(LOW)
    cross_normed[...] = normed
    question[...] = multiply(normed, cross(0)).astype(LOW)
    attend(*cross_refs(question, pair), bias, shares, inverse, result, hook)
    mid_out[...] = target_stream + multiply(result[...], cross(1))


def forward_shapes():
    return [
        ((ROW, D), FULL), ((ROW, D), FULL), ((ROW, D), LOW), ((ROW, FF), LOW), ((ROW, FF), LOW), ((ROW, 2 * D), LOW),
        ((ROW, D), LOW), ((ROW, D), LOW), ((HEADS, ROW, ROW), LOW), ((ROW, 2 * HD), FULL), ((ROW, D), LOW),
    ]


def cross_refs(question, pair):
    return (
        lambda number: question[:, columns(number, 2 * HD)],
        lambda number: pair[:, columns(number, 2 * HD)],
        lambda number: pair[:, columns(PAIRS + number, 2 * HD)],
    )


def counts_of(source_counts, target_counts, row):
    return [[counts[row, piece] for piece in range(PACK)] for counts in (source_counts, target_counts)]


def no_hook():
    pass


def per_row(*shape, last=None, start=0, buffers=2):
    def index(row):
        return (start + (row if last is None else jnp.minimum(row, last)),) + (0,) * len(shape)

    return pl.BlockSpec((1,) + shape, index, pipeline_mode=pl.Buffered(buffers) if buffers != 2 else None)


def constant(*shape):
    return pl.BlockSpec(shape, lambda row: (0,) * len(shape), pipeline_mode=pl.Buffered(1))


ANYWHERE = pl.BlockSpec(memory_space=pl.ANY)
SCALARS = pl.BlockSpec(memory_space=pltpu.SMEM)
PARAMS = pltpu.CompilerParams(vmem_limit_bytes=VMEM_LIMIT)


def shape_of(shape, kind):
    return jax.ShapeDtypeStruct(shape, kind)


MESH = pl.DeviceIdType.MESH
UNITS = BLOCKS + SLABS
UNIT = 32
DEPTHS, SIDES, CORES = 4, 2, 2


class Place:
    def __init__(self):
        self.layer = lax.axis_index("pipe")
        self.rank = lax.axis_index("dp")
        self.core = self.rank % CORES
        self.side = self.rank // CORES % SIDES
        self.depth = self.rank // (CORES * SIDES)

    def sibling(self):
        return (self.layer, self.rank + 1 - 2 * self.core)

    def across_side(self):
        return (self.layer, self.rank + CORES * (1 - 2 * self.side))

    def across_layer(self):
        return (1 - self.layer, self.rank)

    def other_depth(self, step):
        return (self.depth + step) % DEPTHS

    def along_depth(self, step):
        return (self.layer, self.rank + CORES * SIDES * (self.other_depth(step) - self.depth))

    def greet(self):
        partners = [self.sibling(), self.across_side(), self.across_layer()]
        partners += [self.along_depth(step) for step in range(1, DEPTHS)]
        barrier = pltpu.get_barrier_semaphore()
        for partner in partners:
            pl.semaphore_signal(barrier, inc=1, device_id=partner, device_id_type=MESH)
        pl.semaphore_wait(barrier, len(partners))


def row_of(layer, slot, count):
    return (slot + count * (1 - layer)) % (2 * count)


class Plan:
    def __init__(self, rate, hooks):
        self.rate, self.hooks = rate, hooks
        self.steps = {}
        self.index = 0

    def fill(self, thunks, rows):
        late = []
        for number, thunk in enumerate(thunks):
            place = int(number * self.rate)
            if place < rows * self.hooks:
                self.steps.setdefault(divmod(place, self.hooks), []).append(thunk)
            else:
                late.append(thunk)
        return late

    def hook(self, step):
        index, self.index = self.index, self.index + 1
        for (row, place), thunks in sorted(self.steps.items(), key=lambda item: item[0]):
            if place == index:

                @pl.when(step == row)
                def _(thunks=thunks):
                    for thunk in thunks:
                        thunk()


class Copies:
    def __init__(self):
        self.made = {}

    def define(self, key, parts):
        def make():
            source, target, sent, arrived, device = parts()
            return pltpu.make_async_remote_copy(
                src_ref=source, dst_ref=target, send_sem=sent, recv_sem=arrived, device_id=device,
                device_id_type=MESH,
            )

        self.made[key] = make

    def start(self, *keys):
        for key in keys:
            self.made[key]().start()

    def arrived(self, *keys):
        for key in keys:
            self.made[key]().wait_recv()

    def finish(self, *keys):
        for key in keys or self.made:
            self.made[key]().wait_send()


class Spread:
    LAYER, SIDE, CORE, RELAY = 3, 4, 5, 6

    def __init__(self, place, copies, units, sent, done, kept):
        self.place, self.copies, self.units = place, copies, units
        self.sent, self.done, self.kept = sent, done, kept
        for number in range(len(units)):
            for stage in range(self.RELAY + DEPTHS - 1):
                copies.define((self, number, stage), partial(self.parts, number, stage))

    def parts(self, number, stage):
        place, (_, late, source, spot) = self.place, self.units[number]
        own, slot, everything = spot(place.depth, place.side, place.core), stage, slice(None)
        if stage < self.LAYER:
            block, target, device = source(), own, place.along_depth(stage + 1)
        elif stage == self.LAYER:
            block, target, device = source(), own, place.across_layer()
            if late:
                block = target = spot(everything, everything, place.core)
        elif stage == self.SIDE:
            block = target = spot(everything, place.side, place.core)
            device = place.across_side()
        elif stage == self.CORE:
            block = target = spot(everything, everything, place.core)
            device = place.sibling()
        else:
            slot = stage - self.RELAY
            block, target, device = own, own, place.along_depth(slot + 1)
        return block, target, self.sent.at[number, slot], self.done.at[number, slot], device

    def keys(self, number, *stages):
        return [(self, number, stage) for stage in stages]

    def along(self, number):
        return self.keys(number, *range(DEPTHS - 1))

    def relayed(self, number):
        return self.keys(number, *range(self.RELAY, self.RELAY + DEPTHS - 1))

    def keep(self, number):
        _, _, source, spot = self.units[number]
        place = self.place
        return pltpu.make_async_copy(source(), spot(place.depth, place.side, place.core), self.kept.at[number])

    def owned(self, number):
        return pl.when(self.place.layer == self.units[number][0])

    def foreign(self, number):
        return pl.when(self.place.layer != self.units[number][0])

    def late(self, number):
        return self.units[number][1]

    def announce(self):
        for number in range(len(self.units)):
            if not self.late(number):

                @self.owned(number)
                def _(number=number):
                    self.copies.start(*self.keys(number, self.LAYER))

    def begin(self, number):
        @self.owned(number)
        def _():
            self.copies.start(*self.along(number))
            self.keep(number).start()

    def relay(self, number):
        if not self.late(number):

            @self.foreign(number)
            def _():
                self.copies.arrived(*self.keys(number, self.LAYER))
                self.copies.start(*self.relayed(number))

    def cross(self, number):
        def work():
            self.copies.arrived(*self.along(number))
            self.copies.start(*self.keys(number, self.SIDE))

        @self.owned(number)
        def _():
            self.keep(number).wait()
            if self.late(number):
                work()

        if not self.late(number):
            work()

    def share(self, number):
        def work():
            self.copies.arrived(*self.keys(number, self.SIDE))
            self.copies.start(*self.keys(number, self.CORE))

        if self.late(number):

            @self.owned(number)
            def _():
                work()
                self.copies.start(*self.keys(number, self.LAYER))

        else:
            work()

    def pass_on(self, number):
        if self.late(number):

            @self.foreign(number)
            def _():
                self.copies.arrived(*self.keys(number, self.LAYER))
                self.copies.start(*self.keys(number, self.CORE))

    def end(self, number):
        self.copies.arrived(*self.keys(number, self.CORE))

    def finish(self):
        for number in range(len(self.units)):
            first = self.along(number) + self.keys(number, self.SIDE)

            @self.owned(number)
            def _(number=number, first=first):
                self.copies.finish(*self.keys(number, self.LAYER))
                if self.late(number):
                    self.copies.finish(*first)

            if not self.late(number):
                self.copies.finish(*first)
            self.copies.finish(*self.keys(number, self.CORE))

    def steps(self, ahead, gap):
        def one(number):
            if ahead <= number + ahead < len(self.units):
                self.begin(number + ahead)
                self.relay(number + ahead)
            if number < len(self.units):
                self.cross(number)
            if 0 <= number - gap < len(self.units):
                self.share(number - gap)
            if 0 <= number - 2 * gap < len(self.units):
                self.pass_on(number - 2 * gap)

        return [partial(one, number) for number in range(len(self.units) + 2 * gap)]


def add_low(left, right):
    return (left.astype(FULL) + right.astype(FULL)).astype(LOW)


class Collect:
    SIDE, DEPTH, LAYER = 1, 2, 5

    def __init__(self, place, copies, units, buffers, sent, done):
        self.place, self.copies, self.units = place, copies, units
        self.from_core, self.from_side, self.from_depth, self.from_layer = buffers
        self.sent, self.done = sent, done
        for number in range(len(units)):
            for stage in range(self.LAYER + 1):
                copies.define((self, number, stage), partial(self.parts, number, stage))

    def parts(self, number, stage):
        place, (_, outgoing, total, _, _) = self.place, self.units[number]
        if stage == 0:
            source, target, device = outgoing(), self.from_core.at[number], place.sibling()
        elif stage == self.SIDE:
            source = total(slice(None), 1 - place.side)
            target, device = self.from_side.at[number], place.across_side()
        elif stage < self.LAYER:
            away_by = stage - self.DEPTH + 1
            source = total(place.other_depth(away_by), place.side)
            target, device = self.from_depth.at[number, away_by - 1], place.along_depth(away_by)
        else:
            source, target = total(place.depth, place.side), self.from_layer.at[number]
            device = place.across_layer()
        return source, target, self.sent.at[number, stage], self.done.at[number, stage], device

    def keys(self, number, *stages):
        return [(self, number, stage) for stage in stages]

    def along(self, number):
        return self.keys(number, *range(self.DEPTH, self.LAYER))

    def begin(self, number):
        load = self.units[number][3]
        if load is not None:
            load().start()
        self.copies.start(*self.keys(number, 0))

    def chip(self, number):
        _, _, total, load, _ = self.units[number]
        if load is not None:
            load().wait()
        self.copies.arrived(*self.keys(number, 0))

        def add(depth, carry):
            share = total(depth, slice(None))
            share[...] = add_low(share[...], self.from_core[number, depth])
            return carry

        lax.fori_loop(0, DEPTHS, add, 0)
        self.copies.start(*self.keys(number, self.SIDE))

    def sides(self, number):
        total = self.units[number][2]
        self.copies.arrived(*self.keys(number, self.SIDE))

        def add(depth, carry):
            share = total(depth, self.place.side)
            share[...] = add_low(share[...], self.from_side[number, depth])
            return carry

        lax.fori_loop(0, DEPTHS, add, 0)
        self.copies.start(*self.along(number))

    def depths(self, number):
        owner, _, total, _, target = self.units[number]
        self.copies.arrived(*self.along(number))
        share = total(self.place.depth, self.place.side)
        value = share[...].astype(FULL)
        for other in range(DEPTHS - 1):
            value = value + self.from_depth[number, other].astype(FULL)
        if owner is None:
            target()[...] = value
            return

        @pl.when(self.place.layer == owner)
        def _():
            target()[...] = value

        @pl.when(self.place.layer != owner)
        def _():
            share[...] = value.astype(LOW)
            self.copies.start(*self.keys(number, self.LAYER))

    def layers(self, number):
        owner, target = self.units[number][0], self.units[number][4]
        if owner is not None:

            @pl.when(self.place.layer == owner)
            def _():
                self.copies.arrived(*self.keys(number, self.LAYER))
                target()[...] = target()[...] + self.from_layer[number].astype(FULL)

    def finish(self):
        for number, unit in enumerate(self.units):
            self.copies.finish(*self.keys(number, 0, self.SIDE), *self.along(number))
            if unit[0] is not None:

                @pl.when(self.place.layer != unit[0])
                def _(number=number):
                    self.copies.finish(*self.keys(number, self.LAYER))

    def steps(self, ahead, gap):
        count = len(self.units)

        def one(number):
            if ahead <= number + ahead < count:
                self.begin(number + ahead)
            for place, work in enumerate((self.chip, self.sides, self.depths, self.layers)):
                if 0 <= number - place * gap < count:
                    work(number - place * gap)

        return [partial(one, number) for number in range(count + 3 * gap)]


def collect_scratch(count, layers=True):
    low = lambda *shape: pltpu.VMEM(shape, LOW)
    return [
        low(count, DEPTHS, SIDES, UNIT, D), low(count, DEPTHS, UNIT, D), low(count, DEPTHS - 1, UNIT, D),
        low(count if layers else 1, UNIT, D),
        pltpu.SemaphoreType.DMA((count, 6)), pltpu.SemaphoreType.DMA((count, 6)),
    ]


GATHER_RATE, GATHER_AHEAD, GATHER_GAP, GATHER_EARLY, FORWARD_RATE = 1.9, 6, 3, 4, 3.0
GATHER_ORDER = (
    tuple((0, unit, False) for unit in (2, 6, 3, 7, 4, 8, 5, 9, 0, 1))
    + ((1, 0, False), (1, 1, False))
    + tuple((1, unit, False) for unit in (6, 7, 8, 9, 2, 3, 4, 5))
)
SOON = 12
FORWARD_HOOKS = SLABS + PAIRS + 1
SCATTER_RATE, SCATTER_AHEAD, SCATTER_GAP = 2.0, 4, 3
SCATTER_ORDER = ((1, 0), (1, 1)) + tuple((0, unit) for unit in (2, 6, 3, 7, 4, 8, 5, 9, 0, 1))
TURN_RATE, TURN_GAP, TURN_HOOKS = 1.3, 5, PAIRS + 3
HOOKS = PAIRS + 2


def near_self_kernel(
    source_counts, target_counts, attention_in, attention_out, cross, expand, contract, gains, rows,
    square_out, tall_out, cross_out, target_rest, target_tall, own_square, every_gain, away,
    triple, shares, inverse, result, first,
    end, mid, source_normed, active, change, pair, cross_normed, question, cross_shares, cross_inverse, cross_result,
    blocks, tiles, streams, firsts, landing, bias, own, source_square, source_tall, target_cross, share_rows,
    share_done, fetched, block_sent, block_done, block_out, tile_sent, tile_done,
    spread_sent, spread_done, spread_kept, away_sent, away_done, copied,
):
    place = Place()
    layer, depth, side, core = place.layer, place.depth, place.side, place.core
    step, total = pl.program_id(0), 2 * away.shape[0]
    count = away.shape[0]
    copies = Copies()
    share_row = share_rows.at[step % 2]

    def kept_share(target):
        return pltpu.make_async_copy(share_row, target, share_done.at[step % 2])

    kept = [
        ref.at[0]
        for ref in (end, mid, source_normed, active, change, pair, cross_normed, question, cross_inverse, cross_result)
    ]
    kept.insert(8, share_row)
    selfs = [attention_in.at[:, columns(j)] for j in range(3)] + [attention_out]
    sources = [cross.at[:, columns(j)] for j in range(2)] + [expand.at[:, columns(j)] for j in range(SLABS)]
    sources += [contract.at[columns(j, UNIT), :] for j in range(SLABS)]

    def spot(owner, unit, *index):
        if owner == 0:
            if unit < BLOCKS:
                return source_square.at[(unit,) + index]
            return source_tall.at[index + (unit - BLOCKS,)]
        if unit < EXPAND:
            return target_cross.at[(unit,) + index]
        if unit < BLOCKS:
            return target_rest.at[(unit - EXPAND,) + index]
        return target_tall.at[index + (unit - BLOCKS,)]

    units = [
        (owner, late, partial(own.at.__getitem__, unit), partial(spot, owner, unit))
        for owner, unit, late in GATHER_ORDER
    ]
    spread = Spread(place, copies, units, spread_sent, spread_done, spread_kept)

    def away_parts(slot):
        return firsts.at[slot], landing.at[slot], away_sent.at[slot], away_done.at[slot], place.across_layer()

    def block_parts(unit, stage):
        if stage == 0:
            block, target = blocks.at[unit, :, :, core], place.sibling()
        elif stage < DEPTHS:
            block, target = blocks.at[unit, depth, side, core], place.along_depth(stage)
        else:
            block, target = blocks.at[unit, :, side, core], place.across_side()
        return block, block, block_sent.at[unit, stage], block_done.at[unit, stage], target

    def tile_parts(stage):
        if stage == 0:
            block, target = tiles.at[layer], place.across_layer()
        elif stage < DEPTHS:
            block, target = tiles.at[layer, depth, side, core], place.along_depth(stage)
        elif stage == DEPTHS:
            block, target = tiles.at[layer, :, side, core], place.across_side()
        else:
            block, target = tiles.at[layer, :, :, core], place.sibling()
        return block, block, tile_sent.at[stage], tile_done.at[stage], target

    for stage in range(DEPTHS + 2):
        copies.define(("tile", stage), partial(tile_parts, stage))
    for unit in range(SELFS):
        for stage in range(DEPTHS + 1):
            copies.define(("block", unit, stage), partial(block_parts, unit, stage))
    for slot in range(count):
        copies.define(("away", slot), partial(away_parts, slot))

    def lay_gains(which):
        for row in range(DEPTHS):
            value = tiles[which, row, 0, 0].astype(FULL)
            for other in ((0, 1), (1, 0), (1, 1)):
                value = value + tiles[(which, row) + other].astype(FULL)
            every_gain[which, :, columns(row, 128)] = value[:8]

    def fetch(slot):
        return pltpu.make_async_copy(
            rows.at[row_of(layer, slot, count)], streams.at[slot % 2], fetched.at[slot % 2]
        )

    @pl.when(step == 0)
    def _():
        fetch(step).start()
        for unit in range(SELFS):
            blocks[unit, depth, side, core] = selfs[unit][...].astype(LOW)
        for unit in range(UNITS):
            own[unit] = sources[unit][...].astype(LOW)
        tiles[layer, depth, side, core] = gains[...]
        place.greet()
        across = range(1, DEPTHS)
        early = iter(spread.steps(GATHER_AHEAD, GATHER_GAP)[:GATHER_EARLY])
        copies.start(*[("tile", stage) for stage in across])
        for unit in range(SELFS):
            copies.start(*[("block", unit, stage) for stage in across])
        spread.announce()
        for number in range(GATHER_AHEAD):
            spread.begin(number)
        copies.arrived(*[("tile", stage) for stage in across])
        copies.start(("tile", DEPTHS))
        for number in range(GATHER_AHEAD):
            spread.relay(number)
        for unit in range(SELFS):
            copies.arrived(*[("block", unit, stage) for stage in across])
            copies.start(("block", unit, DEPTHS))
        copies.arrived(("tile", DEPTHS))
        copies.start(("tile", DEPTHS + 1))
        for unit in range(SELFS):
            for _ in range(GATHER_EARLY // SELFS):
                next(early)()
            copies.arrived(("block", unit, DEPTHS))
            copies.start(("block", unit, 0))
        copies.arrived(("tile", DEPTHS + 1))
        copies.start(("tile", 0))
        lay_gains(layer)
        copies.arrived(*[("block", unit, 0) for unit in range(OUT)])

    def last_block():
        copies.arrived(("block", OUT, 0))
        pltpu.make_async_copy(blocks, own_square, block_out).start()

    plan = Plan(GATHER_RATE, HOOKS)
    late = plan.fill([last_block] + spread.steps(GATHER_AHEAD, GATHER_GAP)[GATHER_EARLY:], total)
    forward_plan = Plan(FORWARD_RATE, FORWARD_HOOKS)
    late = forward_plan.fill(late, count)

    @pl.when(step + 1 < total)
    def _():
        fetch(step + 1).start()

    @pl.when(step >= 2)
    def _():
        kept_share(shares.at[0]).wait()

    @pl.when(step < total)
    def _():
        row = row_of(layer, step, count)
        causal = layer == 1
        both = [jnp.where(causal, *pair_of) for pair_of in zip(*counts_of(target_counts, source_counts, row))]
        fill_bias(bias, *segments(both), causal)
        fetch(step).wait()
        stream = self_forward(
            streams[step % 2].astype(FULL), every_gain[layer, 0:1, :], lambda unit: blocks[unit].reshape(D, D), bias,
            triple.at[0], share_row, inverse.at[0], result.at[0], partial(plan.hook, step),
        )
        kept_share(shares.at[step]).start()
        stream = stream.astype(LOW)
        first[0] = stream
        firsts[step] = stream
        for slot in range(count):

            @pl.when(step == slot)
            def _(slot=slot):
                copies.start(("away", slot))

        plan.hook(step)

    outward = [
        pltpu.make_async_copy(source, target, copied.at[index])
        for index, (source, target) in enumerate(
            ((source_square, square_out), (source_tall, tall_out), (target_cross, cross_out), (landing, away))
        )
    ]

    @pl.when(step == total)
    def _():
        copies.arrived(("tile", 0))
        lay_gains(1 - layer)
        for number in range(SOON):
            spread.end(number)
        copies.arrived(*[("away", slot) for slot in range(count)])
        for copy in outward:
            copy.start()

    @pl.when(step >= total)
    def _():
        index = step - total
        source_pieces, target_pieces = counts_of(source_counts, target_counts, layer * count + index)
        forward(
            layer, firsts[step - count], landing[index], segments(source_pieces), segments(target_pieces), every_gain,
            lambda slab: source_square[EXPAND + slab].reshape(D, D), lambda slab: source_tall[slab].reshape(D, D),
            lambda part: source_square[CROSS + part].reshape(D, D), lambda part: target_cross[part].reshape(D, D),
            bias, kept, partial(forward_plan.hook, index),
        )
        kept_share(cross_shares.at[index]).start()

    @pl.when(step == total + count - 1)
    def _():
        for thunk in late:
            thunk()
        for number in range(SOON, len(units)):
            spread.end(number)
        copies.finish(*[("away", slot) for slot in range(count)])
        copies.finish(*[("tile", stage) for stage in range(DEPTHS + 2)])
        copies.finish(*[("block", unit, stage) for unit in range(SELFS) for stage in range(DEPTHS + 1)])
        spread.finish()
        pltpu.make_async_copy(blocks, own_square, block_out).wait()
        for copy in outward:
            copy.wait()
        for number in range(2):
            pltpu.make_async_copy(share_rows.at[number], cross_shares.at[number], share_done.at[number]).wait()


def kept_shapes():
    return [
        ((ROW, 3 * D), LOW), ((HEADS, ROW, ROW), LOW), ((ROW, 2 * HD), FULL), ((ROW, D), LOW), ((ROW, D), LOW)
    ]


def near_self(source_counts, target_counts, weights, gains, rows):
    total = rows.shape[0]
    tile = jnp.tile(gains.astype(LOW), (1, 4))
    lane_part = lax.broadcasted_iota(jnp.int32, tile.shape, 1) // UNIT
    tile = jnp.where(lane_part == lax.axis_index("dp") % 4, tile, jnp.zeros_like(tile))
    tile = jnp.pad(tile, ((0, 16 - tile.shape[0]), (0, 0)))
    dma = pltpu.SemaphoreType.DMA
    kept, ahead = kept_shapes(), forward_shapes()
    count = total // 2
    square_shape = (BLOCKS, DEPTHS, SIDES, CORES, UNIT, D)
    tall_shape = (DEPTHS, SIDES, CORES, SLABS, UNIT, D)
    cross_shape, rest_shape = (2,) + square_shape[1:], (SLABS,) + square_shape[1:]
    own_shape = (SELFS,) + square_shape[1:]
    outs = [
        shape_of(shape, LOW) for shape in (square_shape, tall_shape, cross_shape, rest_shape, tall_shape, own_shape)
    ] + [shape_of((2, 8, D), FULL), shape_of((count, ROW, D), LOW)]
    low = lambda *shape: pltpu.VMEM(shape, LOW)

    def later(*shape):
        return pl.BlockSpec((1,) + shape, lambda step: (jnp.maximum(step - total, 0),) + (0,) * len(shape))

    def spec(shape, make):
        return ANYWHERE if shape == (HEADS, ROW, ROW) else make(*shape)

    results = pl.pallas_call(
        near_self_kernel,
        grid=(total + count,),
        in_specs=[SCALARS, SCALARS] + [constant(*value.shape) for value in weights] + [constant(16, 128), ANYWHERE],
        out_specs=[ANYWHERE] * 6
        + [pl.BlockSpec((2, 8, D), lambda row: (0, 0, 0)), ANYWHERE]
        + [spec(shape, partial(per_row, last=total - 1)) for shape, _ in kept]
        + [spec(shape, later) for shape, _ in ahead],
        out_shape=outs
        + [shape_of((total,) + shape, kind) for shape, kind in kept]
        + [shape_of((count,) + shape, kind) for shape, kind in ahead],
        scratch_shapes=[
            low(*own_shape), low(2, DEPTHS, SIDES, CORES, 16, 128), low(2, ROW, D), low(total, ROW, D),
            low(count, ROW, D), low(ROW, ROW), low(UNITS, UNIT, D), low(*square_shape), low(*tall_shape),
            low(*cross_shape), low(2, HEADS, ROW, ROW),
            dma((2,)), dma((2,)), dma((SELFS, 5)), dma((SELFS, 5)), dma, dma((6,)), dma((6,)),
            dma((len(GATHER_ORDER), 6)), dma((len(GATHER_ORDER), 6)), dma((len(GATHER_ORDER),)),
            dma((count,)), dma((count,)), dma((4,)),
        ],
        compiler_params=pltpu.CompilerParams(
            vmem_limit_bytes=VMEM_LIMIT, collective_id=0, has_side_effects=True
        ),
        name="self_forward",
    )(source_counts, target_counts, *weights, tile, rows)
    weights, (own_square, every_gain, away), results = results[:5], results[5:8], results[8:]
    weights = weights[0].reshape(BLOCKS, D, D), weights[1].reshape(FF, D), weights[2].reshape(2, D, D), *weights[3:]
    return weights, own_square, every_gain, away, results[: len(kept)], results[len(kept) :]


def middle_kernel(
    near,
    first, away, cotangent, source_square, source_tall, target_cross, rest, rest_tall, gains,
    kept_end, kept_mid, kept_normed, kept_active, kept_change, kept_pair, kept_cross, kept_question, kept_shares,
    kept_inverse, kept_result,
    section_output, sent_output, kept_delta, sent_delta, square_out, tall_out, gain_out, expand_out, contract_out,
    target_expand, target_contract, shares, inverse, cross_result, source_end, target_mid, value, sending, keeping,
    source_normed, active, memory_low, cross_normed, feed_normed,
    source_change, source_low, delta_pair, delta_question, cross_low, target_change, target_low,
    loaded, stored, kept, ready, output_sent, output_done, delta_sent, delta_done, fetched,
    turn_core, turn_side, turn_depth, turn_layer, turn_sent, turn_done,
):
    place = Place()
    layer = place.layer
    count = away.shape[0]
    copies = Copies()

    def source_expand(slab):
        return source_square[EXPAND + slab]

    def source_contract(slab):
        return source_tall[columns(slab), :]

    if near:

        def spot(unit, *index):
            if unit < SLABS:
                return target_expand.at[(unit,) + index]
            return target_contract.at[index + (unit - SLABS,)]

        def turn_unit(unit):
            def target():
                if unit < SLABS:
                    return expand_out.at[:, columns(unit)]
                return contract_out.at[columns(unit - SLABS, UNIT), :]

            return (
                1,
                lambda: spot(unit, slice(None), slice(None), 1 - place.core),
                lambda *index: spot(unit, *index, place.core),
                None,
                target,
            )

        collect = Collect(
            place, copies, [turn_unit(unit) for unit in range(2 * SLABS)],
            (turn_core, turn_side, turn_depth, turn_layer), turn_sent, turn_done,
        )

        def expand_of(slab):
            return target_expand[slab].reshape(D, D)

        def contract_of(slab):
            return target_contract[slab].reshape(D, D)

    else:

        def expand_of(slab):
            return target_expand[slab]

        def contract_of(slab):
            return target_contract[columns(slab), :]

    whole_rest = [
        pltpu.make_async_copy(rest, target_expand, fetched.at[0]),
        pltpu.make_async_copy(rest_tall, target_contract, fetched.at[1]),
    ]

    def rows_of(row):
        return pl.ds(pl.multiple_of(row * ROW, ROW), ROW)

    def load(row):
        return pltpu.make_async_copy(
            cotangent.at[layer * count + row], target_low.at[columns(row, ROW), :], loaded.at[row]
        )

    def store(row):
        return pltpu.make_async_copy(value, section_output.at[layer * count + row], stored)

    def keep(row):
        return pltpu.make_async_copy(keeping.at[row], kept_delta.at[row], kept.at[row])

    class Parcels:
        def __init__(self, name, target, sent, done):
            self.name, self.target, self.sent, self.done = name, target, sent, done
            for row in range(count):
                copies.define((name, row), partial(self.parts, row))

        def parts(self, row):
            return sending.at[row], self.target.at[row], self.sent.at[row], self.done.at[row], place.across_layer()

        def local(self, row):
            return pltpu.make_async_copy(sending.at[row], self.target.at[row], self.sent.at[row])

        def put(self, row, block):
            for static in range(count):

                @pl.when(row == static)
                def _(static=static):
                    sending[static] = block
                    if near:
                        copies.start((self.name, static))
                    else:
                        self.local(static).start()

        def left(self, row):
            for static in range(count):

                @pl.when(row == static)
                def _(static=static):
                    if near:
                        copies.finish((self.name, static))
                    else:
                        self.local(static).wait()

    outputs = Parcels("output", sent_output, output_sent, output_done)
    deltas = Parcels("delta", sent_delta, delta_sent, delta_done)

    def streams(row):
        own, other = first[row].astype(FULL), away[row].astype(FULL)
        return jnp.where(layer == 0, own, other), jnp.where(layer == 0, other, own)

    def publish(row, owner, block):
        @pl.when(layer == owner)
        def _():
            @pl.when(jnp.asarray(row) > 0)
            def _():
                store(row - 1).wait()

            value[...] = block
            store(row).start()

        @pl.when(layer != owner)
        def _():
            outputs.put(row, block.astype(LOW))

    for row in range(count):
        load(row).start()
    gain_out[...] = jnp.zeros(gain_out.shape, FULL)
    if near:
        place.greet()
    takes = [
        pltpu.make_async_copy(source, target, fetched.at[2 + index])
        for index, (source, target) in enumerate(
            (
                (kept_end, source_end), (kept_mid, target_mid), (kept_normed, source_normed), (kept_cross, cross_normed),
                (kept_result, cross_result), (kept_pair, delta_pair), (kept_question, delta_question),
                (kept_inverse, inverse), (kept_shares.at[count - 1], shares), (kept_change, source_change),
            )
        )
    ]
    take_active = pltpu.make_async_copy(kept_active, active, fetched.at[12])
    for copy in takes[:2] + whole_rest + takes[2:]:
        copy.start()

    def cross_parts(row):
        at = rows_of(row)
        return cross_refs(delta_question.at[at, :], delta_pair.at[at, :])

    def take_shares(row):
        return pltpu.make_async_copy(kept_shares.at[row], shares, fetched.at[13])

    takes[0].wait()
    for row in range(count):
        memory = normalize(source_end[row])[0] * gains[0, 2:3, :]
        memory_low[columns(row, ROW), :] = memory.astype(LOW)
        publish(row, 0, memory)
    for copy in takes[1:2] + whole_rest:
        copy.wait()

    @pl.when(layer == 0)
    def _():
        store(count - 1).wait()

    def turn(row, carry):
        at = rows_of(row)
        stream = target_mid[row]
        normed = (normalize(stream)[0] * gains[1, 2:3, :]).astype(LOW)
        feed_normed[at, :] = normed
        output = feed(
            normed, stream, expand_of, contract_of, active.at[at, :], target_change.at[at, :], no_hook
        )
        publish(row, 1, output)
        for static in range(count):

            @pl.when(row == static)
            def _(static=static):
                load(static).wait()

        delta, delta_gain = feed_back(
            target_low[at, :].astype(FULL), stream, gains[1, 2:3, :], expand_of, contract_of, target_change.at[at, :]
        )
        gain_out[1, 2:3, :] += delta_gain
        target_mid[row] = delta
        return carry

    lax.fori_loop(0, count, turn, 0)

    emitted, late = [], []

    def emit(block, holder, target):
        holder[...] = block.astype(LOW)
        copy = pltpu.make_async_copy(holder, target, ready.at[len(emitted)])
        copy.start()
        emitted.append(copy)
        if late:
            late.pop(0)()

    def feed_grads(which, normed, change, low):
        turned = normed[...].T
        for slab in range(SLABS):
            grown = multiply(turned, change[:, columns(slab)])
            shrunk = multiply(active[:, columns(slab)], low[...], TN)
            emit(grown, change.at[pl.ds(0, D), columns(slab)], square_out.at[which, EXPAND + slab])
            emit(shrunk, change.at[pl.ds(D, D), columns(slab)], tall_out.at[which, columns(slab), :])

    if near:
        turned = feed_normed[...].T
        for slab in range(SLABS):
            grown = multiply(turned, target_change[:, columns(slab)])
            target_expand[slab] = grown.astype(LOW).reshape(DEPTHS, SIDES, CORES, UNIT, D)
            collect.begin(slab)
            shrunk = multiply(active[:, columns(slab)], target_low[...], TN)
            target_contract[slab] = shrunk.astype(LOW).reshape(SIDES, CORES, SLABS, UNIT, D)
        for slab in range(SLABS):
            collect.begin(SLABS + slab)
        plan = Plan(TURN_RATE, TURN_HOOKS)
        late = plan.fill(collect.steps(2 * SLABS, TURN_GAP), count)
    else:
        feed_grads(1, feed_normed, target_change, target_low)
    take_active.start()
    for copy in takes[2:]:
        copy.wait()

    def backward(number, carry):
        row = count - 1 - number
        at = rows_of(row)
        hook = partial(plan.hook, number) if near else no_hook
        source_stream, target_stream = streams(row)

        @pl.when(number > 0)
        def _():
            take_shares(row).wait()

        delta = target_mid[row]
        low = delta.astype(LOW)
        cross_low[at, :] = low
        delta_result = multiply(low, target_cross[1], NT)

        def put(pair, query, keys, values):
            delta_question[at, columns(pair, 2 * HD)] = query
            delta_pair[at, columns(pair, 2 * HD)] = keys
            delta_pair[at, columns(PAIRS + pair, 2 * HD)] = values

        attend_back(
            *cross_parts(row), shares, inverse.at[row], cross_result.at[at, :], delta_result, put, hook
        )

        @pl.when(number < count - 1)
        def _():
            take_shares(row - 1).start()

        unit, scale = normalize(target_stream)
        delta_normed = multiply(delta_question[at, :], target_cross[0], NT)
        delta_stream, delta_gain = norm_back(unit, scale, gains[1, 1:2, :], delta_normed)
        gain_out[1, 1:2, :] += delta_gain
        target_delta = (delta + delta_stream).astype(LOW)
        hook()

        unit, scale = normalize(source_end[row])
        delta_memory = 0.0
        for part in range(2):
            delta_memory = delta_memory + multiply(delta_pair[at, columns(part)], source_square[CROSS + part], NT)
        delta, delta_gain = norm_back(unit, scale, gains[0, 2:3, :], delta_memory)
        gain_out[0, 2:3, :] += delta_gain
        source_low[at, :] = delta.astype(LOW)
        hook()
        delta, delta_gain = feed_back(
            delta, source_stream, gains[0, 1:2, :], source_expand, source_contract, source_change.at[at, :]
        )
        gain_out[0, 1:2, :] += delta_gain
        source_delta = delta.astype(LOW)
        keeping[row] = jnp.where(layer == 0, source_delta, target_delta)
        for static in range(count):

            @pl.when(row == static)
            def _(static=static):
                keep(static).start()

        outputs.left(row)
        deltas.put(row, jnp.where(layer == 0, target_delta, source_delta))
        hook()
        return carry

    lax.fori_loop(0, count, backward, 0)
    take_active.wait()
    feed_grads(0, source_normed, source_change, source_low)
    turned = memory_low[...].T
    for part in range(2):
        grown = multiply(turned, delta_pair[:, columns(part)])
        emit(grown, delta_pair.at[pl.ds(0, D), columns(part)], square_out.at[0, CROSS + part])
    for part, (left, right) in enumerate(((cross_normed, delta_question), (cross_result, cross_low))):
        emit(multiply(left[...], right[...], TN), right.at[pl.ds(0, D), :], square_out.at[1, CROSS + part])
    for thunk in late:
        thunk()
    for copy in emitted:
        copy.wait()

    @pl.when(layer == 1)
    def _():
        store(count - 1).wait()

    for row in range(count):
        keep(row).wait()
        deltas.left(row)
    if near:
        copies.arrived(*[(name, row) for name in ("output", "delta") for row in range(count)])
        collect.finish()


def middle(near, first, away, cotangent, weights, gains, ahead):
    count = away.shape[0]
    tokens = count * ROW
    dma = pltpu.SemaphoreType.DMA
    low = lambda *shape: pltpu.VMEM(shape, LOW)
    full = lambda *shape: pltpu.VMEM(shape, FULL)
    square, tall, cross, rest, rest_tall = weights
    if near:
        expand = low(SLABS, DEPTHS, SIDES, CORES, UNIT, D)
        contract = low(DEPTHS, SIDES, CORES, SLABS, UNIT, D)
    else:
        expand, contract = low(SLABS, D, D), low(FF, D)
    rows_apart = (0, 1, 8, 9)
    ahead = [
        value if place in rows_apart else value.reshape(tokens, value.shape[-1]) for place, value in enumerate(ahead)
    ]
    row_shape = shape_of((count, ROW, D), LOW)
    early_shapes = [(UNIT, FF), (SLABS * UNIT, D)]
    remote = dict(collective_id=2, has_side_effects=True) if near else {}
    outs = pl.pallas_call(
        partial(middle_kernel, near),
        grid=(1,),
        in_specs=[
            pl.BlockSpec((count, ROW, D), lambda step: (1, 0, 0), pipeline_mode=pl.Buffered(1)),
            constant(count, ROW, D), ANYWHERE, constant(BLOCKS, D, D), constant(FF, D), constant(2, D, D),
            ANYWHERE, ANYWHERE, constant(2, 8, D),
        ]
        + [ANYWHERE] * len(ahead),
        out_specs=[ANYWHERE] * 6
        + [pl.BlockSpec((2, 8, D), lambda step: (0, 0, 0))]
        + [pl.BlockSpec(shape, lambda step: (0, 0)) for shape in early_shapes],
        out_shape=[shape_of((2 * count, ROW, D), FULL), row_shape, row_shape, row_shape]
        + [shape_of((2, BLOCKS, D, D), LOW), shape_of((2, FF, D), LOW), shape_of((2, 8, D), FULL)]
        + [shape_of(shape, FULL) for shape in early_shapes],
        scratch_shapes=[
            expand, contract, low(HEADS, ROW, ROW), full(count, ROW, 2 * HD), low(tokens, D),
            full(count, ROW, D), full(count, ROW, D), full(ROW, D), low(count, ROW, D), low(count, ROW, D),
            low(tokens, D), low(tokens, FF), low(tokens, D), low(tokens, D), low(tokens, D),
            low(tokens, FF), low(tokens, D), low(tokens, 2 * D), low(tokens, D), low(tokens, D), low(tokens, FF),
            low(tokens, D),
            dma((count,)), dma, dma((count,)), dma((2 * UNITS,)),
            dma((count,)), dma((count,)), dma((count,)), dma((count,)), dma((14,)),
        ]
        + collect_scratch(2 * SLABS if near else 1),
        compiler_params=pltpu.CompilerParams(vmem_limit_bytes=VMEM_LIMIT, **remote),
        name="middle",
    )(first, away, cotangent, square, tall, cross, rest, rest_tall, gains, *ahead)
    return outs[:7], outs[7:]


def near_back_kernel(
    kept_delta, away_delta, rows, own_square, gains, triple, shares, inverse, result,
    square_sums, tall_sums, gain_sums, early_expand, early_contract,
    gradient, attention_in, attention_out, cross, expand, contract, gain_out,
    deltas, streams, value, delta_triple, sums, low_sums, own_gain, total,
    gain_total, gain_parts, gain_from_layer,
    delta_done, fetched, stored, loaded, gain_sent, gain_done,
    other_core, other_side, other_depth, other_layer, other_sent, other_done,
    own_core, own_side, own_depth, own_layer, own_sent, own_done,
):
    place = Place()
    layer, depth, core = place.layer, place.depth, place.core
    count = kept_delta.shape[0]
    step, steps_in_all = pl.program_id(0), 2 * count
    copies = Copies()

    def other_unit(number):
        which, unit = SCATTER_ORDER[number]

        def share(owner):
            if unit < BLOCKS:
                return square_sums.at[which, unit, :, :, owner]
            return tall_sums.at[which, :, :, owner, unit - BLOCKS]

        def target():
            if unit < EXPAND:
                return cross.at[:, columns(unit - CROSS)]
            if unit < BLOCKS:
                return expand.at[:, columns(unit - EXPAND)]
            return contract.at[columns(unit - BLOCKS, UNIT), :]

        return (
            which,
            lambda: share(1 - core),
            lambda *index: total.at[(number,) + index],
            lambda: pltpu.make_async_copy(share(core), total.at[number], loaded.at[number]),
            target,
        )

    def own_unit(unit):
        return (
            None,
            lambda: low_sums.at[unit, :, :, 1 - core],
            lambda *index: low_sums.at[(unit,) + index + (core,)],
            None,
            lambda: attention_in.at[:, columns(unit)] if unit < OUT else attention_out,
        )

    others = Collect(
        place, copies, [other_unit(number) for number in range(len(SCATTER_ORDER))],
        (other_core, other_side, other_depth, other_layer), other_sent, other_done,
    )
    selfs = Collect(
        place, copies, [own_unit(unit) for unit in range(SELFS)], (own_core, own_side, own_depth, own_layer),
        own_sent, own_done,
    )

    def gain_parts_of(stage):
        if stage == 0:
            source, target, device = gain_sums.at[1 - layer], gain_from_layer, place.across_layer()
        elif stage == 1:
            source, target, device = gain_total.at[0], gain_parts.at[0], place.sibling()
        elif stage == 2:
            source, target, device = gain_total.at[1], gain_parts.at[1], place.across_side()
        else:
            away_by = stage - 2
            source, target = gain_total.at[2, place.other_depth(away_by)], gain_parts.at[2, away_by]
            device = place.along_depth(away_by)
        return source, target, gain_sent.at[stage], gain_done.at[stage], device

    gain_stages = range(3 + DEPTHS - 1)
    for stage in gain_stages:
        copies.define(("gain", stage), partial(gain_parts_of, stage))

    def fetch(index):
        slot = (index + count) % steps_in_all
        return pltpu.make_async_copy(
            rows.at[row_of(layer, slot, count)], streams.at[index % 2], fetched.at[index % 2]
        )

    def store(index):
        slot = (index + count) % steps_in_all
        return pltpu.make_async_copy(
            value.at[index % 2], gradient.at[row_of(layer, slot, count)], stored.at[index % 2]
        )

    takes = [
        pltpu.make_async_copy(source, deltas.at[pl.ds(count * half, count)], delta_done.at[half])
        for half, source in enumerate((kept_delta, away_delta))
    ]

    @pl.when(step == 0)
    def _():
        for take in takes:
            take.start()
        fetch(step).start()
        sums[...] = jnp.zeros(sums.shape, FULL)
        own_gain[...] = jnp.zeros(own_gain.shape, FULL)
        place.greet()
        for number in range(SCATTER_AHEAD):
            others.begin(number)
        copies.start(("gain", 0))

        @pl.when(layer == 1)
        def _():
            expand[...] = early_expand[...]
            contract[...] = early_contract[...]

        for take in takes:
            take.wait()

    plan = Plan(SCATTER_RATE, HOOKS)
    late = plan.fill(others.steps(SCATTER_AHEAD, SCATTER_GAP), steps_in_all)

    def ready(unit):
        low_sums[unit] = sums[unit].astype(LOW).reshape(DEPTHS, SIDES, CORES, UNIT, D)
        selfs.begin(unit)

    for hook, work in ((0, ready), (2, selfs.chip), (4, selfs.sides)):
        plan.steps.setdefault((steps_in_all - 1, hook), []).append(partial(work, OUT))

    @pl.when(step + 1 < steps_in_all)
    def _():
        fetch(step + 1).start()

    fetch(step).wait()
    delta, delta_gain = self_back(
        deltas[step], streams[step % 2].astype(FULL), gains[layer, 0:1, :],
        lambda unit: own_square[unit].reshape(D, D),
        triple.at[0], shares.at[0], inverse.at[0], result.at[0], delta_triple, sums, partial(plan.hook, step),
    )
    own_gain[0:1, :] += delta_gain

    @pl.when(step >= 2)
    def _():
        store(step).wait()

    value[step % 2] = delta.astype(LOW)
    store(step).start()
    plan.hook(step)

    @pl.when(step == steps_in_all - 1)
    def _():
        def more():
            if late:
                late.pop(0)()

        for unit in range(OUT):
            ready(unit)
        copies.arrived(("gain", 0))
        whole = gain_sums[layer] + gain_from_layer[...] + own_gain[...]
        for row in range(DEPTHS):
            gain_total[0, row] = whole[:, 128 * row : 128 * (row + 1)]
        copies.start(("gain", 1))
        more()
        for unit in range(OUT):
            selfs.chip(unit)
        copies.arrived(("gain", 1))
        gain_total[1] = gain_total[0] + gain_parts[0]
        copies.start(("gain", 2))
        for unit in range(OUT):
            more()
            selfs.sides(unit)
        copies.arrived(("gain", 2))
        gain_total[2] = gain_total[1] + gain_parts[1]
        copies.start(*[("gain", 2 + away_by) for away_by in range(1, DEPTHS)])
        for unit in (OUT, *range(OUT)):
            more()
            selfs.depths(unit)
        while late:
            more()
        whole = gain_total[2, depth]
        for away_by in range(1, DEPTHS):
            copies.arrived(("gain", 2 + away_by))
            whole = whole + gain_parts[2, away_by]
        gain_out[...] = whole
        store(step - 1).wait()
        store(step).wait()
        copies.finish(*[("gain", stage) for stage in gain_stages])
        others.finish()
        selfs.finish()


def near_back(kept_delta, away_delta, rows, own_square, gains, kept, square_sums, tall_sums, gain_sums, early):
    count, total = kept_delta.shape[0], rows.shape[0]
    dma = pltpu.SemaphoreType.DMA
    vmem = pl.BlockSpec(memory_space=pltpu.VMEM)
    shapes = kept_shapes()[:4]

    def rotated(*shape):
        return pl.BlockSpec((1,) + shape, lambda step: ((step + count) % total,) + (0,) * len(shape))

    units = len(SCATTER_ORDER)
    weight_shapes = [(UNIT, 3 * D), (UNIT, D), (UNIT, 2 * D), (UNIT, FF), (SLABS * UNIT, D), (8, 128)]
    low = lambda *shape: pltpu.VMEM(shape, LOW)
    full = lambda *shape: pltpu.VMEM(shape, FULL)
    gradient, *weights, gain = pl.pallas_call(
        near_back_kernel,
        grid=(total,),
        in_specs=[ANYWHERE, ANYWHERE, ANYWHERE, constant(SELFS, DEPTHS, SIDES, CORES, UNIT, D), constant(2, 8, D)]
        + [rotated(*shape) for shape, _ in shapes]
        + [ANYWHERE, ANYWHERE, constant(2, 8, D), constant(UNIT, FF), constant(SLABS * UNIT, D)],
        out_specs=[ANYWHERE] + [pl.BlockSpec(shape, lambda step: (0, 0)) for shape in weight_shapes],
        out_shape=[shape_of((total, ROW, D), LOW)] + [shape_of(shape, FULL) for shape in weight_shapes],
        scratch_shapes=[
            low(total, ROW, D), low(2, ROW, D), low(2, ROW, D), low(ROW, 3 * D), full(SELFS, D, D),
            low(SELFS, DEPTHS, SIDES, CORES, UNIT, D), full(8, D), low(units, DEPTHS, SIDES, UNIT, D),
            full(3, DEPTHS, 8, 128), full(3, DEPTHS, 8, 128), full(8, D),
            dma((2,)), dma((2,)), dma((2,)), dma((units,)), dma((6,)), dma((6,)),
        ]
        + collect_scratch(units)
        + collect_scratch(SELFS, False),
        compiler_params=pltpu.CompilerParams(
            vmem_limit_bytes=VMEM_LIMIT, collective_id=1, has_side_effects=True
        ),
        name="self_back",
    )(
        kept_delta, away_delta, rows, own_square, gains, *kept[:4],
        square_sums.reshape(2, BLOCKS, DEPTHS, SIDES, CORES, UNIT, D),
        tall_sums.reshape(2, DEPTHS, SIDES, CORES, SLABS, UNIT, D), gain_sums, *early,
    )
    start = lax.axis_index("dp") % 4 * UNIT
    return gradient.astype(FULL), *weights, lax.dynamic_slice_in_dim(gain[:3], start, UNIT, axis=1)


def far_self_kernel(
    source_counts, target_counts, rows, square, gains, triple, shares, inverse, result, first, bias
):
    layer, step, count = lax.axis_index("pipe"), pl.program_id(0), pl.num_programs(0) // 2
    row = row_of(layer, step, count)
    causal = layer == 1
    both = [jnp.where(causal, target_counts[row, piece], source_counts[row, piece]) for piece in range(PACK)]
    fill_bias(bias, *segments(both), causal)
    first[0] = self_forward(
        rows[0].astype(FULL), gains[layer, 0:1, :], lambda unit: square[unit], bias,
        triple.at[0], shares.at[0], inverse.at[0], result.at[0], no_hook,
    ).astype(LOW)


def far_self(source_counts, target_counts, square, gains, rows):
    total = rows.shape[0]
    kept = kept_shapes()
    return pl.pallas_call(
        far_self_kernel,
        grid=(total,),
        in_specs=[SCALARS, SCALARS, per_row(ROW, D), constant(SELFS, D, D), constant(2, 8, D)],
        out_specs=[per_row(*shape) for shape, _ in kept],
        out_shape=[shape_of((total,) + shape, kind) for shape, kind in kept],
        scratch_shapes=[pltpu.VMEM((ROW, ROW), FULL)],
        compiler_params=PARAMS,
        name="self_forward",
    )(source_counts, target_counts, rows, square, gains)


def far_forward_kernel(
    source_counts, target_counts, first, away, square, tall, cross, gains, *refs
):
    layer, step, count = lax.axis_index("pipe"), pl.program_id(0), pl.num_programs(0)
    source_pieces, target_pieces = counts_of(source_counts, target_counts, layer * count + step)
    forward(
        layer, first[0], away[0], segments(source_pieces), segments(target_pieces), gains,
        lambda slab: square[EXPAND + slab], lambda slab: tall[columns(slab), :],
        lambda part: square[CROSS + part], lambda part: cross[part], refs[-1], [ref.at[0] for ref in refs[:-1]], no_hook,
    )


def far_forward(source_counts, target_counts, first, away, square, tall, cross, gains):
    count = away.shape[0]
    kept = forward_shapes()
    return pl.pallas_call(
        far_forward_kernel,
        grid=(count,),
        in_specs=[
            SCALARS, SCALARS, per_row(ROW, D, start=count), per_row(ROW, D), constant(BLOCKS, D, D), constant(FF, D),
            constant(2, D, D), constant(2, 8, D),
        ],
        out_specs=[per_row(*shape) for shape, _ in kept],
        out_shape=[shape_of((count,) + shape, kind) for shape, kind in kept],
        scratch_shapes=[pltpu.VMEM((ROW, ROW), LOW)],
        compiler_params=PARAMS,
        name="forward",
    )(source_counts, target_counts, first, away, square, tall, cross, gains)


def far_back_kernel(
    deltas, rows, square, gains, triple, shares, inverse, result, gradient, sums, gain_out, delta_triple
):
    layer, step = lax.axis_index("pipe"), pl.program_id(0)

    @pl.when(step == 0)
    def _():
        sums[...] = jnp.zeros(sums.shape, FULL)
        gain_out[...] = jnp.zeros(gain_out.shape, FULL)

    delta, delta_gain = self_back(
        deltas[0], rows[0].astype(FULL), gains[layer, 0:1, :], lambda unit: square[unit],
        triple.at[0], shares.at[0], inverse.at[0], result.at[0], delta_triple, sums, no_hook,
    )
    gain_out[0:1, :] += delta_gain
    gradient[0] = delta


def far_back(deltas, rows, square, gains, kept):
    total = rows.shape[0]
    return pl.pallas_call(
        far_back_kernel,
        grid=(total,),
        in_specs=[per_row(ROW, D), per_row(ROW, D), constant(SELFS, D, D), constant(2, 8, D)]
        + [per_row(*shape) for shape, _ in kept_shapes()[:4]],
        out_specs=[per_row(ROW, D), constant(SELFS, D, D), constant(8, D)],
        out_shape=[shape_of((total, ROW, D), FULL), shape_of((SELFS, D, D), FULL), shape_of((8, D), FULL)],
        scratch_shapes=[pltpu.VMEM((ROW, 3 * D), LOW)],
        compiler_params=PARAMS,
        name="self_back",
    )(deltas, rows, square, gains, *kept[:4])


def spotsof(value):
    return [value[:, start : start + D] for start in range(0, value.shape[1], D)]


def gather_all(value, axes):
    return lax.all_gather(value, axes, axis=0, tiled=False)


def far_weights(weights, gains, shards):
    attention_in, attention_out, cross, expand, contract = (value.astype(LOW) for value in weights)
    both = ("pipe", "dp")
    own = jnp.stack(spotsof(attention_in) + [attention_out])
    own = jnp.swapaxes(gather_all(own, "dp"), 0, 1).reshape(SELFS, D, D)
    square = gather_all(jnp.stack(spotsof(cross) + spotsof(expand)), both)
    square = jnp.swapaxes(square.reshape(2, shards, BLOCKS, D // shards, D), 1, 2)
    tall = gather_all(contract, both)
    gains = gather_all(gains.astype(LOW), both).reshape(2, shards, 3, D // shards)
    gains = jnp.swapaxes(gains, 1, 2).reshape(2, 3, D).astype(FULL)
    return own, square.reshape(2, BLOCKS, D, D), tall.reshape(2, FF, D), jnp.pad(gains, ((0, 0), (0, 5), (0, 0)))


def scattered(value, axes):
    return lax.psum_scatter(value, axes, scatter_dimension=0, tiled=False).astype(FULL)


def far_sums(own, own_gain, square, tall, gains, section, shards):
    both = ("pipe", "dp")
    share = D // shards
    own = scattered(jnp.swapaxes(own.reshape(SELFS, shards, share, D), 0, 1), "dp")
    square = jnp.swapaxes(square.reshape(2, BLOCKS, shards, share, D), 1, 2)
    square = scattered(square.reshape(2 * shards, BLOCKS, share, D), both)
    tall = scattered(tall.reshape(2 * shards, FF // shards, D), both)
    gains = gains + jnp.where(jnp.arange(2)[:, None, None] == section, own_gain[None], 0.0)
    gains = jnp.swapaxes(gains[:, :3].reshape(2, 3, shards, share), 1, 2)
    gains = scattered(gains.reshape(2 * shards, 3, share), both)

    def joined(value, first, last):
        return jnp.concatenate([value[block] for block in range(first, last)], axis=1)

    return (
        joined(own, QKV, OUT), own[OUT], joined(square, CROSS, EXPAND), joined(square, EXPAND, BLOCKS), tall, gains
    )


def swap(value):
    return lax.ppermute(value, "pipe", [(0, 1), (1, 0)])


def local(
    section_input,
    attention_in,
    attention_out,
    cross_weights,
    expand,
    contract,
    norm_gains,
    source_lengths,
    target_lengths,
    cotangent,
):
    section = lax.axis_index("pipe")
    shards = lax.axis_size("dp")
    near = shards == DEPTHS * SIDES * CORES
    rows = section_input[0]
    count = rows.shape[0] // 2
    weights = tuple(value[0] for value in (attention_in, attention_out, cross_weights, expand, contract))
    if near:
        weights, own_square, gains, away, kept, ahead = near_self(
            source_lengths, target_lengths, weights, norm_gains[0], rows
        )
    else:
        turn = jnp.where(section == 0, count, 0)
        own_square, square, tall, gains = far_weights(weights, norm_gains[0], shards)
        weights = square[0], tall[0], square[1, CROSS:EXPAND], square[1, EXPAND:], tall[1]
        slots = jnp.roll(rows, turn, axis=0)
        kept = far_self(source_lengths, target_lengths, own_square, gains, slots)
        away = swap(kept[-1][:count])
        ahead = far_forward(source_lengths, target_lengths, kept[-1], away, *weights[:3], gains)
    (section_output, away_output, kept_delta, away_delta, *sums), early = middle(
        near, kept[-1], away, cotangent, weights, gains, ahead
    )
    if near:
        gradient, *weight_sums = near_back(
            kept_delta, away_delta, rows, own_square, gains, kept, *sums, early
        )
    else:
        away_output, away_delta = swap(away_output), swap(away_delta)
        deltas = jnp.concatenate([away_delta, kept_delta], axis=0)
        gradient, own_sums, own_gain = far_back(deltas, slots, own_square, gains, kept)
        gradient = jnp.roll(gradient, -turn, axis=0)
        weight_sums = far_sums(own_sums, own_gain, *sums, section, shards)
    section_output = lax.dynamic_update_slice_in_dim(
        section_output, away_output.astype(FULL), count * (1 - section), axis=0
    )
    return (section_output[None], gradient[None]) + tuple(value[None] for value in weight_sums)


def solution(mesh):
    in_specs = (
        P("pipe", "dp", None, None),
        P("pipe", "dp", None),
        P("pipe", "dp", None),
        P("pipe", "dp", None),
        P("pipe", "dp", None),
        P("pipe", "dp", None),
        P("pipe", None, "dp"),
        P("dp", None),
        P("dp", None),
        P("dp", None, None),
    )
    out_specs = (
        P("pipe", "dp", None, None),
        P("pipe", "dp", None, None),
        P("pipe", "dp", None),
        P("pipe", "dp", None),
        P("pipe", "dp", None),
        P("pipe", "dp", None),
        P("pipe", "dp", None),
        P("pipe", None, "dp"),
    )
    return jax.shard_map(local, mesh=mesh, in_specs=in_specs, out_specs=out_specs, check_vma=False)
```

```python
from functools import partial
import math

import jax
import jax.numpy as jnp
from jax import lax
from jax.experimental import pallas as pl
from jax.experimental.pallas import tpu as pltpu
from jax.sharding import PartitionSpec as P

D = 512
HEADS = 8
HD = 64
FF = 2048
ROW = 512
PAIRS = HEADS // 2
PACK = 4

QKV, OUT, SELFS = 0, 3, 4
CROSS, EXPAND, BLOCKS = 0, 2, 6
SLABS = FF // D
UNITS = BLOCKS + SLABS

EPSILON = 1e-05
MASKED = -1e30
LOG2E = math.log2(math.e)
EXPONENT = HD**-0.5 * LOG2E
BELL = 1.0 / math.sqrt(2.0 * math.pi)
LOW = jnp.bfloat16
FULL = jnp.float32
VMEM_LIMIT = 63 * 2**20

NN = (((1,), (0,)), ((), ()))
NT = (((1,), (1,)), ((), ()))
TN = (((0,), (0,)), ((), ()))


def multiply(left, right, dims=NN):
    return lax.dot_general(left, right, dims, preferred_element_type=jnp.float32)


def columns(index, width=D):
    return pl.ds(index * width, width)


def normalize(stream):
    centred = stream - jnp.mean(stream, axis=1, keepdims=True)
    scale = lax.rsqrt(jnp.mean(centred * centred, axis=1, keepdims=True) + EPSILON)
    return centred * scale, scale


def norm_back(unit, scale, gain, delta):
    inner = delta * gain
    mean = jnp.mean(inner, axis=1, keepdims=True)
    along = jnp.mean(inner * unit, axis=1, keepdims=True)
    return scale * (inner - mean - unit * along), jnp.sum(delta * unit, axis=0, keepdims=True)


def segment(counts, shape, axis):
    places = lax.broadcasted_iota(jnp.int32, shape, axis)
    end = counts[0]
    found = (places >= end).astype(jnp.int32)
    for count in counts[1:]:
        end = end + count
        found = found + (places >= end).astype(jnp.int32)
    return found


def segments(counts):
    return segment(counts, (ROW, 1), 0), segment(counts, (1, ROW), 1)


def fill_bias(bias, query_segment, key_segment, causal=None):
    keep = query_segment == key_segment
    if causal is not None:
        query = lax.broadcasted_iota(jnp.int32, (ROW, ROW), 0)
        key = lax.broadcasted_iota(jnp.int32, (ROW, ROW), 1)
        keep = keep & (key <= query + jnp.where(causal, 0, ROW))
    bias[...] = jnp.where(keep, 0.0, MASKED).astype(bias.dtype)


def lanes():
    return lax.broadcasted_iota(jnp.int32, (1, 2 * HD), 1)


def only_half(value, half):
    return jnp.where(lanes() // HD == half, value, jnp.zeros_like(value))


def attend(query, keys, values, bias, shares, inverse, result, hook):
    kept = jnp.zeros((ROW, 2 * HD), FULL)
    for pair in range(PAIRS):
        query2, keys2, values2 = query(pair), keys(pair), values(pair)
        parts = []
        for half in range(2):
            head = 2 * pair + half
            scores = multiply(only_half(query2, half), keys2, NT) + bias[...]
            top = jnp.max(scores, axis=1, keepdims=True)
            weights = jnp.exp2((scores - top) * EXPONENT)
            scale = 1.0 / jnp.sum(weights, axis=1, keepdims=True)
            low = weights.astype(LOW)
            shares[head] = low
            parts.append(multiply(low, values2) * scale)
            kept = jnp.where(lanes() == head, scale, kept)
        result[:, columns(pair, 2 * HD)] = jnp.where(lanes() < HD, parts[0], parts[1]).astype(LOW)
        hook()
    inverse[...] = kept


def attend_back(query, keys, values, shares, inverse, result, delta, put, hook):
    for pair in range(PAIRS):
        query2, keys2, values2 = query(pair), keys(pair), values(pair)
        place = slice(2 * HD * pair, 2 * HD * (pair + 1))
        scale = jnp.where(
            lanes() < HD, inverse[:, 2 * pair : 2 * pair + 1], inverse[:, 2 * pair + 1 : 2 * pair + 2]
        )
        low = (delta[:, place] * scale).astype(LOW)
        product = low.astype(FULL) * result[:, columns(pair, 2 * HD)].astype(FULL)
        query_turned, low_turned = query2.T, low.T
        delta_query = 0.0
        delta_keys, delta_values = [], []
        for half in range(2):
            weights = shares[2 * pair + half]
            along = jnp.sum(only_half(product, half), axis=1, keepdims=True)
            delta_shares = multiply(only_half(low, half), values2, NT)
            delta_scores = (weights.astype(FULL) * (delta_shares - along)).astype(LOW)
            delta_query = delta_query + multiply(delta_scores, only_half(keys2, half))
            own = slice(HD * half, HD * (half + 1))
            delta_keys.append(multiply(query_turned[own], delta_scores))
            delta_values.append(multiply(low_turned[own], weights))
        keys_turned = (jnp.concatenate(delta_keys, axis=0) * HD**-0.5).astype(LOW)
        values_turned = jnp.concatenate(delta_values, axis=0).astype(LOW)
        put(pair, (delta_query * HD**-0.5).astype(LOW), keys_turned.T, values_turned.T)
        hook()


def self_parts(triple):
    return tuple(
        (lambda pair, start=part * PAIRS: triple[:, columns(start + pair, 2 * HD)]) for part in range(3)
    )


def put_triple(target):
    def put(pair, *parts):
        for part, value in enumerate(parts):
            target[:, columns(part * PAIRS + pair, 2 * HD)] = value

    return put


def feed(normed, stream, expand, contract, active, slope, hook):
    total = stream
    for slab in range(SLABS):
        hidden = multiply(normed, expand(slab))
        under = 0.5 + 0.5 * lax.erf(hidden * math.sqrt(0.5))
        bell = BELL * jnp.exp2(hidden * hidden * (-0.5 * LOG2E))
        low = (hidden * under).astype(LOW)
        active[:, columns(slab)] = low
        slope[:, columns(slab)] = (under + hidden * bell).astype(LOW)
        total = total + multiply(low, contract(slab))
        hook()
    return total


def feed_back(delta, stream, gain, expand, contract, change):
    unit, scale = normalize(stream)
    low = delta.astype(LOW)
    delta_normed = 0.0
    for slab in range(SLABS):
        delta_active = multiply(low, contract(slab), NT)
        delta_hidden = (delta_active * change[:, columns(slab)].astype(FULL)).astype(LOW)
        change[:, columns(slab)] = delta_hidden
        delta_normed = delta_normed + multiply(delta_hidden, expand(slab), NT)
    delta_stream, delta_gain = norm_back(unit, scale, gain, delta_normed)
    return delta + delta_stream, delta_gain


def self_forward(stream, gain, square, bias, triple, shares, inverse, result, hook):
    normed = (normalize(stream)[0] * gain).astype(LOW)
    for part in range(3):
        triple[:, columns(part)] = multiply(normed, square(QKV + part)).astype(LOW)
    hook()
    attend(*self_parts(triple), bias, shares, inverse, result, hook)
    return stream + multiply(result[...], square(OUT))


def self_back(low, stream, gain, square, triple, shares, inverse, result, delta_triple, sums, hook):
    unit, scale = normalize(stream)
    sums[OUT] += multiply(result[...], low, TN)
    delta_result = multiply(low, square(OUT), NT)
    hook()
    attend_back(*self_parts(triple), shares, inverse, result, delta_result, put_triple(delta_triple), hook)
    turned = (unit * gain).astype(LOW).T
    delta_normed = 0.0
    for part in range(3):
        chunk = delta_triple[:, columns(part)]
        sums[QKV + part] += multiply(turned, chunk)
        delta_normed = delta_normed + multiply(chunk, square(QKV + part), NT)
    delta_stream, delta_gain = norm_back(unit, scale, gain, delta_normed)
    return low.astype(FULL) + delta_stream, delta_gain


def forward(
    layer, own, other, source_segment, target_segment, gains, expand, contract, pair_weights, cross, bias, kept, hook
):
    end_out, mid_out, normed_out, active, change, pair, cross_normed, question, shares, inverse, result = kept
    source_stream = jnp.where(layer == 0, own, other).astype(FULL)
    target_stream = jnp.where(layer == 0, other, own).astype(FULL)
    normed = (normalize(source_stream)[0] * gains[0, 1:2, :]).astype(LOW)
    normed_out[...] = normed
    end = feed(normed, source_stream, expand, contract, active, change, hook)
    end_out[...] = end
    low = (normalize(end)[0] * gains[0, 2:3, :]).astype(LOW)
    for part in range(2):
        pair[:, columns(part)] = multiply(low, pair_weights(part)).astype(LOW)
    hook()
    fill_bias(bias, target_segment[0], source_segment[1])
    normed = (normalize(target_stream)[0] * gains[1, 1:2, :]).astype(LOW)
    cross_normed[...] = normed
    question[...] = multiply(normed, cross(0)).astype(LOW)
    attend(*cross_refs(question, pair), bias, shares, inverse, result, hook)
    mid_out[...] = target_stream + multiply(result[...], cross(1))


def forward_shapes():
    return [
        ((ROW, D), FULL), ((ROW, D), FULL), ((ROW, D), LOW), ((ROW, FF), LOW), ((ROW, FF), LOW), ((ROW, 2 * D), LOW),
        ((ROW, D), LOW), ((ROW, D), LOW), ((HEADS, ROW, ROW), LOW), ((ROW, 2 * HD), FULL), ((ROW, D), LOW),
    ]


def cross_refs(question, pair):
    return (
        lambda number: question[:, columns(number, 2 * HD)],
        lambda number: pair[:, columns(number, 2 * HD)],
        lambda number: pair[:, columns(PAIRS + number, 2 * HD)],
    )


def counts_of(source_counts, target_counts, row):
    return [[counts[row, piece] for piece in range(PACK)] for counts in (source_counts, target_counts)]


def no_hook():
    pass


def per_row(*shape, last=None, start=0, buffers=2):
    def index(row):
        return (start + (row if last is None else jnp.minimum(row, last)),) + (0,) * len(shape)

    return pl.BlockSpec((1,) + shape, index, pipeline_mode=pl.Buffered(buffers) if buffers != 2 else None)


def constant(*shape):
    return pl.BlockSpec(shape, lambda row: (0,) * len(shape), pipeline_mode=pl.Buffered(1))


ANYWHERE = pl.BlockSpec(memory_space=pl.ANY)
SCALARS = pl.BlockSpec(memory_space=pltpu.SMEM)
PARAMS = pltpu.CompilerParams(vmem_limit_bytes=VMEM_LIMIT)


def shape_of(shape, kind):
    return jax.ShapeDtypeStruct(shape, kind)


MESH = pl.DeviceIdType.MESH
UNITS = BLOCKS + SLABS
UNIT = 32
DEPTHS, SIDES, CORES = 4, 2, 2


class Place:
    def __init__(self):
        self.layer = lax.axis_index("pipe")
        self.rank = lax.axis_index("dp")
        self.core = self.rank % CORES
        self.side = self.rank // CORES % SIDES
        self.depth = self.rank // (CORES * SIDES)

    def sibling(self):
        return (self.layer, self.rank + 1 - 2 * self.core)

    def across_side(self):
        return (self.layer, self.rank + CORES * (1 - 2 * self.side))

    def across_layer(self):
        return (1 - self.layer, self.rank)

    def other_depth(self, step):
        return (self.depth + step) % DEPTHS

    def along_depth(self, step):
        return (self.layer, self.rank + CORES * SIDES * (self.other_depth(step) - self.depth))

    def greet(self):
        partners = [self.sibling(), self.across_side(), self.across_layer()]
        partners += [self.along_depth(step) for step in range(1, DEPTHS)]
        barrier = pltpu.get_barrier_semaphore()
        for partner in partners:
            pl.semaphore_signal(barrier, inc=1, device_id=partner, device_id_type=MESH)
        pl.semaphore_wait(barrier, len(partners))


def row_of(layer, slot, count):
    return (slot + count * (1 - layer)) % (2 * count)


class Plan:
    def __init__(self, rate, hooks):
        self.rate, self.hooks = rate, hooks
        self.steps = {}
        self.index = 0

    def fill(self, thunks, rows):
        late = []
        for number, thunk in enumerate(thunks):
            place = int(number * self.rate)
            if place < rows * self.hooks:
                self.steps.setdefault(divmod(place, self.hooks), []).append(thunk)
            else:
                late.append(thunk)
        return late

    def hook(self, step):
        index, self.index = self.index, self.index + 1
        for (row, place), thunks in sorted(self.steps.items(), key=lambda item: item[0]):
            if place == index:

                @pl.when(step == row)
                def _(thunks=thunks):
                    for thunk in thunks:
                        thunk()


class Copies:
    def __init__(self):
        self.made = {}

    def define(self, key, parts):
        def make():
            source, target, sent, arrived, device = parts()
            return pltpu.make_async_remote_copy(
                src_ref=source, dst_ref=target, send_sem=sent, recv_sem=arrived, device_id=device,
                device_id_type=MESH,
            )

        self.made[key] = make

    def start(self, *keys):
        for key in keys:
            self.made[key]().start()

    def arrived(self, *keys):
        for key in keys:
            self.made[key]().wait_recv()

    def finish(self, *keys):
        for key in keys or self.made:
            self.made[key]().wait_send()


class Spread:
    LAYER, SIDE, CORE, RELAY = 3, 4, 5, 6

    def __init__(self, place, copies, units, sent, done, kept):
        self.place, self.copies, self.units = place, copies, units
        self.sent, self.done, self.kept = sent, done, kept
        for number in range(len(units)):
            for stage in range(self.RELAY + DEPTHS - 1):
                copies.define((self, number, stage), partial(self.parts, number, stage))

    def parts(self, number, stage):
        place, (_, late, source, spot) = self.place, self.units[number]
        own, slot, everything = spot(place.depth, place.side, place.core), stage, slice(None)
        if stage < self.LAYER:
            block, target, device = source(), own, place.along_depth(stage + 1)
        elif stage == self.LAYER:
            block, target, device = source(), own, place.across_layer()
            if late:
                block = target = spot(everything, everything, place.core)
        elif stage == self.SIDE:
            block = target = spot(everything, place.side, place.core)
            device = place.across_side()
        elif stage == self.CORE:
            block = target = spot(everything, everything, place.core)
            device = place.sibling()
        else:
            slot = stage - self.RELAY
            block, target, device = own, own, place.along_depth(slot + 1)
        return block, target, self.sent.at[number, slot], self.done.at[number, slot], device

    def keys(self, number, *stages):
        return [(self, number, stage) for stage in stages]

    def along(self, number):
        return self.keys(number, *range(DEPTHS - 1))

    def relayed(self, number):
        return self.keys(number, *range(self.RELAY, self.RELAY + DEPTHS - 1))

    def keep(self, number):
        _, _, source, spot = self.units[number]
        place = self.place
        return pltpu.make_async_copy(source(), spot(place.depth, place.side, place.core), self.kept.at[number])

    def owned(self, number):
        return pl.when(self.place.layer == self.units[number][0])

    def foreign(self, number):
        return pl.when(self.place.layer != self.units[number][0])

    def late(self, number):
        return self.units[number][1]

    def announce(self):
        for number in range(len(self.units)):
            if not self.late(number):

                @self.owned(number)
                def _(number=number):
                    self.copies.start(*self.keys(number, self.LAYER))

    def begin(self, number):
        @self.owned(number)
        def _():
            self.copies.start(*self.along(number))
            self.keep(number).start()

    def relay(self, number):
        if not self.late(number):

            @self.foreign(number)
            def _():
                self.copies.arrived(*self.keys(number, self.LAYER))
                self.copies.start(*self.relayed(number))

    def cross(self, number):
        def work():
            self.copies.arrived(*self.along(number))
            self.copies.start(*self.keys(number, self.SIDE))

        @self.owned(number)
        def _():
            self.keep(number).wait()
            if self.late(number):
                work()

        if not self.late(number):
            work()

    def share(self, number):
        def work():
            self.copies.arrived(*self.keys(number, self.SIDE))
            self.copies.start(*self.keys(number, self.CORE))

        if self.late(number):

            @self.owned(number)
            def _():
                work()
                self.copies.start(*self.keys(number, self.LAYER))

        else:
            work()

    def pass_on(self, number):
        if self.late(number):

            @self.foreign(number)
            def _():
                self.copies.arrived(*self.keys(number, self.LAYER))
                self.copies.start(*self.keys(number, self.CORE))

    def end(self, number):
        self.copies.arrived(*self.keys(number, self.CORE))

    def finish(self):
        for number in range(len(self.units)):
            first = self.along(number) + self.keys(number, self.SIDE)

            @self.owned(number)
            def _(number=number, first=first):
                self.copies.finish(*self.keys(number, self.LAYER))
                if self.late(number):
                    self.copies.finish(*first)

            if not self.late(number):
                self.copies.finish(*first)
            self.copies.finish(*self.keys(number, self.CORE))

    def steps(self, ahead, gap):
        def one(number):
            if ahead <= number + ahead < len(self.units):
                self.begin(number + ahead)
                self.relay(number + ahead)
            if number < len(self.units):
                self.cross(number)
            if 0 <= number - gap < len(self.units):
                self.share(number - gap)
            if 0 <= number - 2 * gap < len(self.units):
                self.pass_on(number - 2 * gap)

        return [partial(one, number) for number in range(len(self.units) + 2 * gap)]


def add_low(left, right):
    return (left.astype(FULL) + right.astype(FULL)).astype(LOW)


class Collect:
    SIDE, DEPTH, LAYER = 1, 2, 5

    def __init__(self, place, copies, units, buffers, sent, done):
        self.place, self.copies, self.units = place, copies, units
        self.from_core, self.from_side, self.from_depth, self.from_layer = buffers
        self.sent, self.done = sent, done
        for number in range(len(units)):
            for stage in range(self.LAYER + 1):
                copies.define((self, number, stage), partial(self.parts, number, stage))

    def parts(self, number, stage):
        place, (_, outgoing, total, _, _) = self.place, self.units[number]
        if stage == 0:
            source, target, device = outgoing(), self.from_core.at[number], place.sibling()
        elif stage == self.SIDE:
            source = total(slice(None), 1 - place.side)
            target, device = self.from_side.at[number], place.across_side()
        elif stage < self.LAYER:
            away_by = stage - self.DEPTH + 1
            source = total(place.other_depth(away_by), place.side)
            target, device = self.from_depth.at[number, away_by - 1], place.along_depth(away_by)
        else:
            source, target = total(place.depth, place.side), self.from_layer.at[number]
            device = place.across_layer()
        return source, target, self.sent.at[number, stage], self.done.at[number, stage], device

    def keys(self, number, *stages):
        return [(self, number, stage) for stage in stages]

    def along(self, number):
        return self.keys(number, *range(self.DEPTH, self.LAYER))

    def begin(self, number):
        load = self.units[number][3]
        if load is not None:
            load().start()
        self.copies.start(*self.keys(number, 0))

    def chip(self, number):
        _, _, total, load, _ = self.units[number]
        if load is not None:
            load().wait()
        self.copies.arrived(*self.keys(number, 0))

        def add(depth, carry):
            share = total(depth, slice(None))
            share[...] = add_low(share[...], self.from_core[number, depth])
            return carry

        lax.fori_loop(0, DEPTHS, add, 0)
        self.copies.start(*self.keys(number, self.SIDE))

    def sides(self, number):
        total = self.units[number][2]
        self.copies.arrived(*self.keys(number, self.SIDE))

        def add(depth, carry):
            share = total(depth, self.place.side)
            share[...] = add_low(share[...], self.from_side[number, depth])
            return carry

        lax.fori_loop(0, DEPTHS, add, 0)
        self.copies.start(*self.along(number))

    def depths(self, number):
        owner, _, total, _, target = self.units[number]
        self.copies.arrived(*self.along(number))
        share = total(self.place.depth, self.place.side)
        value = share[...].astype(FULL)
        for other in range(DEPTHS - 1):
            value = value + self.from_depth[number, other].astype(FULL)
        if owner is None:
            target()[...] = value
            return

        @pl.when(self.place.layer == owner)
        def _():
            target()[...] = value

        @pl.when(self.place.layer != owner)
        def _():
            share[...] = value.astype(LOW)
            self.copies.start(*self.keys(number, self.LAYER))

    def layers(self, number):
        owner, target = self.units[number][0], self.units[number][4]
        if owner is not None:

            @pl.when(self.place.layer == owner)
            def _():
                self.copies.arrived(*self.keys(number, self.LAYER))
                target()[...] = target()[...] + self.from_layer[number].astype(FULL)

    def finish(self):
        for number, unit in enumerate(self.units):
            self.copies.finish(*self.keys(number, 0, self.SIDE), *self.along(number))
            if unit[0] is not None:

                @pl.when(self.place.layer != unit[0])
                def _(number=number):
                    self.copies.finish(*self.keys(number, self.LAYER))

    def steps(self, ahead, gap):
        count = len(self.units)

        def one(number):
            if ahead <= number + ahead < count:
                self.begin(number + ahead)
            for place, work in enumerate((self.chip, self.sides, self.depths, self.layers)):
                if 0 <= number - place * gap < count:
                    work(number - place * gap)

        return [partial(one, number) for number in range(count + 3 * gap)]


def collect_scratch(count, layers=True):
    low = lambda *shape: pltpu.VMEM(shape, LOW)
    return [
        low(count, DEPTHS, SIDES, UNIT, D), low(count, DEPTHS, UNIT, D), low(count, DEPTHS - 1, UNIT, D),
        low(count if layers else 1, UNIT, D),
        pltpu.SemaphoreType.DMA((count, 6)), pltpu.SemaphoreType.DMA((count, 6)),
    ]


GATHER_RATE, GATHER_AHEAD, GATHER_GAP, GATHER_EARLY, FORWARD_RATE = 1.9, 6, 3, 4, 3.0
GATHER_ORDER = (
    tuple((0, unit, False) for unit in (2, 6, 3, 7, 4, 8, 5, 9, 0, 1))
    + ((1, 0, False), (1, 1, False))
    + tuple((1, unit, False) for unit in (6, 7, 8, 9, 2, 3, 4, 5))
)
SOON = 12
FORWARD_HOOKS = SLABS + PAIRS + 1
SCATTER_RATE, SCATTER_AHEAD, SCATTER_GAP = 2.0, 4, 3
SCATTER_ORDER = ((1, 0), (1, 1)) + tuple((0, unit) for unit in (2, 6, 3, 7, 4, 8, 5, 9, 0, 1))
TURN_RATE, TURN_GAP, TURN_HOOKS = 1.3, 5, PAIRS + 3
HOOKS = PAIRS + 2


def near_self_kernel(
    source_counts, target_counts, attention_in, attention_out, cross, expand, contract, gains, rows,
    square_out, tall_out, cross_out, target_rest, target_tall, own_square, every_gain, away,
    triple, shares, inverse, result, first,
    end, mid, source_normed, active, change, pair, cross_normed, question, cross_shares, cross_inverse, cross_result,
    blocks, tiles, streams, firsts, landing, bias, own, source_square, source_tall, target_cross, share_rows,
    share_done, fetched, block_sent, block_done, block_out, tile_sent, tile_done,
    spread_sent, spread_done, spread_kept, away_sent, away_done, copied,
):
    place = Place()
    layer, depth, side, core = place.layer, place.depth, place.side, place.core
    step, total = pl.program_id(0), 2 * away.shape[0]
    count = away.shape[0]
    copies = Copies()
    share_row = share_rows.at[step % 2]

    def kept_share(target):
        return pltpu.make_async_copy(share_row, target, share_done.at[step % 2])

    kept = [
        ref.at[0]
        for ref in (end, mid, source_normed, active, change, pair, cross_normed, question, cross_inverse, cross_result)
    ]
    kept.insert(8, share_row)
    selfs = [attention_in.at[:, columns(j)] for j in range(3)] + [attention_out]
    sources = [cross.at[:, columns(j)] for j in range(2)] + [expand.at[:, columns(j)] for j in range(SLABS)]
    sources += [contract.at[columns(j, UNIT), :] for j in range(SLABS)]

    def spot(owner, unit, *index):
        if owner == 0:
            if unit < BLOCKS:
                return source_square.at[(unit,) + index]
            return source_tall.at[index + (unit - BLOCKS,)]
        if unit < EXPAND:
            return target_cross.at[(unit,) + index]
        if unit < BLOCKS:
            return target_rest.at[(unit - EXPAND,) + index]
        return target_tall.at[index + (unit - BLOCKS,)]

    units = [
        (owner, late, partial(own.at.__getitem__, unit), partial(spot, owner, unit))
        for owner, unit, late in GATHER_ORDER
    ]
    spread = Spread(place, copies, units, spread_sent, spread_done, spread_kept)

    def away_parts(slot):
        return firsts.at[slot], landing.at[slot], away_sent.at[slot], away_done.at[slot], place.across_layer()

    def block_parts(unit, stage):
        if stage == 0:
            block, target = blocks.at[unit, :, :, core], place.sibling()
        elif stage < DEPTHS:
            block, target = blocks.at[unit, depth, side, core], place.along_depth(stage)
        else:
            block, target = blocks.at[unit, :, side, core], place.across_side()
        return block, block, block_sent.at[unit, stage], block_done.at[unit, stage], target

    def tile_parts(stage):
        if stage == 0:
            block, target = tiles.at[layer], place.across_layer()
        elif stage < DEPTHS:
            block, target = tiles.at[layer, depth, side, core], place.along_depth(stage)
        elif stage == DEPTHS:
            block, target = tiles.at[layer, :, side, core], place.across_side()
        else:
            block, target = tiles.at[layer, :, :, core], place.sibling()
        return block, block, tile_sent.at[stage], tile_done.at[stage], target

    for stage in range(DEPTHS + 2):
        copies.define(("tile", stage), partial(tile_parts, stage))
    for unit in range(SELFS):
        for stage in range(DEPTHS + 1):
            copies.define(("block", unit, stage), partial(block_parts, unit, stage))
    for slot in range(count):
        copies.define(("away", slot), partial(away_parts, slot))

    def lay_gains(which):
        for row in range(DEPTHS):
            value = tiles[which, row, 0, 0].astype(FULL)
            for other in ((0, 1), (1, 0), (1, 1)):
                value = value + tiles[(which, row) + other].astype(FULL)
            every_gain[which, :, columns(row, 128)] = value[:8]

    def fetch(slot):
        return pltpu.make_async_copy(
            rows.at[row_of(layer, slot, count)], streams.at[slot % 2], fetched.at[slot % 2]
        )

    @pl.when(step == 0)
    def _():
        fetch(step).start()
        for unit in range(SELFS):
            blocks[unit, depth, side, core] = selfs[unit][...].astype(LOW)
        for unit in range(UNITS):
            own[unit] = sources[unit][...].astype(LOW)
        tiles[layer, depth, side, core] = gains[...]
        place.greet()
        across = range(1, DEPTHS)
        early = iter(spread.steps(GATHER_AHEAD, GATHER_GAP)[:GATHER_EARLY])
        copies.start(*[("tile", stage) for stage in across])
        for unit in range(SELFS):
            copies.start(*[("block", unit, stage) for stage in across])
        spread.announce()
        for number in range(GATHER_AHEAD):
            spread.begin(number)
        copies.arrived(*[("tile", stage) for stage in across])
        copies.start(("tile", DEPTHS))
        for number in range(GATHER_AHEAD):
            spread.relay(number)
        for unit in range(SELFS):
            copies.arrived(*[("block", unit, stage) for stage in across])
            copies.start(("block", unit, DEPTHS))
        copies.arrived(("tile", DEPTHS))
        copies.start(("tile", DEPTHS + 1))
        for unit in range(SELFS):
            for _ in range(GATHER_EARLY // SELFS):
                next(early)()
            copies.arrived(("block", unit, DEPTHS))
            copies.start(("block", unit, 0))
        copies.arrived(("tile", DEPTHS + 1))
        copies.start(("tile", 0))
        lay_gains(layer)
        copies.arrived(*[("block", unit, 0) for unit in range(OUT)])

    def last_block():
        copies.arrived(("block", OUT, 0))
        pltpu.make_async_copy(blocks, own_square, block_out).start()

    plan = Plan(GATHER_RATE, HOOKS)
    late = plan.fill([last_block] + spread.steps(GATHER_AHEAD, GATHER_GAP)[GATHER_EARLY:], total)
    forward_plan = Plan(FORWARD_RATE, FORWARD_HOOKS)
    late = forward_plan.fill(late, count)

    @pl.when(step + 1 < total)
    def _():
        fetch(step + 1).start()

    @pl.when(step >= 2)
    def _():
        kept_share(shares.at[0]).wait()

    @pl.when(step < total)
    def _():
        row = row_of(layer, step, count)
        causal = layer == 1
        both = [jnp.where(causal, *pair_of) for pair_of in zip(*counts_of(target_counts, source_counts, row))]
        fill_bias(bias, *segments(both), causal)
        fetch(step).wait()
        stream = self_forward(
            streams[step % 2].astype(FULL), every_gain[layer, 0:1, :], lambda unit: blocks[unit].reshape(D, D), bias,
            triple.at[0], share_row, inverse.at[0], result.at[0], partial(plan.hook, step),
        )
        kept_share(shares.at[step]).start()
        stream = stream.astype(LOW)
        first[0] = stream
        firsts[step] = stream
        for slot in range(count):

            @pl.when(step == slot)
            def _(slot=slot):
                copies.start(("away", slot))

        plan.hook(step)

    outward = [
        pltpu.make_async_copy(source, target, copied.at[index])
        for index, (source, target) in enumerate(
            ((source_square, square_out), (source_tall, tall_out), (target_cross, cross_out), (landing, away))
        )
    ]

    @pl.when(step == total)
    def _():
        copies.arrived(("tile", 0))
        lay_gains(1 - layer)
        for number in range(SOON):
            spread.end(number)
        copies.arrived(*[("away", slot) for slot in range(count)])
        for copy in outward:
            copy.start()

    @pl.when(step >= total)
    def _():
        index = step - total
        source_pieces, target_pieces = counts_of(source_counts, target_counts, layer * count + index)
        forward(
            layer, firsts[step - count], landing[index], segments(source_pieces), segments(target_pieces), every_gain,
            lambda slab: source_square[EXPAND + slab].reshape(D, D), lambda slab: source_tall[slab].reshape(D, D),
            lambda part: source_square[CROSS + part].reshape(D, D), lambda part: target_cross[part].reshape(D, D),
            bias, kept, partial(forward_plan.hook, index),
        )
        kept_share(cross_shares.at[index]).start()

    @pl.when(step == total + count - 1)
    def _():
        for thunk in late:
            thunk()
        for number in range(SOON, len(units)):
            spread.end(number)
        copies.finish(*[("away", slot) for slot in range(count)])
        copies.finish(*[("tile", stage) for stage in range(DEPTHS + 2)])
        copies.finish(*[("block", unit, stage) for unit in range(SELFS) for stage in range(DEPTHS + 1)])
        spread.finish()
        pltpu.make_async_copy(blocks, own_square, block_out).wait()
        for copy in outward:
            copy.wait()
        for number in range(2):
            pltpu.make_async_copy(share_rows.at[number], cross_shares.at[number], share_done.at[number]).wait()


def kept_shapes():
    return [
        ((ROW, 3 * D), LOW), ((HEADS, ROW, ROW), LOW), ((ROW, 2 * HD), FULL), ((ROW, D), LOW), ((ROW, D), LOW)
    ]


def near_self(source_counts, target_counts, weights, gains, rows):
    total = rows.shape[0]
    tile = jnp.tile(gains.astype(LOW), (1, 4))
    lane_part = lax.broadcasted_iota(jnp.int32, tile.shape, 1) // UNIT
    tile = jnp.where(lane_part == lax.axis_index("dp") % 4, tile, jnp.zeros_like(tile))
    tile = jnp.pad(tile, ((0, 16 - tile.shape[0]), (0, 0)))
    dma = pltpu.SemaphoreType.DMA
    kept, ahead = kept_shapes(), forward_shapes()
    count = total // 2
    square_shape = (BLOCKS, DEPTHS, SIDES, CORES, UNIT, D)
    tall_shape = (DEPTHS, SIDES, CORES, SLABS, UNIT, D)
    cross_shape, rest_shape = (2,) + square_shape[1:], (SLABS,) + square_shape[1:]
    own_shape = (SELFS,) + square_shape[1:]
    outs = [
        shape_of(shape, LOW) for shape in (square_shape, tall_shape, cross_shape, rest_shape, tall_shape, own_shape)
    ] + [shape_of((2, 8, D), FULL), shape_of((count, ROW, D), LOW)]
    low = lambda *shape: pltpu.VMEM(shape, LOW)

    def later(*shape):
        return pl.BlockSpec((1,) + shape, lambda step: (jnp.maximum(step - total, 0),) + (0,) * len(shape))

    def spec(shape, make):
        return ANYWHERE if shape == (HEADS, ROW, ROW) else make(*shape)

    results = pl.pallas_call(
        near_self_kernel,
        grid=(total + count,),
        in_specs=[SCALARS, SCALARS] + [constant(*value.shape) for value in weights] + [constant(16, 128), ANYWHERE],
        out_specs=[ANYWHERE] * 6
        + [pl.BlockSpec((2, 8, D), lambda row: (0, 0, 0)), ANYWHERE]
        + [spec(shape, partial(per_row, last=total - 1)) for shape, _ in kept]
        + [spec(shape, later) for shape, _ in ahead],
        out_shape=outs
        + [shape_of((total,) + shape, kind) for shape, kind in kept]
        + [shape_of((count,) + shape, kind) for shape, kind in ahead],
        scratch_shapes=[
            low(*own_shape), low(2, DEPTHS, SIDES, CORES, 16, 128), low(2, ROW, D), low(total, ROW, D),
            low(count, ROW, D), low(ROW, ROW), low(UNITS, UNIT, D), low(*square_shape), low(*tall_shape),
            low(*cross_shape), low(2, HEADS, ROW, ROW),
            dma((2,)), dma((2,)), dma((SELFS, 5)), dma((SELFS, 5)), dma, dma((6,)), dma((6,)),
            dma((len(GATHER_ORDER), 6)), dma((len(GATHER_ORDER), 6)), dma((len(GATHER_ORDER),)),
            dma((count,)), dma((count,)), dma((4,)),
        ],
        compiler_params=pltpu.CompilerParams(
            vmem_limit_bytes=VMEM_LIMIT, collective_id=0, has_side_effects=True
        ),
        name="self_forward",
    )(source_counts, target_counts, *weights, tile, rows)
    weights, (own_square, every_gain, away), results = results[:5], results[5:8], results[8:]
    weights = weights[0].reshape(BLOCKS, D, D), weights[1].reshape(FF, D), weights[2].reshape(2, D, D), *weights[3:]
    return weights, own_square, every_gain, away, results[: len(kept)], results[len(kept) :]


def middle_kernel(
    near,
    first, away, cotangent, source_square, source_tall, target_cross, rest, rest_tall, gains,
    kept_end, kept_mid, kept_normed, kept_active, kept_change, kept_pair, kept_cross, kept_question, kept_shares,
    kept_inverse, kept_result,
    section_output, sent_output, kept_delta, sent_delta, square_out, tall_out, gain_out, expand_out, contract_out,
    target_expand, target_contract, shares, inverse, cross_result, source_end, target_mid, value, sending, keeping,
    source_normed, active, memory_low, cross_normed, feed_normed,
    source_change, source_low, delta_pair, delta_question, cross_low, target_change, target_low,
    loaded, stored, kept, ready, output_sent, output_done, delta_sent, delta_done, fetched,
    turn_core, turn_side, turn_depth, turn_layer, turn_sent, turn_done,
):
    place = Place()
    layer = place.layer
    count = away.shape[0]
    copies = Copies()

    def source_expand(slab):
        return source_square[EXPAND + slab]

    def source_contract(slab):
        return source_tall[columns(slab), :]

    if near:

        def spot(unit, *index):
            if unit < SLABS:
                return target_expand.at[(unit,) + index]
            return target_contract.at[index + (unit - SLABS,)]

        def turn_unit(unit):
            def target():
                if unit < SLABS:
                    return expand_out.at[:, columns(unit)]
                return contract_out.at[columns(unit - SLABS, UNIT), :]

            return (
                1,
                lambda: spot(unit, slice(None), slice(None), 1 - place.core),
                lambda *index: spot(unit, *index, place.core),
                None,
                target,
            )

        collect = Collect(
            place, copies, [turn_unit(unit) for unit in range(2 * SLABS)],
            (turn_core, turn_side, turn_depth, turn_layer), turn_sent, turn_done,
        )

        def expand_of(slab):
            return target_expand[slab].reshape(D, D)

        def contract_of(slab):
            return target_contract[slab].reshape(D, D)

    else:

        def expand_of(slab):
            return target_expand[slab]

        def contract_of(slab):
            return target_contract[columns(slab), :]

    whole_rest = [
        pltpu.make_async_copy(rest, target_expand, fetched.at[0]),
        pltpu.make_async_copy(rest_tall, target_contract, fetched.at[1]),
    ]

    def rows_of(row):
        return pl.ds(pl.multiple_of(row * ROW, ROW), ROW)

    def load(row):
        return pltpu.make_async_copy(
            cotangent.at[layer * count + row], target_low.at[columns(row, ROW), :], loaded.at[row]
        )

    def store(row):
        return pltpu.make_async_copy(value, section_output.at[row], stored)

    def keep(row):
        return pltpu.make_async_copy(keeping.at[row], kept_delta.at[row], kept.at[row])

    class Parcels:
        def __init__(self, name, target, sent, done):
            self.name, self.target, self.sent, self.done = name, target, sent, done
            for row in range(count):
                copies.define((name, row), partial(self.parts, row))

        def parts(self, row):
            return sending.at[row], self.target.at[row], self.sent.at[row], self.done.at[row], place.across_layer()

        def local(self, row):
            return pltpu.make_async_copy(sending.at[row], self.target.at[row], self.sent.at[row])

        def put(self, row, block):
            for static in range(count):

                @pl.when(row == static)
                def _(static=static):
                    sending[static] = block
                    if near:
                        copies.start((self.name, static))
                    else:
                        self.local(static).start()

        def left(self, row):
            for static in range(count):

                @pl.when(row == static)
                def _(static=static):
                    if near:
                        copies.finish((self.name, static))
                    else:
                        self.local(static).wait()

    outputs = Parcels("output", sent_output, output_sent, output_done)
    deltas = Parcels("delta", sent_delta, delta_sent, delta_done)

    def streams(row):
        own, other = first[row].astype(FULL), away[row].astype(FULL)
        return jnp.where(layer == 0, own, other), jnp.where(layer == 0, other, own)

    def publish(row, owner, block):
        @pl.when(layer == owner)
        def _():
            @pl.when(jnp.asarray(row) > 0)
            def _():
                store(row - 1).wait()

            value[...] = block
            store(row).start()

        @pl.when(layer != owner)
        def _():
            outputs.put(row, block.astype(LOW))

    for row in range(count):
        load(row).start()
    gain_out[...] = jnp.zeros(gain_out.shape, FULL)
    if near:
        place.greet()
    takes = [
        pltpu.make_async_copy(source, target, fetched.at[2 + index])
        for index, (source, target) in enumerate(
            (
                (kept_end, source_end), (kept_mid, target_mid), (kept_normed, source_normed), (kept_cross, cross_normed),
                (kept_result, cross_result), (kept_pair, delta_pair), (kept_question, delta_question),
                (kept_inverse, inverse), (kept_shares.at[count - 1], shares), (kept_change, source_change),
            )
        )
    ]
    take_active = pltpu.make_async_copy(kept_active, active, fetched.at[12])
    for copy in takes[:2] + whole_rest + takes[2:]:
        copy.start()

    def cross_parts(row):
        at = rows_of(row)
        return cross_refs(delta_question.at[at, :], delta_pair.at[at, :])

    def take_shares(row):
        return pltpu.make_async_copy(kept_shares.at[row], shares, fetched.at[13])

    takes[0].wait()
    for row in range(count):
        memory = normalize(source_end[row])[0] * gains[0, 2:3, :]
        memory_low[columns(row, ROW), :] = memory.astype(LOW)
        publish(row, 0, memory)
    for copy in takes[1:2] + whole_rest:
        copy.wait()

    @pl.when(layer == 0)
    def _():
        store(count - 1).wait()

    def turn(row, carry):
        at = rows_of(row)
        stream = target_mid[row]
        normed = (normalize(stream)[0] * gains[1, 2:3, :]).astype(LOW)
        feed_normed[at, :] = normed
        output = feed(
            normed, stream, expand_of, contract_of, active.at[at, :], target_change.at[at, :], no_hook
        )
        publish(row, 1, output)
        for static in range(count):

            @pl.when(row == static)
            def _(static=static):
                load(static).wait()

        delta, delta_gain = feed_back(
            target_low[at, :].astype(FULL), stream, gains[1, 2:3, :], expand_of, contract_of, target_change.at[at, :]
        )
        gain_out[1, 2:3, :] += delta_gain
        target_mid[row] = delta
        return carry

    lax.fori_loop(0, count, turn, 0)

    emitted, late = [], []

    def emit(block, holder, target):
        holder[...] = block.astype(LOW)
        copy = pltpu.make_async_copy(holder, target, ready.at[len(emitted)])
        copy.start()
        emitted.append(copy)
        if late:
            late.pop(0)()

    def feed_grads(which, normed, change, low):
        turned = normed[...].T
        for slab in range(SLABS):
            grown = multiply(turned, change[:, columns(slab)])
            shrunk = multiply(active[:, columns(slab)], low[...], TN)
            emit(grown, change.at[pl.ds(0, D), columns(slab)], square_out.at[which, EXPAND + slab])
            emit(shrunk, change.at[pl.ds(D, D), columns(slab)], tall_out.at[which, columns(slab), :])

    if near:
        turned = feed_normed[...].T
        for slab in range(SLABS):
            grown = multiply(turned, target_change[:, columns(slab)])
            target_expand[slab] = grown.astype(LOW).reshape(DEPTHS, SIDES, CORES, UNIT, D)
            collect.begin(slab)
            shrunk = multiply(active[:, columns(slab)], target_low[...], TN)
            target_contract[slab] = shrunk.astype(LOW).reshape(SIDES, CORES, SLABS, UNIT, D)
        for slab in range(SLABS):
            collect.begin(SLABS + slab)
        plan = Plan(TURN_RATE, TURN_HOOKS)
        late = plan.fill(collect.steps(2 * SLABS, TURN_GAP), count)
    else:
        feed_grads(1, feed_normed, target_change, target_low)
    take_active.start()
    for copy in takes[2:]:
        copy.wait()

    def backward(number, carry):
        row = count - 1 - number
        at = rows_of(row)
        hook = partial(plan.hook, number) if near else no_hook
        source_stream, target_stream = streams(row)

        @pl.when(number > 0)
        def _():
            take_shares(row).wait()

        delta = target_mid[row]
        low = delta.astype(LOW)
        cross_low[at, :] = low
        delta_result = multiply(low, target_cross[1], NT)

        def put(pair, query, keys, values):
            delta_question[at, columns(pair, 2 * HD)] = query
            delta_pair[at, columns(pair, 2 * HD)] = keys
            delta_pair[at, columns(PAIRS + pair, 2 * HD)] = values

        attend_back(
            *cross_parts(row), shares, inverse.at[row], cross_result.at[at, :], delta_result, put, hook
        )

        @pl.when(number < count - 1)
        def _():
            take_shares(row - 1).start()

        unit, scale = normalize(target_stream)
        delta_normed = multiply(delta_question[at, :], target_cross[0], NT)
        delta_stream, delta_gain = norm_back(unit, scale, gains[1, 1:2, :], delta_normed)
        gain_out[1, 1:2, :] += delta_gain
        target_delta = (delta + delta_stream).astype(LOW)
        hook()

        unit, scale = normalize(source_end[row])
        delta_memory = 0.0
        for part in range(2):
            delta_memory = delta_memory + multiply(delta_pair[at, columns(part)], source_square[CROSS + part], NT)
        delta, delta_gain = norm_back(unit, scale, gains[0, 2:3, :], delta_memory)
        gain_out[0, 2:3, :] += delta_gain
        source_low[at, :] = delta.astype(LOW)
        hook()
        delta, delta_gain = feed_back(
            delta, source_stream, gains[0, 1:2, :], source_expand, source_contract, source_change.at[at, :]
        )
        gain_out[0, 1:2, :] += delta_gain
        source_delta = delta.astype(LOW)
        keeping[row] = jnp.where(layer == 0, source_delta, target_delta)
        for static in range(count):

            @pl.when(row == static)
            def _(static=static):
                keep(static).start()

        outputs.left(row)
        deltas.put(row, jnp.where(layer == 0, target_delta, source_delta))
        hook()
        return carry

    lax.fori_loop(0, count, backward, 0)
    take_active.wait()
    feed_grads(0, source_normed, source_change, source_low)
    turned = memory_low[...].T
    for part in range(2):
        grown = multiply(turned, delta_pair[:, columns(part)])
        emit(grown, delta_pair.at[pl.ds(0, D), columns(part)], square_out.at[0, CROSS + part])
    for part, (left, right) in enumerate(((cross_normed, delta_question), (cross_result, cross_low))):
        emit(multiply(left[...], right[...], TN), right.at[pl.ds(0, D), :], square_out.at[1, CROSS + part])
    for thunk in late:
        thunk()
    for copy in emitted:
        copy.wait()

    @pl.when(layer == 1)
    def _():
        store(count - 1).wait()

    for row in range(count):
        keep(row).wait()
        deltas.left(row)
    if near:
        copies.arrived(*[(name, row) for name in ("output", "delta") for row in range(count)])
        collect.finish()


def middle(near, first, away, cotangent, weights, gains, ahead):
    count = away.shape[0]
    tokens = count * ROW
    dma = pltpu.SemaphoreType.DMA
    low = lambda *shape: pltpu.VMEM(shape, LOW)
    full = lambda *shape: pltpu.VMEM(shape, FULL)
    square, tall, cross, rest, rest_tall = weights
    if near:
        expand = low(SLABS, DEPTHS, SIDES, CORES, UNIT, D)
        contract = low(DEPTHS, SIDES, CORES, SLABS, UNIT, D)
    else:
        expand, contract = low(SLABS, D, D), low(FF, D)
    rows_apart = (0, 1, 8, 9)
    ahead = [
        value if place in rows_apart else value.reshape(tokens, value.shape[-1]) for place, value in enumerate(ahead)
    ]
    row_shape = shape_of((count, ROW, D), LOW)
    early_shapes = [(UNIT, FF), (SLABS * UNIT, D)]
    remote = dict(collective_id=2, has_side_effects=True) if near else {}
    outs = pl.pallas_call(
        partial(middle_kernel, near),
        grid=(1,),
        in_specs=[
            pl.BlockSpec((count, ROW, D), lambda step: (1, 0, 0), pipeline_mode=pl.Buffered(1)),
            constant(count, ROW, D), ANYWHERE, constant(BLOCKS, D, D), constant(FF, D), constant(2, D, D),
            ANYWHERE, ANYWHERE, constant(2, 8, D),
        ]
        + [ANYWHERE] * len(ahead),
        out_specs=[ANYWHERE] * 6
        + [pl.BlockSpec((2, 8, D), lambda step: (0, 0, 0))]
        + [pl.BlockSpec(shape, lambda step: (0, 0)) for shape in early_shapes],
        out_shape=[shape_of((count, ROW, D), FULL), row_shape, row_shape, row_shape]
        + [shape_of((2, BLOCKS, D, D), LOW), shape_of((2, FF, D), LOW), shape_of((2, 8, D), FULL)]
        + [shape_of(shape, FULL) for shape in early_shapes],
        scratch_shapes=[
            expand, contract, low(HEADS, ROW, ROW), full(count, ROW, 2 * HD), low(tokens, D),
            full(count, ROW, D), full(count, ROW, D), full(ROW, D), low(count, ROW, D), low(count, ROW, D),
            low(tokens, D), low(tokens, FF), low(tokens, D), low(tokens, D), low(tokens, D),
            low(tokens, FF), low(tokens, D), low(tokens, 2 * D), low(tokens, D), low(tokens, D), low(tokens, FF),
            low(tokens, D),
            dma((count,)), dma, dma((count,)), dma((2 * UNITS,)),
            dma((count,)), dma((count,)), dma((count,)), dma((count,)), dma((14,)),
        ]
        + collect_scratch(2 * SLABS if near else 1),
        compiler_params=pltpu.CompilerParams(vmem_limit_bytes=VMEM_LIMIT, **remote),
        name="middle",
    )(first, away, cotangent, square, tall, cross, rest, rest_tall, gains, *ahead)
    return outs[:7], outs[7:]


def near_back_kernel(
    kept_delta, away_delta, rows, own_square, gains, triple, shares, inverse, result,
    square_sums, tall_sums, gain_sums, early_expand, early_contract,
    gradient, attention_in, attention_out, cross, expand, contract, gain_out,
    deltas, streams, value, delta_triple, sums, low_sums, own_gain, total,
    gain_total, gain_parts, gain_from_layer,
    delta_done, fetched, stored, loaded, gain_sent, gain_done,
    other_core, other_side, other_depth, other_layer, other_sent, other_done,
    own_core, own_side, own_depth, own_layer, own_sent, own_done,
):
    place = Place()
    layer, depth, core = place.layer, place.depth, place.core
    count = kept_delta.shape[0]
    step, steps_in_all = pl.program_id(0), 2 * count
    copies = Copies()

    def other_unit(number):
        which, unit = SCATTER_ORDER[number]

        def share(owner):
            if unit < BLOCKS:
                return square_sums.at[which, unit, :, :, owner]
            return tall_sums.at[which, :, :, owner, unit - BLOCKS]

        def target():
            if unit < EXPAND:
                return cross.at[:, columns(unit - CROSS)]
            if unit < BLOCKS:
                return expand.at[:, columns(unit - EXPAND)]
            return contract.at[columns(unit - BLOCKS, UNIT), :]

        return (
            which,
            lambda: share(1 - core),
            lambda *index: total.at[(number,) + index],
            lambda: pltpu.make_async_copy(share(core), total.at[number], loaded.at[number]),
            target,
        )

    def own_unit(unit):
        return (
            None,
            lambda: low_sums.at[unit, :, :, 1 - core],
            lambda *index: low_sums.at[(unit,) + index + (core,)],
            None,
            lambda: attention_in.at[:, columns(unit)] if unit < OUT else attention_out,
        )

    others = Collect(
        place, copies, [other_unit(number) for number in range(len(SCATTER_ORDER))],
        (other_core, other_side, other_depth, other_layer), other_sent, other_done,
    )
    selfs = Collect(
        place, copies, [own_unit(unit) for unit in range(SELFS)], (own_core, own_side, own_depth, own_layer),
        own_sent, own_done,
    )

    def gain_parts_of(stage):
        if stage == 0:
            source, target, device = gain_sums.at[1 - layer], gain_from_layer, place.across_layer()
        elif stage == 1:
            source, target, device = gain_total.at[0], gain_parts.at[0], place.sibling()
        elif stage == 2:
            source, target, device = gain_total.at[1], gain_parts.at[1], place.across_side()
        else:
            away_by = stage - 2
            source, target = gain_total.at[2, place.other_depth(away_by)], gain_parts.at[2, away_by]
            device = place.along_depth(away_by)
        return source, target, gain_sent.at[stage], gain_done.at[stage], device

    gain_stages = range(3 + DEPTHS - 1)
    for stage in gain_stages:
        copies.define(("gain", stage), partial(gain_parts_of, stage))

    def fetch(index):
        slot = (index + count) % steps_in_all
        return pltpu.make_async_copy(
            rows.at[row_of(layer, slot, count)], streams.at[index % 2], fetched.at[index % 2]
        )

    def store(index):
        slot = (index + count) % steps_in_all
        return pltpu.make_async_copy(
            value.at[index % 2], gradient.at[row_of(layer, slot, count)], stored.at[index % 2]
        )

    takes = [
        pltpu.make_async_copy(source, deltas.at[pl.ds(count * half, count)], delta_done.at[half])
        for half, source in enumerate((kept_delta, away_delta))
    ]

    @pl.when(step == 0)
    def _():
        for take in takes:
            take.start()
        fetch(step).start()
        sums[...] = jnp.zeros(sums.shape, FULL)
        own_gain[...] = jnp.zeros(own_gain.shape, FULL)
        place.greet()
        for number in range(SCATTER_AHEAD):
            others.begin(number)
        copies.start(("gain", 0))

        @pl.when(layer == 1)
        def _():
            expand[...] = early_expand[...]
            contract[...] = early_contract[...]

        for take in takes:
            take.wait()

    plan = Plan(SCATTER_RATE, HOOKS)
    late = plan.fill(others.steps(SCATTER_AHEAD, SCATTER_GAP), steps_in_all)

    def ready(unit):
        low_sums[unit] = sums[unit].astype(LOW).reshape(DEPTHS, SIDES, CORES, UNIT, D)
        selfs.begin(unit)

    for hook, work in ((0, ready), (2, selfs.chip), (4, selfs.sides)):
        plan.steps.setdefault((steps_in_all - 1, hook), []).append(partial(work, OUT))

    @pl.when(step + 1 < steps_in_all)
    def _():
        fetch(step + 1).start()

    fetch(step).wait()
    delta, delta_gain = self_back(
        deltas[step], streams[step % 2].astype(FULL), gains[layer, 0:1, :],
        lambda unit: own_square[unit].reshape(D, D),
        triple.at[0], shares.at[0], inverse.at[0], result.at[0], delta_triple, sums, partial(plan.hook, step),
    )
    own_gain[0:1, :] += delta_gain

    @pl.when(step >= 2)
    def _():
        store(step).wait()

    value[step % 2] = delta.astype(LOW)
    store(step).start()
    plan.hook(step)

    @pl.when(step == steps_in_all - 1)
    def _():
        def more():
            if late:
                late.pop(0)()

        for unit in range(OUT):
            ready(unit)
        copies.arrived(("gain", 0))
        whole = gain_sums[layer] + gain_from_layer[...] + own_gain[...]
        for row in range(DEPTHS):
            gain_total[0, row] = whole[:, 128 * row : 128 * (row + 1)]
        copies.start(("gain", 1))
        more()
        for unit in range(OUT):
            selfs.chip(unit)
        copies.arrived(("gain", 1))
        gain_total[1] = gain_total[0] + gain_parts[0]
        copies.start(("gain", 2))
        for unit in range(OUT):
            more()
            selfs.sides(unit)
        copies.arrived(("gain", 2))
        gain_total[2] = gain_total[1] + gain_parts[1]
        copies.start(*[("gain", 2 + away_by) for away_by in range(1, DEPTHS)])
        for unit in (OUT, *range(OUT)):
            more()
            selfs.depths(unit)
        while late:
            more()
        whole = gain_total[2, depth]
        for away_by in range(1, DEPTHS):
            copies.arrived(("gain", 2 + away_by))
            whole = whole + gain_parts[2, away_by]
        gain_out[...] = whole
        store(step - 1).wait()
        store(step).wait()
        copies.finish(*[("gain", stage) for stage in gain_stages])
        others.finish()
        selfs.finish()


def near_back(kept_delta, away_delta, rows, own_square, gains, kept, square_sums, tall_sums, gain_sums, early):
    count, total = kept_delta.shape[0], rows.shape[0]
    dma = pltpu.SemaphoreType.DMA
    vmem = pl.BlockSpec(memory_space=pltpu.VMEM)
    shapes = kept_shapes()[:4]

    def rotated(*shape):
        return pl.BlockSpec((1,) + shape, lambda step: ((step + count) % total,) + (0,) * len(shape))

    units = len(SCATTER_ORDER)
    weight_shapes = [(UNIT, 3 * D), (UNIT, D), (UNIT, 2 * D), (UNIT, FF), (SLABS * UNIT, D), (8, 128)]
    low = lambda *shape: pltpu.VMEM(shape, LOW)
    full = lambda *shape: pltpu.VMEM(shape, FULL)
    gradient, *weights, gain = pl.pallas_call(
        near_back_kernel,
        grid=(total,),
        in_specs=[ANYWHERE, ANYWHERE, ANYWHERE, constant(SELFS, DEPTHS, SIDES, CORES, UNIT, D), constant(2, 8, D)]
        + [rotated(*shape) for shape, _ in shapes]
        + [ANYWHERE, ANYWHERE, constant(2, 8, D), constant(UNIT, FF), constant(SLABS * UNIT, D)],
        out_specs=[ANYWHERE] + [pl.BlockSpec(shape, lambda step: (0, 0)) for shape in weight_shapes],
        out_shape=[shape_of((total, ROW, D), LOW)] + [shape_of(shape, FULL) for shape in weight_shapes],
        scratch_shapes=[
            low(total, ROW, D), low(2, ROW, D), low(2, ROW, D), low(ROW, 3 * D), full(SELFS, D, D),
            low(SELFS, DEPTHS, SIDES, CORES, UNIT, D), full(8, D), low(units, DEPTHS, SIDES, UNIT, D),
            full(3, DEPTHS, 8, 128), full(3, DEPTHS, 8, 128), full(8, D),
            dma((2,)), dma((2,)), dma((2,)), dma((units,)), dma((6,)), dma((6,)),
        ]
        + collect_scratch(units)
        + collect_scratch(SELFS, False),
        compiler_params=pltpu.CompilerParams(
            vmem_limit_bytes=VMEM_LIMIT, collective_id=1, has_side_effects=True
        ),
        name="self_back",
    )(
        kept_delta, away_delta, rows, own_square, gains, *kept[:4],
        square_sums.reshape(2, BLOCKS, DEPTHS, SIDES, CORES, UNIT, D),
        tall_sums.reshape(2, DEPTHS, SIDES, CORES, SLABS, UNIT, D), gain_sums, *early,
    )
    start = lax.axis_index("dp") % 4 * UNIT
    return gradient, *weights, lax.dynamic_slice_in_dim(gain[:3], start, UNIT, axis=1)


def settle_kernel(mine, away, low_gradient, *refs):
    step, count = pl.program_id(0), pl.num_programs(0) // 2
    sums = len(refs) // 2 - 1
    whole, gradient = refs[sums], refs[sums + 1]
    whole[...] = jnp.where(step // count == lax.axis_index("pipe"), mine[...], away[...].astype(FULL))
    gradient[...] = low_gradient[...].astype(FULL)

    @pl.when(step == 0)
    def _():
        for source, target in zip(refs[:sums], refs[sums + 2 :]):
            target[...] = source[...]


def settle(mine, away, gradient, sums):
    total, count = gradient.shape[0], away.shape[0]

    def row(step):
        return (step, 0, 0)

    def row_of_half(step):
        return (step % count, 0, 0)

    wide = pl.BlockSpec((1, ROW, D), row)
    half = pl.BlockSpec((1, ROW, D), row_of_half)
    kept = [pl.BlockSpec(value.shape, lambda step: (0, 0)) for value in sums]
    whole = shape_of((total, ROW, D), FULL)
    return pl.pallas_call(
        settle_kernel,
        grid=(total,),
        in_specs=[half, half, wide] + kept,
        out_specs=[wide, wide] + kept,
        out_shape=[whole, whole] + [shape_of(value.shape, FULL) for value in sums],
        compiler_params=PARAMS,
        name="settle",
    )(mine, away, gradient, *sums)


def far_self_kernel(
    source_counts, target_counts, rows, square, gains, triple, shares, inverse, result, first, bias
):
    layer, step, count = lax.axis_index("pipe"), pl.program_id(0), pl.num_programs(0) // 2
    row = row_of(layer, step, count)
    causal = layer == 1
    both = [jnp.where(causal, target_counts[row, piece], source_counts[row, piece]) for piece in range(PACK)]
    fill_bias(bias, *segments(both), causal)
    first[0] = self_forward(
        rows[0].astype(FULL), gains[layer, 0:1, :], lambda unit: square[unit], bias,
        triple.at[0], shares.at[0], inverse.at[0], result.at[0], no_hook,
    ).astype(LOW)


def far_self(source_counts, target_counts, square, gains, rows):
    total = rows.shape[0]
    kept = kept_shapes()
    return pl.pallas_call(
        far_self_kernel,
        grid=(total,),
        in_specs=[SCALARS, SCALARS, per_row(ROW, D), constant(SELFS, D, D), constant(2, 8, D)],
        out_specs=[per_row(*shape) for shape, _ in kept],
        out_shape=[shape_of((total,) + shape, kind) for shape, kind in kept],
        scratch_shapes=[pltpu.VMEM((ROW, ROW), FULL)],
        compiler_params=PARAMS,
        name="self_forward",
    )(source_counts, target_counts, rows, square, gains)


def far_forward_kernel(
    source_counts, target_counts, first, away, square, tall, cross, gains, *refs
):
    layer, step, count = lax.axis_index("pipe"), pl.program_id(0), pl.num_programs(0)
    source_pieces, target_pieces = counts_of(source_counts, target_counts, layer * count + step)
    forward(
        layer, first[0], away[0], segments(source_pieces), segments(target_pieces), gains,
        lambda slab: square[EXPAND + slab], lambda slab: tall[columns(slab), :],
        lambda part: square[CROSS + part], lambda part: cross[part], refs[-1], [ref.at[0] for ref in refs[:-1]], no_hook,
    )


def far_forward(source_counts, target_counts, first, away, square, tall, cross, gains):
    count = away.shape[0]
    kept = forward_shapes()
    return pl.pallas_call(
        far_forward_kernel,
        grid=(count,),
        in_specs=[
            SCALARS, SCALARS, per_row(ROW, D, start=count), per_row(ROW, D), constant(BLOCKS, D, D), constant(FF, D),
            constant(2, D, D), constant(2, 8, D),
        ],
        out_specs=[per_row(*shape) for shape, _ in kept],
        out_shape=[shape_of((count,) + shape, kind) for shape, kind in kept],
        scratch_shapes=[pltpu.VMEM((ROW, ROW), LOW)],
        compiler_params=PARAMS,
        name="forward",
    )(source_counts, target_counts, first, away, square, tall, cross, gains)


def far_back_kernel(
    deltas, rows, square, gains, triple, shares, inverse, result, gradient, sums, gain_out, delta_triple
):
    layer, step = lax.axis_index("pipe"), pl.program_id(0)

    @pl.when(step == 0)
    def _():
        sums[...] = jnp.zeros(sums.shape, FULL)
        gain_out[...] = jnp.zeros(gain_out.shape, FULL)

    delta, delta_gain = self_back(
        deltas[0], rows[0].astype(FULL), gains[layer, 0:1, :], lambda unit: square[unit],
        triple.at[0], shares.at[0], inverse.at[0], result.at[0], delta_triple, sums, no_hook,
    )
    gain_out[0:1, :] += delta_gain
    gradient[0] = delta


def far_back(deltas, rows, square, gains, kept):
    total = rows.shape[0]
    return pl.pallas_call(
        far_back_kernel,
        grid=(total,),
        in_specs=[per_row(ROW, D), per_row(ROW, D), constant(SELFS, D, D), constant(2, 8, D)]
        + [per_row(*shape) for shape, _ in kept_shapes()[:4]],
        out_specs=[per_row(ROW, D), constant(SELFS, D, D), constant(8, D)],
        out_shape=[shape_of((total, ROW, D), FULL), shape_of((SELFS, D, D), FULL), shape_of((8, D), FULL)],
        scratch_shapes=[pltpu.VMEM((ROW, 3 * D), LOW)],
        compiler_params=PARAMS,
        name="self_back",
    )(deltas, rows, square, gains, *kept[:4])


def spotsof(value):
    return [value[:, start : start + D] for start in range(0, value.shape[1], D)]


def gather_all(value, axes):
    return lax.all_gather(value, axes, axis=0, tiled=False)


def far_weights(weights, gains, shards):
    attention_in, attention_out, cross, expand, contract = (value.astype(LOW) for value in weights)
    both = ("pipe", "dp")
    own = jnp.stack(spotsof(attention_in) + [attention_out])
    own = jnp.swapaxes(gather_all(own, "dp"), 0, 1).reshape(SELFS, D, D)
    square = gather_all(jnp.stack(spotsof(cross) + spotsof(expand)), both)
    square = jnp.swapaxes(square.reshape(2, shards, BLOCKS, D // shards, D), 1, 2)
    tall = gather_all(contract, both)
    gains = gather_all(gains.astype(LOW), both).reshape(2, shards, 3, D // shards)
    gains = jnp.swapaxes(gains, 1, 2).reshape(2, 3, D).astype(FULL)
    return own, square.reshape(2, BLOCKS, D, D), tall.reshape(2, FF, D), jnp.pad(gains, ((0, 0), (0, 5), (0, 0)))


def scattered(value, axes):
    return lax.psum_scatter(value, axes, scatter_dimension=0, tiled=False).astype(FULL)


def far_sums(own, own_gain, square, tall, gains, section, shards):
    both = ("pipe", "dp")
    share = D // shards
    own = scattered(jnp.swapaxes(own.reshape(SELFS, shards, share, D), 0, 1), "dp")
    square = jnp.swapaxes(square.reshape(2, BLOCKS, shards, share, D), 1, 2)
    square = scattered(square.reshape(2 * shards, BLOCKS, share, D), both)
    tall = scattered(tall.reshape(2 * shards, FF // shards, D), both)
    gains = gains + jnp.where(jnp.arange(2)[:, None, None] == section, own_gain[None], 0.0)
    gains = jnp.swapaxes(gains[:, :3].reshape(2, 3, shards, share), 1, 2)
    gains = scattered(gains.reshape(2 * shards, 3, share), both)

    def joined(value, first, last):
        return jnp.concatenate([value[block] for block in range(first, last)], axis=1)

    return (
        joined(own, QKV, OUT), own[OUT], joined(square, CROSS, EXPAND), joined(square, EXPAND, BLOCKS), tall, gains
    )


def swap(value):
    return lax.ppermute(value, "pipe", [(0, 1), (1, 0)])


def local(
    section_input,
    attention_in,
    attention_out,
    cross_weights,
    expand,
    contract,
    norm_gains,
    source_lengths,
    target_lengths,
    cotangent,
):
    section = lax.axis_index("pipe")
    shards = lax.axis_size("dp")
    near = shards == DEPTHS * SIDES * CORES
    rows = section_input[0]
    count = rows.shape[0] // 2
    weights = tuple(value[0] for value in (attention_in, attention_out, cross_weights, expand, contract))
    if near:
        weights, own_square, gains, away, kept, ahead = near_self(
            source_lengths, target_lengths, weights, norm_gains[0], rows
        )
    else:
        turn = jnp.where(section == 0, count, 0)
        own_square, square, tall, gains = far_weights(weights, norm_gains[0], shards)
        weights = square[0], tall[0], square[1, CROSS:EXPAND], square[1, EXPAND:], tall[1]
        slots = jnp.roll(rows, turn, axis=0)
        kept = far_self(source_lengths, target_lengths, own_square, gains, slots)
        away = swap(kept[-1][:count])
        ahead = far_forward(source_lengths, target_lengths, kept[-1], away, *weights[:3], gains)
    (section_output, away_output, kept_delta, away_delta, *sums), early = middle(
        near, kept[-1], away, cotangent, weights, gains, ahead
    )
    if near:
        gradient, *weight_sums = near_back(
            kept_delta, away_delta, rows, own_square, gains, kept, *sums, early
        )
    else:
        away_output, away_delta = swap(away_output), swap(away_delta)
        deltas = jnp.concatenate([away_delta, kept_delta], axis=0)
        gradient, own_sums, own_gain = far_back(deltas, slots, own_square, gains, kept)
        gradient = jnp.roll(gradient, -turn, axis=0)
        weight_sums = far_sums(own_sums, own_gain, *sums, section, shards)
    results = settle(section_output, away_output, gradient, weight_sums)
    return tuple(value[None] for value in results)


def solution(mesh):
    in_specs = (
        P("pipe", "dp", None, None),
        P("pipe", "dp", None),
        P("pipe", "dp", None),
        P("pipe", "dp", None),
        P("pipe", "dp", None),
        P("pipe", "dp", None),
        P("pipe", None, "dp"),
        P("dp", None),
        P("dp", None),
        P("dp", None, None),
    )
    out_specs = (
        P("pipe", "dp", None, None),
        P("pipe", "dp", None, None),
        P("pipe", "dp", None),
        P("pipe", "dp", None),
        P("pipe", "dp", None),
        P("pipe", "dp", None),
        P("pipe", "dp", None),
        P("pipe", None, "dp"),
    )
    return jax.shard_map(local, mesh=mesh, in_specs=in_specs, out_specs=out_specs, check_vma=False)
```

```python
from functools import partial
import math

import jax
import jax.numpy as jnp
from jax import lax
from jax.experimental import pallas as pl
from jax.experimental.pallas import tpu as pltpu
from jax.sharding import PartitionSpec as P

D = 512
HEADS = 8
HD = 64
FF = 2048
ROW = 512
PAIRS = HEADS // 2
PACK = 4

QKV, OUT, SELFS = 0, 3, 4
CROSS, EXPAND, BLOCKS = 0, 2, 6
SLABS = FF // D
UNITS = BLOCKS + SLABS

EPSILON = 1e-05
MASKED = -1e30
LOG2E = math.log2(math.e)
EXPONENT = HD**-0.5 * LOG2E
BELL = 1.0 / math.sqrt(2.0 * math.pi)
LOW = jnp.bfloat16
FULL = jnp.float32
VMEM_LIMIT = 63 * 2**20

NN = (((1,), (0,)), ((), ()))
NT = (((1,), (1,)), ((), ()))
TN = (((0,), (0,)), ((), ()))


def multiply(left, right, dims=NN):
    return lax.dot_general(left, right, dims, preferred_element_type=jnp.float32)


def columns(index, width=D):
    return pl.ds(index * width, width)


def normalize(stream):
    centred = stream - jnp.mean(stream, axis=1, keepdims=True)
    scale = lax.rsqrt(jnp.mean(centred * centred, axis=1, keepdims=True) + EPSILON)
    return centred * scale, scale


def norm_back(unit, scale, gain, delta):
    inner = delta * gain
    mean = jnp.mean(inner, axis=1, keepdims=True)
    along = jnp.mean(inner * unit, axis=1, keepdims=True)
    return scale * (inner - mean - unit * along), jnp.sum(delta * unit, axis=0, keepdims=True)


def segment(counts, shape, axis):
    places = lax.broadcasted_iota(jnp.int32, shape, axis)
    end = counts[0]
    found = (places >= end).astype(jnp.int32)
    for count in counts[1:]:
        end = end + count
        found = found + (places >= end).astype(jnp.int32)
    return found


def segments(counts):
    return segment(counts, (ROW, 1), 0), segment(counts, (1, ROW), 1)


def fill_bias(bias, query_segment, key_segment, causal=None):
    keep = query_segment == key_segment
    if causal is not None:
        query = lax.broadcasted_iota(jnp.int32, (ROW, ROW), 0)
        key = lax.broadcasted_iota(jnp.int32, (ROW, ROW), 1)
        keep = keep & (key <= query + jnp.where(causal, 0, ROW))
    bias[...] = jnp.where(keep, 0.0, MASKED).astype(bias.dtype)


def lanes():
    return lax.broadcasted_iota(jnp.int32, (1, 2 * HD), 1)


def only_half(value, half):
    return jnp.where(lanes() // HD == half, value, jnp.zeros_like(value))


def attend(query, keys, values, bias, shares, inverse, result, hook):
    kept = jnp.zeros((ROW, 2 * HD), FULL)
    for pair in range(PAIRS):
        query2, keys2, values2 = query(pair), keys(pair), values(pair)
        parts = []
        for half in range(2):
            head = 2 * pair + half
            scores = multiply(only_half(query2, half), keys2, NT) + bias[...]
            top = jnp.max(scores, axis=1, keepdims=True)
            weights = jnp.exp2((scores - top) * EXPONENT)
            scale = 1.0 / jnp.sum(weights, axis=1, keepdims=True)
            low = weights.astype(LOW)
            shares[head] = low
            parts.append(multiply(low, values2) * scale)
            kept = jnp.where(lanes() == head, scale, kept)
        result[:, columns(pair, 2 * HD)] = jnp.where(lanes() < HD, parts[0], parts[1]).astype(LOW)
        hook()
    inverse[...] = kept


def attend_back(query, keys, values, shares, inverse, result, delta, put, hook):
    for pair in range(PAIRS):
        query2, keys2, values2 = query(pair), keys(pair), values(pair)
        place = slice(2 * HD * pair, 2 * HD * (pair + 1))
        scale = jnp.where(
            lanes() < HD, inverse[:, 2 * pair : 2 * pair + 1], inverse[:, 2 * pair + 1 : 2 * pair + 2]
        )
        low = (delta[:, place] * scale).astype(LOW)
        product = low.astype(FULL) * result[:, columns(pair, 2 * HD)].astype(FULL)
        query_turned, low_turned = query2.T, low.T
        delta_query = 0.0
        delta_keys, delta_values = [], []
        for half in range(2):
            weights = shares[2 * pair + half]
            along = jnp.sum(only_half(product, half), axis=1, keepdims=True)
            delta_shares = multiply(only_half(low, half), values2, NT)
            delta_scores = (weights.astype(FULL) * (delta_shares - along)).astype(LOW)
            delta_query = delta_query + multiply(delta_scores, only_half(keys2, half))
            own = slice(HD * half, HD * (half + 1))
            delta_keys.append(multiply(query_turned[own], delta_scores))
            delta_values.append(multiply(low_turned[own], weights))
        keys_turned = (jnp.concatenate(delta_keys, axis=0) * HD**-0.5).astype(LOW)
        values_turned = jnp.concatenate(delta_values, axis=0).astype(LOW)
        put(pair, (delta_query * HD**-0.5).astype(LOW), keys_turned.T, values_turned.T)
        hook()


def self_parts(triple):
    return tuple(
        (lambda pair, start=part * PAIRS: triple[:, columns(start + pair, 2 * HD)]) for part in range(3)
    )


def put_triple(target):
    def put(pair, *parts):
        for part, value in enumerate(parts):
            target[:, columns(part * PAIRS + pair, 2 * HD)] = value

    return put


def feed(normed, stream, expand, contract, active, slope, hook):
    total = stream
    for slab in range(SLABS):
        hidden = multiply(normed, expand(slab))
        under = 0.5 + 0.5 * lax.erf(hidden * math.sqrt(0.5))
        bell = BELL * jnp.exp2(hidden * hidden * (-0.5 * LOG2E))
        low = (hidden * under).astype(LOW)
        active[:, columns(slab)] = low
        slope[:, columns(slab)] = (under + hidden * bell).astype(LOW)
        total = total + multiply(low, contract(slab))
        hook()
    return total


def feed_back(delta, stream, gain, expand, contract, change):
    unit, scale = normalize(stream)
    low = delta.astype(LOW)
    delta_normed = 0.0
    for slab in range(SLABS):
        delta_active = multiply(low, contract(slab), NT)
        delta_hidden = (delta_active * change[:, columns(slab)].astype(FULL)).astype(LOW)
        change[:, columns(slab)] = delta_hidden
        delta_normed = delta_normed + multiply(delta_hidden, expand(slab), NT)
    delta_stream, delta_gain = norm_back(unit, scale, gain, delta_normed)
    return delta + delta_stream, delta_gain


def self_forward(stream, gain, square, bias, triple, shares, inverse, result, hook):
    normed = (normalize(stream)[0] * gain).astype(LOW)
    for part in range(3):
        triple[:, columns(part)] = multiply(normed, square(QKV + part)).astype(LOW)
    hook()
    attend(*self_parts(triple), bias, shares, inverse, result, hook)
    return stream + multiply(result[...], square(OUT))


def self_back(low, stream, gain, square, triple, shares, inverse, result, delta_triple, sums, hook):
    unit, scale = normalize(stream)
    sums[OUT] += multiply(result[...], low, TN)
    delta_result = multiply(low, square(OUT), NT)
    hook()
    attend_back(*self_parts(triple), shares, inverse, result, delta_result, put_triple(delta_triple), hook)
    turned = (unit * gain).astype(LOW).T
    delta_normed = 0.0
    for part in range(3):
        chunk = delta_triple[:, columns(part)]
        sums[QKV + part] += multiply(turned, chunk)
        delta_normed = delta_normed + multiply(chunk, square(QKV + part), NT)
    delta_stream, delta_gain = norm_back(unit, scale, gain, delta_normed)
    return low.astype(FULL) + delta_stream, delta_gain


def forward(
    layer, own, other, source_segment, target_segment, gains, expand, contract, pair_weights, cross, bias, kept, hook
):
    end_out, mid_out, normed_out, active, change, pair, cross_normed, question, shares, inverse, result = kept
    source_stream = jnp.where(layer == 0, own, other).astype(FULL)
    target_stream = jnp.where(layer == 0, other, own).astype(FULL)
    normed = (normalize(source_stream)[0] * gains[0, 1:2, :]).astype(LOW)
    normed_out[...] = normed
    end = feed(normed, source_stream, expand, contract, active, change, hook)
    end_out[...] = end
    low = (normalize(end)[0] * gains[0, 2:3, :]).astype(LOW)
    for part in range(2):
        pair[:, columns(part)] = multiply(low, pair_weights(part)).astype(LOW)
    hook()
    fill_bias(bias, target_segment[0], source_segment[1])
    normed = (normalize(target_stream)[0] * gains[1, 1:2, :]).astype(LOW)
    cross_normed[...] = normed
    question[...] = multiply(normed, cross(0)).astype(LOW)
    attend(*cross_refs(question, pair), bias, shares, inverse, result, hook)
    mid_out[...] = target_stream + multiply(result[...], cross(1))


def forward_shapes():
    return [
        ((ROW, D), FULL), ((ROW, D), FULL), ((ROW, D), LOW), ((ROW, FF), LOW), ((ROW, FF), LOW), ((ROW, 2 * D), LOW),
        ((ROW, D), LOW), ((ROW, D), LOW), ((HEADS, ROW, ROW), LOW), ((ROW, 2 * HD), FULL), ((ROW, D), LOW),
    ]


def cross_refs(question, pair):
    return (
        lambda number: question[:, columns(number, 2 * HD)],
        lambda number: pair[:, columns(number, 2 * HD)],
        lambda number: pair[:, columns(PAIRS + number, 2 * HD)],
    )


def counts_of(source_counts, target_counts, row):
    return [[counts[row, piece] for piece in range(PACK)] for counts in (source_counts, target_counts)]


def no_hook():
    pass


def per_row(*shape, last=None, start=0, buffers=2):
    def index(row):
        return (start + (row if last is None else jnp.minimum(row, last)),) + (0,) * len(shape)

    return pl.BlockSpec((1,) + shape, index, pipeline_mode=pl.Buffered(buffers) if buffers != 2 else None)


def constant(*shape):
    return pl.BlockSpec(shape, lambda row: (0,) * len(shape), pipeline_mode=pl.Buffered(1))


ANYWHERE = pl.BlockSpec(memory_space=pl.ANY)
SCALARS = pl.BlockSpec(memory_space=pltpu.SMEM)
PARAMS = pltpu.CompilerParams(vmem_limit_bytes=VMEM_LIMIT)


def shape_of(shape, kind):
    return jax.ShapeDtypeStruct(shape, kind)


MESH = pl.DeviceIdType.MESH
UNITS = BLOCKS + SLABS
UNIT = 32
DEPTHS, SIDES, CORES = 4, 2, 2


class Place:
    def __init__(self):
        self.layer = lax.axis_index("pipe")
        self.rank = lax.axis_index("dp")
        self.core = self.rank % CORES
        self.side = self.rank // CORES % SIDES
        self.depth = self.rank // (CORES * SIDES)

    def sibling(self):
        return (self.layer, self.rank + 1 - 2 * self.core)

    def across_side(self):
        return (self.layer, self.rank + CORES * (1 - 2 * self.side))

    def across_layer(self):
        return (1 - self.layer, self.rank)

    def other_depth(self, step):
        return (self.depth + step) % DEPTHS

    def along_depth(self, step):
        return (self.layer, self.rank + CORES * SIDES * (self.other_depth(step) - self.depth))

    def greet(self):
        partners = [self.sibling(), self.across_side(), self.across_layer()]
        partners += [self.along_depth(step) for step in range(1, DEPTHS)]
        barrier = pltpu.get_barrier_semaphore()
        for partner in partners:
            pl.semaphore_signal(barrier, inc=1, device_id=partner, device_id_type=MESH)
        pl.semaphore_wait(barrier, len(partners))


def row_of(layer, slot, count):
    return (slot + count * (1 - layer)) % (2 * count)


class Plan:
    def __init__(self, rate, hooks):
        self.rate, self.hooks = rate, hooks
        self.steps = {}
        self.index = 0

    def fill(self, thunks, rows):
        late = []
        for number, thunk in enumerate(thunks):
            place = int(number * self.rate)
            if place < rows * self.hooks:
                self.steps.setdefault(divmod(place, self.hooks), []).append(thunk)
            else:
                late.append(thunk)
        return late

    def hook(self, step):
        index, self.index = self.index, self.index + 1
        for (row, place), thunks in sorted(self.steps.items(), key=lambda item: item[0]):
            if place == index:

                @pl.when(step == row)
                def _(thunks=thunks):
                    for thunk in thunks:
                        thunk()


class Copies:
    def __init__(self):
        self.made = {}

    def define(self, key, parts):
        def make():
            source, target, sent, arrived, device = parts()
            return pltpu.make_async_remote_copy(
                src_ref=source, dst_ref=target, send_sem=sent, recv_sem=arrived, device_id=device,
                device_id_type=MESH,
            )

        self.made[key] = make

    def start(self, *keys):
        for key in keys:
            self.made[key]().start()

    def arrived(self, *keys):
        for key in keys:
            self.made[key]().wait_recv()

    def finish(self, *keys):
        for key in keys or self.made:
            self.made[key]().wait_send()


class Spread:
    LAYER, SIDE, CORE, RELAY = 3, 4, 5, 6

    def __init__(self, place, copies, units, sent, done, kept):
        self.place, self.copies, self.units = place, copies, units
        self.sent, self.done, self.kept = sent, done, kept
        for number in range(len(units)):
            for stage in range(self.RELAY + DEPTHS - 1):
                copies.define((self, number, stage), partial(self.parts, number, stage))

    def parts(self, number, stage):
        place, (_, late, source, spot) = self.place, self.units[number]
        own, slot, everything = spot(place.depth, place.side, place.core), stage, slice(None)
        if stage < self.LAYER:
            block, target, device = source(), own, place.along_depth(stage + 1)
        elif stage == self.LAYER:
            block, target, device = source(), own, place.across_layer()
            if late:
                block = target = spot(everything, everything, place.core)
        elif stage == self.SIDE:
            block = target = spot(everything, place.side, place.core)
            device = place.across_side()
        elif stage == self.CORE:
            block = target = spot(everything, everything, place.core)
            device = place.sibling()
        else:
            slot = stage - self.RELAY
            block, target, device = own, own, place.along_depth(slot + 1)
        return block, target, self.sent.at[number, slot], self.done.at[number, slot], device

    def keys(self, number, *stages):
        return [(self, number, stage) for stage in stages]

    def along(self, number):
        return self.keys(number, *range(DEPTHS - 1))

    def relayed(self, number):
        return self.keys(number, *range(self.RELAY, self.RELAY + DEPTHS - 1))

    def keep(self, number):
        _, _, source, spot = self.units[number]
        place = self.place
        return pltpu.make_async_copy(source(), spot(place.depth, place.side, place.core), self.kept.at[number])

    def owned(self, number):
        return pl.when(self.place.layer == self.units[number][0])

    def foreign(self, number):
        return pl.when(self.place.layer != self.units[number][0])

    def late(self, number):
        return self.units[number][1]

    def announce(self):
        for number in range(len(self.units)):
            if not self.late(number):

                @self.owned(number)
                def _(number=number):
                    self.copies.start(*self.keys(number, self.LAYER))

    def begin(self, number):
        @self.owned(number)
        def _():
            self.copies.start(*self.along(number))
            self.keep(number).start()

    def relay(self, number):
        if not self.late(number):

            @self.foreign(number)
            def _():
                self.copies.arrived(*self.keys(number, self.LAYER))
                self.copies.start(*self.relayed(number))

    def cross(self, number):
        def work():
            self.copies.arrived(*self.along(number))
            self.copies.start(*self.keys(number, self.SIDE))

        @self.owned(number)
        def _():
            self.keep(number).wait()
            if self.late(number):
                work()

        if not self.late(number):
            work()

    def share(self, number):
        def work():
            self.copies.arrived(*self.keys(number, self.SIDE))
            self.copies.start(*self.keys(number, self.CORE))

        if self.late(number):

            @self.owned(number)
            def _():
                work()
                self.copies.start(*self.keys(number, self.LAYER))

        else:
            work()

    def pass_on(self, number):
        if self.late(number):

            @self.foreign(number)
            def _():
                self.copies.arrived(*self.keys(number, self.LAYER))
                self.copies.start(*self.keys(number, self.CORE))

    def end(self, number):
        self.copies.arrived(*self.keys(number, self.CORE))

    def finish(self):
        for number in range(len(self.units)):
            first = self.along(number) + self.keys(number, self.SIDE)

            @self.owned(number)
            def _(number=number, first=first):
                self.copies.finish(*self.keys(number, self.LAYER))
                if self.late(number):
                    self.copies.finish(*first)

            if not self.late(number):
                self.copies.finish(*first)
            self.copies.finish(*self.keys(number, self.CORE))

    def steps(self, ahead, gap):
        def one(number):
            if ahead <= number + ahead < len(self.units):
                self.begin(number + ahead)
                self.relay(number + ahead)
            if number < len(self.units):
                self.cross(number)
            if 0 <= number - gap < len(self.units):
                self.share(number - gap)
            if 0 <= number - 2 * gap < len(self.units):
                self.pass_on(number - 2 * gap)

        return [partial(one, number) for number in range(len(self.units) + 2 * gap)]


def add_low(left, right):
    return (left.astype(FULL) + right.astype(FULL)).astype(LOW)


class Collect:
    SIDE, DEPTH, LAYER = 1, 2, 5

    def __init__(self, place, copies, units, buffers, sent, done):
        self.place, self.copies, self.units = place, copies, units
        self.from_core, self.from_side, self.from_depth, self.from_layer = buffers
        self.sent, self.done = sent, done
        for number in range(len(units)):
            for stage in range(self.LAYER + 1):
                copies.define((self, number, stage), partial(self.parts, number, stage))

    def parts(self, number, stage):
        place, (_, outgoing, total, _, _) = self.place, self.units[number]
        if stage == 0:
            source, target, device = outgoing(), self.from_core.at[number], place.sibling()
        elif stage == self.SIDE:
            source = total(slice(None), 1 - place.side)
            target, device = self.from_side.at[number], place.across_side()
        elif stage < self.LAYER:
            away_by = stage - self.DEPTH + 1
            source = total(place.other_depth(away_by), place.side)
            target, device = self.from_depth.at[number, away_by - 1], place.along_depth(away_by)
        else:
            source, target = total(place.depth, place.side), self.from_layer.at[number]
            device = place.across_layer()
        return source, target, self.sent.at[number, stage], self.done.at[number, stage], device

    def keys(self, number, *stages):
        return [(self, number, stage) for stage in stages]

    def along(self, number):
        return self.keys(number, *range(self.DEPTH, self.LAYER))

    def begin(self, number):
        load = self.units[number][3]
        if load is not None:
            load().start()
        self.copies.start(*self.keys(number, 0))

    def chip(self, number):
        _, _, total, load, _ = self.units[number]
        if load is not None:
            load().wait()
        self.copies.arrived(*self.keys(number, 0))

        def add(depth, carry):
            share = total(depth, slice(None))
            share[...] = add_low(share[...], self.from_core[number, depth])
            return carry

        lax.fori_loop(0, DEPTHS, add, 0)
        self.copies.start(*self.keys(number, self.SIDE))

    def sides(self, number):
        total = self.units[number][2]
        self.copies.arrived(*self.keys(number, self.SIDE))

        def add(depth, carry):
            share = total(depth, self.place.side)
            share[...] = add_low(share[...], self.from_side[number, depth])
            return carry

        lax.fori_loop(0, DEPTHS, add, 0)
        self.copies.start(*self.along(number))

    def depths(self, number):
        owner, _, total, _, target = self.units[number]
        self.copies.arrived(*self.along(number))
        share = total(self.place.depth, self.place.side)
        value = share[...].astype(FULL)
        for other in range(DEPTHS - 1):
            value = value + self.from_depth[number, other].astype(FULL)
        if owner is None:
            target()[...] = value
            return

        @pl.when(self.place.layer == owner)
        def _():
            target()[...] = value

        @pl.when(self.place.layer != owner)
        def _():
            share[...] = value.astype(LOW)
            self.copies.start(*self.keys(number, self.LAYER))

    def layers(self, number):
        owner, target = self.units[number][0], self.units[number][4]
        if owner is not None:

            @pl.when(self.place.layer == owner)
            def _():
                self.copies.arrived(*self.keys(number, self.LAYER))
                target()[...] = target()[...] + self.from_layer[number].astype(FULL)

    def finish(self):
        for number, unit in enumerate(self.units):
            self.copies.finish(*self.keys(number, 0, self.SIDE), *self.along(number))
            if unit[0] is not None:

                @pl.when(self.place.layer != unit[0])
                def _(number=number):
                    self.copies.finish(*self.keys(number, self.LAYER))

    def steps(self, ahead, gap):
        count = len(self.units)

        def one(number):
            if ahead <= number + ahead < count:
                self.begin(number + ahead)
            for place, work in enumerate((self.chip, self.sides, self.depths, self.layers)):
                if 0 <= number - place * gap < count:
                    work(number - place * gap)

        return [partial(one, number) for number in range(count + 3 * gap)]


def collect_scratch(count, layers=True):
    low = lambda *shape: pltpu.VMEM(shape, LOW)
    return [
        low(count, DEPTHS, SIDES, UNIT, D), low(count, DEPTHS, UNIT, D), low(count, DEPTHS - 1, UNIT, D),
        low(count if layers else 1, UNIT, D),
        pltpu.SemaphoreType.DMA((count, 6)), pltpu.SemaphoreType.DMA((count, 6)),
    ]


GATHER_RATE, GATHER_AHEAD, GATHER_GAP, GATHER_EARLY, FORWARD_RATE = 1.9, 4, 3, 4, 4.0
GATHER_ORDER = (
    tuple((0, unit, False) for unit in (2, 6, 3, 7, 4, 8, 5, 9, 0, 1))
    + ((1, 0, False), (1, 1, False))
    + tuple((1, unit, False) for unit in (6, 7, 8, 9, 2, 3, 4, 5))
)
SOON = 12
FORWARD_HOOKS = SLABS + PAIRS + 1
SCATTER_RATE, SCATTER_AHEAD, SCATTER_GAP = 2.0, 4, 3
SCATTER_ORDER = ((1, 0), (1, 1)) + tuple((0, unit) for unit in (2, 6, 3, 7, 4, 8, 5, 9, 0, 1))
TURN_RATE, TURN_GAP, TURN_HOOKS = 1.3, 5, PAIRS + 3
HOOKS = PAIRS + 2


def near_self_kernel(
    source_counts, target_counts, attention_in, attention_out, cross, expand, contract, gains, rows,
    square_out, tall_out, cross_out, target_rest, target_tall, own_square, every_gain, away,
    triple, shares, inverse, result, first,
    end, mid, source_normed, active, change, pair, cross_normed, question, cross_shares, cross_inverse, cross_result,
    blocks, tiles, streams, firsts, landing, bias, own, source_square, source_tall, target_cross, share_rows,
    share_done, fetched, block_sent, block_done, block_out, tile_sent, tile_done,
    spread_sent, spread_done, spread_kept, away_sent, away_done, copied,
):
    place = Place()
    layer, depth, side, core = place.layer, place.depth, place.side, place.core
    step, total = pl.program_id(0), 2 * away.shape[0]
    count = away.shape[0]
    copies = Copies()
    share_row = share_rows.at[step % 2]

    def kept_share(target):
        return pltpu.make_async_copy(share_row, target, share_done.at[step % 2])

    kept = [
        ref.at[0]
        for ref in (end, mid, source_normed, active, change, pair, cross_normed, question, cross_inverse, cross_result)
    ]
    kept.insert(8, share_row)
    selfs = [attention_in.at[:, columns(j)] for j in range(3)] + [attention_out]
    sources = [cross.at[:, columns(j)] for j in range(2)] + [expand.at[:, columns(j)] for j in range(SLABS)]
    sources += [contract.at[columns(j, UNIT), :] for j in range(SLABS)]

    def spot(owner, unit, *index):
        if owner == 0:
            if unit < BLOCKS:
                return source_square.at[(unit,) + index]
            return source_tall.at[index + (unit - BLOCKS,)]
        if unit < EXPAND:
            return target_cross.at[(unit,) + index]
        if unit < BLOCKS:
            return target_rest.at[(unit - EXPAND,) + index]
        return target_tall.at[index + (unit - BLOCKS,)]

    units = [
        (owner, late, partial(own.at.__getitem__, unit), partial(spot, owner, unit))
        for owner, unit, late in GATHER_ORDER
    ]
    spread = Spread(place, copies, units, spread_sent, spread_done, spread_kept)

    def away_parts(slot):
        return firsts.at[slot], landing.at[slot], away_sent.at[slot], away_done.at[slot], place.across_layer()

    def block_parts(unit, stage):
        if stage == 0:
            block, target = blocks.at[unit, :, :, core], place.sibling()
        elif stage < DEPTHS:
            block, target = blocks.at[unit, depth, side, core], place.along_depth(stage)
        else:
            block, target = blocks.at[unit, :, side, core], place.across_side()
        return block, block, block_sent.at[unit, stage], block_done.at[unit, stage], target

    def tile_parts(stage):
        if stage == 0:
            block, target = tiles.at[layer], place.across_layer()
        elif stage < DEPTHS:
            block, target = tiles.at[layer, depth, side, core], place.along_depth(stage)
        elif stage == DEPTHS:
            block, target = tiles.at[layer, :, side, core], place.across_side()
        else:
            block, target = tiles.at[layer, :, :, core], place.sibling()
        return block, block, tile_sent.at[stage], tile_done.at[stage], target

    for stage in range(DEPTHS + 2):
        copies.define(("tile", stage), partial(tile_parts, stage))
    for unit in range(SELFS):
        for stage in range(DEPTHS + 1):
            copies.define(("block", unit, stage), partial(block_parts, unit, stage))
    for slot in range(count):
        copies.define(("away", slot), partial(away_parts, slot))

    def lay_gains(which):
        for row in range(DEPTHS):
            value = tiles[which, row, 0, 0].astype(FULL)
            for other in ((0, 1), (1, 0), (1, 1)):
                value = value + tiles[(which, row) + other].astype(FULL)
            every_gain[which, :, columns(row, 128)] = value[:8]

    def fetch(slot):
        return pltpu.make_async_copy(
            rows.at[row_of(layer, slot, count)], streams.at[slot % 2], fetched.at[slot % 2]
        )

    @pl.when(step == 0)
    def _():
        fetch(step).start()
        for unit in range(SELFS):
            blocks[unit, depth, side, core] = selfs[unit][...].astype(LOW)
        for unit in range(UNITS):
            own[unit] = sources[unit][...].astype(LOW)
        tiles[layer, depth, side, core] = gains[...]
        place.greet()
        across = range(1, DEPTHS)
        early = iter(spread.steps(GATHER_AHEAD, GATHER_GAP)[:GATHER_EARLY])
        copies.start(*[("tile", stage) for stage in across])
        for unit in range(SELFS):
            copies.start(*[("block", unit, stage) for stage in across])
        spread.announce()
        for number in range(GATHER_AHEAD):
            spread.begin(number)
        copies.arrived(*[("tile", stage) for stage in across])
        copies.start(("tile", DEPTHS))
        for number in range(GATHER_AHEAD):
            spread.relay(number)
        for unit in range(SELFS):
            copies.arrived(*[("block", unit, stage) for stage in across])
            copies.start(("block", unit, DEPTHS))
        copies.arrived(("tile", DEPTHS))
        copies.start(("tile", DEPTHS + 1))
        for unit in range(SELFS):
            for _ in range(GATHER_EARLY // SELFS):
                next(early)()
            copies.arrived(("block", unit, DEPTHS))
            copies.start(("block", unit, 0))
        copies.arrived(("tile", DEPTHS + 1))
        copies.start(("tile", 0))
        lay_gains(layer)
        copies.arrived(*[("block", unit, 0) for unit in range(OUT)])

    def last_block():
        copies.arrived(("block", OUT, 0))
        pltpu.make_async_copy(blocks, own_square, block_out).start()

    plan = Plan(GATHER_RATE, HOOKS)
    late = plan.fill([last_block] + spread.steps(GATHER_AHEAD, GATHER_GAP)[GATHER_EARLY:], total)
    forward_plan = Plan(FORWARD_RATE, FORWARD_HOOKS)
    late = forward_plan.fill(late, count)

    @pl.when(step + 1 < total)
    def _():
        fetch(step + 1).start()

    @pl.when(step >= 2)
    def _():
        kept_share(shares.at[0]).wait()

    @pl.when(step < total)
    def _():
        row = row_of(layer, step, count)
        causal = layer == 1
        both = [jnp.where(causal, *pair_of) for pair_of in zip(*counts_of(target_counts, source_counts, row))]
        fill_bias(bias, *segments(both), causal)
        fetch(step).wait()
        stream = self_forward(
            streams[step % 2].astype(FULL), every_gain[layer, 0:1, :], lambda unit: blocks[unit].reshape(D, D), bias,
            triple.at[0], share_row, inverse.at[0], result.at[0], partial(plan.hook, step),
        )
        kept_share(shares.at[step]).start()
        stream = stream.astype(LOW)
        first[0] = stream
        firsts[step] = stream
        for slot in range(count):

            @pl.when(step == slot)
            def _(slot=slot):
                copies.start(("away", slot))

        plan.hook(step)

    outward = [
        pltpu.make_async_copy(source, target, copied.at[index])
        for index, (source, target) in enumerate(
            ((source_square, square_out), (source_tall, tall_out), (target_cross, cross_out), (landing, away))
        )
    ]

    @pl.when(step == total)
    def _():
        copies.arrived(("tile", 0))
        lay_gains(1 - layer)
        for number in range(SOON):
            spread.end(number)
        copies.arrived(*[("away", slot) for slot in range(count)])
        for copy in outward:
            copy.start()

    @pl.when(step >= total)
    def _():
        index = step - total
        source_pieces, target_pieces = counts_of(source_counts, target_counts, layer * count + index)
        forward(
            layer, firsts[step - count], landing[index], segments(source_pieces), segments(target_pieces), every_gain,
            lambda slab: source_square[EXPAND + slab].reshape(D, D), lambda slab: source_tall[slab].reshape(D, D),
            lambda part: source_square[CROSS + part].reshape(D, D), lambda part: target_cross[part].reshape(D, D),
            bias, kept, partial(forward_plan.hook, index),
        )
        kept_share(cross_shares.at[index]).start()

    @pl.when(step == total + count - 1)
    def _():
        for thunk in late:
            thunk()
        for number in range(SOON, len(units)):
            spread.end(number)
        copies.finish(*[("away", slot) for slot in range(count)])
        copies.finish(*[("tile", stage) for stage in range(DEPTHS + 2)])
        copies.finish(*[("block", unit, stage) for unit in range(SELFS) for stage in range(DEPTHS + 1)])
        spread.finish()
        pltpu.make_async_copy(blocks, own_square, block_out).wait()
        for copy in outward:
            copy.wait()
        for number in range(2):
            pltpu.make_async_copy(share_rows.at[number], cross_shares.at[number], share_done.at[number]).wait()


def kept_shapes():
    return [
        ((ROW, 3 * D), LOW), ((HEADS, ROW, ROW), LOW), ((ROW, 2 * HD), FULL), ((ROW, D), LOW), ((ROW, D), LOW)
    ]


def near_self(source_counts, target_counts, weights, gains, rows):
    total = rows.shape[0]
    tile = jnp.tile(gains.astype(LOW), (1, 4))
    lane_part = lax.broadcasted_iota(jnp.int32, tile.shape, 1) // UNIT
    tile = jnp.where(lane_part == lax.axis_index("dp") % 4, tile, jnp.zeros_like(tile))
    tile = jnp.pad(tile, ((0, 16 - tile.shape[0]), (0, 0)))
    dma = pltpu.SemaphoreType.DMA
    kept, ahead = kept_shapes(), forward_shapes()
    count = total // 2
    square_shape = (BLOCKS, DEPTHS, SIDES, CORES, UNIT, D)
    tall_shape = (DEPTHS, SIDES, CORES, SLABS, UNIT, D)
    cross_shape, rest_shape = (2,) + square_shape[1:], (SLABS,) + square_shape[1:]
    own_shape = (SELFS,) + square_shape[1:]
    outs = [
        shape_of(shape, LOW) for shape in (square_shape, tall_shape, cross_shape, rest_shape, tall_shape, own_shape)
    ] + [shape_of((2, 8, D), FULL), shape_of((count, ROW, D), LOW)]
    low = lambda *shape: pltpu.VMEM(shape, LOW)

    def later(*shape):
        return pl.BlockSpec((1,) + shape, lambda step: (jnp.maximum(step - total, 0),) + (0,) * len(shape))

    def spec(shape, make):
        return ANYWHERE if shape == (HEADS, ROW, ROW) else make(*shape)

    results = pl.pallas_call(
        near_self_kernel,
        grid=(total + count,),
        in_specs=[SCALARS, SCALARS] + [constant(*value.shape) for value in weights] + [constant(16, 128), ANYWHERE],
        out_specs=[ANYWHERE] * 6
        + [pl.BlockSpec((2, 8, D), lambda row: (0, 0, 0)), ANYWHERE]
        + [spec(shape, partial(per_row, last=total - 1)) for shape, _ in kept]
        + [spec(shape, later) for shape, _ in ahead],
        out_shape=outs
        + [shape_of((total,) + shape, kind) for shape, kind in kept]
        + [shape_of((count,) + shape, kind) for shape, kind in ahead],
        scratch_shapes=[
            low(*own_shape), low(2, DEPTHS, SIDES, CORES, 16, 128), low(2, ROW, D), low(total, ROW, D),
            low(count, ROW, D), low(ROW, ROW), low(UNITS, UNIT, D), low(*square_shape), low(*tall_shape),
            low(*cross_shape), low(2, HEADS, ROW, ROW),
            dma((2,)), dma((2,)), dma((SELFS, 5)), dma((SELFS, 5)), dma, dma((6,)), dma((6,)),
            dma((len(GATHER_ORDER), 6)), dma((len(GATHER_ORDER), 6)), dma((len(GATHER_ORDER),)),
            dma((count,)), dma((count,)), dma((4,)),
        ],
        compiler_params=pltpu.CompilerParams(
            vmem_limit_bytes=VMEM_LIMIT, collective_id=0, has_side_effects=True
        ),
        name="self_forward",
    )(source_counts, target_counts, *weights, tile, rows)
    weights, (own_square, every_gain, away), results = results[:5], results[5:8], results[8:]
    weights = weights[0].reshape(BLOCKS, D, D), weights[1].reshape(FF, D), weights[2].reshape(2, D, D), *weights[3:]
    return weights, own_square, every_gain, away, results[: len(kept)], results[len(kept) :]


def middle_kernel(
    near,
    first, away, cotangent, source_square, source_tall, target_cross, rest, rest_tall, gains,
    kept_end, kept_mid, kept_normed, kept_active, kept_change, kept_pair, kept_cross, kept_question, kept_shares,
    kept_inverse, kept_result,
    section_output, sent_output, kept_delta, sent_delta, square_out, tall_out, gain_out, expand_out, contract_out,
    target_expand, target_contract, shares, inverse, cross_result, source_end, target_mid, value, sending, keeping,
    source_normed, active, memory_low, cross_normed, feed_normed,
    source_change, source_low, delta_pair, delta_question, cross_low, target_change, target_low,
    loaded, stored, kept, ready, output_sent, output_done, delta_sent, delta_done, fetched,
    turn_core, turn_side, turn_depth, turn_layer, turn_sent, turn_done,
):
    place = Place()
    layer = place.layer
    count = away.shape[0]
    copies = Copies()

    def source_expand(slab):
        return source_square[EXPAND + slab]

    def source_contract(slab):
        return source_tall[columns(slab), :]

    if near:

        def spot(unit, *index):
            if unit < SLABS:
                return target_expand.at[(unit,) + index]
            return target_contract.at[index + (unit - SLABS,)]

        def turn_unit(unit):
            def target():
                if unit < SLABS:
                    return expand_out.at[:, columns(unit)]
                return contract_out.at[columns(unit - SLABS, UNIT), :]

            return (
                1,
                lambda: spot(unit, slice(None), slice(None), 1 - place.core),
                lambda *index: spot(unit, *index, place.core),
                None,
                target,
            )

        collect = Collect(
            place, copies, [turn_unit(unit) for unit in range(2 * SLABS)],
            (turn_core, turn_side, turn_depth, turn_layer), turn_sent, turn_done,
        )

        def expand_of(slab):
            return target_expand[slab].reshape(D, D)

        def contract_of(slab):
            return target_contract[slab].reshape(D, D)

    else:

        def expand_of(slab):
            return target_expand[slab]

        def contract_of(slab):
            return target_contract[columns(slab), :]

    whole_rest = [
        pltpu.make_async_copy(rest, target_expand, fetched.at[0]),
        pltpu.make_async_copy(rest_tall, target_contract, fetched.at[1]),
    ]

    def rows_of(row):
        return pl.ds(pl.multiple_of(row * ROW, ROW), ROW)

    def load(row):
        return pltpu.make_async_copy(
            cotangent.at[layer * count + row], target_low.at[columns(row, ROW), :], loaded.at[row]
        )

    def store(row):
        return pltpu.make_async_copy(value, section_output.at[row], stored)

    def keep(row):
        return pltpu.make_async_copy(keeping.at[row], kept_delta.at[row], kept.at[row])

    class Parcels:
        def __init__(self, name, target, sent, done):
            self.name, self.target, self.sent, self.done = name, target, sent, done
            for row in range(count):
                copies.define((name, row), partial(self.parts, row))

        def parts(self, row):
            return sending.at[row], self.target.at[row], self.sent.at[row], self.done.at[row], place.across_layer()

        def local(self, row):
            return pltpu.make_async_copy(sending.at[row], self.target.at[row], self.sent.at[row])

        def put(self, row, block):
            for static in range(count):

                @pl.when(row == static)
                def _(static=static):
                    sending[static] = block
                    if near:
                        copies.start((self.name, static))
                    else:
                        self.local(static).start()

        def left(self, row):
            for static in range(count):

                @pl.when(row == static)
                def _(static=static):
                    if near:
                        copies.finish((self.name, static))
                    else:
                        self.local(static).wait()

    outputs = Parcels("output", sent_output, output_sent, output_done)
    deltas = Parcels("delta", sent_delta, delta_sent, delta_done)

    def streams(row):
        own, other = first[row].astype(FULL), away[row].astype(FULL)
        return jnp.where(layer == 0, own, other), jnp.where(layer == 0, other, own)

    def publish(row, owner, block):
        @pl.when(layer == owner)
        def _():
            @pl.when(jnp.asarray(row) > 0)
            def _():
                store(row - 1).wait()

            value[...] = block
            store(row).start()

        @pl.when(layer != owner)
        def _():
            outputs.put(row, block.astype(LOW))

    for row in range(count):
        load(row).start()
    gain_out[...] = jnp.zeros(gain_out.shape, FULL)
    if near:
        place.greet()
    takes = [
        pltpu.make_async_copy(source, target, fetched.at[2 + index])
        for index, (source, target) in enumerate(
            (
                (kept_end, source_end), (kept_mid, target_mid), (kept_normed, source_normed), (kept_cross, cross_normed),
                (kept_result, cross_result), (kept_pair, delta_pair), (kept_question, delta_question),
                (kept_inverse, inverse), (kept_shares.at[count - 1], shares), (kept_change, source_change),
            )
        )
    ]
    take_active = pltpu.make_async_copy(kept_active, active, fetched.at[12])
    for copy in takes[:2] + whole_rest + takes[2:]:
        copy.start()

    def cross_parts(row):
        at = rows_of(row)
        return cross_refs(delta_question.at[at, :], delta_pair.at[at, :])

    def take_shares(row):
        return pltpu.make_async_copy(kept_shares.at[row], shares, fetched.at[13])

    takes[0].wait()
    for row in range(count):
        memory = normalize(source_end[row])[0] * gains[0, 2:3, :]
        memory_low[columns(row, ROW), :] = memory.astype(LOW)
        publish(row, 0, memory)
    for copy in takes[1:2] + whole_rest:
        copy.wait()

    @pl.when(layer == 0)
    def _():
        store(count - 1).wait()

    def turn(row, carry):
        at = rows_of(row)
        stream = target_mid[row]
        normed = (normalize(stream)[0] * gains[1, 2:3, :]).astype(LOW)
        feed_normed[at, :] = normed
        output = feed(
            normed, stream, expand_of, contract_of, active.at[at, :], target_change.at[at, :], no_hook
        )
        publish(row, 1, output)
        for static in range(count):

            @pl.when(row == static)
            def _(static=static):
                load(static).wait()

        delta, delta_gain = feed_back(
            target_low[at, :].astype(FULL), stream, gains[1, 2:3, :], expand_of, contract_of, target_change.at[at, :]
        )
        gain_out[1, 2:3, :] += delta_gain
        target_mid[row] = delta
        return carry

    lax.fori_loop(0, count, turn, 0)

    emitted, late = [], []

    def emit(block, holder, target):
        holder[...] = block.astype(LOW)
        copy = pltpu.make_async_copy(holder, target, ready.at[len(emitted)])
        copy.start()
        emitted.append(copy)
        if late:
            late.pop(0)()

    def feed_grads(which, normed, change, low):
        turned = normed[...].T
        for slab in range(SLABS):
            grown = multiply(turned, change[:, columns(slab)])
            shrunk = multiply(active[:, columns(slab)], low[...], TN)
            emit(grown, change.at[pl.ds(0, D), columns(slab)], square_out.at[which, EXPAND + slab])
            emit(shrunk, change.at[pl.ds(D, D), columns(slab)], tall_out.at[which, columns(slab), :])

    if near:
        turned = feed_normed[...].T
        for slab in range(SLABS):
            grown = multiply(turned, target_change[:, columns(slab)])
            target_expand[slab] = grown.astype(LOW).reshape(DEPTHS, SIDES, CORES, UNIT, D)
            collect.begin(slab)
            shrunk = multiply(active[:, columns(slab)], target_low[...], TN)
            target_contract[slab] = shrunk.astype(LOW).reshape(SIDES, CORES, SLABS, UNIT, D)
        for slab in range(SLABS):
            collect.begin(SLABS + slab)
        plan = Plan(TURN_RATE, TURN_HOOKS)
        late = plan.fill(collect.steps(2 * SLABS, TURN_GAP), count)
    else:
        feed_grads(1, feed_normed, target_change, target_low)
    take_active.start()
    for copy in takes[2:]:
        copy.wait()

    def backward(number, carry):
        row = count - 1 - number
        at = rows_of(row)
        hook = partial(plan.hook, number) if near else no_hook
        source_stream, target_stream = streams(row)

        @pl.when(number > 0)
        def _():
            take_shares(row).wait()

        delta = target_mid[row]
        low = delta.astype(LOW)
        cross_low[at, :] = low
        delta_result = multiply(low, target_cross[1], NT)

        def put(pair, query, keys, values):
            delta_question[at, columns(pair, 2 * HD)] = query
            delta_pair[at, columns(pair, 2 * HD)] = keys
            delta_pair[at, columns(PAIRS + pair, 2 * HD)] = values

        attend_back(
            *cross_parts(row), shares, inverse.at[row], cross_result.at[at, :], delta_result, put, hook
        )

        @pl.when(number < count - 1)
        def _():
            take_shares(row - 1).start()

        unit, scale = normalize(target_stream)
        delta_normed = multiply(delta_question[at, :], target_cross[0], NT)
        delta_stream, delta_gain = norm_back(unit, scale, gains[1, 1:2, :], delta_normed)
        gain_out[1, 1:2, :] += delta_gain
        target_delta = (delta + delta_stream).astype(LOW)
        hook()

        unit, scale = normalize(source_end[row])
        delta_memory = 0.0
        for part in range(2):
            delta_memory = delta_memory + multiply(delta_pair[at, columns(part)], source_square[CROSS + part], NT)
        delta, delta_gain = norm_back(unit, scale, gains[0, 2:3, :], delta_memory)
        gain_out[0, 2:3, :] += delta_gain
        source_low[at, :] = delta.astype(LOW)
        hook()
        delta, delta_gain = feed_back(
            delta, source_stream, gains[0, 1:2, :], source_expand, source_contract, source_change.at[at, :]
        )
        gain_out[0, 1:2, :] += delta_gain
        source_delta = delta.astype(LOW)
        keeping[row] = jnp.where(layer == 0, source_delta, target_delta)
        for static in range(count):

            @pl.when(row == static)
            def _(static=static):
                keep(static).start()

        outputs.left(row)
        deltas.put(row, jnp.where(layer == 0, target_delta, source_delta))
        hook()
        return carry

    lax.fori_loop(0, count, backward, 0)
    take_active.wait()
    feed_grads(0, source_normed, source_change, source_low)
    turned = memory_low[...].T
    for part in range(2):
        grown = multiply(turned, delta_pair[:, columns(part)])
        emit(grown, delta_pair.at[pl.ds(0, D), columns(part)], square_out.at[0, CROSS + part])
    for part, (left, right) in enumerate(((cross_normed, delta_question), (cross_result, cross_low))):
        emit(multiply(left[...], right[...], TN), right.at[pl.ds(0, D), :], square_out.at[1, CROSS + part])
    for thunk in late:
        thunk()
    for copy in emitted:
        copy.wait()

    @pl.when(layer == 1)
    def _():
        store(count - 1).wait()

    for row in range(count):
        keep(row).wait()
        deltas.left(row)
    if near:
        copies.arrived(*[(name, row) for name in ("output", "delta") for row in range(count)])
        collect.finish()


def middle(near, first, away, cotangent, weights, gains, ahead):
    count = away.shape[0]
    tokens = count * ROW
    dma = pltpu.SemaphoreType.DMA
    low = lambda *shape: pltpu.VMEM(shape, LOW)
    full = lambda *shape: pltpu.VMEM(shape, FULL)
    square, tall, cross, rest, rest_tall = weights
    if near:
        expand = low(SLABS, DEPTHS, SIDES, CORES, UNIT, D)
        contract = low(DEPTHS, SIDES, CORES, SLABS, UNIT, D)
    else:
        expand, contract = low(SLABS, D, D), low(FF, D)
    rows_apart = (0, 1, 8, 9)
    ahead = [
        value if place in rows_apart else value.reshape(tokens, value.shape[-1]) for place, value in enumerate(ahead)
    ]
    row_shape = shape_of((count, ROW, D), LOW)
    early_shapes = [(UNIT, FF), (SLABS * UNIT, D)]
    remote = dict(collective_id=2, has_side_effects=True) if near else {}
    outs = pl.pallas_call(
        partial(middle_kernel, near),
        grid=(1,),
        in_specs=[
            pl.BlockSpec((count, ROW, D), lambda step: (1, 0, 0), pipeline_mode=pl.Buffered(1)),
            constant(count, ROW, D), ANYWHERE, constant(BLOCKS, D, D), constant(FF, D), constant(2, D, D),
            ANYWHERE, ANYWHERE, constant(2, 8, D),
        ]
        + [ANYWHERE] * len(ahead),
        out_specs=[ANYWHERE] * 6
        + [pl.BlockSpec((2, 8, D), lambda step: (0, 0, 0))]
        + [pl.BlockSpec(shape, lambda step: (0, 0)) for shape in early_shapes],
        out_shape=[shape_of((count, ROW, D), FULL), row_shape, row_shape, row_shape]
        + [shape_of((2, BLOCKS, D, D), LOW), shape_of((2, FF, D), LOW), shape_of((2, 8, D), FULL)]
        + [shape_of(shape, FULL) for shape in early_shapes],
        scratch_shapes=[
            expand, contract, low(HEADS, ROW, ROW), full(count, ROW, 2 * HD), low(tokens, D),
            full(count, ROW, D), full(count, ROW, D), full(ROW, D), low(count, ROW, D), low(count, ROW, D),
            low(tokens, D), low(tokens, FF), low(tokens, D), low(tokens, D), low(tokens, D),
            low(tokens, FF), low(tokens, D), low(tokens, 2 * D), low(tokens, D), low(tokens, D), low(tokens, FF),
            low(tokens, D),
            dma((count,)), dma, dma((count,)), dma((2 * UNITS,)),
            dma((count,)), dma((count,)), dma((count,)), dma((count,)), dma((14,)),
        ]
        + collect_scratch(2 * SLABS if near else 1),
        compiler_params=pltpu.CompilerParams(vmem_limit_bytes=VMEM_LIMIT, **remote),
        name="middle",
    )(first, away, cotangent, square, tall, cross, rest, rest_tall, gains, *ahead)
    return outs[:7], outs[7:]


def near_back_kernel(
    kept_delta, away_delta, rows, own_square, gains, triple, shares, inverse, result,
    square_sums, tall_sums, gain_sums, early_expand, early_contract,
    gradient, attention_in, attention_out, cross, expand, contract, gain_out,
    deltas, streams, value, delta_triple, sums, low_sums, own_gain, total,
    gain_total, gain_parts, gain_from_layer,
    delta_done, fetched, stored, loaded, gain_sent, gain_done,
    other_core, other_side, other_depth, other_layer, other_sent, other_done,
    own_core, own_side, own_depth, own_layer, own_sent, own_done,
):
    place = Place()
    layer, depth, core = place.layer, place.depth, place.core
    count = kept_delta.shape[0]
    step, steps_in_all = pl.program_id(0), 2 * count
    copies = Copies()

    def other_unit(number):
        which, unit = SCATTER_ORDER[number]

        def share(owner):
            if unit < BLOCKS:
                return square_sums.at[which, unit, :, :, owner]
            return tall_sums.at[which, :, :, owner, unit - BLOCKS]

        def target():
            if unit < EXPAND:
                return cross.at[:, columns(unit - CROSS)]
            if unit < BLOCKS:
                return expand.at[:, columns(unit - EXPAND)]
            return contract.at[columns(unit - BLOCKS, UNIT), :]

        return (
            which,
            lambda: share(1 - core),
            lambda *index: total.at[(number,) + index],
            lambda: pltpu.make_async_copy(share(core), total.at[number], loaded.at[number]),
            target,
        )

    def own_unit(unit):
        return (
            None,
            lambda: low_sums.at[unit, :, :, 1 - core],
            lambda *index: low_sums.at[(unit,) + index + (core,)],
            None,
            lambda: attention_in.at[:, columns(unit)] if unit < OUT else attention_out,
        )

    others = Collect(
        place, copies, [other_unit(number) for number in range(len(SCATTER_ORDER))],
        (other_core, other_side, other_depth, other_layer), other_sent, other_done,
    )
    selfs = Collect(
        place, copies, [own_unit(unit) for unit in range(SELFS)], (own_core, own_side, own_depth, own_layer),
        own_sent, own_done,
    )

    def gain_parts_of(stage):
        if stage == 0:
            source, target, device = gain_sums.at[1 - layer], gain_from_layer, place.across_layer()
        elif stage == 1:
            source, target, device = gain_total.at[0], gain_parts.at[0], place.sibling()
        elif stage == 2:
            source, target, device = gain_total.at[1], gain_parts.at[1], place.across_side()
        else:
            away_by = stage - 2
            source, target = gain_total.at[2, place.other_depth(away_by)], gain_parts.at[2, away_by]
            device = place.along_depth(away_by)
        return source, target, gain_sent.at[stage], gain_done.at[stage], device

    gain_stages = range(3 + DEPTHS - 1)
    for stage in gain_stages:
        copies.define(("gain", stage), partial(gain_parts_of, stage))

    def fetch(index):
        slot = (index + count) % steps_in_all
        return pltpu.make_async_copy(
            rows.at[row_of(layer, slot, count)], streams.at[index % 2], fetched.at[index % 2]
        )

    def store(index):
        slot = (index + count) % steps_in_all
        return pltpu.make_async_copy(
            value.at[index % 2], gradient.at[row_of(layer, slot, count)], stored.at[index % 2]
        )

    takes = [
        pltpu.make_async_copy(source, deltas.at[pl.ds(count * half, count)], delta_done.at[half])
        for half, source in enumerate((kept_delta, away_delta))
    ]

    @pl.when(step == 0)
    def _():
        for take in takes:
            take.start()
        fetch(step).start()
        sums[...] = jnp.zeros(sums.shape, FULL)
        own_gain[...] = jnp.zeros(own_gain.shape, FULL)
        place.greet()
        for number in range(SCATTER_AHEAD):
            others.begin(number)
        copies.start(("gain", 0))

        @pl.when(layer == 1)
        def _():
            expand[...] = early_expand[...]
            contract[...] = early_contract[...]

        for take in takes:
            take.wait()

    plan = Plan(SCATTER_RATE, HOOKS)
    late = plan.fill(others.steps(SCATTER_AHEAD, SCATTER_GAP), steps_in_all)

    def ready(unit):
        low_sums[unit] = sums[unit].astype(LOW).reshape(DEPTHS, SIDES, CORES, UNIT, D)
        selfs.begin(unit)

    @pl.when(step + 1 < steps_in_all)
    def _():
        fetch(step + 1).start()

    fetch(step).wait()
    delta, delta_gain = self_back(
        deltas[step], streams[step % 2].astype(FULL), gains[layer, 0:1, :],
        lambda unit: own_square[unit].reshape(D, D),
        triple.at[0], shares.at[0], inverse.at[0], result.at[0], delta_triple, sums, partial(plan.hook, step),
    )
    own_gain[0:1, :] += delta_gain

    @pl.when(step >= 2)
    def _():
        store(step).wait()

    value[step % 2] = delta.astype(LOW)
    store(step).start()
    plan.hook(step)

    @pl.when(step == steps_in_all - 1)
    def _():
        def more():
            if late:
                late.pop(0)()

        for unit in range(SELFS):
            ready(unit)
        copies.arrived(("gain", 0))
        whole = gain_sums[layer] + gain_from_layer[...] + own_gain[...]
        for row in range(DEPTHS):
            gain_total[0, row] = whole[:, 128 * row : 128 * (row + 1)]
        copies.start(("gain", 1))
        more()
        for unit in range(SELFS):
            selfs.chip(unit)
        copies.arrived(("gain", 1))
        gain_total[1] = gain_total[0] + gain_parts[0]
        copies.start(("gain", 2))
        for unit in range(SELFS):
            more()
            selfs.sides(unit)
        copies.arrived(("gain", 2))
        gain_total[2] = gain_total[1] + gain_parts[1]
        copies.start(*[("gain", 2 + away_by) for away_by in range(1, DEPTHS)])
        for unit in range(SELFS):
            more()
            selfs.depths(unit)
        while late:
            more()
        whole = gain_total[2, depth]
        for away_by in range(1, DEPTHS):
            copies.arrived(("gain", 2 + away_by))
            whole = whole + gain_parts[2, away_by]
        gain_out[...] = whole
        store(step - 1).wait()
        store(step).wait()
        copies.finish(*[("gain", stage) for stage in gain_stages])
        others.finish()
        selfs.finish()


def near_back(kept_delta, away_delta, rows, own_square, gains, kept, square_sums, tall_sums, gain_sums, early):
    count, total = kept_delta.shape[0], rows.shape[0]
    dma = pltpu.SemaphoreType.DMA
    vmem = pl.BlockSpec(memory_space=pltpu.VMEM)
    shapes = kept_shapes()[:4]

    def rotated(*shape):
        return pl.BlockSpec((1,) + shape, lambda step: ((step + count) % total,) + (0,) * len(shape))

    units = len(SCATTER_ORDER)
    weight_shapes = [(UNIT, 3 * D), (UNIT, D), (UNIT, 2 * D), (UNIT, FF), (SLABS * UNIT, D), (8, 128)]
    low = lambda *shape: pltpu.VMEM(shape, LOW)
    full = lambda *shape: pltpu.VMEM(shape, FULL)
    gradient, *weights, gain = pl.pallas_call(
        near_back_kernel,
        grid=(total,),
        in_specs=[ANYWHERE, ANYWHERE, ANYWHERE, constant(SELFS, DEPTHS, SIDES, CORES, UNIT, D), constant(2, 8, D)]
        + [rotated(*shape) for shape, _ in shapes]
        + [ANYWHERE, ANYWHERE, constant(2, 8, D), constant(UNIT, FF), constant(SLABS * UNIT, D)],
        out_specs=[ANYWHERE] + [pl.BlockSpec(shape, lambda step: (0, 0)) for shape in weight_shapes],
        out_shape=[shape_of((total, ROW, D), LOW)] + [shape_of(shape, FULL) for shape in weight_shapes],
        scratch_shapes=[
            low(total, ROW, D), low(2, ROW, D), low(2, ROW, D), low(ROW, 3 * D), full(SELFS, D, D),
            low(SELFS, DEPTHS, SIDES, CORES, UNIT, D), full(8, D), low(units, DEPTHS, SIDES, UNIT, D),
            full(3, DEPTHS, 8, 128), full(3, DEPTHS, 8, 128), full(8, D),
            dma((2,)), dma((2,)), dma((2,)), dma((units,)), dma((6,)), dma((6,)),
        ]
        + collect_scratch(units)
        + collect_scratch(SELFS, False),
        compiler_params=pltpu.CompilerParams(
            vmem_limit_bytes=VMEM_LIMIT, collective_id=1, has_side_effects=True
        ),
        name="self_back",
    )(
        kept_delta, away_delta, rows, own_square, gains, *kept[:4],
        square_sums.reshape(2, BLOCKS, DEPTHS, SIDES, CORES, UNIT, D),
        tall_sums.reshape(2, DEPTHS, SIDES, CORES, SLABS, UNIT, D), gain_sums, *early,
    )
    start = lax.axis_index("dp") % 4 * UNIT
    return gradient, *weights, lax.dynamic_slice_in_dim(gain[:3], start, UNIT, axis=1)


def settle_kernel(mine, away, low_gradient, *refs):
    step, count = pl.program_id(0), pl.num_programs(0) // 2
    sums = len(refs) // 2 - 1
    whole, gradient = refs[sums], refs[sums + 1]
    whole[...] = jnp.where(step // count == lax.axis_index("pipe"), mine[...], away[...].astype(FULL))
    gradient[...] = low_gradient[...].astype(FULL)

    @pl.when(step == 0)
    def _():
        for source, target in zip(refs[:sums], refs[sums + 2 :]):
            target[...] = source[...]


def settle(mine, away, gradient, sums):
    total, count = gradient.shape[0], away.shape[0]

    def row(step):
        return (step, 0, 0)

    def row_of_half(step):
        return (step % count, 0, 0)

    wide = pl.BlockSpec((1, ROW, D), row)
    half = pl.BlockSpec((1, ROW, D), row_of_half)
    kept = [pl.BlockSpec(value.shape, lambda step: (0, 0)) for value in sums]
    whole = shape_of((total, ROW, D), FULL)
    return pl.pallas_call(
        settle_kernel,
        grid=(total,),
        in_specs=[half, half, wide] + kept,
        out_specs=[wide, wide] + kept,
        out_shape=[whole, whole] + [shape_of(value.shape, FULL) for value in sums],
        compiler_params=PARAMS,
        name="settle",
    )(mine, away, gradient, *sums)


def far_self_kernel(
    source_counts, target_counts, rows, square, gains, triple, shares, inverse, result, first, bias
):
    layer, step, count = lax.axis_index("pipe"), pl.program_id(0), pl.num_programs(0) // 2
    row = row_of(layer, step, count)
    causal = layer == 1
    both = [jnp.where(causal, target_counts[row, piece], source_counts[row, piece]) for piece in range(PACK)]
    fill_bias(bias, *segments(both), causal)
    first[0] = self_forward(
        rows[0].astype(FULL), gains[layer, 0:1, :], lambda unit: square[unit], bias,
        triple.at[0], shares.at[0], inverse.at[0], result.at[0], no_hook,
    ).astype(LOW)


def far_self(source_counts, target_counts, square, gains, rows):
    total = rows.shape[0]
    kept = kept_shapes()
    return pl.pallas_call(
        far_self_kernel,
        grid=(total,),
        in_specs=[SCALARS, SCALARS, per_row(ROW, D), constant(SELFS, D, D), constant(2, 8, D)],
        out_specs=[per_row(*shape) for shape, _ in kept],
        out_shape=[shape_of((total,) + shape, kind) for shape, kind in kept],
        scratch_shapes=[pltpu.VMEM((ROW, ROW), FULL)],
        compiler_params=PARAMS,
        name="self_forward",
    )(source_counts, target_counts, rows, square, gains)


def far_forward_kernel(
    source_counts, target_counts, first, away, square, tall, cross, gains, *refs
):
    layer, step, count = lax.axis_index("pipe"), pl.program_id(0), pl.num_programs(0)
    source_pieces, target_pieces = counts_of(source_counts, target_counts, layer * count + step)
    forward(
        layer, first[0], away[0], segments(source_pieces), segments(target_pieces), gains,
        lambda slab: square[EXPAND + slab], lambda slab: tall[columns(slab), :],
        lambda part: square[CROSS + part], lambda part: cross[part], refs[-1], [ref.at[0] for ref in refs[:-1]], no_hook,
    )


def far_forward(source_counts, target_counts, first, away, square, tall, cross, gains):
    count = away.shape[0]
    kept = forward_shapes()
    return pl.pallas_call(
        far_forward_kernel,
        grid=(count,),
        in_specs=[
            SCALARS, SCALARS, per_row(ROW, D, start=count), per_row(ROW, D), constant(BLOCKS, D, D), constant(FF, D),
            constant(2, D, D), constant(2, 8, D),
        ],
        out_specs=[per_row(*shape) for shape, _ in kept],
        out_shape=[shape_of((count,) + shape, kind) for shape, kind in kept],
        scratch_shapes=[pltpu.VMEM((ROW, ROW), LOW)],
        compiler_params=PARAMS,
        name="forward",
    )(source_counts, target_counts, first, away, square, tall, cross, gains)


def far_back_kernel(
    deltas, rows, square, gains, triple, shares, inverse, result, gradient, sums, gain_out, delta_triple
):
    layer, step = lax.axis_index("pipe"), pl.program_id(0)

    @pl.when(step == 0)
    def _():
        sums[...] = jnp.zeros(sums.shape, FULL)
        gain_out[...] = jnp.zeros(gain_out.shape, FULL)

    delta, delta_gain = self_back(
        deltas[0], rows[0].astype(FULL), gains[layer, 0:1, :], lambda unit: square[unit],
        triple.at[0], shares.at[0], inverse.at[0], result.at[0], delta_triple, sums, no_hook,
    )
    gain_out[0:1, :] += delta_gain
    gradient[0] = delta


def far_back(deltas, rows, square, gains, kept):
    total = rows.shape[0]
    return pl.pallas_call(
        far_back_kernel,
        grid=(total,),
        in_specs=[per_row(ROW, D), per_row(ROW, D), constant(SELFS, D, D), constant(2, 8, D)]
        + [per_row(*shape) for shape, _ in kept_shapes()[:4]],
        out_specs=[per_row(ROW, D), constant(SELFS, D, D), constant(8, D)],
        out_shape=[shape_of((total, ROW, D), FULL), shape_of((SELFS, D, D), FULL), shape_of((8, D), FULL)],
        scratch_shapes=[pltpu.VMEM((ROW, 3 * D), LOW)],
        compiler_params=PARAMS,
        name="self_back",
    )(deltas, rows, square, gains, *kept[:4])


def spotsof(value):
    return [value[:, start : start + D] for start in range(0, value.shape[1], D)]


def gather_all(value, axes):
    return lax.all_gather(value, axes, axis=0, tiled=False)


def far_weights(weights, gains, shards):
    attention_in, attention_out, cross, expand, contract = (value.astype(LOW) for value in weights)
    both = ("pipe", "dp")
    own = jnp.stack(spotsof(attention_in) + [attention_out])
    own = jnp.swapaxes(gather_all(own, "dp"), 0, 1).reshape(SELFS, D, D)
    square = gather_all(jnp.stack(spotsof(cross) + spotsof(expand)), both)
    square = jnp.swapaxes(square.reshape(2, shards, BLOCKS, D // shards, D), 1, 2)
    tall = gather_all(contract, both)
    gains = gather_all(gains.astype(LOW), both).reshape(2, shards, 3, D // shards)
    gains = jnp.swapaxes(gains, 1, 2).reshape(2, 3, D).astype(FULL)
    return own, square.reshape(2, BLOCKS, D, D), tall.reshape(2, FF, D), jnp.pad(gains, ((0, 0), (0, 5), (0, 0)))


def scattered(value, axes):
    return lax.psum_scatter(value, axes, scatter_dimension=0, tiled=False).astype(FULL)


def far_sums(own, own_gain, square, tall, gains, section, shards):
    both = ("pipe", "dp")
    share = D // shards
    own = scattered(jnp.swapaxes(own.reshape(SELFS, shards, share, D), 0, 1), "dp")
    square = jnp.swapaxes(square.reshape(2, BLOCKS, shards, share, D), 1, 2)
    square = scattered(square.reshape(2 * shards, BLOCKS, share, D), both)
    tall = scattered(tall.reshape(2 * shards, FF // shards, D), both)
    gains = gains + jnp.where(jnp.arange(2)[:, None, None] == section, own_gain[None], 0.0)
    gains = jnp.swapaxes(gains[:, :3].reshape(2, 3, shards, share), 1, 2)
    gains = scattered(gains.reshape(2 * shards, 3, share), both)

    def joined(value, first, last):
        return jnp.concatenate([value[block] for block in range(first, last)], axis=1)

    return (
        joined(own, QKV, OUT), own[OUT], joined(square, CROSS, EXPAND), joined(square, EXPAND, BLOCKS), tall, gains
    )


def swap(value):
    return lax.ppermute(value, "pipe", [(0, 1), (1, 0)])


def local(
    section_input,
    attention_in,
    attention_out,
    cross_weights,
    expand,
    contract,
    norm_gains,
    source_lengths,
    target_lengths,
    cotangent,
):
    section = lax.axis_index("pipe")
    shards = lax.axis_size("dp")
    near = shards == DEPTHS * SIDES * CORES
    rows = section_input[0]
    count = rows.shape[0] // 2
    weights = tuple(value[0] for value in (attention_in, attention_out, cross_weights, expand, contract))
    if near:
        weights, own_square, gains, away, kept, ahead = near_self(
            source_lengths, target_lengths, weights, norm_gains[0], rows
        )
    else:
        turn = jnp.where(section == 0, count, 0)
        own_square, square, tall, gains = far_weights(weights, norm_gains[0], shards)
        weights = square[0], tall[0], square[1, CROSS:EXPAND], square[1, EXPAND:], tall[1]
        slots = jnp.roll(rows, turn, axis=0)
        kept = far_self(source_lengths, target_lengths, own_square, gains, slots)
        away = swap(kept[-1][:count])
        ahead = far_forward(source_lengths, target_lengths, kept[-1], away, *weights[:3], gains)
    (section_output, away_output, kept_delta, away_delta, *sums), early = middle(
        near, kept[-1], away, cotangent, weights, gains, ahead
    )
    if near:
        gradient, *weight_sums = near_back(
            kept_delta, away_delta, rows, own_square, gains, kept, *sums, early
        )
    else:
        away_output, away_delta = swap(away_output), swap(away_delta)
        deltas = jnp.concatenate([away_delta, kept_delta], axis=0)
        gradient, own_sums, own_gain = far_back(deltas, slots, own_square, gains, kept)
        gradient = jnp.roll(gradient, -turn, axis=0)
        weight_sums = far_sums(own_sums, own_gain, *sums, section, shards)
    results = settle(section_output, away_output, gradient, weight_sums)
    return tuple(value[None] for value in results)


def solution(mesh):
    in_specs = (
        P("pipe", "dp", None, None),
        P("pipe", "dp", None),
        P("pipe", "dp", None),
        P("pipe", "dp", None),
        P("pipe", "dp", None),
        P("pipe", "dp", None),
        P("pipe", None, "dp"),
        P("dp", None),
        P("dp", None),
        P("dp", None, None),
    )
    out_specs = (
        P("pipe", "dp", None, None),
        P("pipe", "dp", None, None),
        P("pipe", "dp", None),
        P("pipe", "dp", None),
        P("pipe", "dp", None),
        P("pipe", "dp", None),
        P("pipe", "dp", None),
        P("pipe", None, "dp"),
    )
    return jax.shard_map(local, mesh=mesh, in_specs=in_specs, out_specs=out_specs, check_vma=False)
```
